32 devices in a mesh: wide: 16 (over z, x, core), narrow: 2 (over y).
Axes of the slice: x: 2, y: 2, z: 4, core: 2. Of those that a mesh axis runs over, the one named last changes fastest.
Arguments:
- tokens: bfloat16 [16384, 768], P(('wide', 'narrow')), may hold values from -6 to 6
- w_qkv: bfloat16 [768, 2304], P('wide'), may hold values from -0.21875 to 0.21875
- w_out: bfloat16 [768, 768], P('wide'), may hold values from -0.625 to 0.625
- w_gate: bfloat16 [768, 3072], P('wide', 'narrow'), may hold values from -0.21875 to 0.21875
- w_value: bfloat16 [768, 3072], P('wide', 'narrow'), may hold values from -0.21875 to 0.21875
- w_down: bfloat16 [3072, 768], P('narrow', 'wide'), may hold values from -0.109375 to 0.109375
- norm_gains: bfloat16 [2, 768], P(None, 'wide'), may hold values from 0.5 to 1.5
- norm_biases: bfloat16 [2, 768], P(None, 'wide'), may hold values from -1.5 to 1.5
- long_count: int32 [16, 2], P('wide', 'narrow'), may hold values from 0 to 1, as said below
- cotangent: bfloat16 [16384, 768], P(('wide', 'narrow')), may hold values from -6 to 6
Outputs:
- layer_output: bfloat16 [16384, 768], P(('wide', 'narrow'))
- input_grad: float32 [16384, 768], P(('wide', 'narrow'))
- grad_qkv: float32 [768, 2304], P('wide')
- grad_out: float32 [768, 768], P('wide')
- grad_gate: float32 [768, 3072], P('wide', 'narrow')
- grad_value: float32 [768, 3072], P('wide', 'narrow')
- grad_down: float32 [3072, 768], P('narrow', 'wide')
- grad_gains: float32 [2, 768], P(None, 'wide')
- grad_biases: float32 [2, 768], P(None, 'wide')
The draws below stay inside these ranges and needn't reach their ends.
Inputs may be any that keep to these rules, and one draw needn't show every extreme that they name: long_count[w, n] sequences of 512 tokens open the 512 rows of device (w, n); the rest of its rows are sequences of 128 tokens. Every draw has a device with the most and a device with none.
All inputs are finite; a program needn't handle non-finite values.
Results may differ from the reference program's by a relative error of at most 0.02.
Values may be sent and summed in bfloat16 or wider, within the bound.
No kernel may reach another device: no remote copies, remote signals or barrier semaphores. Data moves between devices by JAX's collectives and lax.ppermute only.
A program may use at most 128 MiB of HBM per device.

```python
import jax
import jax.numpy as jnp
from jax import lax

D = 768
HEADS = 12
HEAD_DIM = 64
FF = 3072
LONG = 512
SHORT = 128
TOK_DEV = 512
TOKENS = 16384
N_WIDE = 16
N_NARROW = 2


def draw_long_count(key, part):
    most_long = TOK_DEV // LONG
    total_dev = N_WIDE * N_NARROW
    key_a = jax.random.fold_in(key, 11)
    key_b = jax.random.fold_in(key, 12)
    key_c = jax.random.fold_in(key, 13)
    drawn = jax.random.randint(key_a, (total_dev,), 0, most_long + 1)
    kept_mask = jax.random.randint(key_b, (total_dev,), 0, 2)
    counts = drawn * kept_mask
    chosen = jax.random.permutation(key_c, total_dev)
    counts = counts.at[chosen[0]].set(most_long).at[chosen[1]].set(0)
    return counts.reshape(N_WIDE, N_NARROW).astype(jnp.int32)


def levels(key, shape, shards, smallest, top_value):
    def one(dim, shards_of):
        steps = jax.random.uniform(jax.random.fold_in(jax.random.fold_in(key, 6), dim), (shards_of,), jnp.float32, smallest / len(shards), top_value / len(shards))
        return jnp.repeat(jnp.exp(steps), shape[dim] // shards_of).reshape((-1,) + (1,) * (len(shape) - dim - 1))

    loudness = one(*shards[0])
    for cut in shards[1:]:
        loudness = loudness * one(*cut)
    return loudness


def scatter_about(key, dims, scale, reach, split=(), kind=jnp.bfloat16):
    values = jax.random.normal(key, dims, jnp.float32) * scale
    if len(split) > 0:
        values = levels(key, dims, split, -0.22, 0.18) * values
    return jnp.clip(values, min=-reach, max=reach).astype(kind)


def setup_inputs(seed: int = 0) -> dict:
    splits = jax.random.split(jax.random.key(seed), 11)
    return {
        "tokens": scatter_about(splits[0], (TOKENS, D), 1.0, 6.0, ((0, 32),)),
        "w_qkv": scatter_about(splits[1], (D, 3 * D), D ** -0.5, 0.21875, ((0, 16),)),
        "w_out": scatter_about(splits[2], (D, D), (D // 8) ** -0.5, 0.625, ((0, 16),)),
        "w_gate": scatter_about(splits[3], (D, FF), D ** -0.5, 0.21875, ((0, 16), (1, 2))),
        "w_value": scatter_about(splits[4], (D, FF), D ** -0.5, 0.21875, ((0, 16), (1, 2))),
        "w_down": scatter_about(splits[5], (FF, D), FF ** -0.5, 0.109375, ((0, 2), (1, 16))),
        "norm_gains": jnp.clip(1.0 + 0.1 * jax.random.normal(splits[6], (2, D), jnp.float32), 0.5, 1.5).astype(jnp.bfloat16),
        "norm_biases": scatter_about(splits[7], (2, D), 0.3, 1.5, ((1, 16),)),
        "long_count": draw_long_count(jax.random.fold_in(splits[10], 71), 0),
        "cotangent": scatter_about(splits[9], (TOKENS, D), 1.0, 6.0, ((0, 32),)),
    }


@jax.custom_vjp
def low(v):
    return lax.optimization_barrier(v.astype(jnp.bfloat16)).astype(jnp.float32)

@jax.custom_vjp
def low_back(v):
    return v

def low_keep(v):
    return (low(v), None)

def low_pass(kept, grad):
    return (grad,)

def back_keep(v):
    return (v, None)

def back_low(kept, grad):
    return (low(grad),)
low.defvjp(low_keep, low_pass)
low_back.defvjp(back_keep, back_low)

def alibi_slopes(heads):
    power = 1 << heads.bit_length() - 1
    first = [2.0 ** (-8.0 * (index + 1) / power) for index in range(power)]
    second = [2.0 ** (-8.0 * (2 * index + 1) / (2 * power)) for index in range(heads - power)]
    return jnp.array(first + second, dtype=jnp.float32)

def matmul(left, right):
    return jnp.dot(left, right, precision=lax.Precision.HIGHEST, preferred_element_type=jnp.float32)

def round_both(values):
    return low_back(low(values))

def norm_rows(values, gain_row, bias_row):
    center = lax.optimization_barrier(jnp.mean(values, axis=-1, keepdims=True))
    shifted = values - center
    spread = lax.optimization_barrier(jnp.mean(shifted * shifted, axis=-1, keepdims=True))
    return shifted * lax.rsqrt(spread + 1e-05) * gain_row + bias_row

def layer(params, block_in, is_long):
    w_qkv, w_out, w_gate, w_value, w_down, gains, biases = params
    rows = block_in.shape[0]
    mixed = round_both(matmul(block_in, w_qkv))
    queries = mixed[:, :D].reshape(rows, HEADS, HEAD_DIM)
    key_rows = mixed[:, D:2 * D].reshape(rows, HEADS, HEAD_DIM)
    value_rows = mixed[:, 2 * D:].reshape(rows, HEADS, HEAD_DIM)
    position = jnp.arange(rows)
    segment = jnp.where(is_long, 0, position // SHORT)
    same_seq = segment[:, None] == segment[None, :]
    distance = jnp.abs(position[:, None] - position[None, :]).astype(jnp.float32)
    slopes = alibi_slopes(HEADS)
    scores = jnp.einsum('qhd,khd->hqk', queries, key_rows, precision=lax.Precision.HIGHEST) * HEAD_DIM ** (-0.5)
    scores = low_back(scores - slopes[:, None, None] * distance)
    scores = jnp.where(same_seq[None, :, :], scores, -1e+30)
    top = lax.optimization_barrier(jnp.max(scores, axis=-1, keepdims=True))
    expd = jnp.exp(scores - top)
    probs = expd / lax.optimization_barrier(jnp.sum(expd, axis=-1, keepdims=True))
    context = jnp.einsum('hqk,khd->qhd', low(probs), value_rows, precision=lax.Precision.HIGHEST).reshape(rows, D)
    context = round_both(context)
    branch = low_back(matmul(context, w_out))
    normed = norm_rows(block_in + branch, gains[0], biases[0])
    normed_low = low(normed)
    gate = low_back(matmul(normed_low, w_gate))
    value_up = low_back(matmul(normed_low, w_value))
    product = low(jax.nn.gelu(gate, approximate=False) * value_up)
    ffn_out = low_back(matmul(product, w_down))
    return norm_rows(normed + ffn_out, gains[1], biases[1])

def reference(tokens, w_qkv, w_out, w_gate, w_value, w_down, norm_gains, norm_biases, long_count, cotangent):
    params = tuple((array.astype(jnp.float32) for array in (w_qkv, w_out, w_gate, w_value, w_down, norm_gains, norm_biases)))
    per_device = TOK_DEV // LONG
    n_blocks = TOKENS // LONG
    counts = long_count.reshape(-1)
    block_index = jnp.arange(n_blocks)
    flags = block_index % per_device < counts[block_index // per_device]
    blocks_in = tokens.astype(jnp.float32).reshape(n_blocks, LONG, D)
    blocks_cot = cotangent.astype(jnp.float32).reshape(n_blocks, LONG, D)

    def step(totals, entry):
        block_in, block_cot, is_long = entry
        result, pull = jax.vjp(lambda weights, rows_in: layer(weights, rows_in, is_long), params, block_in)
        d_params, d_rows = pull(block_cot)
        return (tuple((total + grad for total, grad in zip(totals, d_params))), (result, d_rows))
    zeros = tuple((jnp.zeros_like(array) for array in params))
    totals, (outputs, d_inputs) = lax.scan(step, zeros, (blocks_in, blocks_cot, flags))
    return (outputs.reshape(TOKENS, D).astype(jnp.bfloat16), d_inputs.reshape(TOKENS, D), totals[0], totals[1], totals[2], totals[3], totals[4], totals[5], totals[6])
```

```python
import functools

import jax
import jax.numpy as jnp
import numpy as np
from jax import lax
from jax.experimental import pallas as pl
from jax.experimental.pallas import tpu as pltpu
from jax.sharding import PartitionSpec as P

D = 768
HEADS = 12
HEAD_DIM = 64
LONG = 512
SHORT = 128


def norm_rows(values, gain_row, bias_row):
    center = jnp.mean(values, axis=-1, keepdims=True)
    shifted = values - center
    spread = jnp.mean(shifted * shifted, axis=-1, keepdims=True)
    return shifted * lax.rsqrt(spread + 1e-05) * gain_row + bias_row


def gelu_product(gate_in, value_in):
    return jax.nn.gelu(gate_in, approximate=False) * value_in


def alibi_slopes(heads):
    power = 1 << heads.bit_length() - 1
    first = [2.0 ** (-8.0 * (index + 1) / power) for index in range(power)]
    second = [2.0 ** (-8.0 * (2 * index + 1) / (2 * power)) for index in range(heads - power)]
    return jnp.array(first + second, dtype=jnp.float32)


def alibi_bias(span, heads):
    position = jnp.arange(span)
    distance = jnp.abs(position[:, None] - position[None, :]).astype(jnp.float32)
    slopes = alibi_slopes(heads)
    return slopes[:, None, None] * distance


def block_scores(query_g, key_g, span):
    width = query_g.shape[-1]
    scores = jnp.einsum(
        "bqhd,bkhd->bhqk", query_g, key_g, preferred_element_type=jnp.float32
    ) * width ** (-0.5)
    return scores - alibi_bias(span, query_g.shape[2])


def attend(query_rows, key_rows, value_rows, span):
    rows, heads, width = query_rows.shape
    groups = rows // span
    shape_g = (groups, span, heads, width)
    query_g = query_rows.reshape(shape_g)
    key_g = key_rows.reshape(shape_g)
    value_g = value_rows.reshape(shape_g)
    scores = block_scores(query_g, key_g, span)
    top = jnp.max(scores, axis=-1, keepdims=True)
    expd = jnp.exp(scores - top)
    total = jnp.sum(expd, axis=-1, keepdims=True)
    probs_low = (expd / total).astype(jnp.bfloat16)
    context = jnp.einsum("bhqk,bkhd->bqhd", probs_low, value_g, preferred_element_type=jnp.float32)
    log_total = jnp.transpose((top + jnp.log(total))[..., 0], (0, 2, 1)).reshape(rows, heads)
    return (context.reshape(rows, heads * width), log_total)


def attend_back(query_rows, key_rows, value_rows, log_total, d_context, span):
    rows, heads, width = query_rows.shape
    groups = rows // span
    shape_g = (groups, span, heads, width)
    query_g = query_rows.reshape(shape_g)
    key_g = key_rows.reshape(shape_g)
    value_g = value_rows.reshape(shape_g)
    d_context_g = d_context.reshape(shape_g)
    lse_g = jnp.transpose(log_total.reshape(groups, span, heads), (0, 2, 1))
    scores = block_scores(query_g, key_g, span)
    probs = jnp.exp(scores - lse_g[..., None])
    probs_low = probs.astype(jnp.bfloat16)
    d_probs = jnp.einsum(
        "bqhd,bkhd->bhqk", d_context_g, value_g, preferred_element_type=jnp.float32
    )
    d_values = jnp.einsum(
        "bhqk,bqhd->bkhd", probs_low, d_context_g, preferred_element_type=jnp.float32
    )
    row_dot = jnp.sum(probs * d_probs, axis=-1, keepdims=True)
    d_scores = (probs * (d_probs - row_dot)).astype(jnp.bfloat16)
    scale = width ** (-0.5)
    d_queries = (
        jnp.einsum("bhqk,bkhd->bqhd", d_scores, key_g, preferred_element_type=jnp.float32) * scale
    )
    d_keys = (
        jnp.einsum("bhqk,bqhd->bkhd", d_scores, query_g, preferred_element_type=jnp.float32) * scale
    )
    return jnp.stack([d_queries, d_keys, d_values], axis=2).reshape(rows, 3, heads, width)


def contract_rows(left, right):
    return lax.dot_general(
        left, right, (((0,), (0,)), ((), ())), preferred_element_type=jnp.float32
    )


def contract_cols(left, right):
    return lax.dot_general(
        left, right, (((1,), (1,)), ((), ())), preferred_element_type=jnp.float32
    )


def general_shards(
    tokens, w_qkv, w_out, w_gate, w_value, w_down, norm_gains, norm_biases, long_count, cotangent
):
    gathered = (
        lax.all_gather(w_qkv, "wide", axis=0, tiled=True),
        lax.all_gather(w_out, "wide", axis=0, tiled=True),
        lax.all_gather(w_gate, "wide", axis=0, tiled=True),
        lax.all_gather(w_value, "wide", axis=0, tiled=True),
        lax.all_gather(w_down, "wide", axis=1, tiled=True),
        lax.all_gather(norm_gains, "wide", axis=1, tiled=True),
        lax.all_gather(norm_biases, "wide", axis=1, tiled=True),
    )
    full_qkv, full_out, wide_gate, wide_value, wide_down, gains_all, biases_all = gathered
    gains_f = gains_all.astype(jnp.float32)
    biases_f = biases_all.astype(jnp.float32)
    rows_dev = tokens.shape[0]
    n_blocks = rows_dev // LONG
    long_here = long_count[0, 0]
    tokens_f = tokens.astype(jnp.float32)
    mixed = jnp.dot(tokens, full_qkv, preferred_element_type=jnp.float32).astype(jnp.bfloat16)
    heads_view = mixed.reshape(n_blocks, LONG, 3, HEADS, HEAD_DIM)
    query_blk = heads_view[:, :, 0]
    key_blk = heads_view[:, :, 1]
    value_blk = heads_view[:, :, 2]
    block_ids = jnp.arange(n_blocks)

    def forward_block(entry):
        block_id, query_rows, key_rows, value_rows = entry
        return lax.cond(
            block_id < long_here,
            lambda operands: attend(operands[0], operands[1], operands[2], LONG),
            lambda operands: attend(operands[0], operands[1], operands[2], SHORT),
            (query_rows, key_rows, value_rows),
        )

    context_f, lse_rows = lax.map(forward_block, (block_ids, query_blk, key_blk, value_blk))
    context = context_f.reshape(rows_dev, D).astype(jnp.bfloat16)
    branch = jnp.dot(context, full_out, preferred_element_type=jnp.float32)
    hidden_in = tokens_f + branch
    normed = norm_rows(hidden_in, gains_f[0], biases_f[0])
    normed_low = normed.astype(jnp.bfloat16)
    all_rows = lax.all_gather(normed_low, "narrow", axis=0, tiled=True)
    gate = jnp.dot(all_rows, wide_gate, preferred_element_type=jnp.float32)
    value_up = jnp.dot(all_rows, wide_value, preferred_element_type=jnp.float32)
    product_f, pull_product = jax.vjp(gelu_product, gate, value_up)
    product = product_f.astype(jnp.bfloat16)
    ffn_out = lax.psum_scatter(
        jnp.dot(product, wide_down, preferred_element_type=jnp.float32),
        "narrow",
        scatter_dimension=0,
        tiled=True,
    )
    out_in = normed + ffn_out
    layer_out, pull_second = jax.vjp(norm_rows, out_in, gains_f[1], biases_f[1])
    d_out, d_gain_two, d_bias_two = pull_second(cotangent.astype(jnp.float32))
    d_ffn = d_out.astype(jnp.bfloat16)
    d_rows = lax.all_gather(d_ffn, "narrow", axis=0, tiled=True)
    grad_down = contract_rows(product, d_rows)
    d_product = contract_cols(d_rows, wide_down)
    d_gate, d_up = pull_product(d_product)
    d_gate_low = d_gate.astype(jnp.bfloat16)
    d_up_low = d_up.astype(jnp.bfloat16)
    grad_gate = contract_rows(all_rows, d_gate_low)
    grad_value = contract_rows(all_rows, d_up_low)
    d_normed = lax.psum_scatter(
        contract_cols(d_gate_low, wide_gate) + contract_cols(d_up_low, wide_value),
        "narrow",
        scatter_dimension=0,
        tiled=True,
    )
    d_normed_total = d_out + d_normed
    unused_out, pull_first = jax.vjp(norm_rows, hidden_in, gains_f[0], biases_f[0])
    d_hidden, d_gain_one, d_bias_one = pull_first(d_normed_total)
    d_branch = d_hidden.astype(jnp.bfloat16)
    grad_out = contract_rows(context, d_branch)
    d_context = contract_cols(d_branch, full_out).astype(jnp.bfloat16)
    d_context_blk = d_context.reshape(n_blocks, LONG, HEADS, HEAD_DIM)

    def backward_block(entry):
        block_id, query_rows, key_rows, value_rows, log_total, d_ctx = entry
        return lax.cond(
            block_id < long_here,
            lambda operands: attend_back(
                operands[0], operands[1], operands[2], operands[3], operands[4], LONG
            ),
            lambda operands: attend_back(
                operands[0], operands[1], operands[2], operands[3], operands[4], SHORT
            ),
            (query_rows, key_rows, value_rows, log_total, d_ctx),
        )

    d_mixed_f = lax.map(
        backward_block, (block_ids, query_blk, key_blk, value_blk, lse_rows, d_context_blk)
    )
    d_mixed = d_mixed_f.reshape(rows_dev, 3 * D).astype(jnp.bfloat16)
    grad_qkv = contract_rows(tokens, d_mixed)
    input_grad = d_hidden + contract_cols(d_mixed, full_qkv)
    grad_gains = jnp.stack([d_gain_one, d_gain_two])
    grad_biases = jnp.stack([d_bias_one, d_bias_two])
    pieces = (
        lax.psum_scatter(
            grad_qkv.astype(jnp.bfloat16), "wide", scatter_dimension=0, tiled=True
        ).astype(jnp.float32),
        lax.psum_scatter(
            grad_out.astype(jnp.bfloat16), "wide", scatter_dimension=0, tiled=True
        ).astype(jnp.float32),
        lax.psum_scatter(
            grad_gate.astype(jnp.bfloat16), "wide", scatter_dimension=0, tiled=True
        ).astype(jnp.float32),
        lax.psum_scatter(
            grad_value.astype(jnp.bfloat16), "wide", scatter_dimension=0, tiled=True
        ).astype(jnp.float32),
        lax.psum_scatter(
            grad_down.astype(jnp.bfloat16), "wide", scatter_dimension=1, tiled=True
        ).astype(jnp.float32),
        lax.psum_scatter(
            grad_gains.astype(jnp.bfloat16), "wide", scatter_dimension=1, tiled=True
        ).astype(jnp.float32),
        lax.psum_scatter(
            grad_biases.astype(jnp.bfloat16), "wide", scatter_dimension=1, tiled=True
        ).astype(jnp.float32),
    )
    qkv_piece, out_piece, gate_piece, value_piece, down_piece, gains_piece, biases_piece = pieces
    qkv_piece, out_piece, gains_piece, biases_piece = (
        lax.psum(qkv_piece.astype(jnp.bfloat16), "narrow").astype(jnp.float32),
        lax.psum(out_piece.astype(jnp.bfloat16), "narrow").astype(jnp.float32),
        lax.psum(gains_piece.astype(jnp.bfloat16), "narrow").astype(jnp.float32),
        lax.psum(biases_piece.astype(jnp.bfloat16), "narrow").astype(jnp.float32),
    )
    return (
        layer_out.astype(jnp.bfloat16),
        input_grad,
        qkv_piece,
        out_piece,
        gate_piece,
        value_piece,
        down_piece,
        gains_piece,
        biases_piece,
    )


AXES = ("wide", "narrow")
F32 = jnp.float32
BF16 = jnp.bfloat16
VMEM_LIMIT = 56 * 1024 * 1024
PAIR = 2 * HEAD_DIM


def dot(left, right):
    return jnp.dot(left, right, preferred_element_type=F32)


class Plane:
    def __init__(self, wide, narrow):
        self.size = {"z": wide // 4, "a": 2, "b": 2, "core": 2, "y": narrow}
        self.pairs = {}
        count = wide * narrow
        for dim, size in self.size.items():
            for step in range(1, size):
                self.pairs[dim, step] = [(i, self.partner(i, dim, step)) for i in range(count)]
        w = lax.axis_index("wide")
        self.z, self.x, self.core = w // 4, (w // 2) % 2, w % 2
        self.y = lax.axis_index("narrow")

    @staticmethod
    def partner(i, dim, step):
        z, x, c, y = i // 8, (i // 4) % 2, (i // 2) % 2, i % 2
        if dim == "z":
            z ^= step
        elif dim == "core":
            c ^= 1
        elif dim == "y" or (dim == "a") == (c == 1):
            y ^= 1
        else:
            x ^= 1
        return ((z * 2 + x) * 2 + c) * 2 + y

    def swap(self, value, dim, step=1):
        return lax.ppermute(value, AXES, self.pairs[dim, step])

    def gather(self, value, order):
        held = value[None]
        for place, dim in enumerate(order):
            parts = [held] + [self.swap(held, dim, k) for k in range(1, self.size[dim])]
            if place == len(order) - 1:
                return parts
            held = jnp.concatenate(parts, axis=0)

    def reduce(self, blocks, order):
        for dim in reversed(order):
            size = self.size[dim]
            blocks = blocks.reshape((size, -1) + blocks.shape[1:])
            got = [self.swap(blocks[k], dim, k) for k in range(1, size)]
            total = blocks[0].astype(F32)
            for part in got:
                total = total + part.astype(F32)
            blocks = total.astype(BF16)
        return total[0]

    def tables(self, order, numbered):
        sizes = [self.size[dim] for dim in order]
        number = np.arange(int(np.prod(sizes)))
        rest, digit = number, {}
        for dim, size in zip(order, sizes):
            digit[dim] = rest % size
            rest = rest // size
        first = self.core == 0
        a_here = jnp.where(first, self.x, self.y)
        b_here = jnp.where(first, self.y, self.x)
        z = digit["z"] ^ self.z
        a = digit["a"] ^ a_here
        b = digit["b"] ^ b_here
        x, y = jnp.where(first, a, b), jnp.where(first, b, a)
        forward = numbered(z, x, y).astype(jnp.int32)
        places = {(zz, xx, yy): int(numbered(zz, xx, yy)) for zz in range(self.size["z"]) for xx in range(2) for yy in range(2)}
        by_place = sorted(places, key=places.get)
        pz, px, py = (np.array(v) for v in zip(*by_place))
        rel = {"z": pz ^ self.z, "a": jnp.where(first, px, py) ^ a_here, "b": jnp.where(first, py, px) ^ b_here}
        back, scale = 0, 1
        for dim, size in zip(order, sizes):
            back = back + rel[dim] * scale
            scale *= size
        return forward, back.astype(jnp.int32)


def smem():
    return pl.BlockSpec(memory_space=pltpu.SMEM)


def whole(shape):
    zeros = (0,) * len(shape)
    return pl.BlockSpec(tuple(shape), lambda *_: zeros)


def kernel_call(body, grid, ins, outs, scratch=(), flops=0, name=None):
    size = sum(a.size * a.dtype.itemsize for a, _ in ins)
    size += sum(int(np.prod(s)) * np.dtype(d).itemsize for s, d, _ in outs)
    return pl.pallas_call(
        body,
        grid=grid,
        in_specs=[spec for _, spec in ins],
        out_specs=[spec for _, _, spec in outs],
        out_shape=[jax.ShapeDtypeStruct(s, d) for s, d, _ in outs],
        scratch_shapes=list(scratch),
        compiler_params=pltpu.CompilerParams(
            dimension_semantics=("arbitrary",) * len(grid), vmem_limit_bytes=VMEM_LIMIT
        ),
        cost_estimate=pl.CostEstimate(flops=flops, bytes_accessed=size, transcendentals=0),
        name=name,
    )(*[a for a, _ in ins])


ROWS = 256


def own_rows(steps, cols):
    return pl.BlockSpec((ROWS, cols), lambda i: (jnp.minimum(i, steps - 1), 0))


def partner_rows(steps, cols):
    return pl.BlockSpec((ROWS, cols), lambda i: (jnp.maximum(i - steps, 0), 0))


def pick_rows(i, steps, own_ref, partner_ref):
    return jnp.where(i < steps, own_ref[...], partner_ref[...])


def qkv_kernel(steps, groups, table, own, partner, first, second, mixed, weight, out_w, norms):
    i = pl.program_id(0)
    count, rows = first.shape[0], first.shape[1]
    part = out_w.shape[2] // 2
    cols = weight.shape[2]

    @pl.when(i == 0)
    def _():
        for k in range(2 * count):
            source = first if k < count else second
            place = table[k % (2 * count)]
            weight[place] = source[k % count, :, :cols]
            norms[place] = source[k % count, :, cols + part :]
            value = source[k % count, :, cols : cols + part]
            for y in range(2):

                @pl.when(lax.rem(place, 2) == y)
                def _():
                    out_w[lax.div(place, 2), :, y * part : (y + 1) * part] = value

    rows_here = pick_rows(i, steps, own, partner)
    for g in range(groups):
        span = slice(g * cols // groups, (g + 1) * cols // groups)
        tile = weight[:, :, span].reshape(2 * count * rows, cols // groups)
        mixed[:, span] = dot(rows_here, tile).astype(BF16)


def lane_masks():
    lane = lax.broadcasted_iota(jnp.int32, (1, PAIR), 1)
    return [lane < HEAD_DIM, lane >= HEAD_DIM]


def keep(mask, value):
    return jnp.where(mask, value, jnp.zeros_like(value))


def fill_distance(distance):
    row = lax.broadcasted_iota(jnp.int32, distance.shape, 0)
    col = lax.broadcasted_iota(jnp.int32, distance.shape, 1)
    distance[...] = jnp.abs(row - col).astype(F32)


def scores_of(queries, keys, slope, distance):
    raw = lax.dot_general(queries, keys, (((1,), (1,)), ((), ())), preferred_element_type=F32)
    return raw - slope * distance


def attend_kernel(flags, slopes, query, key, value, context, logs, distance):
    block, pair = pl.program_id(0), pl.program_id(1)
    masks = lane_masks()

    @pl.when((block == 0) & (pair == 0))
    def _():
        fill_distance(distance)

    def run(is_long):
        keys_all, values_all = key[...], value[...]
        for g in range(LONG // SHORT):
            rows = slice(g * SHORT, (g + 1) * SHORT)
            keys = keys_all if is_long else keys_all[rows]
            values = values_all if is_long else values_all[rows]
            away = distance[rows, :] if is_long else distance[:SHORT, :SHORT]
            total = jnp.zeros((SHORT, PAIR), F32)
            log_rows = []
            for head in range(2):
                q = keep(masks[head], query[rows, :]) * (HEAD_DIM**-0.5)
                s = scores_of(q.astype(BF16), keys, slopes[pair * 2 + head], away)
                top = jnp.max(s, axis=-1, keepdims=True)
                e = jnp.exp(s - top)
                norm = jnp.sum(e, axis=-1, keepdims=True)
                p = (e * (1.0 / norm)).astype(BF16)
                total = total + dot(p, keep(masks[head], values))
                log_rows.append(top + jnp.log(norm))
            context[rows, :] = total.astype(BF16)
            logs[rows, :] = jnp.where(masks[0], log_rows[0], log_rows[1])

    @pl.when(flags[block] > 0)
    def _():
        run(True)

    @pl.when(flags[block] <= 0)
    def _():
        run(False)


def attend_back_kernel(
    blocks, flags, slopes, query, key, value, d_own, d_partner, logs, d_query, d_key, d_value, distance, key_t, value_t
):
    block, pair = pl.program_id(0), pl.program_id(1)
    masks = lane_masks()
    scale = HEAD_DIM**-0.5

    @pl.when((block == 0) & (pair == 0))
    def _():
        fill_distance(distance)

    def run(is_long):
        keys_all, values_all = key[...], value[...]
        for g in range(LONG // SHORT):
            rows = slice(g * SHORT, (g + 1) * SHORT)
            keys = keys_all if is_long else keys_all[rows]
            values = values_all if is_long else values_all[rows]
            away = distance[rows, :] if is_long else distance[:SHORT, :SHORT]
            d_here = jnp.where(block == 0, d_own[rows, :], d_partner[rows, :])
            d_q = jnp.zeros((SHORT, PAIR), F32)
            d_k = jnp.zeros((PAIR, keys.shape[0]), F32)
            d_v = jnp.zeros((PAIR, keys.shape[0]), F32)
            for head in range(2):
                q = (keep(masks[head], query[rows, :]) * scale).astype(BF16)
                d_c = keep(masks[head], d_here)
                s = scores_of(q, keys, slopes[pair * 2 + head], away)
                log_row = logs[rows, head * HEAD_DIM : head * HEAD_DIM + 1]
                p = jnp.exp(s - log_row)
                d_p = lax.dot_general(d_c, values, (((1,), (1,)), ((), ())), preferred_element_type=F32)
                d_s = (p * (d_p - jnp.sum(p * d_p, axis=-1, keepdims=True))).astype(BF16)
                d_q = d_q + dot(d_s, (keep(masks[head], keys) * scale).astype(BF16))
                d_k = d_k + dot(q.T, d_s)
                d_v = d_v + dot(d_c.T, p.astype(BF16))
            d_query[rows, :] = d_q.astype(BF16)
            if not is_long:
                d_key[rows, :] = d_k.T.astype(BF16)
                d_value[rows, :] = d_v.T.astype(BF16)
            elif g == 0:
                key_t[...] = d_k
                value_t[...] = d_v
            else:
                key_t[...] += d_k
                value_t[...] += d_v
        if is_long:
            d_key[...] = key_t[...].T.astype(BF16)
            d_value[...] = value_t[...].T.astype(BF16)

    @pl.when(flags[block] > 0)
    def _():
        run(True)

    @pl.when(flags[block] <= 0)
    def _():
        run(False)


def spread(rows):
    center = jnp.mean(rows, axis=-1, keepdims=True)
    shifted = rows - center
    inverse = lax.rsqrt(jnp.mean(shifted * shifted, axis=-1, keepdims=True) + 1e-05)
    return shifted * inverse, inverse


def norm_back(e, unit, inverse):
    mean_e = jnp.mean(e, axis=-1, keepdims=True)
    mean_en = jnp.mean(e * unit, axis=-1, keepdims=True)
    return (e - mean_e - unit * mean_en) * inverse


def first_norm_kernel(place, tokens, ctx_mine, ctx_other, w_mine, w_other, norms, weight, unit, inverse, low):
    core = place[0]

    @pl.when(pl.program_id(0) == 0)
    def _():
        for k in range(w_mine.shape[0]):
            weight[2 * k + core] = w_mine[k]
            weight[2 * k + 1 - core] = w_other[k]

    half = weight.shape[0] // 2
    mine = weight[pl.ds(core * half, half)].reshape(D // 2, D)
    other = weight[pl.ds((1 - core) * half, half)].reshape(D // 2, D)
    hidden = tokens[...].astype(F32) + (dot(ctx_mine[...], mine) + dot(ctx_other[...], other))
    n, inv = spread(hidden)
    unit[...] = n
    inverse[...] = inv
    low[...] = (n * norms[0:1, :] + norms[2:3, :]).astype(BF16)


def gelu_parts(x):
    t = 1.0 / (1.0 + (0.3275911 * 0.5**0.5) * jnp.abs(x))
    poly = t * (
        0.254829592 + t * (-0.284496736 + t * (1.421413741 + t * (-1.453152027 + t * 1.061405429)))
    )
    bell = jnp.exp(-0.5 * (x * x))
    tail = 0.5 * poly * bell
    phi = jnp.where(x >= 0, 1.0 - tail, tail)
    return x * phi, phi + x * bell * 0.3989422804014327


def fill_blocks(table, first, second, weight):
    count = first.shape[0]
    for k in range(2 * count):
        weight[table[k]] = first[k] if k < count else second[k - count]


def columns_of(weight, half, span):
    count = weight.shape[0] // 2
    return weight[half * count : (half + 1) * count, :, span].reshape(D, span.stop - span.start)


def up_kernel(
    steps, table, own, partner, gate_a, gate_b, value_a, value_b, product, active, slope, gate_w, value_w
):
    i = pl.program_id(0)

    @pl.when(i == 0)
    def _():
        fill_blocks(table, gate_a, gate_b, gate_w)
        fill_blocks(table, value_a, value_b, value_w)

    rows = pick_rows(i, steps, own, partner)
    width = gate_w.shape[2]
    for half in range(2):
        for start in range(0, width, 256):
            span = slice(start, start + 256)
            out = slice(half * width + start, half * width + start + 256)
            gate = dot(rows, columns_of(gate_w, half, span))
            up = dot(rows, columns_of(value_w, half, span))
            act, grad = gelu_parts(gate)
            product[:, out] = (act * up).astype(BF16)
            active[:, out] = act.astype(BF16)
            slope[:, out] = (up * grad).astype(BF16)


def down_kernel(steps, table, product, down_a, down_b, own, partner, down_w):
    i = pl.program_id(0)

    @pl.when(i == 0)
    def _():
        fill_blocks(table, down_a, down_b, down_w)

    width = down_w.shape[2]
    total = 0.0
    for half in range(2):
        total = total + contract_cols(product[:, half * width : (half + 1) * width], columns_of(down_w, half, slice(0, width)))

    @pl.when(i < steps)
    def _():
        own[...] = total

    @pl.when(i >= steps)
    def _():
        partner[...] = total.astype(BF16)


def second_norm_kernel(unit_one, norms, part_own, part_got, cotangent, out, d_z, d_ffn, sums):
    normed = unit_one[...] * norms[0:1, :] + norms[2:3, :]
    n, inv = spread(normed + (part_own[...] + part_got[...].astype(F32)))
    gain = norms[1:2, :]
    out[...] = (n * gain + norms[3:4, :]).astype(BF16)
    c = cotangent[...].astype(F32)
    back = norm_back(gain * c, n, inv)
    d_z[...] = back
    d_ffn[...] = back.astype(BF16)
    add_sums(sums, c * n, c)


def add_sums(sums, gain_terms, bias_terms):
    @pl.when(pl.program_id(0) == 0)
    def _():
        sums[...] = jnp.zeros_like(sums)

    sums[0:1, :] += jnp.sum(gain_terms, axis=0, keepdims=True)
    sums[1:2, :] += jnp.sum(bias_terms, axis=0, keepdims=True)


def ffn_back_kernel(
    steps, own, partner, down_w, gate_w, value_w, active, slope, d_gate, d_up, back_own, back_partner
):
    i = pl.program_id(0)
    rows = pick_rows(i, steps, own, partner)
    width = down_w.shape[2]
    total = jnp.zeros((ROWS, D), F32)
    for half in range(2):
        for start in range(0, width, 256):
            span = slice(start, start + 256)
            out = slice(half * width + start, half * width + start + 256)
            d_product = dot(rows, columns_of(down_w, half, span))
            dg = (d_product * slope[:, out].astype(F32)).astype(BF16)
            du = (d_product * active[:, out].astype(F32)).astype(BF16)
            d_gate[:, out] = dg
            d_up[:, out] = du
            total = total + contract_cols(dg, columns_of(gate_w, half, span))
            total = total + contract_cols(du, columns_of(value_w, half, span))

    @pl.when(i < steps)
    def _():
        back_own[...] = total

    @pl.when(i >= steps)
    def _():
        back_partner[...] = total.astype(BF16)


def weight_grad_kernel(per_half, table, left_own, left_partner, right, grad):
    i = pl.program_id(0)
    rows = left_own.shape[1]
    value = dot(left_own[...], right[:rows, :]) + dot(left_partner[...], right[rows:, :])
    value = value.astype(BF16)
    count, tall = grad.shape[0] // 2, grad.shape[1]
    half, start = lax.div(i, per_half), lax.rem(i, per_half) * 256
    for k in range(count):
        grad[table[half * count + k], :, pl.ds(pl.multiple_of(start, 256), 256)] = value[k * tall : (k + 1) * tall]


def first_norm_back_kernel(
    place,
    unit_ref,
    inverse,
    norms,
    d_z,
    part_own,
    part_got,
    ctx_mine,
    ctx_other,
    weight,
    d_hidden,
    d_branch,
    dctx_mine,
    dctx_other,
    grad,
    sums,
):
    core = place[0]
    unit = unit_ref[...]
    d_normed = d_z[...] + (part_own[...] + part_got[...].astype(F32))
    back = norm_back(norms[0:1, :] * d_normed, unit, inverse[...])
    low = back.astype(BF16)
    d_hidden[...] = back
    d_branch[...] = low
    add_sums(sums, d_normed * unit, d_normed)
    half = weight.shape[0] // 2
    dctx_mine[...] = contract_cols(low, weight[pl.ds(core * half, half)].reshape(D // 2, D)).astype(BF16)
    dctx_other[...] = contract_cols(low, weight[pl.ds((1 - core) * half, half)].reshape(D // 2, D)).astype(BF16)

    @pl.when(pl.program_id(0) == 0)
    def _():
        grad[...] = jnp.zeros_like(grad)

    shape = (half,) + grad.shape[1:]
    grad[pl.ds(core * half, half)] += dot(ctx_mine[...].T, low).reshape(shape)
    grad[pl.ds((1 - core) * half, half)] += dot(ctx_other[...].T, low).reshape(shape)


def qkv_grad_kernel(table, left_own, left_partner, d_query, d_key, d_value, out_grad, norm_grad, grad):
    i = pl.program_id(0)
    rows = left_own.shape[1]
    count, tall = grad.shape[0], grad.shape[1]
    cols = d_query.shape[1]
    part = out_grad.shape[2] // 2
    for g, right in enumerate((d_query, d_key, d_value)):

        @pl.when(i == g)
        def _():
            value = (dot(left_own[...], right[:rows, :]) + dot(left_partner[...], right[rows:, :])).astype(BF16)
            for k in range(count):
                grad[table[k], :, g * cols : (g + 1) * cols] = value[k * tall : (k + 1) * tall]
                if g == 0:
                    y = k % 2
                    grad[table[k], :, 3 * cols : 3 * cols + part] = out_grad[k // 2, :, y * part : (y + 1) * part]
                    grad[table[k], :, 3 * cols + part :] = norm_grad[k]


def input_grad_kernel(steps, d_query, d_key, d_value, weight, own, partner):
    i = pl.program_id(0)
    cols = d_query.shape[1]
    total = 0.0
    for g, left in enumerate((d_query, d_key, d_value)):
        tile = weight[:, :, g * cols : (g + 1) * cols].reshape(D, cols)
        total = total + contract_cols(left[...], tile)

    @pl.when(i < steps)
    def _():
        own[...] = total

    @pl.when(i >= steps)
    def _():
        partner[...] = total.astype(BF16)


def by_core(core, mine, other, axis):
    first = core == 0
    return jnp.stack([jnp.where(first, mine, other), jnp.where(first, other, mine)], axis=axis)


def half_of(core, halves, axis):
    zero, one = (lax.index_in_dim(halves, k, axis, keepdims=False) for k in range(2))
    first = core == 0
    return jnp.where(first, zero, one), jnp.where(first, one, zero)


def plane_shards(
    wide,
    narrow,
    tokens,
    w_qkv,
    w_out,
    w_gate,
    w_value,
    w_down,
    norm_gains,
    norm_biases,
    long_count,
    cotangent,
):
    plane = Plane(wide, narrow)
    core, y_here = plane.core, plane.y
    rows = tokens.shape[0]
    steps = rows // ROWS
    tall = w_qkv.shape[0]
    blocks = wide * narrow // 2
    z_size = plane.size["z"]
    head_cols = D // 2
    width = w_gate.shape[1] // 2
    hidden = 2 * width
    order = ("z", "a", "b")
    qkv_to, qkv_from = plane.tables(order, lambda z, x, y: (z * 2 + x) * 2 + y)
    ffn_to, ffn_from = plane.tables(order, lambda z, x, y: y * (2 * z_size) + z * 2 + x)
    place = jnp.reshape(core, (1,)).astype(jnp.int32)

    qkv_mine, qkv_other = half_of(core, w_qkv.reshape(tall, 3, 2, head_cols), 2)
    norm_cols = jnp.concatenate([norm_gains, norm_biases], axis=0).T
    norm_cols = jnp.pad(norm_cols, ((0, 0), (0, 128 - norm_cols.shape[1])))
    head_part = jnp.concatenate([qkv_mine.reshape(tall, 3 * head_cols), norm_cols], axis=1)
    head_send = jnp.concatenate([qkv_other.reshape(tall, 3 * head_cols), norm_cols], axis=1)
    head_got = plane.swap(head_send, "core")
    tokens_other = plane.swap(tokens, "core")
    head_part = jnp.where(y_here == core, head_part, head_got)
    out_cols = lax.dynamic_slice_in_dim(w_out, y_here * (D // narrow), D // narrow, axis=1)
    head_part = jnp.concatenate(
        [head_part[:, : 3 * head_cols], out_cols, head_part[:, 3 * head_cols :]], axis=1
    )
    qkv_blocks = plane.gather(head_part, order)

    ffn_parts = jnp.stack([w_gate, w_value, w_down.T], axis=0).reshape(3, tall, 2, width)
    ffn_mine, ffn_other = half_of(core, ffn_parts, 2)
    ffn_got = plane.swap(ffn_other, "core")
    ffn_chip = by_core(core, ffn_mine, ffn_got, 1).reshape(3, 2 * tall, width)
    gate_blocks = plane.gather(ffn_chip[0], order)
    value_blocks = plane.gather(ffn_chip[1], order)
    down_blocks = plane.gather(ffn_chip[2], order)

    flag = jnp.broadcast_to(long_count.astype(F32), (8, 128))
    flags = jnp.stack([long_count[0, 0], plane.swap(flag, "core")[0, 0].astype(jnp.int32)])
    slopes = lax.dynamic_slice_in_dim(alibi_slopes(HEADS), core * (HEADS // 2), HEADS // 2)

    half_blocks = blocks // 2
    piece = qkv_blocks[0].shape
    mixed, qkv_w, out_mine, norm_table = kernel_call(
        functools.partial(qkv_kernel, steps, 3),
        (2 * steps,),
        [
            (qkv_to, smem()),
            (tokens, own_rows(steps, D)),
            (tokens_other, partner_rows(steps, D)),
            (qkv_blocks[0], whole(piece)),
            (qkv_blocks[1], whole(piece)),
        ],
        [
            ((2 * rows, 3 * head_cols), BF16, pl.BlockSpec((ROWS, 3 * head_cols), lambda i: (i, 0))),
            ((blocks, tall, 3 * head_cols), BF16, whole((blocks, tall, 3 * head_cols))),
            ((half_blocks, tall, D), BF16, whole((half_blocks, tall, D))),
            ((blocks, tall, 128), BF16, whole((blocks, tall, 128))),
        ],
        flops=2 * 2 * rows * D * 3 * head_cols,
        name="mixed",
    )
    out_other = plane.swap(out_mine, "core")
    norms = norm_table.reshape(D, 128)[:, :4].T.astype(F32)
    norms = jnp.stack([norms[0], norms[1], norms[2], norms[3]])

    pairs = head_cols // PAIR

    def head_block(first):
        return pl.BlockSpec((rows, PAIR), lambda b, p: (b, first + p))

    context, logs = kernel_call(
        attend_kernel,
        (2, pairs),
        [
            (flags, smem()),
            (slopes, smem()),
            (mixed, head_block(0)),
            (mixed, head_block(pairs)),
            (mixed, head_block(2 * pairs)),
        ],
        [
            ((2 * rows, head_cols), BF16, head_block(0)),
            ((2 * rows, head_cols), F32, head_block(0)),
        ],
        scratch=[pltpu.VMEM((LONG, LONG), F32)],
        flops=4 * 2 * rows * LONG * D,
        name="attend",
    )
    ctx_mine = context[:rows]
    ctx_other = plane.swap(context[rows:], "core")

    def step_rows(cols):
        return pl.BlockSpec((ROWS, cols), lambda i: (i, 0))

    out_w, unit_one, inverse_one, low = kernel_call(
        first_norm_kernel,
        (steps,),
        [
            (place, smem()),
            (tokens, step_rows(D)),
            (ctx_mine, step_rows(head_cols)),
            (ctx_other, step_rows(head_cols)),
            (out_mine, whole(out_mine.shape)),
            (out_other, whole(out_mine.shape)),
            (norms, whole(norms.shape)),
        ],
        [
            ((blocks, tall, D), BF16, whole((blocks, tall, D))),
            ((rows, D), F32, step_rows(D)),
            ((rows, 1), F32, step_rows(1)),
            ((rows, D), BF16, step_rows(D)),
        ],
        flops=2 * rows * D * D,
        name="first_norm",
    )
    low_other = plane.swap(low, "core")

    w_shape = (blocks, 2 * tall, width)
    product, active, slope, gate_w, value_w = kernel_call(
        functools.partial(up_kernel, steps),
        (2 * steps,),
        [
            (ffn_to, smem()),
            (low, own_rows(steps, D)),
            (low_other, partner_rows(steps, D)),
        ]
        + [(part, whole(part.shape)) for part in gate_blocks + value_blocks],
        [((2 * rows, hidden), BF16, step_rows(hidden))] * 3 + [(w_shape, BF16, whole(w_shape))] * 2,
        flops=2 * 2 * rows * D * 2 * hidden,
        name="up",
    )
    part_own, part_send, down_w = kernel_call(
        functools.partial(down_kernel, steps),
        (2 * steps,),
        [(ffn_to, smem()), (product, step_rows(hidden))] + [(part, whole(part.shape)) for part in down_blocks],
        [
            ((rows, D), F32, own_rows(steps, D)),
            ((rows, D), BF16, partner_rows(steps, D)),
            (w_shape, BF16, whole(w_shape)),
        ],
        flops=2 * 2 * rows * D * hidden,
        name="down",
    )
    part_got = plane.swap(part_send, "core")
    layer_out, d_z, d_ffn, sums_two = kernel_call(
        second_norm_kernel,
        (steps,),
        [
            (unit_one, step_rows(D)),
            (norms, whole(norms.shape)),
            (part_own, step_rows(D)),
            (part_got, step_rows(D)),
            (cotangent, step_rows(D)),
        ],
        [
            ((rows, D), BF16, step_rows(D)),
            ((rows, D), F32, step_rows(D)),
            ((rows, D), BF16, step_rows(D)),
            ((8, D), F32, whole((8, D))),
        ],
        name="second_norm",
    )
    d_ffn_other = plane.swap(d_ffn, "core")

    def weight_grad(left, left_other, right):
        return kernel_call(
            functools.partial(weight_grad_kernel, width // 256),
            (hidden // 256,),
            [
                (ffn_from, smem()),
                (left.T, whole((D, rows))),
                (left_other.T, whole((D, rows))),
                (right, pl.BlockSpec((2 * rows, 256), lambda i: (0, i))),
            ],
            [(w_shape, BF16, whole(w_shape))],
            flops=2 * 2 * rows * D * hidden,
            name="weight_grad",
        )[0]

    grad_down = plane.reduce(weight_grad(d_ffn, d_ffn_other, product), order)
    d_gate, d_up, back_own, back_send = kernel_call(
        functools.partial(ffn_back_kernel, steps),
        (2 * steps,),
        [
            (d_ffn, own_rows(steps, D)),
            (d_ffn_other, partner_rows(steps, D)),
            (down_w, whole(w_shape)),
            (gate_w, whole(w_shape)),
            (value_w, whole(w_shape)),
            (active, step_rows(hidden)),
            (slope, step_rows(hidden)),
        ],
        [((2 * rows, hidden), BF16, step_rows(hidden))] * 2
        + [((rows, D), F32, own_rows(steps, D)), ((rows, D), BF16, partner_rows(steps, D))],
        flops=3 * 2 * 2 * rows * D * hidden,
        name="ffn_back",
    )
    back_got = plane.swap(back_send, "core")
    grad_gate = plane.reduce(weight_grad(low, low_other, d_gate), order)
    grad_value = plane.reduce(weight_grad(low, low_other, d_up), order)

    d_hidden, d_branch, dctx_mine, dctx_send, out_grad, sums_one = kernel_call(
        first_norm_back_kernel,
        (steps,),
        [
            (place, smem()),
            (unit_one, step_rows(D)),
            (inverse_one, step_rows(1)),
            (norms, whole(norms.shape)),
            (d_z, step_rows(D)),
            (back_own, step_rows(D)),
            (back_got, step_rows(D)),
            (ctx_mine, step_rows(head_cols)),
            (ctx_other, step_rows(head_cols)),
            (out_w, whole(out_w.shape)),
        ],
        [
            ((rows, D), F32, step_rows(D)),
            ((rows, D), BF16, step_rows(D)),
            ((rows, head_cols), BF16, step_rows(head_cols)),
            ((rows, head_cols), BF16, step_rows(head_cols)),
            ((blocks, tall, D), F32, whole((blocks, tall, D))),
            ((8, D), F32, whole((8, D))),
        ],
        flops=2 * 2 * rows * D * D,
        name="first_norm_back",
    )
    dctx_got = plane.swap(dctx_send, "core")
    out_keep, out_send = half_of(core, out_grad.reshape(half_blocks, 2, tall, D), 1)
    out_sum = (out_keep + plane.swap(out_send.astype(BF16), "core").astype(F32)).astype(BF16)
    sums = jnp.stack([sums_one[0], sums_two[0], sums_one[1], sums_two[1]], axis=1)
    norm_grad = jnp.pad(sums, ((0, 0), (0, 124))).astype(BF16).reshape(blocks, tall, 128)

    def whole_pair(first):
        return pl.BlockSpec((rows, PAIR), lambda b, p: (0, first + p))

    d_query, d_key, d_value = kernel_call(
        functools.partial(attend_back_kernel, 2),
        (2, pairs),
        [
            (flags, smem()),
            (slopes, smem()),
            (mixed, head_block(0)),
            (mixed, head_block(pairs)),
            (mixed, head_block(2 * pairs)),
            (dctx_mine, whole_pair(0)),
            (dctx_got, whole_pair(0)),
            (logs, head_block(0)),
        ],
        [((2 * rows, head_cols), BF16, head_block(0))] * 3,
        scratch=[
            pltpu.VMEM((LONG, LONG), F32),
            pltpu.VMEM((PAIR, LONG), F32),
            pltpu.VMEM((PAIR, LONG), F32),
        ],
        flops=10 * 2 * rows * LONG * D,
        name="attend_back",
    )
    grad_shape = (blocks, tall, 3 * head_cols + D // 2 + 128)
    parts = [(v, whole((2 * rows, head_cols))) for v in (d_query, d_key, d_value)]
    grad_head = kernel_call(
        qkv_grad_kernel,
        (3,),
        [
            (qkv_from, smem()),
            (tokens.T, whole((D, rows))),
            (tokens_other.T, whole((D, rows))),
        ]
        + parts
        + [(out_sum, whole(out_sum.shape)), (norm_grad, whole(norm_grad.shape))],
        [(grad_shape, BF16, whole(grad_shape))],
        flops=2 * 2 * rows * D * 3 * head_cols,
        name="qkv_grad",
    )[0]
    head_sum = plane.reduce(grad_head, order).astype(BF16)
    in_own, in_send = kernel_call(
        functools.partial(input_grad_kernel, steps),
        (2 * steps,),
        [(v, step_rows(head_cols)) for v in (d_query, d_key, d_value)] + [(qkv_w, whole(qkv_w.shape))],
        [((rows, D), F32, own_rows(steps, D)), ((rows, D), BF16, partner_rows(steps, D))],
        flops=2 * 2 * rows * D * 3 * head_cols,
        name="input_grad",
    )
    input_grad = d_hidden + in_own + plane.swap(in_send, "core").astype(F32)

    def ffn_piece(total):
        mine, other = half_of(core, total.astype(BF16).reshape(2, tall, width), 0)
        return by_core(core, mine, plane.swap(other, "core"), 1).reshape(tall, 2 * width).astype(F32)

    gate_piece, value_piece = ffn_piece(grad_gate), ffn_piece(grad_value)
    down_piece = ffn_piece(grad_down).T
    both = by_core(y_here, head_sum, plane.swap(head_sum, "y"), 0)
    out_piece = both[:, :, 3 * head_cols : 3 * head_cols + D // 2]
    out_piece = jnp.transpose(out_piece, (1, 0, 2)).reshape(tall, D).astype(F32)
    rest = jnp.concatenate([both[:, :, : 3 * head_cols], both[:, :, 3 * head_cols + D // 2 :]], axis=2)
    mine, other = half_of(core, rest, 0)
    got = plane.swap(other, "core")
    qkv_piece = by_core(
        core, mine[:, : 3 * head_cols].reshape(tall, 3, head_cols), got[:, : 3 * head_cols].reshape(tall, 3, head_cols), 2
    )
    qkv_piece = qkv_piece.reshape(tall, 6 * head_cols).astype(F32)
    norm_piece = (mine[:, 3 * head_cols : 3 * head_cols + 4].astype(F32) + got[:, 3 * head_cols : 3 * head_cols + 4].astype(F32)).T
    return (
        layer_out,
        input_grad,
        qkv_piece,
        out_piece,
        gate_piece,
        value_piece,
        down_piece,
        norm_piece[:2],
        norm_piece[2:],
    )


def solution(mesh):
    wide, narrow = mesh.shape["wide"], mesh.shape["narrow"]
    placed = (
        P(("wide", "narrow"), None),
        P("wide", None),
        P("wide", None),
        P("wide", "narrow"),
        P("wide", "narrow"),
        P("narrow", "wide"),
        P(None, "wide"),
        P(None, "wide"),
        P("wide", "narrow"),
        P(("wide", "narrow"), None),
    )
    if narrow == 2 and wide % 16 == 0 and D % (16 * wide) == 0:
        body = functools.partial(plane_shards, wide, narrow)
    else:
        body = general_shards
    return jax.shard_map(
        body,
        mesh=mesh,
        in_specs=placed,
        out_specs=(
            P(("wide", "narrow"), None),
            P(("wide", "narrow"), None),
            P("wide", None),
            P("wide", None),
            P("wide", "narrow"),
            P("wide", "narrow"),
            P("narrow", "wide"),
            P(None, "wide"),
            P(None, "wide"),
        ),
        check_vma=False,
    )
```

```python
import functools

import jax
import jax.numpy as jnp
import numpy as np
from jax import lax
from jax.experimental import pallas as pl
from jax.experimental.pallas import tpu as pltpu
from jax.sharding import PartitionSpec as P

D = 768
HEADS = 12
HEAD_DIM = 64
LONG = 512
SHORT = 128


def norm_rows(values, gain_row, bias_row):
    center = jnp.mean(values, axis=-1, keepdims=True)
    shifted = values - center
    spread = jnp.mean(shifted * shifted, axis=-1, keepdims=True)
    return shifted * lax.rsqrt(spread + 1e-05) * gain_row + bias_row


def gelu_product(gate_in, value_in):
    return jax.nn.gelu(gate_in, approximate=False) * value_in


def alibi_slopes(heads):
    power = 1 << heads.bit_length() - 1
    first = [2.0 ** (-8.0 * (index + 1) / power) for index in range(power)]
    second = [2.0 ** (-8.0 * (2 * index + 1) / (2 * power)) for index in range(heads - power)]
    return jnp.array(first + second, dtype=jnp.float32)


def alibi_bias(span, heads):
    position = jnp.arange(span)
    distance = jnp.abs(position[:, None] - position[None, :]).astype(jnp.float32)
    slopes = alibi_slopes(heads)
    return slopes[:, None, None] * distance


def block_scores(query_g, key_g, span):
    width = query_g.shape[-1]
    scores = jnp.einsum(
        "bqhd,bkhd->bhqk", query_g, key_g, preferred_element_type=jnp.float32
    ) * width ** (-0.5)
    return scores - alibi_bias(span, query_g.shape[2])


def attend(query_rows, key_rows, value_rows, span):
    rows, heads, width = query_rows.shape
    groups = rows // span
    shape_g = (groups, span, heads, width)
    query_g = query_rows.reshape(shape_g)
    key_g = key_rows.reshape(shape_g)
    value_g = value_rows.reshape(shape_g)
    scores = block_scores(query_g, key_g, span)
    top = jnp.max(scores, axis=-1, keepdims=True)
    expd = jnp.exp(scores - top)
    total = jnp.sum(expd, axis=-1, keepdims=True)
    probs_low = (expd / total).astype(jnp.bfloat16)
    context = jnp.einsum("bhqk,bkhd->bqhd", probs_low, value_g, preferred_element_type=jnp.float32)
    log_total = jnp.transpose((top + jnp.log(total))[..., 0], (0, 2, 1)).reshape(rows, heads)
    return (context.reshape(rows, heads * width), log_total)


def attend_back(query_rows, key_rows, value_rows, log_total, d_context, span):
    rows, heads, width = query_rows.shape
    groups = rows // span
    shape_g = (groups, span, heads, width)
    query_g = query_rows.reshape(shape_g)
    key_g = key_rows.reshape(shape_g)
    value_g = value_rows.reshape(shape_g)
    d_context_g = d_context.reshape(shape_g)
    lse_g = jnp.transpose(log_total.reshape(groups, span, heads), (0, 2, 1))
    scores = block_scores(query_g, key_g, span)
    probs = jnp.exp(scores - lse_g[..., None])
    probs_low = probs.astype(jnp.bfloat16)
    d_probs = jnp.einsum(
        "bqhd,bkhd->bhqk", d_context_g, value_g, preferred_element_type=jnp.float32
    )
    d_values = jnp.einsum(
        "bhqk,bqhd->bkhd", probs_low, d_context_g, preferred_element_type=jnp.float32
    )
    row_dot = jnp.sum(probs * d_probs, axis=-1, keepdims=True)
    d_scores = (probs * (d_probs - row_dot)).astype(jnp.bfloat16)
    scale = width ** (-0.5)
    d_queries = (
        jnp.einsum("bhqk,bkhd->bqhd", d_scores, key_g, preferred_element_type=jnp.float32) * scale
    )
    d_keys = (
        jnp.einsum("bhqk,bqhd->bkhd", d_scores, query_g, preferred_element_type=jnp.float32) * scale
    )
    return jnp.stack([d_queries, d_keys, d_values], axis=2).reshape(rows, 3, heads, width)


def contract_rows(left, right):
    return lax.dot_general(
        left, right, (((0,), (0,)), ((), ())), preferred_element_type=jnp.float32
    )


def contract_cols(left, right):
    return lax.dot_general(
        left, right, (((1,), (1,)), ((), ())), preferred_element_type=jnp.float32
    )


def general_shards(
    tokens, w_qkv, w_out, w_gate, w_value, w_down, norm_gains, norm_biases, long_count, cotangent
):
    gathered = (
        lax.all_gather(w_qkv, "wide", axis=0, tiled=True),
        lax.all_gather(w_out, "wide", axis=0, tiled=True),
        lax.all_gather(w_gate, "wide", axis=0, tiled=True),
        lax.all_gather(w_value, "wide", axis=0, tiled=True),
        lax.all_gather(w_down, "wide", axis=1, tiled=True),
        lax.all_gather(norm_gains, "wide", axis=1, tiled=True),
        lax.all_gather(norm_biases, "wide", axis=1, tiled=True),
    )
    full_qkv, full_out, wide_gate, wide_value, wide_down, gains_all, biases_all = gathered
    gains_f = gains_all.astype(jnp.float32)
    biases_f = biases_all.astype(jnp.float32)
    rows_dev = tokens.shape[0]
    n_blocks = rows_dev // LONG
    long_here = long_count[0, 0]
    tokens_f = tokens.astype(jnp.float32)
    mixed = jnp.dot(tokens, full_qkv, preferred_element_type=jnp.float32).astype(jnp.bfloat16)
    heads_view = mixed.reshape(n_blocks, LONG, 3, HEADS, HEAD_DIM)
    query_blk = heads_view[:, :, 0]
    key_blk = heads_view[:, :, 1]
    value_blk = heads_view[:, :, 2]
    block_ids = jnp.arange(n_blocks)

    def forward_block(entry):
        block_id, query_rows, key_rows, value_rows = entry
        return lax.cond(
            block_id < long_here,
            lambda operands: attend(operands[0], operands[1], operands[2], LONG),
            lambda operands: attend(operands[0], operands[1], operands[2], SHORT),
            (query_rows, key_rows, value_rows),
        )

    context_f, lse_rows = lax.map(forward_block, (block_ids, query_blk, key_blk, value_blk))
    context = context_f.reshape(rows_dev, D).astype(jnp.bfloat16)
    branch = jnp.dot(context, full_out, preferred_element_type=jnp.float32)
    hidden_in = tokens_f + branch
    normed = norm_rows(hidden_in, gains_f[0], biases_f[0])
    normed_low = normed.astype(jnp.bfloat16)
    all_rows = lax.all_gather(normed_low, "narrow", axis=0, tiled=True)
    gate = jnp.dot(all_rows, wide_gate, preferred_element_type=jnp.float32)
    value_up = jnp.dot(all_rows, wide_value, preferred_element_type=jnp.float32)
    product_f, pull_product = jax.vjp(gelu_product, gate, value_up)
    product = product_f.astype(jnp.bfloat16)
    ffn_out = lax.psum_scatter(
        jnp.dot(product, wide_down, preferred_element_type=jnp.float32),
        "narrow",
        scatter_dimension=0,
        tiled=True,
    )
    out_in = normed + ffn_out
    layer_out, pull_second = jax.vjp(norm_rows, out_in, gains_f[1], biases_f[1])
    d_out, d_gain_two, d_bias_two = pull_second(cotangent.astype(jnp.float32))
    d_ffn = d_out.astype(jnp.bfloat16)
    d_rows = lax.all_gather(d_ffn, "narrow", axis=0, tiled=True)
    grad_down = contract_rows(product, d_rows)
    d_product = contract_cols(d_rows, wide_down)
    d_gate, d_up = pull_product(d_product)
    d_gate_low = d_gate.astype(jnp.bfloat16)
    d_up_low = d_up.astype(jnp.bfloat16)
    grad_gate = contract_rows(all_rows, d_gate_low)
    grad_value = contract_rows(all_rows, d_up_low)
    d_normed = lax.psum_scatter(
        contract_cols(d_gate_low, wide_gate) + contract_cols(d_up_low, wide_value),
        "narrow",
        scatter_dimension=0,
        tiled=True,
    )
    d_normed_total = d_out + d_normed
    unused_out, pull_first = jax.vjp(norm_rows, hidden_in, gains_f[0], biases_f[0])
    d_hidden, d_gain_one, d_bias_one = pull_first(d_normed_total)
    d_branch = d_hidden.astype(jnp.bfloat16)
    grad_out = contract_rows(context, d_branch)
    d_context = contract_cols(d_branch, full_out).astype(jnp.bfloat16)
    d_context_blk = d_context.reshape(n_blocks, LONG, HEADS, HEAD_DIM)

    def backward_block(entry):
        block_id, query_rows, key_rows, value_rows, log_total, d_ctx = entry
        return lax.cond(
            block_id < long_here,
            lambda operands: attend_back(
                operands[0], operands[1], operands[2], operands[3], operands[4], LONG
            ),
            lambda operands: attend_back(
                operands[0], operands[1], operands[2], operands[3], operands[4], SHORT
            ),
            (query_rows, key_rows, value_rows, log_total, d_ctx),
        )

    d_mixed_f = lax.map(
        backward_block, (block_ids, query_blk, key_blk, value_blk, lse_rows, d_context_blk)
    )
    d_mixed = d_mixed_f.reshape(rows_dev, 3 * D).astype(jnp.bfloat16)
    grad_qkv = contract_rows(tokens, d_mixed)
    input_grad = d_hidden + contract_cols(d_mixed, full_qkv)
    grad_gains = jnp.stack([d_gain_one, d_gain_two])
    grad_biases = jnp.stack([d_bias_one, d_bias_two])
    pieces = (
        lax.psum_scatter(
            grad_qkv.astype(jnp.bfloat16), "wide", scatter_dimension=0, tiled=True
        ).astype(jnp.float32),
        lax.psum_scatter(
            grad_out.astype(jnp.bfloat16), "wide", scatter_dimension=0, tiled=True
        ).astype(jnp.float32),
        lax.psum_scatter(
            grad_gate.astype(jnp.bfloat16), "wide", scatter_dimension=0, tiled=True
        ).astype(jnp.float32),
        lax.psum_scatter(
            grad_value.astype(jnp.bfloat16), "wide", scatter_dimension=0, tiled=True
        ).astype(jnp.float32),
        lax.psum_scatter(
            grad_down.astype(jnp.bfloat16), "wide", scatter_dimension=1, tiled=True
        ).astype(jnp.float32),
        lax.psum_scatter(
            grad_gains.astype(jnp.bfloat16), "wide", scatter_dimension=1, tiled=True
        ).astype(jnp.float32),
        lax.psum_scatter(
            grad_biases.astype(jnp.bfloat16), "wide", scatter_dimension=1, tiled=True
        ).astype(jnp.float32),
    )
    qkv_piece, out_piece, gate_piece, value_piece, down_piece, gains_piece, biases_piece = pieces
    qkv_piece, out_piece, gains_piece, biases_piece = (
        lax.psum(qkv_piece.astype(jnp.bfloat16), "narrow").astype(jnp.float32),
        lax.psum(out_piece.astype(jnp.bfloat16), "narrow").astype(jnp.float32),
        lax.psum(gains_piece.astype(jnp.bfloat16), "narrow").astype(jnp.float32),
        lax.psum(biases_piece.astype(jnp.bfloat16), "narrow").astype(jnp.float32),
    )
    return (
        layer_out.astype(jnp.bfloat16),
        input_grad,
        qkv_piece,
        out_piece,
        gate_piece,
        value_piece,
        down_piece,
        gains_piece,
        biases_piece,
    )


AXES = ("wide", "narrow")
F32 = jnp.float32
BF16 = jnp.bfloat16
MIB = 1024 * 1024
KEPT = ("mixed", "up", "down")
PAIR = 2 * HEAD_DIM


def dot(left, right):
    return jnp.dot(left, right, preferred_element_type=F32)


class Plane:
    def __init__(self, wide, narrow):
        self.size = {"z": wide // 4, "a": 2, "b": 2, "core": 2, "y": narrow}
        self.pairs = {}
        count = wide * narrow
        for dim, size in self.size.items():
            for step in range(1, size):
                self.pairs[dim, step] = [(i, self.partner(i, dim, step)) for i in range(count)]
        w = lax.axis_index("wide")
        self.z, self.x, self.core = w // 4, (w // 2) % 2, w % 2
        self.y = lax.axis_index("narrow")

    @staticmethod
    def partner(i, dim, step):
        z, x, c, y = i // 8, (i // 4) % 2, (i // 2) % 2, i % 2
        if dim == "z":
            z ^= step
        elif dim == "core":
            c ^= 1
        elif dim == "y" or (dim == "a") == (c == 1):
            y ^= 1
        else:
            x ^= 1
        return ((z * 2 + x) * 2 + c) * 2 + y

    def swap(self, value, dim, step=1):
        return lax.ppermute(value, AXES, self.pairs[dim, step])

    def gather_z(self, value):
        return jnp.stack([value] + [self.swap(value, "z", k) for k in range(1, self.size["z"])])

    def double_z(self, value):
        held, step = value[None], 1
        while step < self.size["z"]:
            held = jnp.concatenate([held, self.swap(held, "z", step)], axis=0)
            step *= 2
        return held

    def sum_pair(self, near, far, dim, step=1):
        return near.astype(F32) + self.swap(far, dim, step).astype(F32)

    def halve(self, held, dim, step=1, events=()):
        count = held.shape[0] // 2
        got = after(self.swap(held[count:], dim, step), *events)
        return (held[:count].astype(F32) + got.astype(F32)).astype(BF16)

    def sum_z(self, held):
        total = held[0].astype(F32)
        for k in range(1, self.size["z"]):
            total = total + self.swap(held[k], "z", k).astype(F32)
        return total

    def tables(self, order, numbered):
        sizes = [self.size[dim] for dim in order]
        number = np.arange(int(np.prod(sizes)))
        rest, digit = number, {}
        for dim, size in zip(order, sizes):
            digit[dim] = rest % size
            rest = rest // size
        first = self.core == 0
        a_here = jnp.where(first, self.x, self.y)
        b_here = jnp.where(first, self.y, self.x)
        z = digit["z"] ^ self.z
        a = digit["a"] ^ a_here
        b = digit["b"] ^ b_here
        x, y = jnp.where(first, a, b), jnp.where(first, b, a)
        return numbered(z, x, y).astype(jnp.int32)


def after(value, *events):
    return lax.optimization_barrier((value,) + events)[0]


def fence(*values):
    return lax.optimization_barrier(values)


def smem():
    return pl.BlockSpec(memory_space=pltpu.SMEM)


def whole(shape):
    zeros = (0,) * len(shape)
    return pl.BlockSpec(tuple(shape), lambda *_: zeros)


def kernel_call(body, grid, ins, outs, scratch=(), flops=0, name=None, room=6):
    blocks = [(spec.block_shape, a.dtype) for a, spec in ins] + [(spec.block_shape, d) for _, d, spec in outs]
    held = sum(2 * int(np.prod(shape)) * np.dtype(d).itemsize for shape, d in blocks if shape is not None)
    held += sum(int(np.prod(v.shape)) * np.dtype(v.dtype).itemsize for v in scratch)
    size = sum(a.size * a.dtype.itemsize for a, _ in ins)
    size += sum(int(np.prod(s)) * np.dtype(d).itemsize for s, d, _ in outs)
    return pl.pallas_call(
        body,
        grid=grid,
        in_specs=[spec for _, spec in ins],
        out_specs=[spec for _, _, spec in outs],
        out_shape=[pltpu.VMEM(s, d) if name in KEPT else jax.ShapeDtypeStruct(s, d) for s, d, _ in outs],
        scratch_shapes=list(scratch),
        compiler_params=pltpu.CompilerParams(
            dimension_semantics=("arbitrary",) * len(grid), vmem_limit_bytes=held + room * MIB
        ),
        cost_estimate=pl.CostEstimate(flops=0, bytes_accessed=0, transcendentals=0),
        name=name,
    )(*[a for a, _ in ins])


ROWS = 256


def own_rows(steps, cols):
    return pl.BlockSpec((ROWS, cols), lambda i: (jnp.minimum(i, steps - 1), 0))


def partner_rows(steps, cols):
    return pl.BlockSpec((ROWS, cols), lambda i: (jnp.maximum(i - steps, 0), 0))


def pick_rows(i, steps, own_ref, partner_ref):
    return jnp.where(i < steps, own_ref[...], partner_ref[...])


def split_kernel(place, w_qkv, w_out, norm_cols, mine, send):
    first = place[0] == 0
    half = D // 2
    for n in range(4):
        source, start = (w_qkv, n * D) if n < 3 else (w_out, 0)
        low, high = source[:, start : start + half], source[:, start + half : start + D]
        mine[:, n * half : (n + 1) * half] = jnp.where(first, low, high)
        send[:, n * half : (n + 1) * half] = jnp.where(first, high, low)
    mine[:, 4 * half :] = norm_cols[...]
    send[:, 4 * half :] = norm_cols[...]


def fill_blocks(table, pieces, weight, cols=slice(None)):
    count = pieces[0].shape[0]
    for n, piece in enumerate(pieces):
        for k in range(count):
            weight[table[n * count + k]] = piece[k, :, cols]


def qkv_kernel(steps, groups, pieces, table, own, partner, *refs):
    i = pl.program_id(0)
    parts = refs[:pieces]
    mixed_own, mixed_partner, weight, out_w, norms = refs[pieces:]
    cols, part = weight.shape[2], out_w.shape[2]
    tall = weight.shape[0] * weight.shape[1]

    @pl.when(i == 0)
    def _():
        fill_blocks(table, parts, weight, slice(0, cols))
        fill_blocks(table, parts, out_w, slice(cols, cols + part))
        fill_blocks(table, parts, norms, slice(cols + part, None))

    rows_here = pick_rows(i, steps, own, partner)
    for g in range(groups):
        span = slice(g * cols // groups, (g + 1) * cols // groups)
        tile = weight[:, :, span].reshape(tall, cols // groups)
        value = dot(rows_here, tile).astype(BF16)

        @pl.when(i < steps)
        def _():
            mixed_own[:, span] = value

        @pl.when(i >= steps)
        def _():
            mixed_partner[:, span] = value


def lane_masks():
    lane = lax.broadcasted_iota(jnp.int32, (1, PAIR), 1)
    return [lane < HEAD_DIM, lane >= HEAD_DIM]


def keep(mask, value):
    return jnp.where(mask, value, jnp.zeros_like(value))


def fill_distance(distance):
    row = lax.broadcasted_iota(jnp.int32, distance.shape, 0)
    col = lax.broadcasted_iota(jnp.int32, distance.shape, 1)
    distance[...] = jnp.abs(row - col).astype(F32)


def scores_of(queries, keys, slope, distance):
    raw = lax.dot_general(queries, keys, (((1,), (1,)), ((), ())), preferred_element_type=F32)
    return raw - slope * distance


def attend_rows(queries, keys, values, slope, away):
    s = jnp.concatenate([scores_of(q, k, slope, away) for q, k in zip(queries, keys)], axis=0)
    top = jnp.max(s, axis=-1, keepdims=True)
    e = jnp.exp(s - top)
    norm = jnp.sum(e, axis=-1, keepdims=True)
    p = (e * (1.0 / norm)).astype(BF16)
    tall = queries[0].shape[0]
    out = [dot(p[n * tall : (n + 1) * tall], v) for n, v in enumerate(values)]
    return jnp.concatenate(out, axis=0), top + jnp.log(norm)


def tiles(value, tall):
    return [value[n : n + tall] for n in range(0, value.shape[0], tall)]


def pair_cols(part, pair):
    return pl.ds(pl.multiple_of(part * (D // 2) + pair * PAIR, PAIR), PAIR)


def attend_kernel(place, flags, slopes, mixed, context, logs, distance):
    masks = lane_masks()
    scale = HEAD_DIM**-0.5
    lane = lax.broadcasted_iota(jnp.int32, (1, 128), 1)
    fill_distance(distance)

    def run(is_long):
        tall = 2 * SHORT if is_long else LONG

        def one_pair(pair, _):
            q_all, k_all, v_all = (mixed[:, pair_cols(part, pair)] for part in range(3))
            totals = [0.0] * (LONG // tall)
            for head in range(2):
                slope = slopes[pair * 2 + head]
                q = (keep(masks[head], q_all) * scale).astype(BF16)
                v = keep(masks[head], v_all)
                for n in range(LONG // tall):
                    rows = slice(n * tall, (n + 1) * tall)
                    if is_long:
                        out = attend_rows([q[rows]], [k_all], [v], slope, distance[rows, :])
                    else:
                        out = attend_rows(
                            tiles(q, SHORT), tiles(k_all, SHORT), tiles(v, SHORT), slope, distance[:SHORT, :SHORT]
                        )
                    totals[n] = totals[n] + out[0]
                    logs[rows, :] = jnp.where(lane == pair * 2 + head, out[1], logs[rows, :])
            for n in range(LONG // tall):
                context[n * tall : (n + 1) * tall, pair_cols(0, pair)] = totals[n].astype(BF16)
            return 0

        lax.fori_loop(0, D // 2 // PAIR, one_pair, 0)

    logs[...] = jnp.zeros_like(logs)
    flag = flags[place[1]]

    @pl.when(flag > 0)
    def _():
        run(True)

    @pl.when(flag <= 0)
    def _():
        run(False)


def back_rows(queries, keys, values, d_rows, log_rows, slope, away, scaled_keys):
    s = jnp.concatenate([scores_of(q, k, slope, away) for q, k in zip(queries, keys)], axis=0)
    p = jnp.exp(s - log_rows)
    d_p = jnp.concatenate([contract_cols(d, v) for d, v in zip(d_rows, values)], axis=0)
    d_s = (p * (d_p - jnp.sum(p * d_p, axis=-1, keepdims=True))).astype(BF16)
    p = p.astype(BF16)
    tall = queries[0].shape[0]
    d_s, p = tiles(d_s, tall), tiles(p, tall)
    d_q = jnp.concatenate([dot(d, k) for d, k in zip(d_s, scaled_keys)], axis=0)
    d_k = [dot(q.T, d) for q, d in zip(queries, d_s)]
    d_v = [dot(d.T, w) for d, w in zip(d_rows, p)]
    return d_q, d_k, d_v


def attend_back_kernel(
    pairs, flags, slopes, mixed_own, mixed_partner, d_own, d_partner, logs_own, logs_partner, d_query, d_key, d_value, distance
):
    block = pl.program_id(0)
    masks = lane_masks()
    scale = HEAD_DIM**-0.5

    @pl.when(block == 0)
    def _():
        fill_distance(distance)

    def run(is_long):
        tall = 2 * SHORT if is_long else LONG
        logs = jnp.where(block == 0, logs_own[...], logs_partner[...])
        lane = lax.broadcasted_iota(jnp.int32, (1, 128), 1)

        def one_pair(place, _):
            pair = pairs[0] + place
            q_all, k_all, v_all = (
                jnp.where(block == 0, mixed_own[:, cols], mixed_partner[:, cols])
                for cols in (pair_cols(part, pair) for part in range(3))
            )
            d_all = jnp.where(block == 0, d_own[:, pair_cols(0, pair)], d_partner[:, pair_cols(0, pair)])
            d_q, d_k, d_v = [0.0] * (LONG // tall), 0.0, 0.0
            for head in range(2):
                slope = slopes[pair * 2 + head]
                q = (keep(masks[head], q_all) * scale).astype(BF16)
                k = (keep(masks[head], k_all) * scale).astype(BF16)
                d_c = keep(masks[head], d_all)
                log_all = jnp.sum(jnp.where(lane == pair * 2 + head, logs, 0.0), axis=-1, keepdims=True)
                for n in range(LONG // tall):
                    rows = slice(n * tall, (n + 1) * tall)
                    if is_long:
                        out = back_rows(
                            [q[rows]], [k_all], [v_all], [d_c[rows]], log_all[rows], slope, distance[rows, :], [k]
                        )
                        new_k, new_v = out[1][0], out[2][0]
                    else:
                        out = back_rows(
                            tiles(q, SHORT),
                            tiles(k_all, SHORT),
                            tiles(v_all, SHORT),
                            tiles(d_c, SHORT),
                            log_all,
                            slope,
                            distance[:SHORT, :SHORT],
                            tiles(k, SHORT),
                        )
                        new_k, new_v = (jnp.concatenate(part, axis=1) for part in out[1:])
                    d_q[n] = d_q[n] + out[0]
                    d_k, d_v = d_k + new_k, d_v + new_v
            cols = pair_cols(0, place)
            for n in range(LONG // tall):
                d_query[n * tall : (n + 1) * tall, cols] = d_q[n].astype(BF16)
            d_key[:, cols] = d_k.T.astype(BF16)
            d_value[:, cols] = d_v.T.astype(BF16)
            return 0

        lax.fori_loop(0, len(pairs), one_pair, 0)

    @pl.when(flags[block] > 0)
    def _():
        run(True)

    @pl.when(flags[block] <= 0)
    def _():
        run(False)


def spread(rows):
    center = jnp.mean(rows, axis=-1, keepdims=True)
    shifted = rows - center
    inverse = lax.rsqrt(jnp.mean(shifted * shifted, axis=-1, keepdims=True) + 1e-05)
    return shifted * inverse, inverse


def norm_back(e, unit, inverse):
    mean_e = jnp.mean(e, axis=-1, keepdims=True)
    mean_en = jnp.mean(e * unit, axis=-1, keepdims=True)
    return (e - mean_e - unit * mean_en) * inverse


def first_norm_kernel(place, tokens, ctx_mine, ctx_other, w_mine, w_other, norms, unit, inverse, low):
    core = place[0]
    half = w_mine.shape[0] // 2
    wide = w_mine.shape[2]

    def branch(weight):
        near = weight[pl.ds(core * half, half)].reshape(D // 2, wide)
        far = weight[pl.ds((1 - core) * half, half)].reshape(D // 2, wide)
        return dot(ctx_mine[...], near) + dot(ctx_other[...], far)

    mine, other = branch(w_mine), branch(w_other)
    first = core == 0
    added = jnp.concatenate([jnp.where(first, mine, other), jnp.where(first, other, mine)], axis=1)
    n, inv = spread(tokens[...].astype(F32) + added)
    unit[...] = n
    inverse[...] = inv
    low[...] = (n * norms[0:1, :] + norms[2:3, :]).astype(BF16)


def gelu_parts(x):
    t = 1.0 / (1.0 + (0.3275911 * 0.5**0.5) * jnp.abs(x))
    poly = t * (
        0.254829592 + t * (-0.284496736 + t * (1.421413741 + t * (-1.453152027 + t * 1.061405429)))
    )
    bell = jnp.exp(-0.5 * (x * x))
    tail = 0.5 * poly * bell
    phi = jnp.where(x >= 0, 1.0 - tail, tail)
    return x * phi, phi + x * bell * 0.3989422804014327


def columns_of(weight, half, span):
    count = weight.shape[0] // 2
    return weight[half * count : (half + 1) * count, :, span].reshape(D, span.stop - span.start)


def up_kernel(steps, pieces, table, own, partner, *refs):
    i = pl.program_id(0)
    parts = refs[: 2 * pieces]
    product, active, slope, gate_w, value_w = refs[2 * pieces :]

    @pl.when(i == 0)
    def _():
        fill_blocks(table, parts[:pieces], gate_w)
        fill_blocks(table, parts[pieces:], value_w)

    rows = pick_rows(i, steps, own, partner)
    width = gate_w.shape[2]
    for half in range(2):
        for start in range(0, width, 256):
            span = slice(start, start + 256)
            out = slice(half * width + start, half * width + start + 256)
            gate = dot(rows, columns_of(gate_w, half, span))
            up = dot(rows, columns_of(value_w, half, span))
            act, grad = gelu_parts(gate)
            product[:, out] = (act * up).astype(BF16)
            active[:, out] = act.astype(BF16)
            slope[:, out] = (up * grad).astype(BF16)


def down_kernel(steps, table, product, *refs):
    i = pl.program_id(0)
    own, partner, down_w = refs[-3:]

    @pl.when(i == 0)
    def _():
        fill_blocks(table, refs[:-3], down_w)

    width = down_w.shape[2]
    total = 0.0
    for half in range(2):
        total = total + contract_cols(product[:, half * width : (half + 1) * width], columns_of(down_w, half, slice(0, width)))

    @pl.when(i < steps)
    def _():
        own[...] = total

    @pl.when(i >= steps)
    def _():
        partner[...] = total.astype(BF16)


def second_norm_kernel(unit_one, norms, part_own, part_got, cotangent, out, d_z, d_ffn, sums):
    normed = unit_one[...] * norms[0:1, :] + norms[2:3, :]
    n, inv = spread(normed + (part_own[...] + part_got[...].astype(F32)))
    gain = norms[1:2, :]
    out[...] = (n * gain + norms[3:4, :]).astype(BF16)
    c = cotangent[...].astype(F32)
    back = norm_back(gain * c, n, inv)
    d_z[...] = back
    d_ffn[...] = back.astype(BF16)
    add_sums(sums, c * n, c)


def add_sums(sums, gain_terms, bias_terms):
    @pl.when(pl.program_id(0) == 0)
    def _():
        sums[...] = jnp.zeros_like(sums)

    sums[0:1, :] += jnp.sum(gain_terms, axis=0, keepdims=True)
    sums[1:2, :] += jnp.sum(bias_terms, axis=0, keepdims=True)


def ffn_back_kernel(
    steps, own, partner, down_w, gate_w, value_w, active, slope, d_gate, d_up, back_own, back_partner
):
    i = pl.program_id(0)
    rows = pick_rows(i, steps, own, partner)
    width = down_w.shape[2]
    total = jnp.zeros((ROWS, D), F32)
    for half in range(2):
        for start in range(0, width, 256):
            span = slice(start, start + 256)
            out = slice(half * width + start, half * width + start + 256)
            d_product = dot(rows, columns_of(down_w, half, span))
            dg = (d_product * slope[:, out].astype(F32)).astype(BF16)
            du = (d_product * active[:, out].astype(F32)).astype(BF16)
            d_gate[:, out] = dg
            d_up[:, out] = du
            total = total + contract_cols(dg, columns_of(gate_w, half, span))
            total = total + contract_cols(du, columns_of(value_w, half, span))

    @pl.when(i < steps)
    def _():
        back_own[...] = total

    @pl.when(i >= steps)
    def _():
        back_partner[...] = total.astype(BF16)


def weight_grad_kernel(table, left_own, left_partner, right_a, right_b, near, far, blocks):
    i = pl.program_id(0)
    rows = left_own.shape[0]
    count, tall, cols = blocks.shape
    for half, right in enumerate((right_a, right_b)):
        value = contract_rows(left_own[...], right[:rows, :]) + contract_rows(left_partner[...], right[rows:, :])
        value = value.astype(BF16).reshape(count // 2, tall, cols)
        blocks[half * (count // 2) : (half + 1) * (count // 2)] = value
    span = pl.ds(pl.multiple_of(i * cols, cols), cols)
    for k in range(count):
        target = near if k < count // 2 else far
        target[k % (count // 2), :, span] = blocks[table[k]]


def first_norm_back_kernel(
    place,
    unit_ref,
    inverse,
    norms,
    d_z,
    part_own,
    part_got,
    ctx_mine,
    ctx_other,
    w_mine,
    w_other,
    d_hidden,
    dctx_mine,
    dctx_other,
    grad_keep,
    grad_send,
    sums,
    grad,
):
    core = place[0]
    first = core == 0
    unit = unit_ref[...]
    d_normed = d_z[...] + (part_own[...] + part_got[...].astype(F32))
    back = norm_back(norms[0:1, :] * d_normed, unit, inverse[...])
    low = back.astype(BF16)
    d_hidden[...] = back
    add_sums(sums, d_normed * unit, d_normed)
    half, wide = w_mine.shape[0] // 2, w_mine.shape[2]
    low_mine = jnp.where(first, low[:, :wide], low[:, wide:])
    low_other = jnp.where(first, low[:, wide:], low[:, :wide])
    for head_core, out in ((core, dctx_mine), (1 - core, dctx_other)):
        near = w_mine[pl.ds(head_core * half, half)].reshape(D // 2, wide)
        far = w_other[pl.ds(head_core * half, half)].reshape(D // 2, wide)
        out[...] = (contract_cols(low_mine, near) + contract_cols(low_other, far)).astype(BF16)

    @pl.when(pl.program_id(0) == 0)
    def _():
        grad[...] = jnp.zeros_like(grad)

    shape = (half,) + grad.shape[1:]
    grad[pl.ds(core * half, half)] += contract_rows(ctx_mine[...], low).reshape(shape)
    grad[pl.ds((1 - core) * half, half)] += contract_rows(ctx_other[...], low).reshape(shape)

    @pl.when(pl.program_id(0) == pl.num_programs(0) - 1)
    def _():
        left, right = grad[:, :, :wide], grad[:, :, wide:]
        grad_keep[...] = jnp.where(first, left, right)
        grad_send[...] = jnp.where(first, right, left).astype(BF16)


def qkv_grad_kernel(table, left_own, left_partner, d_query, d_key, d_value, *refs):
    i = pl.program_id(0)
    near, far, blocks = refs[-3:]
    extra = refs[:-3]
    rows = left_own.shape[0]
    count, tall, cols = blocks.shape
    for g, right in enumerate((d_query, d_key, d_value)):

        @pl.when(i == g)
        def _():
            value = contract_rows(left_own[...], right[:rows, :]) + contract_rows(left_partner[...], right[rows:, :])
            blocks[...] = value.astype(BF16).reshape(blocks.shape)
            for k in range(count):
                target, place = (near if k < count // 2 else far), table[k]
                target[k % (count // 2), :, g * cols : (g + 1) * cols] = blocks[place]
                if g == 0:
                    start = 3 * cols
                    for more in extra:
                        stop = start + more.shape[2]
                        target[k % (count // 2), :, start:stop] = more[place]
                        start = stop


def input_grad_kernel(steps, parts, *refs):
    i = pl.program_id(0)
    weight, own, partner = refs[-3:]
    total = 0.0
    for n, first in enumerate(parts):
        for g in range(3):
            left = refs[3 * n + g]
            start = g * (D // 2) + first * PAIR
            tile = weight[:, :, start : start + left.shape[1]].reshape(D, left.shape[1])
            total = total + contract_cols(left[...], tile)

    @pl.when(i < steps)
    def _():
        own[...] = total

    @pl.when(i >= steps)
    def _():
        partner[...] = total.astype(BF16)


def by_core(core, mine, other, axis):
    first = core == 0
    return jnp.stack([jnp.where(first, mine, other), jnp.where(first, other, mine)], axis=axis)


def half_of(core, halves, axis):
    zero, one = (lax.index_in_dim(halves, k, axis, keepdims=False) for k in range(2))
    first = core == 0
    return jnp.where(first, zero, one), jnp.where(first, one, zero)


def plane_shards(
    wide,
    narrow,
    tokens,
    w_qkv,
    w_out,
    w_gate,
    w_value,
    w_down,
    norm_gains,
    norm_biases,
    long_count,
    cotangent,
):
    plane = Plane(wide, narrow)
    swap = plane.swap
    core, y_here = plane.core, plane.y
    rows = tokens.shape[0]
    steps = rows // ROWS
    tall = w_qkv.shape[0]
    blocks = wide * narrow // 2
    z_size = plane.size["z"]
    head_cols = D // 2
    width = w_gate.shape[1] // 2
    hidden = 2 * width
    pairs = head_cols // PAIR
    qkv_to = plane.tables(("z", "a", "b"), lambda z, x, y: (z * 2 + x) * 2 + y)
    ffn_to = plane.tables(("z", "a", "b"), lambda z, x, y: y * (2 * z_size) + z * 2 + x)
    place = jnp.reshape(core, (1,)).astype(jnp.int32)
    first = core == 0

    def wholes(arrays):
        return [(v, whole(v.shape)) for v in arrays]

    def step_rows(cols):
        return pl.BlockSpec((ROWS, cols), lambda i: (i, 0))

    norm_cols = jnp.concatenate([norm_gains, norm_biases], axis=0).T
    norm_cols = jnp.pad(norm_cols, ((0, 0), (0, 128 - norm_cols.shape[1])))
    head_shape = (tall, 4 * head_cols + 128)
    head_part, head_send = kernel_call(
        split_kernel,
        (1,),
        [(place, smem())] + wholes([w_qkv, w_out, norm_cols]),
        [(head_shape, BF16, whole(head_shape))] * 2,
        name="split",
    )
    head_got = swap(head_send, "core")
    head_part = jnp.where(y_here == core, head_part, head_got)
    qkv_z = plane.gather_z(head_part)
    ffn_parts = [w_gate, w_value, w_down.T]
    ffn_other = jnp.concatenate([jnp.where(first, v[:, width:], v[:, :width]) for v in ffn_parts], axis=1)
    ffn_got = swap(after(ffn_other, head_part), "core")
    tokens_other = swap(after(tokens, head_part), "core")
    flag = jnp.broadcast_to(long_count.astype(F32), (8, 128))
    flag_got = swap(after(flag, head_part), "core")
    flags = jnp.stack([long_count[0, 0], flag_got[0, 0].astype(jnp.int32)])
    slopes = lax.dynamic_slice_in_dim(alibi_slopes(HEADS), core * (HEADS // 2), HEADS // 2)

    def ffn_chip(n):
        v, got = ffn_parts[n], ffn_got[:, n * width : (n + 1) * width]
        mine = jnp.where(first, v[:, :width], v[:, width:])
        return jnp.concatenate([jnp.where(first, mine, got), jnp.where(first, got, mine)], axis=0)

    def doubled(value, step, *events):
        got = swap(value, "z", step)
        return jnp.concatenate(lax.optimization_barrier((value, got) + events)[:2], axis=0)

    def along_plane(held):
        near = swap(held, "a")
        return held, near, swap(held, "b")

    def joined(value, got):
        return jnp.concatenate([value, got], axis=0)

    gate_one, value_one, down_one = (ffn_chip(n)[None] for n in range(3))
    gate_got = swap(gate_one, "z", 1)
    qkv_z, gate_got, tokens_other, flags = fence(qkv_z, gate_got, tokens_other, flags)
    gate_two = joined(gate_one, gate_got)

    head_near, head_far = swap(qkv_z, "a"), swap(qkv_z, "b")
    gate_got = swap(gate_two, "z", 2)
    value_got = swap(after(value_one, qkv_z), "z", 1)
    down_got = swap(after(down_one, qkv_z), "z", 1)
    head_near, head_far, gate_got, value_got, down_got = fence(head_near, head_far, gate_got, value_got, down_got)
    gate_z, value_two, down_two = joined(gate_two, gate_got), joined(value_one, value_got), joined(down_one, down_got)

    head_last = swap(head_near, "b")
    gate_near, gate_far = swap(gate_z, "a"), swap(gate_z, "b")
    value_got = swap(value_two, "z", 2)
    head_last, gate_near, gate_far, value_got, down_two = fence(head_last, gate_near, gate_far, value_got, down_two)
    value_z = joined(value_two, value_got)
    qkv_blocks = [qkv_z, head_near, head_far, head_last]

    gate_last = swap(gate_near, "b")
    value_near, value_far = swap(value_z, "a"), swap(value_z, "b")
    down_got = swap(down_two, "z", 2)
    block_row = (blocks, tall)
    mixed_own, mixed_partner, qkv_w, out_mine, norm_table = kernel_call(
        functools.partial(qkv_kernel, steps, 3, len(qkv_blocks)),
        (2 * steps,),
        [
            (qkv_to, smem()),
            (tokens, own_rows(steps, D)),
            (tokens_other, partner_rows(steps, D)),
        ]
        + wholes(qkv_blocks),
        [((rows, 3 * head_cols), BF16, own_rows(steps, 3 * head_cols))]
        + [((rows, 3 * head_cols), BF16, partner_rows(steps, 3 * head_cols))]
        + [(block_row + (n,), BF16, whole(block_row + (n,))) for n in (3 * head_cols, head_cols, 128)],
        flops=2 * 2 * rows * D * 3 * head_cols,
        name="mixed",
    )
    norms = norm_table.reshape(D, 128)[:, :4].T.astype(F32)

    def attend(block, mixed):
        return kernel_call(
            attend_kernel,
            (1,),
            [(jnp.array([0, block], jnp.int32), smem()), (flags, smem()), (slopes, smem())] + wholes([mixed]),
            [((rows, head_cols), BF16, whole((rows, head_cols))), ((rows, 128), F32, whole((rows, 128)))],
            scratch=[pltpu.VMEM((LONG, LONG), F32)],
            flops=4 * rows * LONG * D,
            name="attend",
            room=12,
        )

    ctx_send, logs_partner = attend(1, mixed_partner)
    ctx_other = swap(ctx_send, "core")
    ctx_mine, logs_own = attend(0, after(mixed_own, ctx_send))
    out_other = swap(after(out_mine, ctx_send), "core")
    gate_last, value_near, value_far, down_got, ctx_mine, ctx_other, out_other = fence(
        gate_last, value_near, value_far, down_got, ctx_mine, ctx_other, out_other
    )
    down_z = joined(down_two, down_got)
    gate_blocks = [gate_z, gate_near, gate_far, gate_last]

    value_last = swap(value_near, "b")
    down_near, down_far = swap(down_z, "a"), swap(down_z, "b")
    unit_one, inverse_one, low = kernel_call(
        first_norm_kernel,
        (steps,),
        [
            (place, smem()),
            (tokens, step_rows(D)),
            (ctx_mine, step_rows(head_cols)),
            (ctx_other, step_rows(head_cols)),
        ]
        + wholes([out_mine, out_other, norms]),
        [
            ((rows, D), F32, step_rows(D)),
            ((rows, 1), F32, step_rows(1)),
            ((rows, D), BF16, step_rows(D)),
        ],
        flops=2 * rows * D * D,
        name="first_norm",
    )
    low_other = swap(low, "core")
    value_last, down_near, down_far, low, low_other = fence(value_last, down_near, down_far, low, low_other)
    value_blocks = [value_z, value_near, value_far, value_last]
    down_blocks = [down_z, down_near, down_far, swap(down_near, "b")]

    w_shape = (blocks, 2 * tall, width)
    product, active, slope, gate_w, value_w = kernel_call(
        functools.partial(up_kernel, steps, len(gate_blocks)),
        (2 * steps,),
        [
            (ffn_to, smem()),
            (low, own_rows(steps, D)),
            (low_other, partner_rows(steps, D)),
        ]
        + wholes(gate_blocks + value_blocks),
        [((2 * rows, hidden), BF16, step_rows(hidden))] * 3 + [(w_shape, BF16, whole(w_shape))] * 2,
        flops=2 * 2 * rows * D * 2 * hidden,
        name="up",
    )
    part_own, part_send, down_w = kernel_call(
        functools.partial(down_kernel, steps),
        (2 * steps,),
        [(ffn_to, smem()), (product, step_rows(hidden))] + wholes(down_blocks),
        [
            ((rows, D), F32, own_rows(steps, D)),
            ((rows, D), BF16, partner_rows(steps, D)),
            (w_shape, BF16, whole(w_shape)),
        ],
        flops=2 * 2 * rows * D * hidden,
        name="down",
    )
    part_got = swap(part_send, "core")
    layer_out, d_z, d_ffn, sums_two = kernel_call(
        second_norm_kernel,
        (steps,),
        [(unit_one, step_rows(D))]
        + wholes([norms])
        + [(part_own, step_rows(D)), (part_got, step_rows(D)), (cotangent, step_rows(D))],
        [
            ((rows, D), BF16, step_rows(D)),
            ((rows, D), F32, step_rows(D)),
            ((rows, D), BF16, step_rows(D)),
            ((8, D), F32, whole((8, D))),
        ],
        name="second_norm",
    )
    d_ffn_other = swap(d_ffn, "core")

    def weight_grad(left, left_other, right):
        near = (blocks // 2, 2 * tall, width)
        cols = width // 3
        return kernel_call(
            weight_grad_kernel,
            (3,),
            [
                (ffn_to, smem()),
                (left, whole((rows, D))),
                (left_other, whole((rows, D))),
                (right, pl.BlockSpec((2 * rows, cols), lambda i: (0, i))),
                (right, pl.BlockSpec((2 * rows, cols), lambda i: (0, 3 + i))),
            ],
            [(near, BF16, whole(near))] * 2,
            scratch=[pltpu.VMEM((blocks, 2 * tall, cols), BF16)],
            flops=2 * 2 * rows * D * hidden,
            name="weight_grad",
        )

    def added(keep, got):
        return (keep.astype(F32) + got.astype(F32)).astype(BF16)

    def halves(held):
        count = held.shape[0] // 2
        return held[:count], held[count:]

    down_keep, down_send = weight_grad(d_ffn, d_ffn_other, product)
    d_gate, d_up, back_own, back_send = kernel_call(
        functools.partial(ffn_back_kernel, steps),
        (2 * steps,),
        [(after(d_ffn, down_send), own_rows(steps, D)), (d_ffn_other, partner_rows(steps, D))]
        + wholes([down_w, gate_w, value_w])
        + [(active, step_rows(hidden)), (slope, step_rows(hidden))],
        [((2 * rows, hidden), BF16, step_rows(hidden))] * 2
        + [((rows, D), F32, own_rows(steps, D)), ((rows, D), BF16, partner_rows(steps, D))],
        flops=3 * 2 * 2 * rows * D * hidden,
        name="ffn_back",
    )
    down_got, back_send, d_gate = fence(swap(down_send, "b"), back_send, d_gate)
    down_keep, down_send = halves(added(down_keep, down_got))

    back_got = swap(back_send, "core")
    down_got = swap(down_send, "a")
    gate_keep, gate_send = weight_grad(after(low, down_send), low_other, d_gate)
    d_hidden, dctx_mine, dctx_send, out_keep, out_send, sums_one = kernel_call(
        first_norm_back_kernel,
        (steps,),
        [
            (place, smem()),
            (unit_one, step_rows(D)),
            (inverse_one, step_rows(1)),
            (norms, whole(norms.shape)),
            (d_z, step_rows(D)),
            (back_own, step_rows(D)),
            (after(back_got, gate_send), step_rows(D)),
            (ctx_mine, step_rows(head_cols)),
            (ctx_other, step_rows(head_cols)),
        ]
        + wholes([out_mine, out_other]),
        [
            ((rows, D), F32, step_rows(D)),
            ((rows, head_cols), BF16, step_rows(head_cols)),
            ((rows, head_cols), BF16, step_rows(head_cols)),
            (out_mine.shape, F32, whole(out_mine.shape)),
            (out_mine.shape, BF16, whole(out_mine.shape)),
            ((8, D), F32, whole((8, D))),
        ],
        scratch=[pltpu.VMEM((blocks, tall, D), F32)],
        flops=2 * 2 * rows * D * D,
        name="first_norm_back",
    )
    down_got, d_hidden, dctx_send, out_send, gate_send = fence(down_got, d_hidden, dctx_send, out_send, gate_send)
    down_keep, down_send = halves(added(down_keep, down_got))

    gate_got = swap(gate_send, "b")
    down_got = swap(down_send, "z", 2)
    dctx_got, out_got = swap(dctx_send, "core"), swap(out_send, "core")
    value_keep, value_send = weight_grad(after(low, down_send), low_other, d_up)
    dctx_got, out_got, value_send = fence(dctx_got, out_got, value_send)
    out_sum = (out_keep + out_got.astype(F32)).astype(BF16)
    sums = jnp.stack([sums_one[0], sums_two[0], sums_one[1], sums_two[1]], axis=1)
    norm_grad = jnp.pad(sums, ((0, 0), (0, 124))).astype(BF16).reshape(blocks, tall, 128)

    def attend_back(chosen, d_mine):
        cols = len(chosen) * PAIR
        return kernel_call(
            functools.partial(attend_back_kernel, chosen),
            (2,),
            [(flags, smem()), (slopes, smem())]
            + wholes([mixed_own, mixed_partner, d_mine, dctx_got, logs_own, logs_partner]),
            [((2 * rows, cols), BF16, pl.BlockSpec((rows, cols), lambda b: (b, 0)))] * 3,
            scratch=[pltpu.VMEM((LONG, LONG), F32)],
            flops=10 * 2 * rows * LONG * cols * 2,
            name="attend_back",
            room=16,
        )

    def qkv_grad(left, d_parts, extra):
        cols = d_parts[0].shape[1]
        shape = (blocks // 2, tall, 3 * cols + sum(v.shape[2] for v in extra))
        return kernel_call(
            qkv_grad_kernel,
            (3,),
            [(qkv_to, smem())] + wholes([left, tokens_other] + list(d_parts) + extra),
            [(shape, BF16, whole(shape))] * 2,
            scratch=[pltpu.VMEM(block_row + (cols,), BF16)],
            flops=2 * 2 * rows * D * 3 * cols,
            name="qkv_grad",
        )

    split = pairs - 1
    d_first = attend_back(tuple(range(split)), after(dctx_mine, value_send))
    gate_got, down_got, d_first, value_send = fence(gate_got, down_got, d_first, value_send)
    gate_keep, gate_send = halves(added(gate_keep, gate_got))
    down_keep, down_send = halves(added(down_keep, down_got))

    gate_got = swap(gate_send, "a")
    value_got = swap(value_send, "b")
    down_got = swap(down_send, "z", 1)
    keep_one, send_one = qkv_grad(after(tokens, gate_send), d_first, [out_sum, norm_grad])
    d_last = attend_back(tuple(range(split, pairs)), after(dctx_mine, send_one))
    keep_two, send_two = qkv_grad(tokens, d_last, [])
    gate_got, value_got, down_got, send_two, send_one = fence(gate_got, value_got, down_got, send_two, send_one)
    grad_down = down_keep[0].astype(F32) + down_got[0].astype(F32)
    gate_keep, gate_send = halves(added(gate_keep, gate_got))
    value_keep, value_send = halves(added(value_keep, value_got))

    one_got, two_got = swap(send_one, "b"), swap(send_two, "b")
    value_got = swap(value_send, "a")
    gate_got = swap(gate_send, "z", 2)
    in_own, in_send = kernel_call(
        functools.partial(input_grad_kernel, steps, (0, split)),
        (2 * steps,),
        [(v, step_rows(v.shape[1])) for v in [after(d_first[0], value_send)] + list(d_first[1:]) + list(d_last)]
        + wholes([qkv_w]),
        [((rows, D), F32, own_rows(steps, D)), ((rows, D), BF16, partner_rows(steps, D))],
        flops=2 * 2 * rows * D * 3 * head_cols,
        name="input_grad",
    )
    input_grad = d_hidden + in_own + swap(in_send, "core").astype(F32)

    one_got, two_got, value_got, gate_got, input_grad = fence(one_got, two_got, value_got, gate_got, input_grad)
    one_keep, one_send = halves(added(keep_one, one_got))
    two_keep, two_send = halves(added(keep_two, two_got))
    value_keep, value_send = halves(added(value_keep, value_got))
    gate_keep, gate_send = halves(added(gate_keep, gate_got))

    one_got, two_got = swap(one_send, "a"), swap(two_send, "a")
    value_got = swap(value_send, "z", 2)
    gate_got = swap(gate_send, "z", 1)
    one_got, two_got, value_got, gate_got = fence(one_got, two_got, value_got, gate_got)
    one_a, two_a = added(one_keep, one_got), added(two_keep, two_got)
    grad_gate = gate_keep[0].astype(F32) + gate_got[0].astype(F32)
    value_keep, value_send = halves(added(value_keep, value_got))
    value_got = swap(value_send, "z", 1)
    grad_value = value_keep[0].astype(F32) + value_got[0].astype(F32)

    def in_order(mine, other):
        return [jnp.where(first, mine, other), jnp.where(first, other, mine)]

    def ffn_piece(total):
        mine, other = half_of(core, total.astype(BF16).reshape(2, tall, width), 0)
        return jnp.concatenate(in_order(mine, swap(other, "core")), axis=1).astype(F32)

    gate_piece, value_piece = ffn_piece(grad_gate), ffn_piece(grad_value)
    down_piece = ffn_piece(grad_down).T
    parts, cols = [], split * PAIR
    for n in range(3):
        parts += [one_a[:, :, n * cols : (n + 1) * cols], two_a[:, :, n * PAIR : (n + 1) * PAIR]]
    head_sum = plane.sum_z(jnp.concatenate(parts + [one_a[:, :, 3 * cols :]], axis=2)).astype(BF16)
    head_sum = after(head_sum, gate_piece, value_piece, down_piece)
    both = by_core(y_here, head_sum, swap(head_sum, "y"), 0)
    mine, other = half_of(core, both, 0)
    got = swap(other, "core")
    four = 4 * head_cols
    pieces = []
    for n in range(4):
        span = slice(n * head_cols, (n + 1) * head_cols)
        pieces += in_order(mine[:, span], got[:, span])
    qkv_piece = jnp.concatenate(pieces[:6], axis=1).astype(F32)
    out_piece = jnp.concatenate(pieces[6:], axis=1).astype(F32)
    norm_piece = (mine[:, four : four + 4].astype(F32) + got[:, four : four + 4].astype(F32)).T
    return (
        layer_out,
        input_grad,
        qkv_piece,
        out_piece,
        gate_piece,
        value_piece,
        down_piece,
        norm_piece[:2],
        norm_piece[2:],
    )


def solution(mesh):
    wide, narrow = mesh.shape["wide"], mesh.shape["narrow"]
    placed = (
        P(("wide", "narrow"), None),
        P("wide", None),
        P("wide", None),
        P("wide", "narrow"),
        P("wide", "narrow"),
        P("narrow", "wide"),
        P(None, "wide"),
        P(None, "wide"),
        P("wide", "narrow"),
        P(("wide", "narrow"), None),
    )
    if narrow == 2 and wide % 16 == 0 and D % (16 * wide) == 0:
        body = functools.partial(plane_shards, wide, narrow)
    else:
        body = general_shards
    return jax.shard_map(
        body,
        mesh=mesh,
        in_specs=placed,
        out_specs=(
            P(("wide", "narrow"), None),
            P(("wide", "narrow"), None),
            P("wide", None),
            P("wide", None),
            P("wide", "narrow"),
            P("wide", "narrow"),
            P("narrow", "wide"),
            P(None, "wide"),
            P(None, "wide"),
        ),
        check_vma=False,
    )
```

```python
import functools

import jax
import jax.numpy as jnp
import numpy as np
from jax import lax
from jax.experimental import pallas as pl
from jax.experimental.pallas import tpu as pltpu
from jax.sharding import PartitionSpec as P

D = 768
HEADS = 12
HEAD_DIM = 64
LONG = 512
SHORT = 128


def norm_rows(values, gain_row, bias_row):
    center = jnp.mean(values, axis=-1, keepdims=True)
    shifted = values - center
    spread = jnp.mean(shifted * shifted, axis=-1, keepdims=True)
    return shifted * lax.rsqrt(spread + 1e-05) * gain_row + bias_row


def gelu_product(gate_in, value_in):
    return jax.nn.gelu(gate_in, approximate=False) * value_in


def alibi_slopes(heads):
    power = 1 << heads.bit_length() - 1
    first = [2.0 ** (-8.0 * (index + 1) / power) for index in range(power)]
    second = [2.0 ** (-8.0 * (2 * index + 1) / (2 * power)) for index in range(heads - power)]
    return jnp.array(first + second, dtype=jnp.float32)


def alibi_bias(span, heads):
    position = jnp.arange(span)
    distance = jnp.abs(position[:, None] - position[None, :]).astype(jnp.float32)
    slopes = alibi_slopes(heads)
    return slopes[:, None, None] * distance


def block_scores(query_g, key_g, span):
    width = query_g.shape[-1]
    scores = jnp.einsum(
        "bqhd,bkhd->bhqk", query_g, key_g, preferred_element_type=jnp.float32
    ) * width ** (-0.5)
    return scores - alibi_bias(span, query_g.shape[2])


def attend(query_rows, key_rows, value_rows, span):
    rows, heads, width = query_rows.shape
    groups = rows // span
    shape_g = (groups, span, heads, width)
    query_g = query_rows.reshape(shape_g)
    key_g = key_rows.reshape(shape_g)
    value_g = value_rows.reshape(shape_g)
    scores = block_scores(query_g, key_g, span)
    top = jnp.max(scores, axis=-1, keepdims=True)
    expd = jnp.exp(scores - top)
    total = jnp.sum(expd, axis=-1, keepdims=True)
    probs_low = (expd / total).astype(jnp.bfloat16)
    context = jnp.einsum("bhqk,bkhd->bqhd", probs_low, value_g, preferred_element_type=jnp.float32)
    log_total = jnp.transpose((top + jnp.log(total))[..., 0], (0, 2, 1)).reshape(rows, heads)
    return (context.reshape(rows, heads * width), log_total)


def attend_back(query_rows, key_rows, value_rows, log_total, d_context, span):
    rows, heads, width = query_rows.shape
    groups = rows // span
    shape_g = (groups, span, heads, width)
    query_g = query_rows.reshape(shape_g)
    key_g = key_rows.reshape(shape_g)
    value_g = value_rows.reshape(shape_g)
    d_context_g = d_context.reshape(shape_g)
    lse_g = jnp.transpose(log_total.reshape(groups, span, heads), (0, 2, 1))
    scores = block_scores(query_g, key_g, span)
    probs = jnp.exp(scores - lse_g[..., None])
    probs_low = probs.astype(jnp.bfloat16)
    d_probs = jnp.einsum(
        "bqhd,bkhd->bhqk", d_context_g, value_g, preferred_element_type=jnp.float32
    )
    d_values = jnp.einsum(
        "bhqk,bqhd->bkhd", probs_low, d_context_g, preferred_element_type=jnp.float32
    )
    row_dot = jnp.sum(probs * d_probs, axis=-1, keepdims=True)
    d_scores = (probs * (d_probs - row_dot)).astype(jnp.bfloat16)
    scale = width ** (-0.5)
    d_queries = (
        jnp.einsum("bhqk,bkhd->bqhd", d_scores, key_g, preferred_element_type=jnp.float32) * scale
    )
    d_keys = (
        jnp.einsum("bhqk,bqhd->bkhd", d_scores, query_g, preferred_element_type=jnp.float32) * scale
    )
    return jnp.stack([d_queries, d_keys, d_values], axis=2).reshape(rows, 3, heads, width)


def contract_rows(left, right):
    return lax.dot_general(
        left, right, (((0,), (0,)), ((), ())), preferred_element_type=jnp.float32
    )


def contract_cols(left, right):
    return lax.dot_general(
        left, right, (((1,), (1,)), ((), ())), preferred_element_type=jnp.float32
    )


def general_shards(
    tokens, w_qkv, w_out, w_gate, w_value, w_down, norm_gains, norm_biases, long_count, cotangent
):
    gathered = (
        lax.all_gather(w_qkv, "wide", axis=0, tiled=True),
        lax.all_gather(w_out, "wide", axis=0, tiled=True),
        lax.all_gather(w_gate, "wide", axis=0, tiled=True),
        lax.all_gather(w_value, "wide", axis=0, tiled=True),
        lax.all_gather(w_down, "wide", axis=1, tiled=True),
        lax.all_gather(norm_gains, "wide", axis=1, tiled=True),
        lax.all_gather(norm_biases, "wide", axis=1, tiled=True),
    )
    full_qkv, full_out, wide_gate, wide_value, wide_down, gains_all, biases_all = gathered
    gains_f = gains_all.astype(jnp.float32)
    biases_f = biases_all.astype(jnp.float32)
    rows_dev = tokens.shape[0]
    n_blocks = rows_dev // LONG
    long_here = long_count[0, 0]
    tokens_f = tokens.astype(jnp.float32)
    mixed = jnp.dot(tokens, full_qkv, preferred_element_type=jnp.float32).astype(jnp.bfloat16)
    heads_view = mixed.reshape(n_blocks, LONG, 3, HEADS, HEAD_DIM)
    query_blk = heads_view[:, :, 0]
    key_blk = heads_view[:, :, 1]
    value_blk = heads_view[:, :, 2]
    block_ids = jnp.arange(n_blocks)

    def forward_block(entry):
        block_id, query_rows, key_rows, value_rows = entry
        return lax.cond(
            block_id < long_here,
            lambda operands: attend(operands[0], operands[1], operands[2], LONG),
            lambda operands: attend(operands[0], operands[1], operands[2], SHORT),
            (query_rows, key_rows, value_rows),
        )

    context_f, lse_rows = lax.map(forward_block, (block_ids, query_blk, key_blk, value_blk))
    context = context_f.reshape(rows_dev, D).astype(jnp.bfloat16)
    branch = jnp.dot(context, full_out, preferred_element_type=jnp.float32)
    hidden_in = tokens_f + branch
    normed = norm_rows(hidden_in, gains_f[0], biases_f[0])
    normed_low = normed.astype(jnp.bfloat16)
    all_rows = lax.all_gather(normed_low, "narrow", axis=0, tiled=True)
    gate = jnp.dot(all_rows, wide_gate, preferred_element_type=jnp.float32)
    value_up = jnp.dot(all_rows, wide_value, preferred_element_type=jnp.float32)
    product_f, pull_product = jax.vjp(gelu_product, gate, value_up)
    product = product_f.astype(jnp.bfloat16)
    ffn_out = lax.psum_scatter(
        jnp.dot(product, wide_down, preferred_element_type=jnp.float32),
        "narrow",
        scatter_dimension=0,
        tiled=True,
    )
    out_in = normed + ffn_out
    layer_out, pull_second = jax.vjp(norm_rows, out_in, gains_f[1], biases_f[1])
    d_out, d_gain_two, d_bias_two = pull_second(cotangent.astype(jnp.float32))
    d_ffn = d_out.astype(jnp.bfloat16)
    d_rows = lax.all_gather(d_ffn, "narrow", axis=0, tiled=True)
    grad_down = contract_rows(product, d_rows)
    d_product = contract_cols(d_rows, wide_down)
    d_gate, d_up = pull_product(d_product)
    d_gate_low = d_gate.astype(jnp.bfloat16)
    d_up_low = d_up.astype(jnp.bfloat16)
    grad_gate = contract_rows(all_rows, d_gate_low)
    grad_value = contract_rows(all_rows, d_up_low)
    d_normed = lax.psum_scatter(
        contract_cols(d_gate_low, wide_gate) + contract_cols(d_up_low, wide_value),
        "narrow",
        scatter_dimension=0,
        tiled=True,
    )
    d_normed_total = d_out + d_normed
    unused_out, pull_first = jax.vjp(norm_rows, hidden_in, gains_f[0], biases_f[0])
    d_hidden, d_gain_one, d_bias_one = pull_first(d_normed_total)
    d_branch = d_hidden.astype(jnp.bfloat16)
    grad_out = contract_rows(context, d_branch)
    d_context = contract_cols(d_branch, full_out).astype(jnp.bfloat16)
    d_context_blk = d_context.reshape(n_blocks, LONG, HEADS, HEAD_DIM)

    def backward_block(entry):
        block_id, query_rows, key_rows, value_rows, log_total, d_ctx = entry
        return lax.cond(
            block_id < long_here,
            lambda operands: attend_back(
                operands[0], operands[1], operands[2], operands[3], operands[4], LONG
            ),
            lambda operands: attend_back(
                operands[0], operands[1], operands[2], operands[3], operands[4], SHORT
            ),
            (query_rows, key_rows, value_rows, log_total, d_ctx),
        )

    d_mixed_f = lax.map(
        backward_block, (block_ids, query_blk, key_blk, value_blk, lse_rows, d_context_blk)
    )
    d_mixed = d_mixed_f.reshape(rows_dev, 3 * D).astype(jnp.bfloat16)
    grad_qkv = contract_rows(tokens, d_mixed)
    input_grad = d_hidden + contract_cols(d_mixed, full_qkv)
    grad_gains = jnp.stack([d_gain_one, d_gain_two])
    grad_biases = jnp.stack([d_bias_one, d_bias_two])
    pieces = (
        lax.psum_scatter(
            grad_qkv.astype(jnp.bfloat16), "wide", scatter_dimension=0, tiled=True
        ).astype(jnp.float32),
        lax.psum_scatter(
            grad_out.astype(jnp.bfloat16), "wide", scatter_dimension=0, tiled=True
        ).astype(jnp.float32),
        lax.psum_scatter(
            grad_gate.astype(jnp.bfloat16), "wide", scatter_dimension=0, tiled=True
        ).astype(jnp.float32),
        lax.psum_scatter(
            grad_value.astype(jnp.bfloat16), "wide", scatter_dimension=0, tiled=True
        ).astype(jnp.float32),
        lax.psum_scatter(
            grad_down.astype(jnp.bfloat16), "wide", scatter_dimension=1, tiled=True
        ).astype(jnp.float32),
        lax.psum_scatter(
            grad_gains.astype(jnp.bfloat16), "wide", scatter_dimension=1, tiled=True
        ).astype(jnp.float32),
        lax.psum_scatter(
            grad_biases.astype(jnp.bfloat16), "wide", scatter_dimension=1, tiled=True
        ).astype(jnp.float32),
    )
    qkv_piece, out_piece, gate_piece, value_piece, down_piece, gains_piece, biases_piece = pieces
    qkv_piece, out_piece, gains_piece, biases_piece = (
        lax.psum(qkv_piece.astype(jnp.bfloat16), "narrow").astype(jnp.float32),
        lax.psum(out_piece.astype(jnp.bfloat16), "narrow").astype(jnp.float32),
        lax.psum(gains_piece.astype(jnp.bfloat16), "narrow").astype(jnp.float32),
        lax.psum(biases_piece.astype(jnp.bfloat16), "narrow").astype(jnp.float32),
    )
    return (
        layer_out.astype(jnp.bfloat16),
        input_grad,
        qkv_piece,
        out_piece,
        gate_piece,
        value_piece,
        down_piece,
        gains_piece,
        biases_piece,
    )


AXES = ("wide", "narrow")
F32 = jnp.float32
BF16 = jnp.bfloat16
MIB = 1024 * 1024
RING = (0, 1, 3, 2)
PAIR = 2 * HEAD_DIM


def dot(left, right):
    return jnp.dot(left, right, preferred_element_type=F32)


class Plane:
    def __init__(self, wide, narrow):
        self.size = {"z": wide // 4, "ring": len(RING), "a": 2, "b": 2, "core": 2, "y": narrow}
        self.pairs = {}
        count = wide * narrow
        for dim, size in self.size.items():
            for step in range(1, size) if dim != "ring" else ():
                self.pairs[dim, step] = [(i, self.partner(i, dim, step)) for i in range(count)]
        after_z = {z: RING[(n + 1) % len(RING)] for n, z in enumerate(RING)}
        self.pairs["next", 1] = [(i, i % 8 + 8 * after_z[i // 8]) for i in range(count)]
        self.pairs["prev", 1] = [(j, i) for i, j in self.pairs["next", 1]]
        w = lax.axis_index("wide")
        self.z, self.x, self.core = w // 4, (w // 2) % 2, w % 2
        self.y = lax.axis_index("narrow")

    @staticmethod
    def partner(i, dim, step):
        z, x, c, y = i // 8, (i // 4) % 2, (i // 2) % 2, i % 2
        if dim == "z":
            z ^= step
        elif dim == "core":
            c ^= 1
        elif dim == "y" or (dim == "a") == (c == 1):
            y ^= 1
        else:
            x ^= 1
        return ((z * 2 + x) * 2 + c) * 2 + y

    def swap(self, value, dim, step=1):
        return lax.ppermute(value, AXES, self.pairs[dim, step])

    def gather_z(self, value):
        return jnp.stack([value] + [self.swap(value, "z", k) for k in range(1, self.size["z"])])

    def sum_z(self, held):
        total = held[0].astype(F32)
        for k in range(1, self.size["z"]):
            total = total + self.swap(held[k], "z", k).astype(F32)
        return total

    def tables(self, order, numbered):
        sizes = [self.size[dim] for dim in order]
        number = np.arange(int(np.prod(sizes)))
        rest, digit = number, {}
        for dim, size in zip(order, sizes):
            digit[dim] = rest % size
            rest = rest // size
        first = self.core == 0
        a_here = jnp.where(first, self.x, self.y)
        b_here = jnp.where(first, self.y, self.x)
        if "ring" in digit:
            at = sum(jnp.where(self.z == z, n, 0) for n, z in enumerate(RING))
            z = sum(jnp.where((at - digit["ring"]) % len(RING) == n, z, 0) for n, z in enumerate(RING))
        else:
            z = digit["z"] ^ self.z
        a = digit["a"] ^ a_here
        b = digit["b"] ^ b_here
        x, y = jnp.where(first, a, b), jnp.where(first, b, a)
        return numbered(z, x, y).astype(jnp.int32)


def after(value, *events):
    return lax.optimization_barrier((value,) + events)[0]


def fence(*values):
    return lax.optimization_barrier(values)


def smem():
    return pl.BlockSpec(memory_space=pltpu.SMEM)


def whole(shape):
    zeros = (0,) * len(shape)
    return pl.BlockSpec(tuple(shape), lambda *_: zeros)


def kernel_call(body, grid, ins, outs, scratch=(), flops=0, name=None, room=6, far=False):
    blocks = [(spec.block_shape, a.dtype) for a, spec in ins] + [(spec.block_shape, d) for _, d, spec in outs]
    held = sum(2 * int(np.prod(shape)) * np.dtype(d).itemsize for shape, d in blocks if shape is not None)
    held += sum(int(np.prod(v.shape)) * np.dtype(v.dtype).itemsize for v in scratch)
    size = sum(a.size * a.dtype.itemsize for a, _ in ins)
    size += sum(int(np.prod(s)) * np.dtype(d).itemsize for s, d, _ in outs)
    return pl.pallas_call(
        body,
        grid=grid,
        in_specs=[spec for _, spec in ins],
        out_specs=[spec for _, _, spec in outs],
        out_shape=[jax.ShapeDtypeStruct(s, d) for s, d, _ in outs],
        scratch_shapes=list(scratch),
        compiler_params=pltpu.CompilerParams(
            dimension_semantics=("arbitrary",) * len(grid), vmem_limit_bytes=held // 2 + room * MIB
        ),
        cost_estimate=pl.CostEstimate(flops=0, bytes_accessed=0, transcendentals=0),
        name=name,
    )(*[pltpu.with_memory_space_constraint(a, pltpu.HBM) if far and a.ndim > 1 else a for a, _ in ins])


ROWS = 256


def own_rows(steps, cols):
    return pl.BlockSpec((ROWS, cols), lambda i: (jnp.minimum(i, steps - 1), 0))


def partner_rows(steps, cols):
    return pl.BlockSpec((ROWS, cols), lambda i: (jnp.maximum(i - steps, 0), 0))


def pick_rows(i, steps, own_ref, partner_ref):
    return jnp.where(i < steps, own_ref[...], partner_ref[...])


def split_kernel(place, w_qkv, w_out, norm_cols, mine, send):
    first = place[0] == 0
    half = D // 2
    for n in range(4):
        source, start = (w_qkv, n * D) if n < 3 else (w_out, 0)
        low, high = source[:, start : start + half], source[:, start + half : start + D]
        mine[:, n * half : (n + 1) * half] = jnp.where(first, low, high)
        send[:, n * half : (n + 1) * half] = jnp.where(first, high, low)
    mine[:, 4 * half :] = norm_cols[...]
    send[:, 4 * half :] = norm_cols[...]


def fill_blocks(table, pieces, weight, cols=slice(None)):
    count = pieces[0].shape[0]
    for n, piece in enumerate(pieces):
        for k in range(count):
            weight[table[n * count + k]] = piece[k, :, cols]


def qkv_kernel(steps, groups, pieces, table, own, partner, *refs):
    i = pl.program_id(0)
    parts = refs[:pieces]
    mixed_own, mixed_partner, weight, out_w, norms, table_t = refs[pieces:]
    cols, part = weight.shape[2], out_w.shape[2]
    tall = weight.shape[0] * weight.shape[1]

    @pl.when(i == 0)
    def _():
        fill_blocks(table, parts, weight, slice(0, cols))
        fill_blocks(table, parts, out_w, slice(cols, cols + part))
        fill_blocks(table, parts, table_t, slice(cols + part, None))
        norms[...] = table_t[...].reshape(tall, table_t.shape[2]).astype(F32).T[: norms.shape[0]]

    rows_here = pick_rows(i, steps, own, partner)
    for g in range(groups):
        span = slice(g * cols // groups, (g + 1) * cols // groups)
        tile = weight[:, :, span].reshape(tall, cols // groups)
        value = dot(rows_here, tile).astype(BF16)

        @pl.when(i < steps)
        def _():
            mixed_own[:, span] = value

        @pl.when(i >= steps)
        def _():
            mixed_partner[:, span] = value


def lane_masks():
    lane = lax.broadcasted_iota(jnp.int32, (1, PAIR), 1)
    return [lane < HEAD_DIM, lane >= HEAD_DIM]


def keep(mask, value):
    return jnp.where(mask, value, jnp.zeros_like(value))


def fill_distance(distance):
    row = lax.broadcasted_iota(jnp.int32, distance.shape, 0)
    col = lax.broadcasted_iota(jnp.int32, distance.shape, 1)
    distance[...] = jnp.abs(row - col).astype(F32)


def scores_of(queries, keys, slope, distance):
    raw = lax.dot_general(queries, keys, (((1,), (1,)), ((), ())), preferred_element_type=F32)
    return raw - slope * distance


def attend_rows(queries, keys, values, slope, away):
    s = jnp.concatenate([scores_of(q, k, slope, away) for q, k in zip(queries, keys)], axis=0)
    top = jnp.max(s, axis=-1, keepdims=True)
    e = jnp.exp(s - top)
    norm = jnp.sum(e, axis=-1, keepdims=True)
    p = (e * (1.0 / norm)).astype(BF16)
    tall = queries[0].shape[0]
    out = [dot(p[n * tall : (n + 1) * tall], v) for n, v in enumerate(values)]
    return jnp.concatenate(out, axis=0), top + jnp.log(norm)


def tiles(value, tall):
    return [value[n : n + tall] for n in range(0, value.shape[0], tall)]


def pair_cols(part, pair):
    return pl.ds(pl.multiple_of(part * (D // 2) + pair * PAIR, PAIR), PAIR)


def attend_kernel(place, flags, slopes, mixed, context, logs, distance):
    masks = lane_masks()
    scale = HEAD_DIM**-0.5
    lane = lax.broadcasted_iota(jnp.int32, (1, 128), 1)
    fill_distance(distance)

    def run(is_long):
        tall = 2 * SHORT if is_long else LONG

        def one_pair(pair, _):
            q_all, k_all, v_all = (mixed[:, pair_cols(part, pair)] for part in range(3))
            totals = [0.0] * (LONG // tall)
            for head in range(2):
                slope = slopes[pair * 2 + head]
                q = (keep(masks[head], q_all) * scale).astype(BF16)
                v = keep(masks[head], v_all)
                for n in range(LONG // tall):
                    rows = slice(n * tall, (n + 1) * tall)
                    if is_long:
                        out = attend_rows([q[rows]], [k_all], [v], slope, distance[rows, :])
                    else:
                        out = attend_rows(
                            tiles(q, SHORT), tiles(k_all, SHORT), tiles(v, SHORT), slope, distance[:SHORT, :SHORT]
                        )
                    totals[n] = totals[n] + out[0]
                    logs[rows, :] = jnp.where(lane == pair * 2 + head, out[1], logs[rows, :])
            for n in range(LONG // tall):
                context[n * tall : (n + 1) * tall, pair_cols(0, pair)] = totals[n].astype(BF16)
            return 0

        lax.fori_loop(0, D // 2 // PAIR, one_pair, 0)

    logs[...] = jnp.zeros_like(logs)
    flag = flags[place[1]]

    @pl.when(flag > 0)
    def _():
        run(True)

    @pl.when(flag <= 0)
    def _():
        run(False)


def back_rows(queries, keys, values, d_rows, log_rows, slope, away, scaled_keys):
    s = jnp.concatenate([scores_of(q, k, slope, away) for q, k in zip(queries, keys)], axis=0)
    p = jnp.exp(s - log_rows)
    d_p = jnp.concatenate([contract_cols(d, v) for d, v in zip(d_rows, values)], axis=0)
    d_s = (p * (d_p - jnp.sum(p * d_p, axis=-1, keepdims=True))).astype(BF16)
    p = p.astype(BF16)
    tall = queries[0].shape[0]
    d_s, p = tiles(d_s, tall), tiles(p, tall)
    d_q = jnp.concatenate([dot(d, k) for d, k in zip(d_s, scaled_keys)], axis=0)
    d_k = [dot(q.T, d) for q, d in zip(queries, d_s)]
    d_v = [dot(d.T, w) for d, w in zip(d_rows, p)]
    return d_q, d_k, d_v


def attend_back_kernel(
    pairs, flags, slopes, mixed_own, mixed_partner, d_own, d_partner, logs_own, logs_partner, d_query, d_key, d_value, distance
):
    block = pl.program_id(0)
    masks = lane_masks()
    scale = HEAD_DIM**-0.5

    @pl.when(block == 0)
    def _():
        fill_distance(distance)

    def run(is_long):
        tall = 2 * SHORT if is_long else LONG
        logs = jnp.where(block == 0, logs_own[...], logs_partner[...])
        lane = lax.broadcasted_iota(jnp.int32, (1, 128), 1)

        def one_pair(place, _):
            pair = pairs[0] + place
            q_all, k_all, v_all = (
                jnp.where(block == 0, mixed_own[:, cols], mixed_partner[:, cols])
                for cols in (pair_cols(part, pair) for part in range(3))
            )
            d_all = jnp.where(block == 0, d_own[:, pair_cols(0, pair)], d_partner[:, pair_cols(0, pair)])
            d_q, d_k, d_v = [0.0] * (LONG // tall), 0.0, 0.0
            for head in range(2):
                slope = slopes[pair * 2 + head]
                q = (keep(masks[head], q_all) * scale).astype(BF16)
                k = (keep(masks[head], k_all) * scale).astype(BF16)
                d_c = keep(masks[head], d_all)
                log_all = jnp.sum(jnp.where(lane == pair * 2 + head, logs, 0.0), axis=-1, keepdims=True)
                for n in range(LONG // tall):
                    rows = slice(n * tall, (n + 1) * tall)
                    if is_long:
                        out = back_rows(
                            [q[rows]], [k_all], [v_all], [d_c[rows]], log_all[rows], slope, distance[rows, :], [k]
                        )
                        new_k, new_v = out[1][0], out[2][0]
                    else:
                        out = back_rows(
                            tiles(q, SHORT),
                            tiles(k_all, SHORT),
                            tiles(v_all, SHORT),
                            tiles(d_c, SHORT),
                            log_all,
                            slope,
                            distance[:SHORT, :SHORT],
                            tiles(k, SHORT),
                        )
                        new_k, new_v = (jnp.concatenate(part, axis=1) for part in out[1:])
                    d_q[n] = d_q[n] + out[0]
                    d_k, d_v = d_k + new_k, d_v + new_v
            cols = pair_cols(0, place)
            for n in range(LONG // tall):
                d_query[n * tall : (n + 1) * tall, cols] = d_q[n].astype(BF16)
            d_key[:, cols] = d_k.T.astype(BF16)
            d_value[:, cols] = d_v.T.astype(BF16)
            return 0

        lax.fori_loop(0, len(pairs), one_pair, 0)

    @pl.when(flags[block] > 0)
    def _():
        run(True)

    @pl.when(flags[block] <= 0)
    def _():
        run(False)


def spread(rows):
    center = jnp.mean(rows, axis=-1, keepdims=True)
    shifted = rows - center
    inverse = lax.rsqrt(jnp.mean(shifted * shifted, axis=-1, keepdims=True) + 1e-05)
    return shifted * inverse, inverse


def norm_back(e, unit, inverse):
    mean_e = jnp.mean(e, axis=-1, keepdims=True)
    mean_en = jnp.mean(e * unit, axis=-1, keepdims=True)
    return (e - mean_e - unit * mean_en) * inverse


def first_norm_kernel(place, tokens, ctx_mine, ctx_other, w_mine, w_other, norms, unit, inverse, low):
    core = place[0]
    half = w_mine.shape[0] // 2
    wide = w_mine.shape[2]

    def branch(weight):
        near = weight[pl.ds(core * half, half)].reshape(D // 2, wide)
        far = weight[pl.ds((1 - core) * half, half)].reshape(D // 2, wide)
        return dot(ctx_mine[...], near) + dot(ctx_other[...], far)

    mine, other = branch(w_mine), branch(w_other)
    first = core == 0
    added = jnp.concatenate([jnp.where(first, mine, other), jnp.where(first, other, mine)], axis=1)
    n, inv = spread(tokens[...].astype(F32) + added)
    unit[...] = n
    inverse[...] = inv
    low[...] = (n * norms[0:1, :] + norms[2:3, :]).astype(BF16)


def gelu_parts(x):
    t = 1.0 / (1.0 + (0.3275911 * 0.5**0.5) * jnp.abs(x))
    poly = t * (
        0.254829592 + t * (-0.284496736 + t * (1.421413741 + t * (-1.453152027 + t * 1.061405429)))
    )
    bell = jnp.exp(-0.5 * (x * x))
    tail = 0.5 * poly * bell
    phi = jnp.where(x >= 0, 1.0 - tail, tail)
    return x * phi, phi + x * bell * 0.3989422804014327


def columns_of(weight, half, span):
    count = weight.shape[0] // 2
    return weight[half * count : (half + 1) * count, :, span].reshape(D, span.stop - span.start)


def up_kernel(steps, pieces, table, own, partner, *refs):
    i = pl.program_id(0)
    parts = refs[: 2 * pieces]
    product, active, slope, gate_w, value_w = refs[2 * pieces :]

    @pl.when(i == 0)
    def _():
        fill_blocks(table, parts[:pieces], gate_w)
        fill_blocks(table, parts[pieces:], value_w)

    rows = pick_rows(i, steps, own, partner)
    width = gate_w.shape[2]
    for half in range(2):
        for start in range(0, width, 256):
            span = slice(start, start + 256)
            out = slice(half * width + start, half * width + start + 256)
            gate = dot(rows, columns_of(gate_w, half, span))
            up = dot(rows, columns_of(value_w, half, span))
            act, grad = gelu_parts(gate)
            product[:, out] = (act * up).astype(BF16)
            active[:, out] = act.astype(BF16)
            slope[:, out] = (up * grad).astype(BF16)


def down_kernel(steps, table, product, *refs):
    i = pl.program_id(0)
    own, partner, down_w = refs[-3:]

    @pl.when(i == 0)
    def _():
        fill_blocks(table, refs[:-3], down_w)

    width = down_w.shape[2]
    total = 0.0
    for half in range(2):
        total = total + contract_cols(product[:, half * width : (half + 1) * width], columns_of(down_w, half, slice(0, width)))

    @pl.when(i < steps)
    def _():
        own[...] = total

    @pl.when(i >= steps)
    def _():
        partner[...] = total.astype(BF16)


def second_norm_kernel(unit_one, norms, part_own, part_got, cotangent, out, d_z, d_ffn, sums):
    normed = unit_one[...] * norms[0:1, :] + norms[2:3, :]
    n, inv = spread(normed + (part_own[...] + part_got[...].astype(F32)))
    gain = norms[1:2, :]
    out[...] = (n * gain + norms[3:4, :]).astype(BF16)
    c = cotangent[...].astype(F32)
    back = norm_back(gain * c, n, inv)
    d_z[...] = back
    d_ffn[...] = back.astype(BF16)
    add_sums(sums, c * n, c)


def add_sums(sums, gain_terms, bias_terms):
    @pl.when(pl.program_id(0) == 0)
    def _():
        sums[...] = jnp.zeros_like(sums)

    sums[0:1, :] += jnp.sum(gain_terms, axis=0, keepdims=True)
    sums[1:2, :] += jnp.sum(bias_terms, axis=0, keepdims=True)


def ffn_back_kernel(
    steps, own, partner, down_w, gate_w, value_w, active, slope, d_gate, d_up, back_own, back_partner
):
    i = pl.program_id(0)
    rows = pick_rows(i, steps, own, partner)
    width = down_w.shape[2]
    total = jnp.zeros((ROWS, D), F32)
    for half in range(2):
        for start in range(0, width, 256):
            span = slice(start, start + 256)
            out = slice(half * width + start, half * width + start + 256)
            d_product = dot(rows, columns_of(down_w, half, span))
            dg = (d_product * slope[:, out].astype(F32)).astype(BF16)
            du = (d_product * active[:, out].astype(F32)).astype(BF16)
            d_gate[:, out] = dg
            d_up[:, out] = du
            total = total + contract_cols(dg, columns_of(gate_w, half, span))
            total = total + contract_cols(du, columns_of(value_w, half, span))

    @pl.when(i < steps)
    def _():
        back_own[...] = total

    @pl.when(i >= steps)
    def _():
        back_partner[...] = total.astype(BF16)


def weight_grad_kernel(table, left_own, left_partner, right_a, right_b, *refs):
    i = pl.program_id(0)
    parts, blocks = refs[:-1], refs[-1]
    rows = left_own.shape[0]
    count, tall, cols = blocks.shape
    for half, right in enumerate((right_a, right_b)):
        value = contract_rows(left_own[...], right[:rows, :]) + contract_rows(left_partner[...], right[rows:, :])
        value = value.astype(BF16).reshape(count // 2, tall, cols)
        blocks[half * (count // 2) : (half + 1) * (count // 2)] = value
    span = pl.ds(pl.multiple_of(i * cols, cols), cols)
    each = count // len(parts)
    for k in range(count):
        parts[k // each][k % each, :, span] = blocks[table[k]]


def first_norm_back_kernel(
    place,
    unit_ref,
    inverse,
    norms,
    d_z,
    part_own,
    part_got,
    ctx_mine,
    ctx_other,
    w_mine,
    w_other,
    d_hidden,
    dctx_mine,
    dctx_other,
    grad_keep,
    grad_send,
    sums,
    grad,
):
    core = place[0]
    first = core == 0
    unit = unit_ref[...]
    d_normed = d_z[...] + (part_own[...] + part_got[...].astype(F32))
    back = norm_back(norms[0:1, :] * d_normed, unit, inverse[...])
    low = back.astype(BF16)
    d_hidden[...] = back
    add_sums(sums, d_normed * unit, d_normed)
    half, wide = w_mine.shape[0] // 2, w_mine.shape[2]
    low_mine = jnp.where(first, low[:, :wide], low[:, wide:])
    low_other = jnp.where(first, low[:, wide:], low[:, :wide])
    for head_core, out in ((core, dctx_mine), (1 - core, dctx_other)):
        near = w_mine[pl.ds(head_core * half, half)].reshape(D // 2, wide)
        far = w_other[pl.ds(head_core * half, half)].reshape(D // 2, wide)
        out[...] = (contract_cols(low_mine, near) + contract_cols(low_other, far)).astype(BF16)

    @pl.when(pl.program_id(0) == 0)
    def _():
        grad[...] = jnp.zeros_like(grad)

    shape = (half,) + grad.shape[1:]
    grad[pl.ds(core * half, half)] += contract_rows(ctx_mine[...], low).reshape(shape)
    grad[pl.ds((1 - core) * half, half)] += contract_rows(ctx_other[...], low).reshape(shape)

    @pl.when(pl.program_id(0) == pl.num_programs(0) - 1)
    def _():
        left, right = grad[:, :, :wide], grad[:, :, wide:]
        grad_keep[...] = jnp.where(first, left, right)
        grad_send[...] = jnp.where(first, right, left).astype(BF16)


def qkv_grad_kernel(table, left_own, left_partner, d_query, d_key, d_value, out_grad, sums_one, sums_two, near, far, blocks, norm_grad):
    i = pl.program_id(0)
    rows = left_own.shape[0]
    count, tall, cols = blocks.shape

    @pl.when(i == 0)
    def _():
        one, two = sums_one[...], sums_two[...]
        empty = jnp.zeros((norm_grad.shape[2] - 4, D), F32)
        stacked = jnp.concatenate([one[0:1], two[0:1], one[1:2], two[1:2], empty], axis=0)
        norm_grad[...] = stacked.T.astype(BF16).reshape(norm_grad.shape)

    for g, right in enumerate((d_query, d_key, d_value)):

        @pl.when(i == g)
        def _():
            value = contract_rows(left_own[...], right[:rows, :]) + contract_rows(left_partner[...], right[rows:, :])
            blocks[...] = value.astype(BF16).reshape(blocks.shape)
            for k in range(count):
                target, place = (near if k < count // 2 else far), table[k]
                target[k % (count // 2), :, g * cols : (g + 1) * cols] = blocks[place]
                if g == 0:
                    start = 3 * cols
                    for more in (out_grad, norm_grad):
                        stop = start + more.shape[2]
                        target[k % (count // 2), :, start:stop] = more[place]
                        start = stop


def input_grad_kernel(steps, parts, *refs):
    i = pl.program_id(0)
    weight, own, partner = refs[-3:]
    total = 0.0
    for n, first in enumerate(parts):
        for g in range(3):
            left = refs[3 * n + g]
            start = g * (D // 2) + first * PAIR
            tile = weight[:, :, start : start + left.shape[1]].reshape(D, left.shape[1])
            total = total + contract_cols(left[...], tile)

    @pl.when(i < steps)
    def _():
        own[...] = total

    @pl.when(i >= steps)
    def _():
        partner[...] = total.astype(BF16)


def by_core(core, mine, other, axis):
    first = core == 0
    return jnp.stack([jnp.where(first, mine, other), jnp.where(first, other, mine)], axis=axis)


def half_of(core, halves, axis):
    zero, one = (lax.index_in_dim(halves, k, axis, keepdims=False) for k in range(2))
    first = core == 0
    return jnp.where(first, zero, one), jnp.where(first, one, zero)


def plane_shards(
    wide,
    narrow,
    tokens,
    w_qkv,
    w_out,
    w_gate,
    w_value,
    w_down,
    norm_gains,
    norm_biases,
    long_count,
    cotangent,
):
    plane = Plane(wide, narrow)
    swap = plane.swap
    core, y_here = plane.core, plane.y
    rows = tokens.shape[0]
    steps = rows // ROWS
    tall = w_qkv.shape[0]
    blocks = wide * narrow // 2
    z_size = plane.size["z"]
    head_cols = D // 2
    width = w_gate.shape[1] // 2
    hidden = 2 * width
    pairs = head_cols // PAIR
    qkv_to = plane.tables(("z", "a", "b"), lambda z, x, y: (z * 2 + x) * 2 + y)
    ffn_to = plane.tables(("z", "a", "b"), lambda z, x, y: y * (2 * z_size) + z * 2 + x)
    down_to = plane.tables(("a", "b", "ring"), lambda z, x, y: y * (2 * z_size) + z * 2 + x)
    place = jnp.reshape(core, (1,)).astype(jnp.int32)
    first = core == 0

    def wholes(arrays):
        return [(v, whole(v.shape)) for v in arrays]

    def step_rows(cols):
        return pl.BlockSpec((ROWS, cols), lambda i: (i, 0))

    norm_cols = jnp.concatenate([norm_gains, norm_biases], axis=0).T
    norm_cols = jnp.pad(norm_cols, ((0, 0), (0, 128 - norm_cols.shape[1])))
    head_shape = (tall, 4 * head_cols + 128)
    head_part, head_send = kernel_call(
        split_kernel,
        (1,),
        [(place, smem())] + wholes([w_qkv, w_out, norm_cols]),
        [(head_shape, BF16, whole(head_shape))] * 2,
        name="split",
        far=True,
    )
    head_got = swap(head_send, "core")
    head_part = jnp.where(y_here == core, head_part, head_got)
    qkv_z = plane.gather_z(head_part)
    ffn_parts = [after(w_gate, head_part), w_value, w_down.T]
    ffn_other = jnp.concatenate([jnp.where(first, v[:, width:], v[:, :width]) for v in ffn_parts], axis=1)
    ffn_got = swap(ffn_other, "core")
    tokens_other = swap(after(tokens, head_part), "core")
    flag = jnp.broadcast_to(long_count.astype(F32), (8, 128))
    flag_got = swap(after(flag, head_part), "core")
    flags = jnp.stack([long_count[0, 0], flag_got[0, 0].astype(jnp.int32)])
    slopes = lax.dynamic_slice_in_dim(alibi_slopes(HEADS), core * (HEADS // 2), HEADS // 2)

    def ffn_chip(n):
        v, got = ffn_parts[n], ffn_got[:, n * width : (n + 1) * width]
        mine = jnp.where(first, v[:, :width], v[:, width:])
        return jnp.concatenate([jnp.where(first, mine, got), jnp.where(first, got, mine)], axis=0)

    def doubled(value, step, *events):
        got = swap(value, "z", step)
        return jnp.concatenate(lax.optimization_barrier((value, got) + events)[:2], axis=0)

    def along_plane(held):
        near = swap(held, "a")
        return held, near, swap(held, "b")

    def joined(value, got):
        return jnp.concatenate([value, got], axis=0)

    gate_one, value_one, down_one = (ffn_chip(n)[None] for n in range(3))
    pair_one = jnp.concatenate([gate_one, value_one], axis=0)
    pair_got = swap(pair_one, "z", 1)
    down_got = swap(down_one, "a")
    qkv_z, pair_got, down_got = fence(qkv_z, pair_got, down_got)
    gate_two, value_two = (jnp.stack([pair_one[n], pair_got[n]]) for n in range(2))
    down_two = joined(down_one, down_got)

    head_near, head_far = swap(qkv_z, "a"), swap(qkv_z, "b")
    gate_got = swap(gate_two, "z", 2)
    down_got = swap(down_two, "b")
    head_near, head_far, gate_got, down_got, tokens_other, flags, value_two = fence(
        head_near, head_far, gate_got, down_got, tokens_other, flags, value_two
    )
    gate_z, down_four = joined(gate_two, gate_got), joined(down_two, down_got)

    head_last = swap(head_near, "b")
    gate_near = swap(gate_z, "a")
    value_got = swap(value_two, "z", 2)
    head_last, gate_near, value_got, down_four = fence(head_last, gate_near, value_got, down_four)
    value_z = joined(value_two, value_got)
    qkv_blocks = [qkv_z, head_near, head_far, head_last]

    gate_far, gate_last = swap(gate_z, "b"), swap(gate_near, "b")
    ring_one = swap(down_four, "next")
    block_row = (blocks, tall)
    mixed_own, mixed_partner, qkv_w, out_mine, norms = kernel_call(
        functools.partial(qkv_kernel, steps, 3, len(qkv_blocks)),
        (2 * steps,),
        [
            (qkv_to, smem()),
            (tokens, own_rows(steps, D)),
            (tokens_other, partner_rows(steps, D)),
        ]
        + wholes(qkv_blocks),
        [((rows, 3 * head_cols), BF16, own_rows(steps, 3 * head_cols))]
        + [((rows, 3 * head_cols), BF16, partner_rows(steps, 3 * head_cols))]
        + [(block_row + (n,), BF16, whole(block_row + (n,))) for n in (3 * head_cols, head_cols)]
        + [((8, D), F32, whole((8, D)))],
        scratch=[pltpu.VMEM(block_row + (128,), BF16)],
        flops=2 * 2 * rows * D * 3 * head_cols,
        name="mixed",
        far=True,
    )
    def attend(block, mixed):
        return kernel_call(
            attend_kernel,
            (1,),
            [(jnp.array([0, block], jnp.int32), smem()), (flags, smem()), (slopes, smem())] + wholes([mixed]),
            [((rows, head_cols), BF16, whole((rows, head_cols))), ((rows, 128), F32, whole((rows, 128)))],
            scratch=[pltpu.VMEM((LONG, LONG), F32)],
            flops=4 * rows * LONG * D,
            name="attend",
            room=12,
            far=True,
        )

    ctx_send, logs_partner = attend(1, mixed_partner)
    gate_far, gate_last, ring_one, ctx_send, out_mine = fence(gate_far, gate_last, ring_one, ctx_send, out_mine)
    gate_blocks = [gate_z, gate_near, gate_far, gate_last]

    value_near, value_far = swap(value_z, "a"), swap(value_z, "b")
    ring_two = swap(ring_one, "next")
    ctx_other = swap(ctx_send, "core")
    out_other = swap(out_mine, "core")
    ctx_mine, logs_own = attend(0, after(mixed_own, ctx_send))

    unit_one, inverse_one, low = kernel_call(
        first_norm_kernel,
        (steps,),
        [
            (place, smem()),
            (tokens, step_rows(D)),
            (ctx_mine, step_rows(head_cols)),
            (ctx_other, step_rows(head_cols)),
        ]
        + wholes([out_mine, out_other, norms]),
        [
            ((rows, D), F32, step_rows(D)),
            ((rows, 1), F32, step_rows(1)),
            ((rows, D), BF16, step_rows(D)),
        ],
        flops=2 * rows * D * D,
        name="first_norm",
    )
    value_near, value_far, ring_two, low = fence(value_near, value_far, ring_two, low)
    value_last = swap(value_near, "b")
    low_other = swap(low, "core")
    value_last, low_other = fence(value_last, low_other)
    value_blocks = [value_z, value_near, value_far, value_last]
    ring_three = swap(ring_two, "next")

    w_shape = (blocks, 2 * tall, width)
    product, active, slope, gate_w, value_w = kernel_call(
        functools.partial(up_kernel, steps, len(gate_blocks)),
        (2 * steps,),
        [
            (ffn_to, smem()),
            (low, own_rows(steps, D)),
            (low_other, partner_rows(steps, D)),
        ]
        + wholes(gate_blocks + value_blocks),
        [((2 * rows, hidden), BF16, step_rows(hidden))] * 3 + [(w_shape, BF16, whole(w_shape))] * 2,
        flops=2 * 2 * rows * D * 2 * hidden,
        name="up",
        far=True,
    )
    ring_three, product = fence(ring_three, product)
    down_blocks = [down_four, ring_one, ring_two, ring_three]
    part_own, part_send, down_w = kernel_call(
        functools.partial(down_kernel, steps),
        (2 * steps,),
        [(down_to, smem()), (product, step_rows(hidden))] + wholes(down_blocks),
        [
            ((rows, D), F32, own_rows(steps, D)),
            ((rows, D), BF16, partner_rows(steps, D)),
            (w_shape, BF16, whole(w_shape)),
        ],
        flops=2 * 2 * rows * D * hidden,
        name="down",
    )
    part_got = swap(part_send, "core")
    layer_out, d_z, d_ffn, sums_two = kernel_call(
        second_norm_kernel,
        (steps,),
        [(unit_one, step_rows(D))]
        + wholes([norms])
        + [(part_own, step_rows(D)), (part_got, step_rows(D)), (cotangent, step_rows(D))],
        [
            ((rows, D), BF16, step_rows(D)),
            ((rows, D), F32, step_rows(D)),
            ((rows, D), BF16, step_rows(D)),
            ((8, D), F32, whole((8, D))),
        ],
        name="second_norm",
    )
    d_ffn_other = swap(d_ffn, "core")

    def weight_grad(left, left_other, right, to, parts):
        part = (blocks // parts, 2 * tall, width)
        cols = width // 3
        return kernel_call(
            weight_grad_kernel,
            (3,),
            [
                (to, smem()),
                (left, whole((rows, D))),
                (left_other, whole((rows, D))),
                (right, pl.BlockSpec((2 * rows, cols), lambda i: (0, i))),
                (right, pl.BlockSpec((2 * rows, cols), lambda i: (0, 3 + i))),
            ],
            [(part, BF16, whole(part))] * parts,
            scratch=[pltpu.VMEM((blocks, 2 * tall, cols), BF16)],
            flops=2 * 2 * rows * D * hidden,
            name="weight_grad",
        )

    def added(keep, got):
        return (keep.astype(F32) + got.astype(F32)).astype(BF16)

    def halves(keep, got):
        count = keep.shape[0] // 2
        return added(keep[:count], got[:count]), added(keep[count:], got[count:])

    down_parts = weight_grad(d_ffn, d_ffn_other, product, down_to, len(RING))
    d_gate, d_up, back_own, back_send = kernel_call(
        functools.partial(ffn_back_kernel, steps),
        (2 * steps,),
        [(after(d_ffn, down_parts[-1]), own_rows(steps, D)), (d_ffn_other, partner_rows(steps, D))]
        + wholes([down_w, gate_w, value_w])
        + [(active, step_rows(hidden)), (slope, step_rows(hidden))],
        [((2 * rows, hidden), BF16, step_rows(hidden))] * 2
        + [((rows, D), F32, own_rows(steps, D)), ((rows, D), BF16, partner_rows(steps, D))],
        flops=3 * 2 * 2 * rows * D * hidden,
        name="ffn_back",
    )
    down_got = swap(down_parts[3], "prev")
    gate_keep, gate_send = weight_grad(after(low, back_send), low_other, d_gate, ffn_to, 2)
    down_got, back_send, gate_send = fence(down_got, back_send, gate_send)

    gate_got = swap(gate_send, "b")
    down_got = swap(added(down_parts[2], down_got), "prev")
    back_got = swap(back_send, "core")
    d_hidden, dctx_mine, dctx_send, out_keep, out_send, sums_one = kernel_call(
        first_norm_back_kernel,
        (steps,),
        [
            (place, smem()),
            (unit_one, step_rows(D)),
            (inverse_one, step_rows(1)),
            (norms, whole(norms.shape)),
            (d_z, step_rows(D)),
            (back_own, step_rows(D)),
            (back_got, step_rows(D)),
            (ctx_mine, step_rows(head_cols)),
            (ctx_other, step_rows(head_cols)),
        ]
        + wholes([out_mine, out_other]),
        [
            ((rows, D), F32, step_rows(D)),
            ((rows, head_cols), BF16, step_rows(head_cols)),
            ((rows, head_cols), BF16, step_rows(head_cols)),
            (out_mine.shape, F32, whole(out_mine.shape)),
            (out_mine.shape, BF16, whole(out_mine.shape)),
            ((8, D), F32, whole((8, D))),
        ],
        scratch=[pltpu.VMEM((blocks, tall, D), F32)],
        flops=2 * 2 * rows * D * D,
        name="first_norm_back",
    )
    value_keep, value_send = weight_grad(after(low, d_hidden), low_other, d_up, ffn_to, 2)
    down_got, gate_got, dctx_send, out_send, value_send = fence(down_got, gate_got, dctx_send, out_send, value_send)
    dctx_got, out_got = swap(dctx_send, "core"), swap(out_send, "core")
    value_got = swap(value_send, "b")
    gate_keep, gate_send = halves(gate_keep, gate_got)
    down_send = added(down_parts[1], down_got)
    gate_got = swap(gate_send, "a")
    down_got = swap(down_send, "prev")
    out_sum = (out_keep + out_got.astype(F32)).astype(BF16)

    def attend_back(chosen, d_mine):
        cols = len(chosen) * PAIR
        return kernel_call(
            functools.partial(attend_back_kernel, chosen),
            (2,),
            [(flags, smem()), (slopes, smem())]
            + wholes([mixed_own, mixed_partner, d_mine, dctx_got, logs_own, logs_partner]),
            [((2 * rows, cols), BF16, pl.BlockSpec((rows, cols), lambda b: (b, 0)))] * 3,
            scratch=[pltpu.VMEM((LONG, LONG), F32)],
            flops=10 * 2 * rows * LONG * cols * 2,
            name="attend_back",
            room=16,
            far=True,
        )

    def qkv_grad(left, d_parts):
        cols = d_parts[0].shape[1]
        shape = (blocks // 2, tall, 4 * cols + 128)
        return kernel_call(
            qkv_grad_kernel,
            (3,),
            [(qkv_to, smem())] + wholes([left, tokens_other] + list(d_parts) + [out_sum, sums_one, sums_two]),
            [(shape, BF16, whole(shape))] * 2,
            scratch=[pltpu.VMEM(block_row + (cols,), BF16), pltpu.VMEM(block_row + (128,), BF16)],
            flops=2 * 2 * rows * D * 3 * cols,
            name="qkv_grad",
        )

    d_parts = attend_back(tuple(range(pairs)), after(dctx_mine, gate_send, down_send))
    head_keep, head_send = qkv_grad(tokens, d_parts)
    down_got, gate_got, value_got, head_send = fence(down_got, gate_got, value_got, head_send)
    down_keep, down_send = halves(down_parts[0], down_got)
    gate_z = added(gate_keep, gate_got)
    value_keep, value_send = halves(value_keep, value_got)

    head_got = swap(head_send, "b")
    value_got = swap(value_send, "a")
    gate_sum = plane.sum_z(gate_z).astype(BF16)
    in_own, in_send = kernel_call(
        functools.partial(input_grad_kernel, steps, (0,)),
        (2 * steps,),
        [(v, step_rows(v.shape[1])) for v in [after(d_parts[0], value_send, gate_z)] + list(d_parts[1:])]
        + wholes([qkv_w]),
        [((rows, D), F32, own_rows(steps, D)), ((rows, D), BF16, partner_rows(steps, D))],
        flops=2 * 2 * rows * D * 3 * head_cols,
        name="input_grad",
    )
    input_grad = d_hidden + in_own + swap(in_send, "core").astype(F32)

    head_got, value_got, gate_sum, down_send, input_grad = fence(head_got, value_got, gate_sum, down_send, input_grad)
    head_keep, head_send = halves(head_keep, head_got)
    value_z = added(value_keep, value_got)

    down_got = swap(down_send, "b")
    head_got = swap(head_send, "a")
    value_sum = plane.sum_z(value_z).astype(BF16)
    head_got, value_sum, down_got = fence(head_got, value_sum, down_got)
    head_z = added(head_keep, head_got)
    down_keep, down_send = halves(down_keep, down_got)

    down_got = swap(down_send, "a")
    head_sum = plane.sum_z(head_z).astype(BF16)
    grads = [gate_sum, value_sum, added(down_keep[0], down_got[0])]

    def in_order(mine, other):
        return [jnp.where(first, mine, other), jnp.where(first, other, mine)]

    kept = [half_of(core, total.reshape(2, tall, width), 0) for total in grads]
    ffn_got = swap(jnp.concatenate([other for _, other in kept], axis=0), "core")
    ffn_pieces = [
        jnp.concatenate(in_order(mine, ffn_got[n * tall : (n + 1) * tall]), axis=1).astype(F32)
        for n, (mine, _) in enumerate(kept)
    ]
    gate_piece, value_piece, down_piece = ffn_pieces[0], ffn_pieces[1], ffn_pieces[2].T
    both = by_core(y_here, head_sum, swap(head_sum, "y"), 0)
    mine, other = half_of(core, both, 0)
    got = swap(other, "core")
    four = 4 * head_cols
    pieces = []
    for n in range(4):
        span = slice(n * head_cols, (n + 1) * head_cols)
        pieces += in_order(mine[:, span], got[:, span])
    qkv_piece = jnp.concatenate(pieces[:6], axis=1).astype(F32)
    out_piece = jnp.concatenate(pieces[6:], axis=1).astype(F32)
    norm_piece = (mine[:, four : four + 4].astype(F32) + got[:, four : four + 4].astype(F32)).T
    return (
        layer_out,
        input_grad,
        qkv_piece,
        out_piece,
        gate_piece,
        value_piece,
        down_piece,
        norm_piece[:2],
        norm_piece[2:],
    )


def solution(mesh):
    wide, narrow = mesh.shape["wide"], mesh.shape["narrow"]
    placed = (
        P(("wide", "narrow"), None),
        P("wide", None),
        P("wide", None),
        P("wide", "narrow"),
        P("wide", "narrow"),
        P("narrow", "wide"),
        P(None, "wide"),
        P(None, "wide"),
        P("wide", "narrow"),
        P(("wide", "narrow"), None),
    )
    if narrow == 2 and wide % 16 == 0 and D % (16 * wide) == 0:
        body = functools.partial(plane_shards, wide, narrow)
    else:
        body = general_shards
    return jax.shard_map(
        body,
        mesh=mesh,
        in_specs=placed,
        out_specs=(
            P(("wide", "narrow"), None),
            P(("wide", "narrow"), None),
            P("wide", None),
            P("wide", None),
            P("wide", "narrow"),
            P("wide", "narrow"),
            P("narrow", "wide"),
            P(None, "wide"),
            P(None, "wide"),
        ),
        check_vma=False,
    )
```

```python
import functools

import jax
import jax.numpy as jnp
import numpy as np
from jax import lax
from jax.experimental import pallas as pl
from jax.experimental.pallas import tpu as pltpu
from jax.sharding import PartitionSpec as P

D = 768
HEADS = 12
HEAD_DIM = 64
LONG = 512
SHORT = 128


def norm_rows(values, gain_row, bias_row):
    center = jnp.mean(values, axis=-1, keepdims=True)
    shifted = values - center
    spread = jnp.mean(shifted * shifted, axis=-1, keepdims=True)
    return shifted * lax.rsqrt(spread + 1e-05) * gain_row + bias_row


def gelu_product(gate_in, value_in):
    return jax.nn.gelu(gate_in, approximate=False) * value_in


def alibi_slopes(heads):
    power = 1 << heads.bit_length() - 1
    first = [2.0 ** (-8.0 * (index + 1) / power) for index in range(power)]
    second = [2.0 ** (-8.0 * (2 * index + 1) / (2 * power)) for index in range(heads - power)]
    return jnp.array(first + second, dtype=jnp.float32)


def alibi_bias(span, heads):
    position = jnp.arange(span)
    distance = jnp.abs(position[:, None] - position[None, :]).astype(jnp.float32)
    slopes = alibi_slopes(heads)
    return slopes[:, None, None] * distance


def block_scores(query_g, key_g, span):
    width = query_g.shape[-1]
    scores = jnp.einsum(
        "bqhd,bkhd->bhqk", query_g, key_g, preferred_element_type=jnp.float32
    ) * width ** (-0.5)
    return scores - alibi_bias(span, query_g.shape[2])


def attend(query_rows, key_rows, value_rows, span):
    rows, heads, width = query_rows.shape
    groups = rows // span
    shape_g = (groups, span, heads, width)
    query_g = query_rows.reshape(shape_g)
    key_g = key_rows.reshape(shape_g)
    value_g = value_rows.reshape(shape_g)
    scores = block_scores(query_g, key_g, span)
    top = jnp.max(scores, axis=-1, keepdims=True)
    expd = jnp.exp(scores - top)
    total = jnp.sum(expd, axis=-1, keepdims=True)
    probs_low = (expd / total).astype(jnp.bfloat16)
    context = jnp.einsum("bhqk,bkhd->bqhd", probs_low, value_g, preferred_element_type=jnp.float32)
    log_total = jnp.transpose((top + jnp.log(total))[..., 0], (0, 2, 1)).reshape(rows, heads)
    return (context.reshape(rows, heads * width), log_total)


def attend_back(query_rows, key_rows, value_rows, log_total, d_context, span):
    rows, heads, width = query_rows.shape
    groups = rows // span
    shape_g = (groups, span, heads, width)
    query_g = query_rows.reshape(shape_g)
    key_g = key_rows.reshape(shape_g)
    value_g = value_rows.reshape(shape_g)
    d_context_g = d_context.reshape(shape_g)
    lse_g = jnp.transpose(log_total.reshape(groups, span, heads), (0, 2, 1))
    scores = block_scores(query_g, key_g, span)
    probs = jnp.exp(scores - lse_g[..., None])
    probs_low = probs.astype(jnp.bfloat16)
    d_probs = jnp.einsum(
        "bqhd,bkhd->bhqk", d_context_g, value_g, preferred_element_type=jnp.float32
    )
    d_values = jnp.einsum(
        "bhqk,bqhd->bkhd", probs_low, d_context_g, preferred_element_type=jnp.float32
    )
    row_dot = jnp.sum(probs * d_probs, axis=-1, keepdims=True)
    d_scores = (probs * (d_probs - row_dot)).astype(jnp.bfloat16)
    scale = width ** (-0.5)
    d_queries = (
        jnp.einsum("bhqk,bkhd->bqhd", d_scores, key_g, preferred_element_type=jnp.float32) * scale
    )
    d_keys = (
        jnp.einsum("bhqk,bqhd->bkhd", d_scores, query_g, preferred_element_type=jnp.float32) * scale
    )
    return jnp.stack([d_queries, d_keys, d_values], axis=2).reshape(rows, 3, heads, width)


def contract_rows(left, right):
    return lax.dot_general(
        left, right, (((0,), (0,)), ((), ())), preferred_element_type=jnp.float32
    )


def contract_cols(left, right):
    return lax.dot_general(
        left, right, (((1,), (1,)), ((), ())), preferred_element_type=jnp.float32
    )


def general_shards(
    tokens, w_qkv, w_out, w_gate, w_value, w_down, norm_gains, norm_biases, long_count, cotangent
):
    gathered = (
        lax.all_gather(w_qkv, "wide", axis=0, tiled=True),
        lax.all_gather(w_out, "wide", axis=0, tiled=True),
        lax.all_gather(w_gate, "wide", axis=0, tiled=True),
        lax.all_gather(w_value, "wide", axis=0, tiled=True),
        lax.all_gather(w_down, "wide", axis=1, tiled=True),
        lax.all_gather(norm_gains, "wide", axis=1, tiled=True),
        lax.all_gather(norm_biases, "wide", axis=1, tiled=True),
    )
    full_qkv, full_out, wide_gate, wide_value, wide_down, gains_all, biases_all = gathered
    gains_f = gains_all.astype(jnp.float32)
    biases_f = biases_all.astype(jnp.float32)
    rows_dev = tokens.shape[0]
    n_blocks = rows_dev // LONG
    long_here = long_count[0, 0]
    tokens_f = tokens.astype(jnp.float32)
    mixed = jnp.dot(tokens, full_qkv, preferred_element_type=jnp.float32).astype(jnp.bfloat16)
    heads_view = mixed.reshape(n_blocks, LONG, 3, HEADS, HEAD_DIM)
    query_blk = heads_view[:, :, 0]
    key_blk = heads_view[:, :, 1]
    value_blk = heads_view[:, :, 2]
    block_ids = jnp.arange(n_blocks)

    def forward_block(entry):
        block_id, query_rows, key_rows, value_rows = entry
        return lax.cond(
            block_id < long_here,
            lambda operands: attend(operands[0], operands[1], operands[2], LONG),
            lambda operands: attend(operands[0], operands[1], operands[2], SHORT),
            (query_rows, key_rows, value_rows),
        )

    context_f, lse_rows = lax.map(forward_block, (block_ids, query_blk, key_blk, value_blk))
    context = context_f.reshape(rows_dev, D).astype(jnp.bfloat16)
    branch = jnp.dot(context, full_out, preferred_element_type=jnp.float32)
    hidden_in = tokens_f + branch
    normed = norm_rows(hidden_in, gains_f[0], biases_f[0])
    normed_low = normed.astype(jnp.bfloat16)
    all_rows = lax.all_gather(normed_low, "narrow", axis=0, tiled=True)
    gate = jnp.dot(all_rows, wide_gate, preferred_element_type=jnp.float32)
    value_up = jnp.dot(all_rows, wide_value, preferred_element_type=jnp.float32)
    product_f, pull_product = jax.vjp(gelu_product, gate, value_up)
    product = product_f.astype(jnp.bfloat16)
    ffn_out = lax.psum_scatter(
        jnp.dot(product, wide_down, preferred_element_type=jnp.float32),
        "narrow",
        scatter_dimension=0,
        tiled=True,
    )
    out_in = normed + ffn_out
    layer_out, pull_second = jax.vjp(norm_rows, out_in, gains_f[1], biases_f[1])
    d_out, d_gain_two, d_bias_two = pull_second(cotangent.astype(jnp.float32))
    d_ffn = d_out.astype(jnp.bfloat16)
    d_rows = lax.all_gather(d_ffn, "narrow", axis=0, tiled=True)
    grad_down = contract_rows(product, d_rows)
    d_product = contract_cols(d_rows, wide_down)
    d_gate, d_up = pull_product(d_product)
    d_gate_low = d_gate.astype(jnp.bfloat16)
    d_up_low = d_up.astype(jnp.bfloat16)
    grad_gate = contract_rows(all_rows, d_gate_low)
    grad_value = contract_rows(all_rows, d_up_low)
    d_normed = lax.psum_scatter(
        contract_cols(d_gate_low, wide_gate) + contract_cols(d_up_low, wide_value),
        "narrow",
        scatter_dimension=0,
        tiled=True,
    )
    d_normed_total = d_out + d_normed
    unused_out, pull_first = jax.vjp(norm_rows, hidden_in, gains_f[0], biases_f[0])
    d_hidden, d_gain_one, d_bias_one = pull_first(d_normed_total)
    d_branch = d_hidden.astype(jnp.bfloat16)
    grad_out = contract_rows(context, d_branch)
    d_context = contract_cols(d_branch, full_out).astype(jnp.bfloat16)
    d_context_blk = d_context.reshape(n_blocks, LONG, HEADS, HEAD_DIM)

    def backward_block(entry):
        block_id, query_rows, key_rows, value_rows, log_total, d_ctx = entry
        return lax.cond(
            block_id < long_here,
            lambda operands: attend_back(
                operands[0], operands[1], operands[2], operands[3], operands[4], LONG
            ),
            lambda operands: attend_back(
                operands[0], operands[1], operands[2], operands[3], operands[4], SHORT
            ),
            (query_rows, key_rows, value_rows, log_total, d_ctx),
        )

    d_mixed_f = lax.map(
        backward_block, (block_ids, query_blk, key_blk, value_blk, lse_rows, d_context_blk)
    )
    d_mixed = d_mixed_f.reshape(rows_dev, 3 * D).astype(jnp.bfloat16)
    grad_qkv = contract_rows(tokens, d_mixed)
    input_grad = d_hidden + contract_cols(d_mixed, full_qkv)
    grad_gains = jnp.stack([d_gain_one, d_gain_two])
    grad_biases = jnp.stack([d_bias_one, d_bias_two])
    pieces = (
        lax.psum_scatter(
            grad_qkv.astype(jnp.bfloat16), "wide", scatter_dimension=0, tiled=True
        ).astype(jnp.float32),
        lax.psum_scatter(
            grad_out.astype(jnp.bfloat16), "wide", scatter_dimension=0, tiled=True
        ).astype(jnp.float32),
        lax.psum_scatter(
            grad_gate.astype(jnp.bfloat16), "wide", scatter_dimension=0, tiled=True
        ).astype(jnp.float32),
        lax.psum_scatter(
            grad_value.astype(jnp.bfloat16), "wide", scatter_dimension=0, tiled=True
        ).astype(jnp.float32),
        lax.psum_scatter(
            grad_down.astype(jnp.bfloat16), "wide", scatter_dimension=1, tiled=True
        ).astype(jnp.float32),
        lax.psum_scatter(
            grad_gains.astype(jnp.bfloat16), "wide", scatter_dimension=1, tiled=True
        ).astype(jnp.float32),
        lax.psum_scatter(
            grad_biases.astype(jnp.bfloat16), "wide", scatter_dimension=1, tiled=True
        ).astype(jnp.float32),
    )
    qkv_piece, out_piece, gate_piece, value_piece, down_piece, gains_piece, biases_piece = pieces
    qkv_piece, out_piece, gains_piece, biases_piece = (
        lax.psum(qkv_piece.astype(jnp.bfloat16), "narrow").astype(jnp.float32),
        lax.psum(out_piece.astype(jnp.bfloat16), "narrow").astype(jnp.float32),
        lax.psum(gains_piece.astype(jnp.bfloat16), "narrow").astype(jnp.float32),
        lax.psum(biases_piece.astype(jnp.bfloat16), "narrow").astype(jnp.float32),
    )
    return (
        layer_out.astype(jnp.bfloat16),
        input_grad,
        qkv_piece,
        out_piece,
        gate_piece,
        value_piece,
        down_piece,
        gains_piece,
        biases_piece,
    )


AXES = ("wide", "narrow")
F32 = jnp.float32
BF16 = jnp.bfloat16
MIB = 1024 * 1024
RING = (0, 1, 3, 2)
PAIR = 2 * HEAD_DIM


def dot(left, right):
    return jnp.dot(left, right, preferred_element_type=F32)


class Plane:
    def __init__(self, wide, narrow):
        self.size = {"z": wide // 4, "ring": len(RING), "a": 2, "b": 2, "core": 2, "y": narrow}
        self.pairs = {}
        count = wide * narrow
        for dim, size in self.size.items():
            for step in range(1, size) if dim != "ring" else ():
                self.pairs[dim, step] = [(i, self.partner(i, dim, step)) for i in range(count)]
        after_z = {z: RING[(n + 1) % len(RING)] for n, z in enumerate(RING)}
        self.pairs["next", 1] = [(i, i % 8 + 8 * after_z[i // 8]) for i in range(count)]
        self.pairs["prev", 1] = [(j, i) for i, j in self.pairs["next", 1]]
        w = lax.axis_index("wide")
        self.z, self.x, self.core = w // 4, (w // 2) % 2, w % 2
        self.y = lax.axis_index("narrow")

    @staticmethod
    def partner(i, dim, step):
        z, x, c, y = i // 8, (i // 4) % 2, (i // 2) % 2, i % 2
        if dim == "z":
            z ^= step
        elif dim == "core":
            c ^= 1
        elif dim == "y" or (dim == "a") == (c == 1):
            y ^= 1
        else:
            x ^= 1
        return ((z * 2 + x) * 2 + c) * 2 + y

    def swap(self, value, dim, step=1):
        return lax.ppermute(value, AXES, self.pairs[dim, step])

    def sum_z(self, parts):
        total = parts[0].astype(F32)
        for k in range(1, self.size["z"]):
            total = total + self.swap(parts[k], "z", k).astype(F32)
        return total.astype(BF16)

    def tables(self, order, numbered):
        sizes = [self.size[dim] for dim in order]
        number = np.arange(int(np.prod(sizes)))
        rest, digit = number, {}
        for dim, size in zip(order, sizes):
            digit[dim] = rest % size
            rest = rest // size
        first = self.core == 0
        a_here = jnp.where(first, self.x, self.y)
        b_here = jnp.where(first, self.y, self.x)
        if "ring" in digit:
            at = sum(jnp.where(self.z == z, n, 0) for n, z in enumerate(RING))
            z = sum(jnp.where((at - digit["ring"]) % len(RING) == n, z, 0) for n, z in enumerate(RING))
        else:
            z = digit["z"] ^ self.z
        a = digit["a"] ^ a_here
        b = digit["b"] ^ b_here
        x, y = jnp.where(first, a, b), jnp.where(first, b, a)
        return numbered(z, x, y).astype(jnp.int32)


def after(value, *events):
    return lax.optimization_barrier((value,) + events)[0]


def fence(*values):
    return lax.optimization_barrier(values)


def smem():
    return pl.BlockSpec(memory_space=pltpu.SMEM)


def whole(shape):
    zeros = (0,) * len(shape)
    return pl.BlockSpec(tuple(shape), lambda *_: zeros)


def kernel_call(body, grid, ins, outs, scratch=(), flops=0, name=None, room=6, far=False):
    blocks = [(spec.block_shape, a.dtype) for a, spec in ins] + [(spec.block_shape, d) for _, d, spec in outs]
    held = sum(2 * int(np.prod(shape)) * np.dtype(d).itemsize for shape, d in blocks if shape is not None)
    held += sum(int(np.prod(v.shape)) * np.dtype(v.dtype).itemsize for v in scratch)
    size = sum(a.size * a.dtype.itemsize for a, _ in ins)
    size += sum(int(np.prod(s)) * np.dtype(d).itemsize for s, d, _ in outs)
    return pl.pallas_call(
        body,
        grid=grid,
        in_specs=[spec for _, spec in ins],
        out_specs=[spec for _, _, spec in outs],
        out_shape=[jax.ShapeDtypeStruct(s, d) for s, d, _ in outs],
        scratch_shapes=list(scratch),
        compiler_params=pltpu.CompilerParams(
            dimension_semantics=("arbitrary",) * len(grid), vmem_limit_bytes=held // 2 + room * MIB
        ),
        cost_estimate=pl.CostEstimate(flops=0, bytes_accessed=0, transcendentals=0),
        name=name,
    )(*[pltpu.with_memory_space_constraint(a, pltpu.HBM) if far and a.ndim > 1 else a for a, _ in ins])


ROWS = 256


def own_rows(steps, cols):
    return pl.BlockSpec((ROWS, cols), lambda i: (jnp.minimum(i, steps - 1), 0))


def partner_rows(steps, cols):
    return pl.BlockSpec((ROWS, cols), lambda i: (jnp.maximum(i - steps, 0), 0))


def pick_rows(i, steps, own_ref, partner_ref):
    return jnp.where(i < steps, own_ref[...], partner_ref[...])


def split_kernel(place, w_qkv, w_out, gains, biases, mine, send):
    first = place[0] == 0
    half = D // 2
    for n in range(4):
        source, start = (w_qkv, n * D) if n < 3 else (w_out, 0)
        low, high = source[:, start : start + half], source[:, start + half : start + D]
        mine[:, n * half : (n + 1) * half] = jnp.where(first, low, high)
        send[:, n * half : (n + 1) * half] = jnp.where(first, high, low)
    rows = jnp.concatenate([gains[...], biases[...]], axis=0).astype(F32)
    eye = jnp.where(
        lax.broadcasted_iota(jnp.int32, (128, rows.shape[0]), 0)
        == lax.broadcasted_iota(jnp.int32, (128, rows.shape[0]), 1),
        1.0,
        0.0,
    )
    norm_cols = contract_cols(rows.T.astype(BF16), eye.astype(BF16)).astype(BF16)
    mine[:, 4 * half :] = norm_cols
    send[:, 4 * half :] = norm_cols


def fill_blocks(table, pieces, weight, cols=slice(None)):
    count = pieces[0].shape[0]
    for n, piece in enumerate(pieces):
        for k in range(count):
            weight[table[n * count + k]] = piece[k, :, cols]


def qkv_kernel(steps, groups, pieces, table, own, partner, *refs):
    i = pl.program_id(0)
    parts = refs[:pieces]
    mixed_own, mixed_partner, weight, out_w, norms, table_t = refs[pieces:]
    cols, part = weight.shape[2], out_w.shape[2]
    tall = weight.shape[0] * weight.shape[1]

    @pl.when(i == 0)
    def _():
        fill_blocks(table, parts, weight, slice(0, cols))
        fill_blocks(table, parts, out_w, slice(cols, cols + part))
        fill_blocks(table, parts, table_t, slice(cols + part, None))
        norms[...] = table_t[...].reshape(tall, table_t.shape[2]).astype(F32).T[: norms.shape[0]]

    rows_here = pick_rows(i, steps, own, partner)
    for g in range(groups):
        span = slice(g * cols // groups, (g + 1) * cols // groups)
        tile = weight[:, :, span].reshape(tall, cols // groups)
        value = dot(rows_here, tile).astype(BF16)

        @pl.when(i < steps)
        def _():
            mixed_own[:, span] = value

        @pl.when(i >= steps)
        def _():
            mixed_partner[:, span] = value


def lane_masks():
    lane = lax.broadcasted_iota(jnp.int32, (1, PAIR), 1)
    return [lane < HEAD_DIM, lane >= HEAD_DIM]


def keep(mask, value):
    return jnp.where(mask, value, jnp.zeros_like(value))


def fill_distance(distance):
    row = lax.broadcasted_iota(jnp.int32, distance.shape, 0)
    col = lax.broadcasted_iota(jnp.int32, distance.shape, 1)
    distance[...] = jnp.abs(row - col).astype(F32)


def scores_of(queries, keys, slope, distance):
    raw = lax.dot_general(queries, keys, (((1,), (1,)), ((), ())), preferred_element_type=F32)
    return raw - slope * distance


def attend_rows(queries, keys, values, slope, away):
    s = jnp.concatenate([scores_of(q, k, slope, away) for q, k in zip(queries, keys)], axis=0)
    top = jnp.max(s, axis=-1, keepdims=True)
    e = jnp.exp(s - top)
    norm = jnp.sum(e, axis=-1, keepdims=True)
    p = (e * (1.0 / norm)).astype(BF16)
    tall = queries[0].shape[0]
    out = [dot(p[n * tall : (n + 1) * tall], v) for n, v in enumerate(values)]
    return jnp.concatenate(out, axis=0), top + jnp.log(norm)


def tiles(value, tall):
    return [value[n : n + tall] for n in range(0, value.shape[0], tall)]


def pair_cols(part, pair):
    return pl.ds(pl.multiple_of(part * (D // 2) + pair * PAIR, PAIR), PAIR)


def attend_kernel(place, flags, slopes, mixed, *refs):
    context, logs, distance = refs[-3:]
    masks = lane_masks()
    scale = HEAD_DIM**-0.5
    lane = lax.broadcasted_iota(jnp.int32, (1, 128), 1)
    fill_distance(distance)
    for extra in refs[:-3]:
        context[LONG:, :] = extra[...].reshape(context.shape[0] - LONG, context.shape[1])

    def run(is_long):
        tall = 2 * SHORT if is_long else LONG

        def one_pair(pair, _):
            q_all, k_all, v_all = (mixed[:, pair_cols(part, pair)] for part in range(3))
            totals = [0.0] * (LONG // tall)
            for head in range(2):
                slope = slopes[pair * 2 + head]
                q = (keep(masks[head], q_all) * scale).astype(BF16)
                v = keep(masks[head], v_all)
                for n in range(LONG // tall):
                    rows = slice(n * tall, (n + 1) * tall)
                    if is_long:
                        out = attend_rows([q[rows]], [k_all], [v], slope, distance[rows, :])
                    else:
                        out = attend_rows(
                            tiles(q, SHORT), tiles(k_all, SHORT), tiles(v, SHORT), slope, distance[:SHORT, :SHORT]
                        )
                    totals[n] = totals[n] + out[0]
                    logs[rows, :] = jnp.where(lane == pair * 2 + head, out[1], logs[rows, :])
            for n in range(LONG // tall):
                context[n * tall : (n + 1) * tall, pair_cols(0, pair)] = totals[n].astype(BF16)
            return 0

        lax.fori_loop(0, D // 2 // PAIR, one_pair, 0)

    logs[...] = jnp.zeros_like(logs)
    flag = flags[place[1]]

    @pl.when(flag > 0)
    def _():
        run(True)

    @pl.when(flag <= 0)
    def _():
        run(False)


def back_rows(queries, keys, values, d_rows, log_rows, slope, away, scaled_keys):
    s = jnp.concatenate([scores_of(q, k, slope, away) for q, k in zip(queries, keys)], axis=0)
    p = jnp.exp(s - log_rows)
    d_p = jnp.concatenate([contract_cols(d, v) for d, v in zip(d_rows, values)], axis=0)
    d_s = (p * (d_p - jnp.sum(p * d_p, axis=-1, keepdims=True))).astype(BF16)
    p = p.astype(BF16)
    tall = queries[0].shape[0]
    d_s, p = tiles(d_s, tall), tiles(p, tall)
    d_q = jnp.concatenate([dot(d, k) for d, k in zip(d_s, scaled_keys)], axis=0)
    d_k = [dot(q.T, d) for q, d in zip(queries, d_s)]
    d_v = [dot(d.T, w) for d, w in zip(d_rows, p)]
    return d_q, d_k, d_v


def attend_back_kernel(place, flags, slopes, mixed, d_context, logs_ref, d_query, d_key, d_value, distance):
    masks = lane_masks()
    scale = HEAD_DIM**-0.5
    fill_distance(distance)

    def run(is_long):
        tall = 2 * SHORT if is_long else LONG
        logs = logs_ref[...]
        lane = lax.broadcasted_iota(jnp.int32, (1, 128), 1)

        def one_pair(pair, _):
            q_all, k_all, v_all = (mixed[:, pair_cols(part, pair)] for part in range(3))
            d_all = d_context[:, pair_cols(0, pair)]
            d_q, d_k, d_v = [0.0] * (LONG // tall), 0.0, 0.0
            for head in range(2):
                slope = slopes[pair * 2 + head]
                q = (keep(masks[head], q_all) * scale).astype(BF16)
                k = (keep(masks[head], k_all) * scale).astype(BF16)
                d_c = keep(masks[head], d_all)
                log_all = jnp.sum(jnp.where(lane == pair * 2 + head, logs, 0.0), axis=-1, keepdims=True)
                for n in range(LONG // tall):
                    rows = slice(n * tall, (n + 1) * tall)
                    if is_long:
                        out = back_rows(
                            [q[rows]], [k_all], [v_all], [d_c[rows]], log_all[rows], slope, distance[rows, :], [k]
                        )
                        new_k, new_v = out[1][0], out[2][0]
                    else:
                        out = back_rows(
                            tiles(q, SHORT),
                            tiles(k_all, SHORT),
                            tiles(v_all, SHORT),
                            tiles(d_c, SHORT),
                            log_all,
                            slope,
                            distance[:SHORT, :SHORT],
                            tiles(k, SHORT),
                        )
                        new_k, new_v = (jnp.concatenate(part, axis=1) for part in out[1:])
                    d_q[n] = d_q[n] + out[0]
                    d_k, d_v = d_k + new_k, d_v + new_v
            cols = pair_cols(0, pair)
            for n in range(LONG // tall):
                d_query[n * tall : (n + 1) * tall, cols] = d_q[n].astype(BF16)
            d_key[:, cols] = d_k.T.astype(BF16)
            d_value[:, cols] = d_v.T.astype(BF16)
            return 0

        lax.fori_loop(0, D // 2 // PAIR, one_pair, 0)

    flag = flags[place[1]]

    @pl.when(flag > 0)
    def _():
        run(True)

    @pl.when(flag <= 0)
    def _():
        run(False)


def spread(rows):
    center = jnp.mean(rows, axis=-1, keepdims=True)
    shifted = rows - center
    inverse = lax.rsqrt(jnp.mean(shifted * shifted, axis=-1, keepdims=True) + 1e-05)
    return shifted * inverse, inverse


def norm_back(e, unit, inverse):
    mean_e = jnp.mean(e, axis=-1, keepdims=True)
    mean_en = jnp.mean(e * unit, axis=-1, keepdims=True)
    return (e - mean_e - unit * mean_en) * inverse


def first_norm_kernel(place, tokens, ctx_mine, ctx_other, w_mine, w_other_rows, norms, unit, inverse, low):
    core = place[0]
    half = w_mine.shape[0] // 2
    wide = w_mine.shape[2]

    def branch(weight):
        return dot(ctx_mine[...], weight(core)) + dot(ctx_other[...], weight(1 - core))

    mine = branch(lambda c: w_mine[pl.ds(c * half, half)].reshape(D // 2, wide))
    other = branch(lambda c: w_other_rows[pl.ds(pl.multiple_of(LONG + c * (D // 2), 128), D // 2), :])
    first = core == 0
    added = jnp.concatenate([jnp.where(first, mine, other), jnp.where(first, other, mine)], axis=1)
    n, inv = spread(tokens[...].astype(F32) + added)
    unit[...] = n
    inverse[...] = inv
    low[...] = (n * norms[0:1, :] + norms[2:3, :]).astype(BF16)


def gelu_parts(x):
    t = 1.0 / (1.0 + (0.3275911 * 0.5**0.5) * jnp.abs(x))
    poly = t * (
        0.254829592 + t * (-0.284496736 + t * (1.421413741 + t * (-1.453152027 + t * 1.061405429)))
    )
    bell = jnp.exp(-0.5 * (x * x))
    tail = 0.5 * poly * bell
    phi = jnp.where(x >= 0, 1.0 - tail, tail)
    return x * phi, phi + x * bell * 0.3989422804014327


def columns_of(weight, half, span):
    count = weight.shape[0] // 2
    return weight[half * count : (half + 1) * count, :, span].reshape(D, span.stop - span.start)


def gate_kernel(steps, pieces, table, own, partner, *refs):
    i = pl.program_id(0)
    active, slope, gate_w = refs[pieces:]

    @pl.when(i == 0)
    def _():
        fill_blocks(table, refs[:pieces], gate_w)

    rows = pick_rows(i, steps, own, partner)
    width = gate_w.shape[2]
    for half in range(2):
        for start in range(0, width, 256):
            out = slice(half * width + start, half * width + start + 256)
            gate = dot(rows, columns_of(gate_w, half, slice(start, start + 256)))
            act, grad = gelu_parts(gate)
            active[:, out] = act.astype(BF16)
            slope[:, out] = grad.astype(BF16)


def value_kernel(steps, pieces, table, own, partner, active, slope, *refs):
    i = pl.program_id(0)
    product, scaled, value_w = refs[pieces:]

    @pl.when(i == 0)
    def _():
        fill_blocks(table, refs[:pieces], value_w)

    rows = pick_rows(i, steps, own, partner)
    width = value_w.shape[2]
    for half in range(2):
        for start in range(0, width, 256):
            out = slice(half * width + start, half * width + start + 256)
            up = dot(rows, columns_of(value_w, half, slice(start, start + 256)))
            product[:, out] = (active[:, out].astype(F32) * up).astype(BF16)
            scaled[:, out] = (slope[:, out].astype(F32) * up).astype(BF16)


def times_down(product, down_w):
    width = down_w.shape[2]
    total = 0.0
    for half in range(2):
        part = product[:, half * width : (half + 1) * width]
        total = total + contract_cols(part, columns_of(down_w, half, slice(0, width)))
    return total


def down_first_kernel(table, product, *refs):
    partner, down_w = refs[-2:]

    @pl.when(pl.program_id(0) == 0)
    def _():
        fill_blocks(table, refs[:-2], down_w)

    partner[...] = times_down(product, down_w).astype(BF16)


def down_kernel(product, down_w, own):
    own[...] = times_down(product, down_w)


def second_norm_kernel(unit_one, norms, part_own, part_got, cotangent, out, d_z, d_ffn, sums):
    normed = unit_one[...] * norms[0:1, :] + norms[2:3, :]
    n, inv = spread(normed + (part_own[...] + part_got[...].astype(F32)))
    gain = norms[1:2, :]
    out[...] = (n * gain + norms[3:4, :]).astype(BF16)
    c = cotangent[...].astype(F32)
    back = norm_back(gain * c, n, inv)
    d_z[...] = back
    d_ffn[...] = back.astype(BF16)
    add_sums(sums, c * n, c)


def add_sums(sums, gain_terms, bias_terms):
    @pl.when(pl.program_id(0) == 0)
    def _():
        sums[...] = jnp.zeros_like(sums)

    sums[0:1, :] += jnp.sum(gain_terms, axis=0, keepdims=True)
    sums[1:2, :] += jnp.sum(bias_terms, axis=0, keepdims=True)


def ffn_back_kernel(
    steps, own, partner, down_w, gate_w, value_w, active, slope, d_gate, d_up, back_own, back_partner
):
    i = pl.program_id(0)
    rows = pick_rows(i, steps, own, partner)
    width = down_w.shape[2]
    total = jnp.zeros((ROWS, D), F32)
    for half in range(2):
        for start in range(0, width, 256):
            span = slice(start, start + 256)
            out = slice(half * width + start, half * width + start + 256)
            d_product = dot(rows, columns_of(down_w, half, span))
            dg = (d_product * slope[:, out].astype(F32)).astype(BF16)
            du = (d_product * active[:, out].astype(F32)).astype(BF16)
            d_gate[:, out] = dg
            d_up[:, out] = du
            total = total + contract_cols(dg, columns_of(gate_w, half, span))
            total = total + contract_cols(du, columns_of(value_w, half, span))

    @pl.when(i < steps)
    def _():
        back_own[...] = total

    @pl.when(i >= steps)
    def _():
        back_partner[...] = total.astype(BF16)


def weight_grad_kernel(table, left_own, left_partner, right_a, right_b, *refs):
    i = pl.program_id(0)
    parts, blocks = refs[:-1], refs[-1]
    rows = left_own.shape[0]
    count, tall, cols = blocks.shape
    for half, right in enumerate((right_a, right_b)):
        value = contract_rows(left_own[...], right[:rows, :]) + contract_rows(left_partner[...], right[rows:, :])
        value = value.astype(BF16).reshape(count // 2, tall, cols)
        blocks[half * (count // 2) : (half + 1) * (count // 2)] = value
    span = pl.ds(pl.multiple_of(i * cols, cols), cols)
    each = count // len(parts)
    for k in range(count):
        parts[k // each][k % each, :, span] = blocks[table[k]]


def first_norm_back_kernel(
    place,
    unit_ref,
    inverse,
    norms,
    d_z,
    part_own,
    part_got,
    ctx_mine,
    ctx_other,
    w_mine,
    w_other,
    d_hidden,
    dctx_mine,
    dctx_other,
    grad_keep,
    grad_send,
    sums,
    grad,
):
    core = place[0]
    first = core == 0
    unit = unit_ref[...]
    d_normed = d_z[...] + (part_own[...] + part_got[...].astype(F32))
    back = norm_back(norms[0:1, :] * d_normed, unit, inverse[...])
    low = back.astype(BF16)
    d_hidden[...] = back
    add_sums(sums, d_normed * unit, d_normed)
    half, wide = w_mine.shape[0] // 2, w_mine.shape[2]
    low_mine = jnp.where(first, low[:, :wide], low[:, wide:])
    low_other = jnp.where(first, low[:, wide:], low[:, :wide])
    for head_core, out in ((core, dctx_mine), (1 - core, dctx_other)):
        near = w_mine[pl.ds(head_core * half, half)].reshape(D // 2, wide)
        far = w_other[pl.ds(pl.multiple_of(LONG + head_core * (D // 2), 128), D // 2), :]
        out[...] = (contract_cols(low_mine, near) + contract_cols(low_other, far)).astype(BF16)

    @pl.when(pl.program_id(0) == 0)
    def _():
        grad[...] = jnp.zeros_like(grad)

    shape = (half,) + grad.shape[1:]
    grad[pl.ds(core * half, half)] += contract_rows(ctx_mine[...], low).reshape(shape)
    grad[pl.ds((1 - core) * half, half)] += contract_rows(ctx_other[...], low).reshape(shape)

    @pl.when(pl.program_id(0) == pl.num_programs(0) - 1)
    def _():
        left, right = grad[:, :, :wide], grad[:, :, wide:]
        grad_keep[...] = jnp.where(first, left, right)
        grad_send[...] = jnp.where(first, right, left).astype(BF16)


def qkv_grad_kernel(table, left_own, left_partner, *refs):
    d_own, d_partner = refs[:3], refs[3:6]
    out_grad, sums_one, sums_two, near, far, blocks, norm_grad = refs[6:]
    i = pl.program_id(0)
    count, tall, cols = blocks.shape

    @pl.when(i == 0)
    def _():
        one, two = sums_one[...], sums_two[...]
        empty = jnp.zeros((norm_grad.shape[2] - 4, D), F32)
        stacked = jnp.concatenate([one[0:1], two[0:1], one[1:2], two[1:2], empty], axis=0)
        norm_grad[...] = stacked.T.astype(BF16).reshape(norm_grad.shape)

    for g in range(3):

        @pl.when(i == g)
        def _():
            value = contract_rows(left_own[...], d_own[g][...]) + contract_rows(left_partner[...], d_partner[g][...])
            blocks[...] = value.astype(BF16).reshape(blocks.shape)
            for k in range(count):
                target, place = (near if k < count // 2 else far), table[k]
                target[k % (count // 2), :, g * cols : (g + 1) * cols] = blocks[place]
                if g == 0:
                    start = 3 * cols
                    for more in (out_grad, norm_grad):
                        stop = start + more.shape[2]
                        target[k % (count // 2), :, start:stop] = more[place]
                        start = stop


def input_grad_kernel(d_query, d_key, d_value, weight, *refs):
    cols = d_query.shape[1]
    total = 0.0
    for g, left in enumerate((d_query, d_key, d_value)):
        tile = weight[:, :, g * cols : (g + 1) * cols].reshape(D, cols)
        total = total + contract_cols(left[...], tile)
    for more in refs[:-1]:
        total = total + more[...].astype(F32)
    refs[-1][...] = total.astype(refs[-1].dtype)


def pieces_kernel(place, here, there, got, qkv, out, gains, biases):
    first, own = place[0] == 0, place[1] == 1
    half = D // 2
    mine = jnp.where(own, here[...], there[...])
    for n in range(4):
        a, b = mine[:, n * half : (n + 1) * half].astype(F32), got[:, n * half : (n + 1) * half].astype(F32)
        target, start = (qkv, n * D) if n < 3 else (out, 0)
        target[:, start : start + half] = jnp.where(first, a, b)
        target[:, start + half : start + D] = jnp.where(first, b, a)
    rows = (mine[:, 4 * half :].astype(F32) + got[:, 4 * half :].astype(F32)).T
    gains[...] = rows[0:2]
    biases[...] = rows[2:4]


def by_core(core, mine, other, axis):
    first = core == 0
    return jnp.stack([jnp.where(first, mine, other), jnp.where(first, other, mine)], axis=axis)


def half_of(core, halves, axis):
    zero, one = (lax.index_in_dim(halves, k, axis, keepdims=False) for k in range(2))
    first = core == 0
    return jnp.where(first, zero, one), jnp.where(first, one, zero)


def plane_shards(
    wide,
    narrow,
    tokens,
    w_qkv,
    w_out,
    w_gate,
    w_value,
    w_down,
    norm_gains,
    norm_biases,
    long_count,
    cotangent,
):
    plane = Plane(wide, narrow)
    swap = plane.swap
    core, y_here = plane.core, plane.y
    rows = tokens.shape[0]
    steps = rows // ROWS
    tall = w_qkv.shape[0]
    blocks = wide * narrow // 2
    z_size = plane.size["z"]
    head_cols = D // 2
    width = w_gate.shape[1] // 2
    hidden = 2 * width
    pairs = head_cols // PAIR
    qkv_to = plane.tables(("z", "a", "b"), lambda z, x, y: (z * 2 + x) * 2 + y)
    ffn_to = plane.tables(("z", "a", "b"), lambda z, x, y: y * (2 * z_size) + z * 2 + x)
    down_to = plane.tables(("a", "b", "ring"), lambda z, x, y: y * (2 * z_size) + z * 2 + x)
    place = jnp.reshape(core, (1,)).astype(jnp.int32)
    first = core == 0

    def wholes(arrays):
        return [(v, whole(v.shape)) for v in arrays]

    def step_rows(cols):
        return pl.BlockSpec((ROWS, cols), lambda i: (i, 0))

    head_shape = (tall, 4 * head_cols + 128)
    head_part, head_send = kernel_call(
        split_kernel,
        (1,),
        [(place, smem())] + wholes([w_qkv, w_out, norm_gains, norm_biases]),
        [(head_shape, BF16, whole(head_shape))] * 2,
        name="split",
        far=True,
    )
    flag = jnp.broadcast_to(long_count.astype(F32), (8, 128))
    head_got, flag_got = fence(swap(head_send, "core"), swap(flag, "core"))
    head_part = jnp.where(y_here == core, head_part, head_got)
    head_parts = [head_part] + [swap(head_part, "z", k) for k in range(1, z_size)]
    ffn_parts = [after(w_gate, head_part), w_value, w_down.T]
    ffn_other = jnp.concatenate([jnp.where(first, v[:, width:], v[:, :width]) for v in ffn_parts], axis=1)
    ffn_got = swap(ffn_other, "core")
    tokens_other = swap(after(tokens, head_part), "core")
    flags = jnp.stack([long_count[0, 0], flag_got[0, 0].astype(jnp.int32)])
    slopes = lax.dynamic_slice_in_dim(alibi_slopes(HEADS), core * (HEADS // 2), HEADS // 2)

    def ffn_chip(n):
        v, got = ffn_parts[n], ffn_got[:, n * width : (n + 1) * width]
        mine = jnp.where(first, v[:, :width], v[:, width:])
        return jnp.concatenate([jnp.where(first, mine, got), jnp.where(first, got, mine)], axis=0)

    def doubled(value, step, *events):
        got = swap(value, "z", step)
        return jnp.concatenate(lax.optimization_barrier((value, got) + events)[:2], axis=0)

    def along_plane(held):
        near = swap(held, "a")
        return held, near, swap(held, "b")

    def joined(value, got):
        return jnp.concatenate([value, got], axis=0)

    gate_one, value_one, down_one = (ffn_chip(n) for n in range(3))

    def all_z(value):
        return [value] + [swap(value, "z", k) for k in range(1, z_size)]

    down_got = swap(down_one, "a")
    *head_parts, down_got, tokens_other = fence(*head_parts, down_got, tokens_other)
    qkv_z = jnp.stack(head_parts)
    down_two = jnp.stack([down_one, down_got])

    head_near, head_far = swap(qkv_z, "a"), swap(qkv_z, "b")
    head_near, head_far, *gate_parts = fence(head_near, head_far, *all_z(after(gate_one, qkv_z)))
    gate_z = jnp.stack(gate_parts)

    head_last = swap(head_near, "b")
    down_got = swap(after(down_two, head_near), "b")
    head_last, down_got, *value_parts = fence(head_last, down_got, *all_z(after(value_one, head_near)))
    value_z, down_four = jnp.stack(value_parts), joined(down_two, down_got)
    qkv_blocks = [qkv_z, head_near, head_far, head_last]

    gate_near, gate_far = swap(after(gate_z, head_last), "a"), swap(after(gate_z, head_last), "b")
    ring_one = swap(down_four, "next")
    block_row = (blocks, tall)
    mixed_own, mixed_partner, qkv_w, out_mine, norms = kernel_call(
        functools.partial(qkv_kernel, steps, 3, len(qkv_blocks)),
        (2 * steps,),
        [
            (qkv_to, smem()),
            (tokens, own_rows(steps, D)),
            (tokens_other, partner_rows(steps, D)),
        ]
        + wholes(qkv_blocks),
        [((rows, 3 * head_cols), BF16, own_rows(steps, 3 * head_cols))]
        + [((rows, 3 * head_cols), BF16, partner_rows(steps, 3 * head_cols))]
        + [(block_row + (n,), BF16, whole(block_row + (n,))) for n in (3 * head_cols, head_cols)]
        + [((8, D), F32, whole((8, D)))],
        scratch=[pltpu.VMEM(block_row + (128,), BF16)],
        flops=2 * 2 * rows * D * 3 * head_cols,
        name="mixed",
        far=True,
    )
    def attend(block, mixed, extra=()):
        tall_out = rows + sum(v.size for v in extra) // head_cols
        return kernel_call(
            attend_kernel,
            (1,),
            [(jnp.array([0, block], jnp.int32), smem()), (flags, smem()), (slopes, smem())] + wholes([mixed, *extra]),
            [((tall_out, head_cols), BF16, whole((tall_out, head_cols))), ((rows, 128), F32, whole((rows, 128)))],
            scratch=[pltpu.VMEM((LONG, LONG), F32)],
            flops=4 * rows * LONG * D,
            name="attend",
            room=12,
            far=True,
        )

    ctx_send, logs_partner = attend(1, mixed_partner, [out_mine])
    gate_near, gate_far, ring_one, ctx_send = fence(gate_near, gate_far, ring_one, ctx_send)

    gate_last = swap(gate_near, "b")
    value_near, value_far = swap(value_z, "a"), swap(value_z, "b")
    ring_two = swap(ring_one, "next")
    ctx_got = swap(ctx_send, "core")
    ctx_mine, logs_own = attend(0, after(mixed_own, ctx_send))

    unit_one, inverse_one, low = kernel_call(
        first_norm_kernel,
        (steps,),
        [
            (place, smem()),
            (tokens, step_rows(D)),
            (ctx_mine, step_rows(head_cols)),
            (ctx_got, step_rows(head_cols)),
        ]
        + wholes([out_mine, ctx_got, norms]),
        [
            ((rows, D), F32, step_rows(D)),
            ((rows, 1), F32, step_rows(1)),
            ((rows, D), BF16, step_rows(D)),
        ],
        flops=2 * rows * D * D,
        name="first_norm",
    )
    gate_last, value_near, value_far, ring_two, low = fence(gate_last, value_near, value_far, ring_two, low)
    gate_blocks = [gate_z, gate_near, gate_far, gate_last]
    value_last = swap(value_near, "b")
    ring_three = swap(ring_two, "next")
    low_other = swap(low, "core")

    w_shape = (blocks, 2 * tall, width)
    both_rows = [(low, own_rows(steps, D)), (low_other, partner_rows(steps, D))]
    active, slope, gate_w = kernel_call(
        functools.partial(gate_kernel, steps, len(gate_blocks)),
        (2 * steps,),
        [(ffn_to, smem())] + both_rows + wholes(gate_blocks),
        [((2 * rows, hidden), BF16, step_rows(hidden))] * 2 + [(w_shape, BF16, whole(w_shape))],
        name="gate",
    )
    value_last, ring_three, active = fence(value_last, ring_three, active)
    value_blocks = [value_z, value_near, value_far, value_last]
    down_blocks = [down_four, ring_one, ring_two, ring_three]
    product, slope, value_w = kernel_call(
        functools.partial(value_kernel, steps, len(value_blocks)),
        (2 * steps,),
        [(ffn_to, smem())] + both_rows + [(active, step_rows(hidden)), (slope, step_rows(hidden))] + wholes(value_blocks),
        [((2 * rows, hidden), BF16, step_rows(hidden))] * 2 + [(w_shape, BF16, whole(w_shape))],
        name="value",
    )
    part_send, down_w = kernel_call(
        down_first_kernel,
        (steps,),
        [(down_to, smem()), (product, pl.BlockSpec((ROWS, hidden), lambda i: (i + steps, 0)))] + wholes(down_blocks),
        [((rows, D), BF16, step_rows(D)), (w_shape, BF16, whole(w_shape))],
        name="down_first",
    )
    (part_own,) = kernel_call(
        down_kernel,
        (steps,),
        [(product, step_rows(hidden))] + wholes([down_w]),
        [((rows, D), F32, step_rows(D))],
        name="down",
    )
    part_got = swap(part_send, "core")
    layer_out, d_z, d_ffn, sums_two = kernel_call(
        second_norm_kernel,
        (steps,),
        [(unit_one, step_rows(D))]
        + wholes([norms])
        + [(part_own, step_rows(D)), (part_got, step_rows(D)), (cotangent, step_rows(D))],
        [
            ((rows, D), BF16, step_rows(D)),
            ((rows, D), F32, step_rows(D)),
            ((rows, D), BF16, step_rows(D)),
            ((8, D), F32, whole((8, D))),
        ],
        name="second_norm",
    )
    d_ffn_other = swap(d_ffn, "core")

    def weight_grad(left, left_other, right, to, parts):
        part = (blocks // parts, 2 * tall, width)
        cols = width // 3
        return kernel_call(
            weight_grad_kernel,
            (3,),
            [
                (to, smem()),
                (left, whole((rows, D))),
                (left_other, whole((rows, D))),
                (right, pl.BlockSpec((2 * rows, cols), lambda i: (0, i))),
                (right, pl.BlockSpec((2 * rows, cols), lambda i: (0, 3 + i))),
            ],
            [(part, BF16, whole(part))] * parts,
            scratch=[pltpu.VMEM((blocks, 2 * tall, cols), BF16)],
            flops=2 * 2 * rows * D * hidden,
            name="weight_grad",
        )

    def added(keep, got):
        return (keep.astype(F32) + got.astype(F32)).astype(BF16)

    def halves(keep, got):
        count = keep.shape[0] // 2
        return added(keep[:count], got[:count]), added(keep[count:], got[count:])

    def quarters(keep, got):
        return [added(keep[k], got[k]) for k in range(z_size)]

    down_parts = weight_grad(d_ffn, d_ffn_other, product, down_to, len(RING))
    d_gate, d_up, back_own, back_send = kernel_call(
        functools.partial(ffn_back_kernel, steps),
        (2 * steps,),
        [(after(d_ffn, down_parts[-1]), own_rows(steps, D)), (d_ffn_other, partner_rows(steps, D))]
        + wholes([down_w, gate_w, value_w])
        + [(active, step_rows(hidden)), (slope, step_rows(hidden))],
        [((2 * rows, hidden), BF16, step_rows(hidden))] * 2
        + [((rows, D), F32, own_rows(steps, D)), ((rows, D), BF16, partner_rows(steps, D))],
        flops=3 * 2 * 2 * rows * D * hidden,
        name="ffn_back",
    )
    down_got = swap(down_parts[3], "prev")
    gate_keep, gate_send = weight_grad(after(low, back_send), low_other, d_gate, ffn_to, 2)
    down_got, back_send, gate_send = fence(down_got, back_send, gate_send)

    gate_got = swap(gate_send, "b")
    down_got = swap(added(down_parts[2], down_got), "prev")
    back_got = swap(back_send, "core")
    d_hidden, dctx_mine, dctx_send, out_keep, out_send, sums_one = kernel_call(
        first_norm_back_kernel,
        (steps,),
        [
            (place, smem()),
            (unit_one, step_rows(D)),
            (inverse_one, step_rows(1)),
            (norms, whole(norms.shape)),
            (d_z, step_rows(D)),
            (back_own, step_rows(D)),
            (back_got, step_rows(D)),
            (ctx_mine, step_rows(head_cols)),
            (ctx_got, step_rows(head_cols)),
        ]
        + wholes([out_mine, ctx_got]),
        [
            ((rows, D), F32, step_rows(D)),
            ((rows, head_cols), BF16, step_rows(head_cols)),
            ((rows, head_cols), BF16, step_rows(head_cols)),
            (out_mine.shape, F32, whole(out_mine.shape)),
            (out_mine.shape, BF16, whole(out_mine.shape)),
            ((8, D), F32, whole((8, D))),
        ],
        scratch=[pltpu.VMEM((blocks, tall, D), F32)],
        flops=2 * 2 * rows * D * D,
        name="first_norm_back",
    )
    def attend_back(block, mixed, d_context, logs):
        return kernel_call(
            attend_back_kernel,
            (1,),
            [(jnp.array([0, block], jnp.int32), smem()), (flags, smem()), (slopes, smem())]
            + wholes([mixed, d_context, logs]),
            [((rows, head_cols), BF16, whole((rows, head_cols)))] * 3,
            scratch=[pltpu.VMEM((LONG, LONG), F32)],
            name="attend_back",
            room=16,
            far=True,
        )

    d_own = attend_back(0, mixed_own, dctx_mine, logs_own)
    value_keep, value_send = weight_grad(after(low, d_own[0]), low_other, d_up, ffn_to, 2)
    down_got, gate_got, dctx_send, out_send, value_send = fence(down_got, gate_got, dctx_send, out_send, value_send)
    dctx_got, out_got = swap(dctx_send, "core"), swap(out_send, "core")
    value_got = swap(value_send, "b")
    gate_keep, gate_send = halves(gate_keep, gate_got)
    down_send = added(down_parts[1], down_got)
    gate_got = swap(gate_send, "a")
    down_got = swap(down_send, "prev")
    out_sum = (out_keep + out_got.astype(F32)).astype(BF16)

    d_partner = attend_back(1, mixed_partner, after(dctx_got, gate_send, down_send), logs_partner)
    grad_shape = (blocks // 2, tall, 4 * head_cols + 128)
    head_keep, head_send = kernel_call(
        qkv_grad_kernel,
        (3,),
        [(qkv_to, smem())]
        + wholes([tokens, tokens_other, *d_own, *d_partner, out_sum, sums_one, sums_two]),
        [(grad_shape, BF16, whole(grad_shape))] * 2,
        scratch=[pltpu.VMEM(block_row + (head_cols,), BF16), pltpu.VMEM(block_row + (128,), BF16)],
        name="qkv_grad",
    )
    down_got, gate_got, value_got, head_send = fence(down_got, gate_got, value_got, head_send)
    gate_parts = quarters(gate_keep, gate_got)
    value_keep, value_send = halves(value_keep, value_got)

    head_got = swap(head_send, "b")
    value_got = swap(value_send, "a")
    gate_sum = plane.sum_z(gate_parts)
    down_keep, down_send = halves(down_parts[0], down_got)

    def input_part(d_parts, more, dtype):
        return kernel_call(
            input_grad_kernel,
            (steps,),
            [(v, step_rows(head_cols)) for v in d_parts] + wholes([qkv_w]) + [(v, step_rows(D)) for v in more],
            [((rows, D), dtype, step_rows(D))],
            name="input_grad",
        )[0]

    in_send = input_part([after(d_partner[0], value_send, *gate_parts), *d_partner[1:]], [], BF16)
    head_got, value_got, gate_sum, down_send, in_send = fence(head_got, value_got, gate_sum, down_send, in_send)
    head_keep, head_send = halves(head_keep, head_got)
    value_parts = quarters(value_keep, value_got)

    in_got = swap(in_send, "core")
    down_got = swap(down_send, "b")
    head_got = swap(head_send, "a")
    value_sum = plane.sum_z(value_parts)
    input_grad = input_part([after(d_own[0], head_send, *value_parts), *d_own[1:]], [d_hidden, in_got], F32)
    head_got, value_sum, down_got, input_grad = fence(head_got, value_sum, down_got, input_grad)
    head_parts = quarters(head_keep, head_got)
    down_keep, down_send = halves(down_keep, down_got)

    down_got = swap(down_send, "a")
    head_sum = plane.sum_z(head_parts)
    grads = [gate_sum, value_sum, added(down_keep[0], down_got[0])]

    def in_order(mine, other):
        return [jnp.where(first, mine, other), jnp.where(first, other, mine)]

    kept = [half_of(core, total.reshape(2, tall, width), 0) for total in grads]
    ffn_got = swap(jnp.concatenate([other for _, other in kept], axis=0), "core")
    ffn_pieces = [
        jnp.concatenate(in_order(mine, ffn_got[n * tall : (n + 1) * tall]), axis=1).astype(F32)
        for n, (mine, _) in enumerate(kept)
    ]
    gate_piece, value_piece, down_piece = ffn_pieces[0], ffn_pieces[1], ffn_pieces[2].T
    there = after(swap(head_sum, "y"), gate_piece, value_piece, down_piece)
    own = y_here == core
    got = swap(jnp.where(own, there, head_sum), "core")
    qkv_piece, out_piece, gains_piece, biases_piece = kernel_call(
        pieces_kernel,
        (1,),
        [(jnp.stack([core, own.astype(jnp.int32)]), smem())] + wholes([head_sum, there, got]),
        [((tall, 3 * D), F32, whole((tall, 3 * D))), ((tall, D), F32, whole((tall, D)))]
        + [((2, tall), F32, whole((2, tall)))] * 2,
        name="pieces",
    )
    return (
        layer_out,
        input_grad,
        qkv_piece,
        out_piece,
        gate_piece,
        value_piece,
        down_piece,
        gains_piece,
        biases_piece,
    )


def solution(mesh):
    wide, narrow = mesh.shape["wide"], mesh.shape["narrow"]
    placed = (
        P(("wide", "narrow"), None),
        P("wide", None),
        P("wide", None),
        P("wide", "narrow"),
        P("wide", "narrow"),
        P("narrow", "wide"),
        P(None, "wide"),
        P(None, "wide"),
        P("wide", "narrow"),
        P(("wide", "narrow"), None),
    )
    if narrow == 2 and wide % 16 == 0 and D % (16 * wide) == 0:
        body = functools.partial(plane_shards, wide, narrow)
    else:
        body = general_shards
    return jax.shard_map(
        body,
        mesh=mesh,
        in_specs=placed,
        out_specs=(
            P(("wide", "narrow"), None),
            P(("wide", "narrow"), None),
            P("wide", None),
            P("wide", None),
            P("wide", "narrow"),
            P("wide", "narrow"),
            P("narrow", "wide"),
            P(None, "wide"),
            P(None, "wide"),
        ),
        check_vma=False,
    )
```

```python
import functools

import jax
import jax.numpy as jnp
import numpy as np
from jax import lax
from jax.experimental import pallas as pl
from jax.experimental.pallas import tpu as pltpu
from jax.sharding import PartitionSpec as P

D = 768
HEADS = 12
HEAD_DIM = 64
LONG = 512
SHORT = 128


def norm_rows(values, gain_row, bias_row):
    center = jnp.mean(values, axis=-1, keepdims=True)
    shifted = values - center
    spread = jnp.mean(shifted * shifted, axis=-1, keepdims=True)
    return shifted * lax.rsqrt(spread + 1e-05) * gain_row + bias_row


def gelu_product(gate_in, value_in):
    return jax.nn.gelu(gate_in, approximate=False) * value_in


def alibi_slopes(heads):
    power = 1 << heads.bit_length() - 1
    first = [2.0 ** (-8.0 * (index + 1) / power) for index in range(power)]
    second = [2.0 ** (-8.0 * (2 * index + 1) / (2 * power)) for index in range(heads - power)]
    return jnp.array(first + second, dtype=jnp.float32)


def alibi_bias(span, heads):
    position = jnp.arange(span)
    distance = jnp.abs(position[:, None] - position[None, :]).astype(jnp.float32)
    slopes = alibi_slopes(heads)
    return slopes[:, None, None] * distance


def block_scores(query_g, key_g, span):
    width = query_g.shape[-1]
    scores = jnp.einsum(
        "bqhd,bkhd->bhqk", query_g, key_g, preferred_element_type=jnp.float32
    ) * width ** (-0.5)
    return scores - alibi_bias(span, query_g.shape[2])


def attend(query_rows, key_rows, value_rows, span):
    rows, heads, width = query_rows.shape
    groups = rows // span
    shape_g = (groups, span, heads, width)
    query_g = query_rows.reshape(shape_g)
    key_g = key_rows.reshape(shape_g)
    value_g = value_rows.reshape(shape_g)
    scores = block_scores(query_g, key_g, span)
    top = jnp.max(scores, axis=-1, keepdims=True)
    expd = jnp.exp(scores - top)
    total = jnp.sum(expd, axis=-1, keepdims=True)
    probs_low = (expd / total).astype(jnp.bfloat16)
    context = jnp.einsum("bhqk,bkhd->bqhd", probs_low, value_g, preferred_element_type=jnp.float32)
    log_total = jnp.transpose((top + jnp.log(total))[..., 0], (0, 2, 1)).reshape(rows, heads)
    return (context.reshape(rows, heads * width), log_total)


def attend_back(query_rows, key_rows, value_rows, log_total, d_context, span):
    rows, heads, width = query_rows.shape
    groups = rows // span
    shape_g = (groups, span, heads, width)
    query_g = query_rows.reshape(shape_g)
    key_g = key_rows.reshape(shape_g)
    value_g = value_rows.reshape(shape_g)
    d_context_g = d_context.reshape(shape_g)
    lse_g = jnp.transpose(log_total.reshape(groups, span, heads), (0, 2, 1))
    scores = block_scores(query_g, key_g, span)
    probs = jnp.exp(scores - lse_g[..., None])
    probs_low = probs.astype(jnp.bfloat16)
    d_probs = jnp.einsum(
        "bqhd,bkhd->bhqk", d_context_g, value_g, preferred_element_type=jnp.float32
    )
    d_values = jnp.einsum(
        "bhqk,bqhd->bkhd", probs_low, d_context_g, preferred_element_type=jnp.float32
    )
    row_dot = jnp.sum(probs * d_probs, axis=-1, keepdims=True)
    d_scores = (probs * (d_probs - row_dot)).astype(jnp.bfloat16)
    scale = width ** (-0.5)
    d_queries = (
        jnp.einsum("bhqk,bkhd->bqhd", d_scores, key_g, preferred_element_type=jnp.float32) * scale
    )
    d_keys = (
        jnp.einsum("bhqk,bqhd->bkhd", d_scores, query_g, preferred_element_type=jnp.float32) * scale
    )
    return jnp.stack([d_queries, d_keys, d_values], axis=2).reshape(rows, 3, heads, width)


def contract_rows(left, right):
    return lax.dot_general(
        left, right, (((0,), (0,)), ((), ())), preferred_element_type=jnp.float32
    )


def contract_cols(left, right):
    return lax.dot_general(
        left, right, (((1,), (1,)), ((), ())), preferred_element_type=jnp.float32
    )


def general_shards(
    tokens, w_qkv, w_out, w_gate, w_value, w_down, norm_gains, norm_biases, long_count, cotangent
):
    gathered = (
        lax.all_gather(w_qkv, "wide", axis=0, tiled=True),
        lax.all_gather(w_out, "wide", axis=0, tiled=True),
        lax.all_gather(w_gate, "wide", axis=0, tiled=True),
        lax.all_gather(w_value, "wide", axis=0, tiled=True),
        lax.all_gather(w_down, "wide", axis=1, tiled=True),
        lax.all_gather(norm_gains, "wide", axis=1, tiled=True),
        lax.all_gather(norm_biases, "wide", axis=1, tiled=True),
    )
    full_qkv, full_out, wide_gate, wide_value, wide_down, gains_all, biases_all = gathered
    gains_f = gains_all.astype(jnp.float32)
    biases_f = biases_all.astype(jnp.float32)
    rows_dev = tokens.shape[0]
    n_blocks = rows_dev // LONG
    long_here = long_count[0, 0]
    tokens_f = tokens.astype(jnp.float32)
    mixed = jnp.dot(tokens, full_qkv, preferred_element_type=jnp.float32).astype(jnp.bfloat16)
    heads_view = mixed.reshape(n_blocks, LONG, 3, HEADS, HEAD_DIM)
    query_blk = heads_view[:, :, 0]
    key_blk = heads_view[:, :, 1]
    value_blk = heads_view[:, :, 2]
    block_ids = jnp.arange(n_blocks)

    def forward_block(entry):
        block_id, query_rows, key_rows, value_rows = entry
        return lax.cond(
            block_id < long_here,
            lambda operands: attend(operands[0], operands[1], operands[2], LONG),
            lambda operands: attend(operands[0], operands[1], operands[2], SHORT),
            (query_rows, key_rows, value_rows),
        )

    context_f, lse_rows = lax.map(forward_block, (block_ids, query_blk, key_blk, value_blk))
    context = context_f.reshape(rows_dev, D).astype(jnp.bfloat16)
    branch = jnp.dot(context, full_out, preferred_element_type=jnp.float32)
    hidden_in = tokens_f + branch
    normed = norm_rows(hidden_in, gains_f[0], biases_f[0])
    normed_low = normed.astype(jnp.bfloat16)
    all_rows = lax.all_gather(normed_low, "narrow", axis=0, tiled=True)
    gate = jnp.dot(all_rows, wide_gate, preferred_element_type=jnp.float32)
    value_up = jnp.dot(all_rows, wide_value, preferred_element_type=jnp.float32)
    product_f, pull_product = jax.vjp(gelu_product, gate, value_up)
    product = product_f.astype(jnp.bfloat16)
    ffn_out = lax.psum_scatter(
        jnp.dot(product, wide_down, preferred_element_type=jnp.float32),
        "narrow",
        scatter_dimension=0,
        tiled=True,
    )
    out_in = normed + ffn_out
    layer_out, pull_second = jax.vjp(norm_rows, out_in, gains_f[1], biases_f[1])
    d_out, d_gain_two, d_bias_two = pull_second(cotangent.astype(jnp.float32))
    d_ffn = d_out.astype(jnp.bfloat16)
    d_rows = lax.all_gather(d_ffn, "narrow", axis=0, tiled=True)
    grad_down = contract_rows(product, d_rows)
    d_product = contract_cols(d_rows, wide_down)
    d_gate, d_up = pull_product(d_product)
    d_gate_low = d_gate.astype(jnp.bfloat16)
    d_up_low = d_up.astype(jnp.bfloat16)
    grad_gate = contract_rows(all_rows, d_gate_low)
    grad_value = contract_rows(all_rows, d_up_low)
    d_normed = lax.psum_scatter(
        contract_cols(d_gate_low, wide_gate) + contract_cols(d_up_low, wide_value),
        "narrow",
        scatter_dimension=0,
        tiled=True,
    )
    d_normed_total = d_out + d_normed
    unused_out, pull_first = jax.vjp(norm_rows, hidden_in, gains_f[0], biases_f[0])
    d_hidden, d_gain_one, d_bias_one = pull_first(d_normed_total)
    d_branch = d_hidden.astype(jnp.bfloat16)
    grad_out = contract_rows(context, d_branch)
    d_context = contract_cols(d_branch, full_out).astype(jnp.bfloat16)
    d_context_blk = d_context.reshape(n_blocks, LONG, HEADS, HEAD_DIM)

    def backward_block(entry):
        block_id, query_rows, key_rows, value_rows, log_total, d_ctx = entry
        return lax.cond(
            block_id < long_here,
            lambda operands: attend_back(
                operands[0], operands[1], operands[2], operands[3], operands[4], LONG
            ),
            lambda operands: attend_back(
                operands[0], operands[1], operands[2], operands[3], operands[4], SHORT
            ),
            (query_rows, key_rows, value_rows, log_total, d_ctx),
        )

    d_mixed_f = lax.map(
        backward_block, (block_ids, query_blk, key_blk, value_blk, lse_rows, d_context_blk)
    )
    d_mixed = d_mixed_f.reshape(rows_dev, 3 * D).astype(jnp.bfloat16)
    grad_qkv = contract_rows(tokens, d_mixed)
    input_grad = d_hidden + contract_cols(d_mixed, full_qkv)
    grad_gains = jnp.stack([d_gain_one, d_gain_two])
    grad_biases = jnp.stack([d_bias_one, d_bias_two])
    pieces = (
        lax.psum_scatter(
            grad_qkv.astype(jnp.bfloat16), "wide", scatter_dimension=0, tiled=True
        ).astype(jnp.float32),
        lax.psum_scatter(
            grad_out.astype(jnp.bfloat16), "wide", scatter_dimension=0, tiled=True
        ).astype(jnp.float32),
        lax.psum_scatter(
            grad_gate.astype(jnp.bfloat16), "wide", scatter_dimension=0, tiled=True
        ).astype(jnp.float32),
        lax.psum_scatter(
            grad_value.astype(jnp.bfloat16), "wide", scatter_dimension=0, tiled=True
        ).astype(jnp.float32),
        lax.psum_scatter(
            grad_down.astype(jnp.bfloat16), "wide", scatter_dimension=1, tiled=True
        ).astype(jnp.float32),
        lax.psum_scatter(
            grad_gains.astype(jnp.bfloat16), "wide", scatter_dimension=1, tiled=True
        ).astype(jnp.float32),
        lax.psum_scatter(
            grad_biases.astype(jnp.bfloat16), "wide", scatter_dimension=1, tiled=True
        ).astype(jnp.float32),
    )
    qkv_piece, out_piece, gate_piece, value_piece, down_piece, gains_piece, biases_piece = pieces
    qkv_piece, out_piece, gains_piece, biases_piece = (
        lax.psum(qkv_piece.astype(jnp.bfloat16), "narrow").astype(jnp.float32),
        lax.psum(out_piece.astype(jnp.bfloat16), "narrow").astype(jnp.float32),
        lax.psum(gains_piece.astype(jnp.bfloat16), "narrow").astype(jnp.float32),
        lax.psum(biases_piece.astype(jnp.bfloat16), "narrow").astype(jnp.float32),
    )
    return (
        layer_out.astype(jnp.bfloat16),
        input_grad,
        qkv_piece,
        out_piece,
        gate_piece,
        value_piece,
        down_piece,
        gains_piece,
        biases_piece,
    )


AXES = ("wide", "narrow")
F32 = jnp.float32
BF16 = jnp.bfloat16
MIB = 1024 * 1024
RING = (0, 1, 3, 2)
PAIR = 2 * HEAD_DIM


def dot(left, right):
    return jnp.dot(left, right, preferred_element_type=F32)


class Plane:
    def __init__(self, wide, narrow):
        self.size = {"z": wide // 4, "ring": len(RING), "a": 2, "b": 2, "core": 2, "y": narrow}
        self.pairs = {}
        count = wide * narrow
        for dim, size in self.size.items():
            for step in range(1, size) if dim != "ring" else ():
                self.pairs[dim, step] = [(i, self.partner(i, dim, step)) for i in range(count)]
        after_z = {z: RING[(n + 1) % len(RING)] for n, z in enumerate(RING)}
        self.pairs["next", 1] = [(i, i % 8 + 8 * after_z[i // 8]) for i in range(count)]
        self.pairs["prev", 1] = [(j, i) for i, j in self.pairs["next", 1]]
        w = lax.axis_index("wide")
        self.z, self.x, self.core = w // 4, (w // 2) % 2, w % 2
        self.y = lax.axis_index("narrow")

    @staticmethod
    def partner(i, dim, step):
        z, x, c, y = i // 8, (i // 4) % 2, (i // 2) % 2, i % 2
        if dim == "z":
            z ^= step
        elif dim == "core":
            c ^= 1
        elif dim == "y" or (dim == "a") == (c == 1):
            y ^= 1
        else:
            x ^= 1
        return ((z * 2 + x) * 2 + c) * 2 + y

    def swap(self, value, dim, step=1):
        return lax.ppermute(value, AXES, self.pairs[dim, step])

    def sum_z(self, parts):
        total = parts[0].astype(F32)
        for k in range(1, self.size["z"]):
            total = total + self.swap(parts[k], "z", k).astype(F32)
        return total.astype(BF16)

    def tables(self, order, numbered):
        sizes = [self.size[dim] for dim in order]
        number = np.arange(int(np.prod(sizes)))
        rest, digit = number, {}
        for dim, size in zip(order, sizes):
            digit[dim] = rest % size
            rest = rest // size
        first = self.core == 0
        a_here = jnp.where(first, self.x, self.y)
        b_here = jnp.where(first, self.y, self.x)
        if "ring" in digit:
            at = sum(jnp.where(self.z == z, n, 0) for n, z in enumerate(RING))
            z = sum(jnp.where((at - digit["ring"]) % len(RING) == n, z, 0) for n, z in enumerate(RING))
        else:
            z = digit["z"] ^ self.z
        a = digit["a"] ^ a_here
        b = digit["b"] ^ b_here
        x, y = jnp.where(first, a, b), jnp.where(first, b, a)
        return numbered(z, x, y).astype(jnp.int32)


def after(value, *events):
    return lax.optimization_barrier((value,) + events)[0]


def fence(*values):
    return lax.optimization_barrier(values)


def smem():
    return pl.BlockSpec(memory_space=pltpu.SMEM)


def whole(shape):
    zeros = (0,) * len(shape)
    return pl.BlockSpec(tuple(shape), lambda *_: zeros)


def kernel_call(body, grid, ins, outs, scratch=(), flops=0, name=None, room=6):
    blocks = [(v[1].block_shape, v[0].dtype) for v in ins] + [(v[2].block_shape, v[1]) for v in outs]
    held = sum(2 * int(np.prod(shape)) * np.dtype(d).itemsize for shape, d in blocks if shape is not None)
    held += sum(int(np.prod(v.shape)) * np.dtype(v.dtype).itemsize for v in scratch)
    return pl.pallas_call(
        body,
        grid=grid,
        in_specs=[v[1] for v in ins],
        out_specs=[v[2] for v in outs],
        out_shape=[(pltpu.HBM if more else jax.ShapeDtypeStruct)(s, d) for s, d, _, *more in outs],
        scratch_shapes=list(scratch),
        compiler_params=pltpu.CompilerParams(
            dimension_semantics=("arbitrary",) * len(grid), vmem_limit_bytes=held // 2 + room * MIB
        ),
        cost_estimate=pl.CostEstimate(flops=0, bytes_accessed=0, transcendentals=0),
        name=name,
    )(*[pltpu.with_memory_space_constraint(a, pltpu.HBM) if more else a for a, _, *more in ins])


ROWS = 512


def own_rows(steps, cols):
    return pl.BlockSpec((ROWS, cols), lambda i: (jnp.minimum(i, steps - 1), 0))


def partner_rows(steps, cols):
    return pl.BlockSpec((ROWS, cols), lambda i: (jnp.maximum(i - steps, 0), 0))


def pick_rows(i, steps, own_ref, partner_ref):
    return jnp.where(i < steps, own_ref[...], partner_ref[...])


def split_kernel(place, w_qkv, w_out, gains, biases, mine, send):
    first = place[0] == 0
    half = D // 2
    for n in range(4):
        source, start = (w_qkv, n * D) if n < 3 else (w_out, 0)
        low, high = source[:, start : start + half], source[:, start + half : start + D]
        mine[:, n * half : (n + 1) * half] = jnp.where(first, low, high)
        send[:, n * half : (n + 1) * half] = jnp.where(first, high, low)
    rows = jnp.concatenate([gains[...], biases[...]], axis=0).astype(F32)
    eye = jnp.where(
        lax.broadcasted_iota(jnp.int32, (128, rows.shape[0]), 0)
        == lax.broadcasted_iota(jnp.int32, (128, rows.shape[0]), 1),
        1.0,
        0.0,
    )
    norm_cols = contract_cols(rows.T.astype(BF16), eye.astype(BF16)).astype(BF16)
    mine[:, 4 * half :] = norm_cols
    send[:, 4 * half :] = norm_cols


def fill_blocks(table, pieces, weight, cols=slice(None)):
    count = pieces[0].shape[0]
    for n, piece in enumerate(pieces):
        for k in range(count):
            weight[table[n * count + k]] = piece[k, :, cols]


def qkv_kernel(steps, groups, pieces, table, own, partner, *refs):
    i = pl.program_id(0)
    parts = refs[:pieces]
    mixed_own, mixed_partner, weight, out_w, norms, table_t = refs[pieces:]
    cols, part = weight.shape[2], out_w.shape[2]
    tall = weight.shape[0] * weight.shape[1]

    @pl.when(i == 0)
    def _():
        fill_blocks(table, parts, weight, slice(0, cols))
        fill_blocks(table, parts, out_w, slice(cols, cols + part))
        fill_blocks(table, parts, table_t, slice(cols + part, None))
        norms[...] = table_t[...].reshape(tall, table_t.shape[2]).astype(F32).T[: norms.shape[0]]

    rows_here = pick_rows(i, steps, own, partner)
    for g in range(groups):
        span = slice(g * cols // groups, (g + 1) * cols // groups)
        tile = weight[:, :, span].reshape(tall, cols // groups)
        value = dot(rows_here, tile).astype(BF16)

        @pl.when(i < steps)
        def _():
            mixed_own[:, span] = value

        @pl.when(i >= steps)
        def _():
            mixed_partner[:, span] = value


def lane_masks():
    lane = lax.broadcasted_iota(jnp.int32, (1, PAIR), 1)
    return [lane < HEAD_DIM, lane >= HEAD_DIM]


def keep(mask, value):
    return jnp.where(mask, value, jnp.zeros_like(value))


def fill_distance(distance):
    row = lax.broadcasted_iota(jnp.int32, distance.shape, 0)
    col = lax.broadcasted_iota(jnp.int32, distance.shape, 1)
    distance[...] = jnp.abs(row - col).astype(F32)


def scores_of(queries, keys, slope, distance):
    raw = lax.dot_general(queries, keys, (((1,), (1,)), ((), ())), preferred_element_type=F32)
    return raw - slope * distance


def attend_rows(queries, keys, values, slope, away):
    s = jnp.concatenate([scores_of(q, k, slope, away) for q, k in zip(queries, keys)], axis=0)
    top = jnp.max(s, axis=-1, keepdims=True)
    e = jnp.exp(s - top)
    norm = jnp.sum(e, axis=-1, keepdims=True)
    p = (e * (1.0 / norm)).astype(BF16)
    tall = queries[0].shape[0]
    out = [dot(p[n * tall : (n + 1) * tall], v) for n, v in enumerate(values)]
    return jnp.concatenate(out, axis=0), top + jnp.log(norm)


def tiles(value, tall):
    return [value[n : n + tall] for n in range(0, value.shape[0], tall)]


def pair_cols(part, pair):
    return pl.ds(pl.multiple_of(part * (D // 2) + pair * PAIR, PAIR), PAIR)


def attend_kernel(place, flags, slopes, mixed, *refs):
    context, logs, distance = refs[-3:]
    masks = lane_masks()
    scale = HEAD_DIM**-0.5
    lane = lax.broadcasted_iota(jnp.int32, (1, 128), 1)
    fill_distance(distance)
    for extra in refs[:-3]:
        context[LONG:, :] = extra[...].reshape(context.shape[0] - LONG, context.shape[1])

    def run(is_long):
        tall = 2 * SHORT if is_long else LONG

        def one_pair(pair, _):
            q_all, k_all, v_all = (mixed[:, pair_cols(part, pair)] for part in range(3))
            totals = [0.0] * (LONG // tall)
            for head in range(2):
                slope = slopes[pair * 2 + head]
                q = (keep(masks[head], q_all) * scale).astype(BF16)
                v = keep(masks[head], v_all)
                for n in range(LONG // tall):
                    rows = slice(n * tall, (n + 1) * tall)
                    if is_long:
                        out = attend_rows([q[rows]], [k_all], [v], slope, distance[rows, :])
                    else:
                        out = attend_rows(
                            tiles(q, SHORT), tiles(k_all, SHORT), tiles(v, SHORT), slope, distance[:SHORT, :SHORT]
                        )
                    totals[n] = totals[n] + out[0]
                    logs[rows, :] = jnp.where(lane == pair * 2 + head, out[1], logs[rows, :])
            for n in range(LONG // tall):
                context[n * tall : (n + 1) * tall, pair_cols(0, pair)] = totals[n].astype(BF16)
            return 0

        lax.fori_loop(0, D // 2 // PAIR, one_pair, 0)

    logs[...] = jnp.zeros_like(logs)
    flag = flags[place[1]]

    @pl.when(flag > 0)
    def _():
        run(True)

    @pl.when(flag <= 0)
    def _():
        run(False)


def back_rows(queries, keys, values, d_rows, log_rows, slope, away, scaled_keys):
    s = jnp.concatenate([scores_of(q, k, slope, away) for q, k in zip(queries, keys)], axis=0)
    p = jnp.exp(s - log_rows)
    d_p = jnp.concatenate([contract_cols(d, v) for d, v in zip(d_rows, values)], axis=0)
    d_s = (p * (d_p - jnp.sum(p * d_p, axis=-1, keepdims=True))).astype(BF16)
    p = p.astype(BF16)
    tall = queries[0].shape[0]
    d_s, p = tiles(d_s, tall), tiles(p, tall)
    d_q = jnp.concatenate([dot(d, k) for d, k in zip(d_s, scaled_keys)], axis=0)
    d_k = [dot(q.T, d) for q, d in zip(queries, d_s)]
    d_v = [dot(d.T, w) for d, w in zip(d_rows, p)]
    return d_q, d_k, d_v


def attend_back_kernel(place, flags, slopes, mixed, logs_ref, d_context, d_query, d_key, d_value, distance):
    masks = lane_masks()
    scale = HEAD_DIM**-0.5
    fill_distance(distance)

    def run(is_long):
        tall = 2 * SHORT if is_long else LONG
        logs = logs_ref[...]
        lane = lax.broadcasted_iota(jnp.int32, (1, 128), 1)

        def one_pair(pair, _):
            q_all, k_all, v_all = (mixed[:, pair_cols(part, pair)] for part in range(3))
            d_all = d_context[:, pair_cols(0, pair)]
            d_q, d_k, d_v = [0.0] * (LONG // tall), 0.0, 0.0
            for head in range(2):
                slope = slopes[pair * 2 + head]
                q = (keep(masks[head], q_all) * scale).astype(BF16)
                k = (keep(masks[head], k_all) * scale).astype(BF16)
                d_c = keep(masks[head], d_all)
                log_all = jnp.sum(jnp.where(lane == pair * 2 + head, logs, 0.0), axis=-1, keepdims=True)
                for n in range(LONG // tall):
                    rows = slice(n * tall, (n + 1) * tall)
                    if is_long:
                        out = back_rows(
                            [q[rows]], [k_all], [v_all], [d_c[rows]], log_all[rows], slope, distance[rows, :], [k]
                        )
                        new_k, new_v = out[1][0], out[2][0]
                    else:
                        out = back_rows(
                            tiles(q, SHORT),
                            tiles(k_all, SHORT),
                            tiles(v_all, SHORT),
                            tiles(d_c, SHORT),
                            log_all,
                            slope,
                            distance[:SHORT, :SHORT],
                            tiles(k, SHORT),
                        )
                        new_k, new_v = (jnp.concatenate(part, axis=1) for part in out[1:])
                    d_q[n] = d_q[n] + out[0]
                    d_k, d_v = d_k + new_k, d_v + new_v
            cols = pair_cols(0, pair)
            for n in range(LONG // tall):
                d_query[n * tall : (n + 1) * tall, cols] = d_q[n].astype(BF16)
            d_key[:, cols] = d_k.T.astype(BF16)
            d_value[:, cols] = d_v.T.astype(BF16)
            return 0

        lax.fori_loop(0, D // 2 // PAIR, one_pair, 0)

    flag = flags[place[1]]

    @pl.when(flag > 0)
    def _():
        run(True)

    @pl.when(flag <= 0)
    def _():
        run(False)


def spread(rows):
    center = jnp.mean(rows, axis=-1, keepdims=True)
    shifted = rows - center
    inverse = lax.rsqrt(jnp.mean(shifted * shifted, axis=-1, keepdims=True) + 1e-05)
    return shifted * inverse, inverse


def norm_back(e, unit, inverse):
    mean_e = jnp.mean(e, axis=-1, keepdims=True)
    mean_en = jnp.mean(e * unit, axis=-1, keepdims=True)
    return (e - mean_e - unit * mean_en) * inverse


def first_norm_kernel(place, tokens, ctx_mine, ctx_other, w_mine, w_other_rows, norms, unit, inverse, low):
    core = place[0]
    half = w_mine.shape[0] // 2
    wide = w_mine.shape[2]

    def branch(weight):
        return dot(ctx_mine[...], weight(core)) + dot(ctx_other[...], weight(1 - core))

    mine = branch(lambda c: w_mine[pl.ds(c * half, half)].reshape(D // 2, wide))
    other = branch(lambda c: w_other_rows[pl.ds(pl.multiple_of(LONG + c * (D // 2), 128), D // 2), :])
    first = core == 0
    added = jnp.concatenate([jnp.where(first, mine, other), jnp.where(first, other, mine)], axis=1)
    n, inv = spread(tokens[...].astype(F32) + added)
    unit[...] = n
    inverse[...] = inv
    low[...] = (n * norms[0:1, :] + norms[2:3, :]).astype(BF16)


def gelu_parts(x):
    t = 1.0 / (1.0 + (0.3275911 * 0.5**0.5) * jnp.abs(x))
    poly = t * (
        0.254829592 + t * (-0.284496736 + t * (1.421413741 + t * (-1.453152027 + t * 1.061405429)))
    )
    bell = jnp.exp(-0.5 * (x * x))
    tail = 0.5 * poly * bell
    phi = jnp.where(x >= 0, 1.0 - tail, tail)
    return x * phi, phi + x * bell * 0.3989422804014327


def columns_of(weight, half, span):
    count = weight.shape[0] // 2
    return weight[half * count : (half + 1) * count, :, span].reshape(D, span.stop - span.start)


def gate_kernel(steps, pieces, table, own, partner, *refs):
    i = pl.program_id(0)
    active, slope, gate_w = refs[pieces:]

    @pl.when(i == 0)
    def _():
        fill_blocks(table, refs[:pieces], gate_w)

    rows = pick_rows(i, steps, own, partner)
    width = gate_w.shape[2]
    for half in range(2):
        for start in range(0, width, 256):
            out = slice(half * width + start, half * width + start + 256)
            gate = dot(rows, columns_of(gate_w, half, slice(start, start + 256)))
            act, grad = gelu_parts(gate)
            active[:, out] = act.astype(BF16)
            slope[:, out] = grad.astype(BF16)


def value_kernel(steps, pieces, table, own, partner, active, slope, *refs):
    i = pl.program_id(0)
    product, scaled, value_w = refs[pieces:]

    @pl.when(i == 0)
    def _():
        fill_blocks(table, refs[:pieces], value_w)

    rows = pick_rows(i, steps, own, partner)
    width = value_w.shape[2]
    for half in range(2):
        for start in range(0, width, 256):
            out = slice(half * width + start, half * width + start + 256)
            up = dot(rows, columns_of(value_w, half, slice(start, start + 256)))
            product[:, out] = (active[:, out].astype(F32) * up).astype(BF16)
            scaled[:, out] = (slope[:, out].astype(F32) * up).astype(BF16)


def times_down(product, down_w):
    width = down_w.shape[2]
    total = 0.0
    for half in range(2):
        part = product[:, half * width : (half + 1) * width]
        total = total + contract_cols(part, columns_of(down_w, half, slice(0, width)))
    return total


def down_first_kernel(table, product, *refs):
    partner, down_w = refs[-2:]

    @pl.when(pl.program_id(0) == 0)
    def _():
        fill_blocks(table, refs[:-2], down_w)

    partner[...] = times_down(product, down_w).astype(BF16)


def down_kernel(product, down_w, own):
    own[...] = times_down(product, down_w)


def second_norm_kernel(unit_one, norms, part_own, part_got, cotangent, out, d_z, d_ffn, sums):
    normed = unit_one[...] * norms[0:1, :] + norms[2:3, :]
    n, inv = spread(normed + (part_own[...] + part_got[...].astype(F32)))
    gain = norms[1:2, :]
    out[...] = (n * gain + norms[3:4, :]).astype(BF16)
    c = cotangent[...].astype(F32)
    back = norm_back(gain * c, n, inv)
    d_z[...] = back
    d_ffn[...] = back.astype(BF16)
    add_sums(sums, c * n, c)


def add_sums(sums, gain_terms, bias_terms):
    @pl.when(pl.program_id(0) == 0)
    def _():
        sums[...] = jnp.zeros_like(sums)

    sums[0:1, :] += jnp.sum(gain_terms, axis=0, keepdims=True)
    sums[1:2, :] += jnp.sum(bias_terms, axis=0, keepdims=True)


def ffn_back_kernel(
    steps, own, partner, down_w, gate_w, value_w, active, slope, d_gate, d_up, back_own, back_partner
):
    i = pl.program_id(0)
    rows = pick_rows(i, steps, own, partner)
    width = down_w.shape[2]
    total = jnp.zeros((ROWS, D), F32)
    for half in range(2):
        for start in range(0, width, 256):
            span = slice(start, start + 256)
            out = slice(half * width + start, half * width + start + 256)
            d_product = dot(rows, columns_of(down_w, half, span))
            dg = (d_product * slope[:, out].astype(F32)).astype(BF16)
            du = (d_product * active[:, out].astype(F32)).astype(BF16)
            d_gate[:, out] = dg
            d_up[:, out] = du
            total = total + contract_cols(dg, columns_of(gate_w, half, span))
            total = total + contract_cols(du, columns_of(value_w, half, span))

    @pl.when(i < steps)
    def _():
        back_own[...] = total

    @pl.when(i >= steps)
    def _():
        back_partner[...] = total.astype(BF16)


def weight_grad_kernel(table, left_own, left_partner, right_a, right_b, *refs):
    i = pl.program_id(0)
    parts, blocks = refs[:-1], refs[-1]
    rows = left_own.shape[0]
    count, tall, cols = blocks.shape
    for half, right in enumerate((right_a, right_b)):
        value = contract_rows(left_own[...], right[:rows, :]) + contract_rows(left_partner[...], right[rows:, :])
        value = value.astype(BF16).reshape(count // 2, tall, cols)
        blocks[half * (count // 2) : (half + 1) * (count // 2)] = value
    span = pl.ds(pl.multiple_of(i * cols, cols), cols)
    each = count // len(parts)
    for k in range(count):
        parts[k // each][k % each, :, span] = blocks[table[k]]


def first_norm_back_kernel(
    place,
    unit_ref,
    inverse,
    norms,
    d_z,
    part_own,
    part_got,
    ctx_mine,
    ctx_other,
    w_mine,
    w_other,
    d_hidden,
    dctx_mine,
    dctx_other,
    grad_keep,
    grad_send,
    sums,
    grad,
):
    core = place[0]
    first = core == 0
    unit = unit_ref[...]
    d_normed = d_z[...] + (part_own[...] + part_got[...].astype(F32))
    back = norm_back(norms[0:1, :] * d_normed, unit, inverse[...])
    low = back.astype(BF16)
    d_hidden[...] = back
    add_sums(sums, d_normed * unit, d_normed)
    half, wide = w_mine.shape[0] // 2, w_mine.shape[2]
    low_mine = jnp.where(first, low[:, :wide], low[:, wide:])
    low_other = jnp.where(first, low[:, wide:], low[:, :wide])
    for head_core, out in ((core, dctx_mine), (1 - core, dctx_other)):
        near = w_mine[pl.ds(head_core * half, half)].reshape(D // 2, wide)
        far = w_other[pl.ds(pl.multiple_of(LONG + head_core * (D // 2), 128), D // 2), :]
        out[...] = (contract_cols(low_mine, near) + contract_cols(low_other, far)).astype(BF16)

    @pl.when(pl.program_id(0) == 0)
    def _():
        grad[...] = jnp.zeros_like(grad)

    shape = (half,) + grad.shape[1:]
    grad[pl.ds(core * half, half)] += contract_rows(ctx_mine[...], low).reshape(shape)
    grad[pl.ds((1 - core) * half, half)] += contract_rows(ctx_other[...], low).reshape(shape)

    @pl.when(pl.program_id(0) == pl.num_programs(0) - 1)
    def _():
        left, right = grad[:, :, :wide], grad[:, :, wide:]
        grad_keep[...] = jnp.where(first, left, right)
        grad_send[...] = jnp.where(first, right, left).astype(BF16)


def qkv_grad_kernel(table, left_own, left_partner, *refs):
    d_own, d_partner = refs[:3], refs[3:6]
    out_grad, sums_one, sums_two, near, far, blocks, norm_grad = refs[6:]
    i = pl.program_id(0)
    count, tall, cols = blocks.shape

    @pl.when(i == 0)
    def _():
        one, two = sums_one[...], sums_two[...]
        empty = jnp.zeros((norm_grad.shape[2] - 4, D), F32)
        stacked = jnp.concatenate([one[0:1], two[0:1], one[1:2], two[1:2], empty], axis=0)
        norm_grad[...] = stacked.T.astype(BF16).reshape(norm_grad.shape)

    for g in range(3):

        @pl.when(i == g)
        def _():
            value = contract_rows(left_own[...], d_own[g][...]) + contract_rows(left_partner[...], d_partner[g][...])
            blocks[...] = value.astype(BF16).reshape(blocks.shape)
            for k in range(count):
                target, place = (near if k < count // 2 else far), table[k]
                target[k % (count // 2), :, g * cols : (g + 1) * cols] = blocks[place]
                if g == 0:
                    start = 3 * cols
                    for more in (out_grad, norm_grad):
                        stop = start + more.shape[2]
                        target[k % (count // 2), :, start:stop] = more[place]
                        start = stop


def input_grad_kernel(d_query, d_key, d_value, weight, *refs):
    cols = d_query.shape[1]
    total = 0.0
    for g, left in enumerate((d_query, d_key, d_value)):
        tile = weight[:, :, g * cols : (g + 1) * cols].reshape(D, cols)
        total = total + contract_cols(left[...], tile)
    for more in refs[:-1]:
        total = total + more[...].astype(F32)
    refs[-1][...] = total.astype(refs[-1].dtype)


def pieces_kernel(place, here, there, got, qkv, out, gains, biases):
    first, own = place[0] == 0, place[1] == 1
    half = D // 2
    mine = jnp.where(own, here[...], there[...])
    for n in range(4):
        a, b = mine[:, n * half : (n + 1) * half].astype(F32), got[:, n * half : (n + 1) * half].astype(F32)
        target, start = (qkv, n * D) if n < 3 else (out, 0)
        target[:, start : start + half] = jnp.where(first, a, b)
        target[:, start + half : start + D] = jnp.where(first, b, a)
    rows = (mine[:, 4 * half :].astype(F32) + got[:, 4 * half :].astype(F32)).T
    gains[...] = rows[0:2]
    biases[...] = rows[2:4]


def by_core(core, mine, other, axis):
    first = core == 0
    return jnp.stack([jnp.where(first, mine, other), jnp.where(first, other, mine)], axis=axis)


def half_of(core, halves, axis):
    zero, one = (lax.index_in_dim(halves, k, axis, keepdims=False) for k in range(2))
    first = core == 0
    return jnp.where(first, zero, one), jnp.where(first, one, zero)


def plane_shards(
    wide,
    narrow,
    tokens,
    w_qkv,
    w_out,
    w_gate,
    w_value,
    w_down,
    norm_gains,
    norm_biases,
    long_count,
    cotangent,
):
    plane = Plane(wide, narrow)
    swap = plane.swap
    core, y_here = plane.core, plane.y
    rows = tokens.shape[0]
    steps = rows // ROWS
    tall = w_qkv.shape[0]
    blocks = wide * narrow // 2
    z_size = plane.size["z"]
    head_cols = D // 2
    width = w_gate.shape[1] // 2
    hidden = 2 * width
    pairs = head_cols // PAIR
    qkv_to = plane.tables(("z", "a", "b"), lambda z, x, y: (z * 2 + x) * 2 + y)
    ffn_to = plane.tables(("z", "a", "b"), lambda z, x, y: y * (2 * z_size) + z * 2 + x)
    down_to = plane.tables(("a", "b", "ring"), lambda z, x, y: y * (2 * z_size) + z * 2 + x)
    place = jnp.reshape(core, (1,)).astype(jnp.int32)
    first = core == 0

    def wholes(arrays):
        return [(v, whole(v.shape)) for v in arrays]

    def far(entries):
        return [entry + (True,) for entry in entries]

    def step_rows(cols):
        return pl.BlockSpec((ROWS, cols), lambda i: (i, 0))

    head_shape = (tall, 4 * head_cols + 128)
    head_part, head_send = kernel_call(
        split_kernel,
        (1,),
        [(place, smem())] + far(wholes([w_qkv, w_out, norm_gains, norm_biases])),
        [(head_shape, BF16, whole(head_shape))] * 2,
        name="split",
    )
    flag = jnp.broadcast_to(long_count.astype(F32), (8, 128))
    head_got, flag_got = fence(swap(head_send, "core"), swap(flag, "core"))
    head_part = jnp.where(y_here == core, head_part, head_got)
    head_parts = [head_part] + [swap(head_part, "z", k) for k in range(1, z_size)]
    ffn_parts = [after(w_gate, head_part), w_value, w_down.T]
    ffn_other = jnp.concatenate([jnp.where(first, v[:, width:], v[:, :width]) for v in ffn_parts], axis=1)
    ffn_got = swap(ffn_other, "core")
    flags = jnp.stack([long_count[0, 0], flag_got[0, 0].astype(jnp.int32)])
    slopes = lax.dynamic_slice_in_dim(alibi_slopes(HEADS), core * (HEADS // 2), HEADS // 2)

    def ffn_chip(n):
        v, got = ffn_parts[n], ffn_got[:, n * width : (n + 1) * width]
        mine = jnp.where(first, v[:, :width], v[:, width:])
        return jnp.concatenate([jnp.where(first, mine, got), jnp.where(first, got, mine)], axis=0)

    def doubled(value, step, *events):
        got = swap(value, "z", step)
        return jnp.concatenate(lax.optimization_barrier((value, got) + events)[:2], axis=0)

    def along_plane(held):
        near = swap(held, "a")
        return held, near, swap(held, "b")

    def joined(value, got):
        return jnp.concatenate([value, got], axis=0)

    gate_one, value_one, down_one = (ffn_chip(n)[None] for n in range(3))
    gate_got = swap(gate_one, "z", 1)
    down_got = swap(down_one, "a")
    *head_parts, gate_got, down_got = fence(*head_parts, gate_got, down_got)
    qkv_z = jnp.stack(head_parts)
    gate_two, down_two = joined(gate_one, gate_got), joined(down_one, down_got)

    head_near, head_far = swap(qkv_z, "a"), swap(qkv_z, "b")
    gate_got = swap(gate_two, "z", 2)
    value_got = swap(after(value_one, qkv_z), "z", 1)
    tokens_other = swap(after(tokens, qkv_z), "core")
    head_near, head_far, gate_got, value_got, tokens_other = fence(head_near, head_far, gate_got, value_got, tokens_other)
    gate_z, value_two = joined(gate_two, gate_got), joined(value_one, value_got)

    head_last = swap(head_near, "b")
    down_got = swap(after(down_two, head_near), "b")
    gate_near = swap(gate_z, "a")
    value_got = swap(value_two, "z", 2)
    head_last, down_got, gate_near, value_got = fence(head_last, down_got, gate_near, value_got)
    value_z, down_four = joined(value_two, value_got), joined(down_two, down_got)
    qkv_blocks = [qkv_z, head_near, head_far, head_last]

    gate_far, gate_last = swap(after(gate_z, head_last), "b"), swap(gate_near, "b")
    ring_one = swap(down_four, "next")
    block_row = (blocks, tall)
    mixed_own, mixed_partner, qkv_w, out_mine, norms = kernel_call(
        functools.partial(qkv_kernel, steps, 3, len(qkv_blocks)),
        (2 * steps,),
        [(qkv_to, smem())]
        + far([(tokens, own_rows(steps, D)), (tokens_other, partner_rows(steps, D))] + wholes(qkv_blocks)),
        far(
            [((rows, 3 * head_cols), BF16, own_rows(steps, 3 * head_cols))]
            + [((rows, 3 * head_cols), BF16, partner_rows(steps, 3 * head_cols))]
            + [(block_row + (n,), BF16, whole(block_row + (n,))) for n in (3 * head_cols, head_cols)]
        )
        + [((8, D), F32, whole((8, D)))],
        scratch=[pltpu.VMEM(block_row + (128,), BF16)],
        flops=2 * 2 * rows * D * 3 * head_cols,
        name="mixed",
    )
    def attend(block, mixed, extra=()):
        tall_out = rows + sum(v.size for v in extra) // head_cols
        return kernel_call(
            attend_kernel,
            (1,),
            [(jnp.array([0, block], jnp.int32), smem()), (flags, smem()), (slopes, smem())]
            + far(wholes([mixed, *extra])),
            [((tall_out, head_cols), BF16, whole((tall_out, head_cols))), ((rows, 128), F32, whole((rows, 128)), True)],
            scratch=[pltpu.VMEM((LONG, LONG), F32)],
            flops=4 * rows * LONG * D,
            name="attend",
            room=12,
        )

    ctx_send, logs_partner = attend(1, mixed_partner, [out_mine])
    gate_far, gate_last, ring_one, ctx_send = fence(gate_far, gate_last, ring_one, ctx_send)

    value_near, value_far = swap(value_z, "a"), swap(value_z, "b")
    ring_two = swap(ring_one, "next")
    ctx_got = swap(ctx_send, "core")
    ctx_mine, logs_own = attend(0, after(mixed_own, ctx_send))

    unit_one, inverse_one, low = kernel_call(
        first_norm_kernel,
        (steps,),
        [
            (place, smem()),
            (tokens, step_rows(D)),
            (ctx_mine, step_rows(head_cols)),
            (ctx_got, step_rows(head_cols)),
        ]
        + wholes([out_mine, ctx_got, norms]),
        [
            ((rows, D), F32, step_rows(D)),
            ((rows, 1), F32, step_rows(1)),
            ((rows, D), BF16, step_rows(D)),
        ],
        flops=2 * rows * D * D,
        name="first_norm",
    )
    value_near, value_far, ring_two, low = fence(value_near, value_far, ring_two, low)
    gate_blocks = [gate_z, gate_near, gate_far, gate_last]
    value_last = swap(value_near, "b")
    ring_three = swap(ring_two, "next")
    low_other = swap(low, "core")

    w_shape = (blocks, 2 * tall, width)
    both_rows = [(low, own_rows(steps, D)), (low_other, partner_rows(steps, D))]
    active, slope, gate_w = kernel_call(
        functools.partial(gate_kernel, steps, len(gate_blocks)),
        (2 * steps,),
        [(ffn_to, smem())] + both_rows + far(wholes(gate_blocks)),
        [((2 * rows, hidden), BF16, step_rows(hidden))] * 2 + [(w_shape, BF16, whole(w_shape))],
        name="gate",
    )
    value_last, active = fence(value_last, active)
    value_blocks = [value_z, value_near, value_far, value_last]
    down_blocks = [down_four, ring_one, ring_two, ring_three]
    product, slope, value_w = kernel_call(
        functools.partial(value_kernel, steps, len(value_blocks)),
        (2 * steps,),
        [(ffn_to, smem())] + both_rows + [(active, step_rows(hidden)), (slope, step_rows(hidden))] + wholes(value_blocks),
        [((2 * rows, hidden), BF16, step_rows(hidden))] * 2 + [(w_shape, BF16, whole(w_shape))],
        name="value",
    )
    part_send, down_w = kernel_call(
        down_first_kernel,
        (steps,),
        [(down_to, smem()), (product, pl.BlockSpec((ROWS, hidden), lambda i: (i + steps, 0)))] + wholes(down_blocks),
        [((rows, D), BF16, step_rows(D)), (w_shape, BF16, whole(w_shape))],
        name="down_first",
    )
    (part_own,) = kernel_call(
        down_kernel,
        (steps,),
        [(product, step_rows(hidden))] + wholes([down_w]),
        [((rows, D), F32, step_rows(D))],
        name="down",
    )
    part_got = swap(part_send, "core")
    layer_out, d_z, d_ffn, sums_two = kernel_call(
        second_norm_kernel,
        (steps,),
        [(unit_one, step_rows(D))]
        + wholes([norms])
        + [(part_own, step_rows(D)), (part_got, step_rows(D)), (cotangent, step_rows(D))],
        [
            ((rows, D), BF16, step_rows(D)),
            ((rows, D), F32, step_rows(D)),
            ((rows, D), BF16, step_rows(D)),
            ((8, D), F32, whole((8, D))),
        ],
        name="second_norm",
    )
    d_ffn_other = swap(d_ffn, "core")

    def weight_grad(left, left_other, right, to, parts):
        part = (blocks // parts, 2 * tall, width)
        cols = width // 3
        return kernel_call(
            weight_grad_kernel,
            (3,),
            [
                (to, smem()),
                (left, whole((rows, D))),
                (left_other, whole((rows, D))),
                (right, pl.BlockSpec((2 * rows, cols), lambda i: (0, i))),
                (right, pl.BlockSpec((2 * rows, cols), lambda i: (0, 3 + i))),
            ],
            [(part, BF16, whole(part))] * parts,
            scratch=[pltpu.VMEM((blocks, 2 * tall, cols), BF16)],
            flops=2 * 2 * rows * D * hidden,
            name="weight_grad",
        )

    def added(keep, got):
        return (keep.astype(F32) + got.astype(F32)).astype(BF16)

    def halves(keep, got):
        count = keep.shape[0] // 2
        return added(keep[:count], got[:count]), added(keep[count:], got[count:])

    def quarters(keep, got):
        return [added(keep[k], got[k]) for k in range(z_size)]

    down_parts = weight_grad(d_ffn, d_ffn_other, product, down_to, len(RING))
    d_gate, d_up, back_own, back_send = kernel_call(
        functools.partial(ffn_back_kernel, steps),
        (2 * steps,),
        [(after(d_ffn, down_parts[-1]), own_rows(steps, D)), (d_ffn_other, partner_rows(steps, D))]
        + wholes([down_w, gate_w, value_w])
        + [(active, step_rows(hidden)), (slope, step_rows(hidden))],
        [((2 * rows, hidden), BF16, step_rows(hidden))] * 2
        + [((rows, D), F32, own_rows(steps, D)), ((rows, D), BF16, partner_rows(steps, D))],
        flops=3 * 2 * 2 * rows * D * hidden,
        name="ffn_back",
    )
    down_got = swap(down_parts[3], "prev")
    gate_keep, gate_send = weight_grad(after(low, back_send), low_other, d_gate, ffn_to, 2)
    down_got, back_send, gate_send = fence(down_got, back_send, gate_send)

    gate_got = swap(gate_send, "b")
    down_got = swap(added(down_parts[2], down_got), "prev")
    back_got = swap(back_send, "core")
    d_hidden, dctx_mine, dctx_send, out_keep, out_send, sums_one = kernel_call(
        first_norm_back_kernel,
        (steps,),
        [
            (place, smem()),
            (unit_one, step_rows(D)),
            (inverse_one, step_rows(1)),
            (norms, whole(norms.shape)),
            (d_z, step_rows(D)),
            (back_own, step_rows(D)),
            (back_got, step_rows(D)),
            (ctx_mine, step_rows(head_cols)),
            (ctx_got, step_rows(head_cols)),
        ]
        + wholes([out_mine, ctx_got]),
        [
            ((rows, D), F32, step_rows(D)),
            ((rows, head_cols), BF16, step_rows(head_cols)),
            ((rows, head_cols), BF16, step_rows(head_cols)),
            (out_mine.shape, F32, whole(out_mine.shape)),
            (out_mine.shape, BF16, whole(out_mine.shape)),
            ((8, D), F32, whole((8, D))),
        ],
        scratch=[pltpu.VMEM((blocks, tall, D), F32)],
        flops=2 * 2 * rows * D * D,
        name="first_norm_back",
    )
    def attend_back(block, mixed, d_context, logs):
        return kernel_call(
            attend_back_kernel,
            (1,),
            [(jnp.array([0, block], jnp.int32), smem()), (flags, smem()), (slopes, smem())]
            + far(wholes([mixed, logs]))
            + wholes([d_context]),
            [((rows, head_cols), BF16, whole((rows, head_cols)))] * 3,
            scratch=[pltpu.VMEM((LONG, LONG), F32)],
            name="attend_back",
            room=16,
        )

    d_own = attend_back(0, mixed_own, dctx_mine, logs_own)
    value_keep, value_send = weight_grad(after(low, d_own[0]), low_other, d_up, ffn_to, 2)
    down_got, gate_got, dctx_send, out_send, value_send = fence(down_got, gate_got, dctx_send, out_send, value_send)
    dctx_got, out_got = swap(dctx_send, "core"), swap(out_send, "core")
    value_got = swap(value_send, "b")
    gate_keep, gate_send = halves(gate_keep, gate_got)
    down_send = added(down_parts[1], down_got)
    gate_got = swap(gate_send, "a")
    down_got = swap(down_send, "prev")
    out_sum = (out_keep + out_got.astype(F32)).astype(BF16)

    d_partner = attend_back(1, mixed_partner, after(dctx_got, gate_send, down_send), logs_partner)
    grad_shape = (blocks // 2, tall, 4 * head_cols + 128)
    head_keep, head_send = kernel_call(
        qkv_grad_kernel,
        (3,),
        [(qkv_to, smem())]
        + wholes([tokens, tokens_other, *d_own, *d_partner, out_sum, sums_one, sums_two]),
        [(grad_shape, BF16, whole(grad_shape))] * 2,
        scratch=[pltpu.VMEM(block_row + (head_cols,), BF16), pltpu.VMEM(block_row + (128,), BF16)],
        name="qkv_grad",
    )
    down_got, gate_got, head_send = fence(down_got, gate_got, head_send)
    head_got = swap(head_send, "b")
    gate_parts = quarters(gate_keep, gate_got)
    value_keep, value_send = halves(value_keep, value_got)

    value_got = swap(value_send, "a")
    gate_sum = plane.sum_z(gate_parts)
    down_keep, down_send = halves(down_parts[0], down_got)

    def input_part(d_parts, more, dtype):
        return kernel_call(
            input_grad_kernel,
            (steps,),
            [(v, step_rows(head_cols)) for v in d_parts] + wholes([qkv_w]) + [(v, step_rows(D)) for v in more],
            [((rows, D), dtype, step_rows(D))],
            name="input_grad",
        )[0]

    in_send = input_part([after(d_partner[0], value_send, *gate_parts), *d_partner[1:]], [], BF16)
    head_got, value_got, gate_sum, down_send, in_send = fence(head_got, value_got, gate_sum, down_send, in_send)
    head_keep, head_send = halves(head_keep, head_got)
    value_parts = quarters(value_keep, value_got)

    in_got = swap(in_send, "core")
    down_got = swap(down_send, "b")
    head_got = swap(head_send, "a")
    value_sum = plane.sum_z(value_parts)
    input_grad = input_part([after(d_own[0], head_send, *value_parts), *d_own[1:]], [d_hidden, in_got], F32)
    head_got, value_sum, down_got, input_grad = fence(head_got, value_sum, down_got, input_grad)
    head_parts = quarters(head_keep, head_got)
    down_keep, down_send = halves(down_keep, down_got)

    down_got = swap(down_send, "a")
    head_sum = plane.sum_z(head_parts)
    grads = [gate_sum, value_sum, added(down_keep[0], down_got[0])]

    def in_order(mine, other):
        return [jnp.where(first, mine, other), jnp.where(first, other, mine)]

    kept = [half_of(core, total.reshape(2, tall, width), 0) for total in grads]
    ffn_got = swap(jnp.concatenate([other for _, other in kept], axis=0), "core")
    ffn_pieces = [
        jnp.concatenate(in_order(mine, ffn_got[n * tall : (n + 1) * tall]), axis=1).astype(F32)
        for n, (mine, _) in enumerate(kept)
    ]
    gate_piece, value_piece, down_piece = ffn_pieces[0], ffn_pieces[1], ffn_pieces[2].T
    there = after(swap(head_sum, "y"), gate_piece, value_piece, down_piece)
    own = y_here == core
    got = swap(jnp.where(own, there, head_sum), "core")
    qkv_piece, out_piece, gains_piece, biases_piece = kernel_call(
        pieces_kernel,
        (1,),
        [(jnp.stack([core, own.astype(jnp.int32)]), smem())] + wholes([head_sum, there, got]),
        [((tall, 3 * D), F32, whole((tall, 3 * D))), ((tall, D), F32, whole((tall, D)))]
        + [((2, tall), F32, whole((2, tall)))] * 2,
        name="pieces",
    )
    return (
        layer_out,
        input_grad,
        qkv_piece,
        out_piece,
        gate_piece,
        value_piece,
        down_piece,
        gains_piece,
        biases_piece,
    )


def solution(mesh):
    wide, narrow = mesh.shape["wide"], mesh.shape["narrow"]
    placed = (
        P(("wide", "narrow"), None),
        P("wide", None),
        P("wide", None),
        P("wide", "narrow"),
        P("wide", "narrow"),
        P("narrow", "wide"),
        P(None, "wide"),
        P(None, "wide"),
        P("wide", "narrow"),
        P(("wide", "narrow"), None),
    )
    if narrow == 2 and wide % 16 == 0 and D % (16 * wide) == 0:
        body = functools.partial(plane_shards, wide, narrow)
    else:
        body = general_shards
    return jax.shard_map(
        body,
        mesh=mesh,
        in_specs=placed,
        out_specs=(
            P(("wide", "narrow"), None),
            P(("wide", "narrow"), None),
            P("wide", None),
            P("wide", None),
            P("wide", "narrow"),
            P("wide", "narrow"),
            P("narrow", "wide"),
            P(None, "wide"),
            P(None, "wide"),
        ),
        check_vma=False,
    )
```

```python
import functools

import jax
import jax.numpy as jnp
import numpy as np
from jax import lax
from jax.experimental import pallas as pl
from jax.experimental.pallas import tpu as pltpu
from jax.sharding import PartitionSpec as P

D = 768
HEADS = 12
HEAD_DIM = 64
LONG = 512
SHORT = 128


def norm_rows(values, gain_row, bias_row):
    center = jnp.mean(values, axis=-1, keepdims=True)
    shifted = values - center
    spread = jnp.mean(shifted * shifted, axis=-1, keepdims=True)
    return shifted * lax.rsqrt(spread + 1e-05) * gain_row + bias_row


def gelu_product(gate_in, value_in):
    return jax.nn.gelu(gate_in, approximate=False) * value_in


def alibi_slopes(heads):
    power = 1 << heads.bit_length() - 1
    first = [2.0 ** (-8.0 * (index + 1) / power) for index in range(power)]
    second = [2.0 ** (-8.0 * (2 * index + 1) / (2 * power)) for index in range(heads - power)]
    return jnp.array(first + second, dtype=jnp.float32)


def alibi_bias(span, heads):
    position = jnp.arange(span)
    distance = jnp.abs(position[:, None] - position[None, :]).astype(jnp.float32)
    slopes = alibi_slopes(heads)
    return slopes[:, None, None] * distance


def block_scores(query_g, key_g, span):
    width = query_g.shape[-1]
    scores = jnp.einsum(
        "bqhd,bkhd->bhqk", query_g, key_g, preferred_element_type=jnp.float32
    ) * width ** (-0.5)
    return scores - alibi_bias(span, query_g.shape[2])


def attend(query_rows, key_rows, value_rows, span):
    rows, heads, width = query_rows.shape
    groups = rows // span
    shape_g = (groups, span, heads, width)
    query_g = query_rows.reshape(shape_g)
    key_g = key_rows.reshape(shape_g)
    value_g = value_rows.reshape(shape_g)
    scores = block_scores(query_g, key_g, span)
    top = jnp.max(scores, axis=-1, keepdims=True)
    expd = jnp.exp(scores - top)
    total = jnp.sum(expd, axis=-1, keepdims=True)
    probs_low = (expd / total).astype(jnp.bfloat16)
    context = jnp.einsum("bhqk,bkhd->bqhd", probs_low, value_g, preferred_element_type=jnp.float32)
    log_total = jnp.transpose((top + jnp.log(total))[..., 0], (0, 2, 1)).reshape(rows, heads)
    return (context.reshape(rows, heads * width), log_total)


def attend_back(query_rows, key_rows, value_rows, log_total, d_context, span):
    rows, heads, width = query_rows.shape
    groups = rows // span
    shape_g = (groups, span, heads, width)
    query_g = query_rows.reshape(shape_g)
    key_g = key_rows.reshape(shape_g)
    value_g = value_rows.reshape(shape_g)
    d_context_g = d_context.reshape(shape_g)
    lse_g = jnp.transpose(log_total.reshape(groups, span, heads), (0, 2, 1))
    scores = block_scores(query_g, key_g, span)
    probs = jnp.exp(scores - lse_g[..., None])
    probs_low = probs.astype(jnp.bfloat16)
    d_probs = jnp.einsum(
        "bqhd,bkhd->bhqk", d_context_g, value_g, preferred_element_type=jnp.float32
    )
    d_values = jnp.einsum(
        "bhqk,bqhd->bkhd", probs_low, d_context_g, preferred_element_type=jnp.float32
    )
    row_dot = jnp.sum(probs * d_probs, axis=-1, keepdims=True)
    d_scores = (probs * (d_probs - row_dot)).astype(jnp.bfloat16)
    scale = width ** (-0.5)
    d_queries = (
        jnp.einsum("bhqk,bkhd->bqhd", d_scores, key_g, preferred_element_type=jnp.float32) * scale
    )
    d_keys = (
        jnp.einsum("bhqk,bqhd->bkhd", d_scores, query_g, preferred_element_type=jnp.float32) * scale
    )
    return jnp.stack([d_queries, d_keys, d_values], axis=2).reshape(rows, 3, heads, width)


def contract_rows(left, right):
    return lax.dot_general(
        left, right, (((0,), (0,)), ((), ())), preferred_element_type=jnp.float32
    )


def contract_cols(left, right):
    return lax.dot_general(
        left, right, (((1,), (1,)), ((), ())), preferred_element_type=jnp.float32
    )


def general_shards(
    tokens, w_qkv, w_out, w_gate, w_value, w_down, norm_gains, norm_biases, long_count, cotangent
):
    gathered = (
        lax.all_gather(w_qkv, "wide", axis=0, tiled=True),
        lax.all_gather(w_out, "wide", axis=0, tiled=True),
        lax.all_gather(w_gate, "wide", axis=0, tiled=True),
        lax.all_gather(w_value, "wide", axis=0, tiled=True),
        lax.all_gather(w_down, "wide", axis=1, tiled=True),
        lax.all_gather(norm_gains, "wide", axis=1, tiled=True),
        lax.all_gather(norm_biases, "wide", axis=1, tiled=True),
    )
    full_qkv, full_out, wide_gate, wide_value, wide_down, gains_all, biases_all = gathered
    gains_f = gains_all.astype(jnp.float32)
    biases_f = biases_all.astype(jnp.float32)
    rows_dev = tokens.shape[0]
    n_blocks = rows_dev // LONG
    long_here = long_count[0, 0]
    tokens_f = tokens.astype(jnp.float32)
    mixed = jnp.dot(tokens, full_qkv, preferred_element_type=jnp.float32).astype(jnp.bfloat16)
    heads_view = mixed.reshape(n_blocks, LONG, 3, HEADS, HEAD_DIM)
    query_blk = heads_view[:, :, 0]
    key_blk = heads_view[:, :, 1]
    value_blk = heads_view[:, :, 2]
    block_ids = jnp.arange(n_blocks)

    def forward_block(entry):
        block_id, query_rows, key_rows, value_rows = entry
        return lax.cond(
            block_id < long_here,
            lambda operands: attend(operands[0], operands[1], operands[2], LONG),
            lambda operands: attend(operands[0], operands[1], operands[2], SHORT),
            (query_rows, key_rows, value_rows),
        )

    context_f, lse_rows = lax.map(forward_block, (block_ids, query_blk, key_blk, value_blk))
    context = context_f.reshape(rows_dev, D).astype(jnp.bfloat16)
    branch = jnp.dot(context, full_out, preferred_element_type=jnp.float32)
    hidden_in = tokens_f + branch
    normed = norm_rows(hidden_in, gains_f[0], biases_f[0])
    normed_low = normed.astype(jnp.bfloat16)
    all_rows = lax.all_gather(normed_low, "narrow", axis=0, tiled=True)
    gate = jnp.dot(all_rows, wide_gate, preferred_element_type=jnp.float32)
    value_up = jnp.dot(all_rows, wide_value, preferred_element_type=jnp.float32)
    product_f, pull_product = jax.vjp(gelu_product, gate, value_up)
    product = product_f.astype(jnp.bfloat16)
    ffn_out = lax.psum_scatter(
        jnp.dot(product, wide_down, preferred_element_type=jnp.float32),
        "narrow",
        scatter_dimension=0,
        tiled=True,
    )
    out_in = normed + ffn_out
    layer_out, pull_second = jax.vjp(norm_rows, out_in, gains_f[1], biases_f[1])
    d_out, d_gain_two, d_bias_two = pull_second(cotangent.astype(jnp.float32))
    d_ffn = d_out.astype(jnp.bfloat16)
    d_rows = lax.all_gather(d_ffn, "narrow", axis=0, tiled=True)
    grad_down = contract_rows(product, d_rows)
    d_product = contract_cols(d_rows, wide_down)
    d_gate, d_up = pull_product(d_product)
    d_gate_low = d_gate.astype(jnp.bfloat16)
    d_up_low = d_up.astype(jnp.bfloat16)
    grad_gate = contract_rows(all_rows, d_gate_low)
    grad_value = contract_rows(all_rows, d_up_low)
    d_normed = lax.psum_scatter(
        contract_cols(d_gate_low, wide_gate) + contract_cols(d_up_low, wide_value),
        "narrow",
        scatter_dimension=0,
        tiled=True,
    )
    d_normed_total = d_out + d_normed
    unused_out, pull_first = jax.vjp(norm_rows, hidden_in, gains_f[0], biases_f[0])
    d_hidden, d_gain_one, d_bias_one = pull_first(d_normed_total)
    d_branch = d_hidden.astype(jnp.bfloat16)
    grad_out = contract_rows(context, d_branch)
    d_context = contract_cols(d_branch, full_out).astype(jnp.bfloat16)
    d_context_blk = d_context.reshape(n_blocks, LONG, HEADS, HEAD_DIM)

    def backward_block(entry):
        block_id, query_rows, key_rows, value_rows, log_total, d_ctx = entry
        return lax.cond(
            block_id < long_here,
            lambda operands: attend_back(
                operands[0], operands[1], operands[2], operands[3], operands[4], LONG
            ),
            lambda operands: attend_back(
                operands[0], operands[1], operands[2], operands[3], operands[4], SHORT
            ),
            (query_rows, key_rows, value_rows, log_total, d_ctx),
        )

    d_mixed_f = lax.map(
        backward_block, (block_ids, query_blk, key_blk, value_blk, lse_rows, d_context_blk)
    )
    d_mixed = d_mixed_f.reshape(rows_dev, 3 * D).astype(jnp.bfloat16)
    grad_qkv = contract_rows(tokens, d_mixed)
    input_grad = d_hidden + contract_cols(d_mixed, full_qkv)
    grad_gains = jnp.stack([d_gain_one, d_gain_two])
    grad_biases = jnp.stack([d_bias_one, d_bias_two])
    pieces = (
        lax.psum_scatter(
            grad_qkv.astype(jnp.bfloat16), "wide", scatter_dimension=0, tiled=True
        ).astype(jnp.float32),
        lax.psum_scatter(
            grad_out.astype(jnp.bfloat16), "wide", scatter_dimension=0, tiled=True
        ).astype(jnp.float32),
        lax.psum_scatter(
            grad_gate.astype(jnp.bfloat16), "wide", scatter_dimension=0, tiled=True
        ).astype(jnp.float32),
        lax.psum_scatter(
            grad_value.astype(jnp.bfloat16), "wide", scatter_dimension=0, tiled=True
        ).astype(jnp.float32),
        lax.psum_scatter(
            grad_down.astype(jnp.bfloat16), "wide", scatter_dimension=1, tiled=True
        ).astype(jnp.float32),
        lax.psum_scatter(
            grad_gains.astype(jnp.bfloat16), "wide", scatter_dimension=1, tiled=True
        ).astype(jnp.float32),
        lax.psum_scatter(
            grad_biases.astype(jnp.bfloat16), "wide", scatter_dimension=1, tiled=True
        ).astype(jnp.float32),
    )
    qkv_piece, out_piece, gate_piece, value_piece, down_piece, gains_piece, biases_piece = pieces
    qkv_piece, out_piece, gains_piece, biases_piece = (
        lax.psum(qkv_piece.astype(jnp.bfloat16), "narrow").astype(jnp.float32),
        lax.psum(out_piece.astype(jnp.bfloat16), "narrow").astype(jnp.float32),
        lax.psum(gains_piece.astype(jnp.bfloat16), "narrow").astype(jnp.float32),
        lax.psum(biases_piece.astype(jnp.bfloat16), "narrow").astype(jnp.float32),
    )
    return (
        layer_out.astype(jnp.bfloat16),
        input_grad,
        qkv_piece,
        out_piece,
        gate_piece,
        value_piece,
        down_piece,
        gains_piece,
        biases_piece,
    )


AXES = ("wide", "narrow")
F32 = jnp.float32
BF16 = jnp.bfloat16
MIB = 1024 * 1024
RING = (0, 1, 3, 2)
PAIR = 2 * HEAD_DIM


def dot(left, right):
    return jnp.dot(left, right, preferred_element_type=F32)


class Plane:
    def __init__(self, wide, narrow):
        self.size = {"z": wide // 4, "ring": len(RING), "a": 2, "b": 2, "core": 2, "y": narrow}
        self.pairs = {}
        count = wide * narrow
        for dim, size in self.size.items():
            for step in range(1, size) if dim != "ring" else ():
                self.pairs[dim, step] = [(i, self.partner(i, dim, step)) for i in range(count)]
        after_z = {z: RING[(n + 1) % len(RING)] for n, z in enumerate(RING)}
        self.pairs["next", 1] = [(i, i % 8 + 8 * after_z[i // 8]) for i in range(count)]
        self.pairs["prev", 1] = [(j, i) for i, j in self.pairs["next", 1]]
        w = lax.axis_index("wide")
        self.z, self.x, self.core = w // 4, (w // 2) % 2, w % 2
        self.y = lax.axis_index("narrow")

    @staticmethod
    def partner(i, dim, step):
        z, x, c, y = i // 8, (i // 4) % 2, (i // 2) % 2, i % 2
        if dim == "z":
            z ^= step
        elif dim == "core":
            c ^= 1
        elif dim == "y" or (dim == "a") == (c == 1):
            y ^= 1
        else:
            x ^= 1
        return ((z * 2 + x) * 2 + c) * 2 + y

    def swap(self, value, dim, step=1):
        return lax.ppermute(value, AXES, self.pairs[dim, step])

    def sum_z(self, parts):
        total = parts[0].astype(F32)
        for k in range(1, self.size["z"]):
            total = total + self.swap(parts[k], "z", k).astype(F32)
        return total.astype(BF16)

    def tables(self, order, numbered):
        sizes = [self.size[dim] for dim in order]
        number = np.arange(int(np.prod(sizes)))
        rest, digit = number, {}
        for dim, size in zip(order, sizes):
            digit[dim] = rest % size
            rest = rest // size
        first = self.core == 0
        a_here = jnp.where(first, self.x, self.y)
        b_here = jnp.where(first, self.y, self.x)
        if "ring" in digit:
            at = sum(jnp.where(self.z == z, n, 0) for n, z in enumerate(RING))
            z = sum(jnp.where((at - digit["ring"]) % len(RING) == n, z, 0) for n, z in enumerate(RING))
        else:
            z = digit["z"] ^ self.z
        a = digit["a"] ^ a_here
        b = digit["b"] ^ b_here
        x, y = jnp.where(first, a, b), jnp.where(first, b, a)
        return numbered(z, x, y).astype(jnp.int32)


def after(value, *events):
    return lax.optimization_barrier((value,) + events)[0]


def fence(*values):
    return lax.optimization_barrier(values)


def smem():
    return pl.BlockSpec(memory_space=pltpu.SMEM)


def whole(shape):
    zeros = (0,) * len(shape)
    return pl.BlockSpec(tuple(shape), lambda *_: zeros)


def kernel_call(body, grid, ins, outs, scratch=(), flops=0, name=None, room=6):
    blocks = [(v[1].block_shape, v[0].dtype) for v in ins] + [(v[2].block_shape, v[1]) for v in outs]
    held = sum(2 * int(np.prod(shape)) * np.dtype(d).itemsize for shape, d in blocks if shape is not None)
    held += sum(int(np.prod(v.shape)) * np.dtype(v.dtype).itemsize for v in scratch)
    return pl.pallas_call(
        body,
        grid=grid,
        in_specs=[v[1] for v in ins],
        out_specs=[v[2] for v in outs],
        out_shape=[(pltpu.HBM if more else jax.ShapeDtypeStruct)(s, d) for s, d, _, *more in outs],
        scratch_shapes=list(scratch),
        compiler_params=pltpu.CompilerParams(
            dimension_semantics=("arbitrary",) * len(grid), vmem_limit_bytes=held // 2 + room * MIB
        ),
        cost_estimate=pl.CostEstimate(flops=0, bytes_accessed=0, transcendentals=0),
        name=name,
    )(*[pltpu.with_memory_space_constraint(a, pltpu.HBM) if more else a for a, _, *more in ins])


ROWS = 512


def own_rows(steps, cols):
    return pl.BlockSpec((ROWS, cols), lambda i: (jnp.minimum(i, steps - 1), 0))


def partner_rows(steps, cols):
    return pl.BlockSpec((ROWS, cols), lambda i: (jnp.maximum(i - steps, 0), 0))


def pick_rows(i, steps, own_ref, partner_ref):
    return jnp.where(i < steps, own_ref[...], partner_ref[...])


def split_kernel(place, w_qkv, w_out, gains, biases, mine, send):
    first = place[0] == 0
    half = D // 2
    for n in range(4):
        source, start = (w_qkv, n * D) if n < 3 else (w_out, 0)
        low, high = source[:, start : start + half], source[:, start + half : start + D]
        mine[:, n * half : (n + 1) * half] = jnp.where(first, low, high)
        send[:, n * half : (n + 1) * half] = jnp.where(first, high, low)
    rows = jnp.concatenate([gains[...], biases[...]], axis=0).astype(F32)
    eye = jnp.where(
        lax.broadcasted_iota(jnp.int32, (128, rows.shape[0]), 0)
        == lax.broadcasted_iota(jnp.int32, (128, rows.shape[0]), 1),
        1.0,
        0.0,
    )
    norm_cols = contract_cols(rows.T.astype(BF16), eye.astype(BF16)).astype(BF16)
    mine[:, 4 * half :] = norm_cols
    send[:, 4 * half :] = norm_cols


def fill_blocks(table, pieces, weight, cols=slice(None)):
    count = pieces[0].shape[0]
    for n, piece in enumerate(pieces):
        for k in range(count):
            weight[table[n * count + k]] = piece[k, :, cols]


def qkv_kernel(steps, groups, pieces, table, own, partner, *refs):
    i = pl.program_id(0)
    parts = refs[:pieces]
    mixed_own, mixed_partner, weight, out_w, norms, table_t = refs[pieces:]
    cols, part = weight.shape[2], out_w.shape[2]
    tall = weight.shape[0] * weight.shape[1]

    @pl.when(i == 0)
    def _():
        fill_blocks(table, parts, weight, slice(0, cols))
        fill_blocks(table, parts, out_w, slice(cols, cols + part))
        fill_blocks(table, parts, table_t, slice(cols + part, None))
        norms[...] = table_t[...].reshape(tall, table_t.shape[2]).astype(F32).T[: norms.shape[0]]

    rows_here = pick_rows(i, steps, own, partner)
    for g in range(groups):
        span = slice(g * cols // groups, (g + 1) * cols // groups)
        tile = weight[:, :, span].reshape(tall, cols // groups)
        value = dot(rows_here, tile).astype(BF16)

        @pl.when(i < steps)
        def _():
            mixed_own[:, span] = value

        @pl.when(i >= steps)
        def _():
            mixed_partner[:, span] = value


def lane_masks():
    lane = lax.broadcasted_iota(jnp.int32, (1, PAIR), 1)
    return [lane < HEAD_DIM, lane >= HEAD_DIM]


def keep(mask, value):
    return jnp.where(mask, value, jnp.zeros_like(value))


def fill_distance(distance):
    row = lax.broadcasted_iota(jnp.int32, distance.shape, 0)
    col = lax.broadcasted_iota(jnp.int32, distance.shape, 1)
    distance[...] = jnp.abs(row - col).astype(F32)


def scores_of(queries, keys, slope, distance):
    raw = lax.dot_general(queries, keys, (((1,), (1,)), ((), ())), preferred_element_type=F32)
    return raw - slope * distance


def tiles(value, tall):
    return [value[n : n + tall] for n in range(0, value.shape[0], tall)]


def pair_cols(part, pair):
    return pl.ds(pl.multiple_of(part * (D // 2) + pair * PAIR, PAIR), PAIR)


def attend_kernel(place, flags, slopes, mixed, *refs):
    context, logs, distance = refs[-3:]
    masks = lane_masks()
    scale = HEAD_DIM**-0.5
    lane = lax.broadcasted_iota(jnp.int32, (1, 128), 1)
    fill_distance(distance)
    for extra in refs[:-3]:
        context[LONG:, :] = extra[...].reshape(context.shape[0] - LONG, context.shape[1])

    def run(is_long):
        tall = 2 * SHORT if is_long else LONG

        def one_pair(pair, _):
            q_all, k_all, v_all = (mixed[:, pair_cols(part, pair)] for part in range(3))
            totals = [0.0] * (LONG // tall)
            mine = (lambda v: [v]) if is_long else (lambda v: tiles(v, SHORT))
            jobs = []
            for head in range(2):
                slope = slopes[pair * 2 + head]
                q = (keep(masks[head], q_all) * scale).astype(BF16)
                v = keep(masks[head], v_all)
                for n in range(LONG // tall):
                    rows = slice(n * tall, (n + 1) * tall)
                    away = distance[rows, :] if is_long else distance[:SHORT, :SHORT]
                    s = [scores_of(a, b, slope, away) for a, b in zip(mine(q[rows]), mine(k_all))]
                    jobs.append((head, n, jnp.concatenate(s, axis=0), v))
            done = []
            for head, n, s, v in jobs:
                top = jnp.max(s, axis=-1, keepdims=True)
                e = jnp.exp(s - top)
                norm = jnp.sum(e, axis=-1, keepdims=True)
                done.append(((e * (1.0 / norm)).astype(BF16), top + jnp.log(norm)))
            for (head, n, s, v), (p, log) in zip(jobs, done):
                totals[n] = totals[n] + jnp.concatenate([dot(a, b) for a, b in zip(mine(p), mine(v))], axis=0)
                rows = slice(n * tall, (n + 1) * tall)
                logs[rows, :] = jnp.where(lane == pair * 2 + head, log, logs[rows, :])
            for n in range(LONG // tall):
                context[n * tall : (n + 1) * tall, pair_cols(0, pair)] = totals[n].astype(BF16)
            return 0

        lax.fori_loop(0, D // 2 // PAIR, one_pair, 0)

    logs[...] = jnp.zeros_like(logs)
    flag = flags[place[1]]

    @pl.when(flag > 0)
    def _():
        run(True)

    @pl.when(flag <= 0)
    def _():
        run(False)


def attend_back_kernel(place, flags, slopes, mixed, logs_ref, d_context, d_query, d_key, d_value, distance):
    masks = lane_masks()
    scale = HEAD_DIM**-0.5
    fill_distance(distance)

    def run(is_long):
        tall = 2 * SHORT if is_long else LONG
        logs = logs_ref[...]
        lane = lax.broadcasted_iota(jnp.int32, (1, 128), 1)

        def one_pair(pair, _):
            q_all, k_all, v_all = (mixed[:, pair_cols(part, pair)] for part in range(3))
            d_all = d_context[:, pair_cols(0, pair)]
            d_q, d_k, d_v = [0.0] * (LONG // tall), 0.0, 0.0
            group = SHORT if not is_long else tall
            jobs = []
            for head in range(2):
                slope = slopes[pair * 2 + head]
                q = (keep(masks[head], q_all) * scale).astype(BF16)
                k = (keep(masks[head], k_all) * scale).astype(BF16)
                d_c = keep(masks[head], d_all)
                log_all = jnp.sum(jnp.where(lane == pair * 2 + head, logs, 0.0), axis=-1, keepdims=True)
                for n in range(LONG // tall):
                    rows = slice(n * tall, (n + 1) * tall)
                    jobs.append((n, slope, q[rows], k, d_c[rows], log_all[rows], distance[rows, :] if is_long else distance[:SHORT, :SHORT]))
            mine = (lambda v: [v]) if is_long else (lambda v: tiles(v, SHORT))
            raw = []
            for n, slope, q, k, d_c, log_rows, away in jobs:
                s = jnp.concatenate([scores_of(a, b, slope, away) for a, b in zip(mine(q), mine(k_all))], axis=0)
                d_p = jnp.concatenate([contract_cols(a, b) for a, b in zip(mine(d_c), mine(v_all))], axis=0)
                raw.append((s, d_p))
            done = []
            for (n, slope, q, k, d_c, log_rows, away), (s, d_p) in zip(jobs, raw):
                p = jnp.exp(s - log_rows)
                d_s = (p * (d_p - jnp.sum(p * d_p, axis=-1, keepdims=True))).astype(BF16)
                done.append((d_s, p.astype(BF16)))
            for (n, slope, q, k, d_c, log_rows, away), (d_s, p) in zip(jobs, done):
                d_q[n] = d_q[n] + jnp.concatenate([dot(a, b) for a, b in zip(mine(d_s), mine(k))], axis=0)
                d_k = d_k + jnp.concatenate([dot(a.T, b) for a, b in zip(mine(q), mine(d_s))], axis=1)
                d_v = d_v + jnp.concatenate([dot(a.T, b) for a, b in zip(mine(d_c), mine(p))], axis=1)
            cols = pair_cols(0, pair)
            for n in range(LONG // tall):
                d_query[n * tall : (n + 1) * tall, cols] = d_q[n].astype(BF16)
            d_key[:, cols] = d_k.T.astype(BF16)
            d_value[:, cols] = d_v.T.astype(BF16)
            return 0

        lax.fori_loop(0, D // 2 // PAIR, one_pair, 0)

    flag = flags[place[1]]

    @pl.when(flag > 0)
    def _():
        run(True)

    @pl.when(flag <= 0)
    def _():
        run(False)


def spread(rows):
    center = jnp.mean(rows, axis=-1, keepdims=True)
    shifted = rows - center
    inverse = lax.rsqrt(jnp.mean(shifted * shifted, axis=-1, keepdims=True) + 1e-05)
    return shifted * inverse, inverse


def norm_back(e, unit, inverse):
    mean_e = jnp.mean(e, axis=-1, keepdims=True)
    mean_en = jnp.mean(e * unit, axis=-1, keepdims=True)
    return (e - mean_e - unit * mean_en) * inverse


def first_norm_kernel(place, tokens, ctx_mine, ctx_other, w_mine, w_other_rows, norms, unit, inverse, low):
    core = place[0]
    half = w_mine.shape[0] // 2
    wide = w_mine.shape[2]

    def branch(weight):
        return dot(ctx_mine[...], weight(core)) + dot(ctx_other[...], weight(1 - core))

    mine = branch(lambda c: w_mine[pl.ds(c * half, half)].reshape(D // 2, wide))
    other = branch(lambda c: w_other_rows[pl.ds(pl.multiple_of(LONG + c * (D // 2), 128), D // 2), :])
    first = core == 0
    added = jnp.concatenate([jnp.where(first, mine, other), jnp.where(first, other, mine)], axis=1)
    n, inv = spread(tokens[...].astype(F32) + added)
    unit[...] = n
    inverse[...] = inv
    low[...] = (n * norms[0:1, :] + norms[2:3, :]).astype(BF16)


def gelu_parts(x):
    phi = 0.5 + 0.5 * lax.erf(x * 0.5**0.5)
    return x * phi, phi + x * jnp.exp(-0.5 * (x * x)) * 0.3989422804014327


def columns_of(weight, half, span):
    count = weight.shape[0] // 2
    return weight[half * count : (half + 1) * count, :, span].reshape(D, span.stop - span.start)


def gate_kernel(steps, pieces, table, own, partner, *refs):
    i = pl.program_id(0)
    active, slope, gate_w = refs[pieces:]

    @pl.when(i == 0)
    def _():
        fill_blocks(table, refs[:pieces], gate_w)

    rows = pick_rows(i, steps, own, partner)
    width = gate_w.shape[2]
    for half in range(2):
        for start in range(0, width, 256):
            out = slice(half * width + start, half * width + start + 256)
            gate = dot(rows, columns_of(gate_w, half, slice(start, start + 256)))
            act, grad = gelu_parts(gate)
            active[:, out] = act.astype(BF16)
            slope[:, out] = grad.astype(BF16)


def value_kernel(steps, pieces, table, own, partner, active, slope, *refs):
    i = pl.program_id(0)
    product, scaled, value_w = refs[pieces:]

    @pl.when(i == 0)
    def _():
        fill_blocks(table, refs[:pieces], value_w)

    rows = pick_rows(i, steps, own, partner)
    width = value_w.shape[2]
    for half in range(2):
        for start in range(0, width, 256):
            out = slice(half * width + start, half * width + start + 256)
            up = dot(rows, columns_of(value_w, half, slice(start, start + 256)))
            product[:, out] = (active[:, out].astype(F32) * up).astype(BF16)
            scaled[:, out] = (slope[:, out].astype(F32) * up).astype(BF16)


def times_down(product, down_w):
    width = down_w.shape[2]
    total = 0.0
    for half in range(2):
        part = product[:, half * width : (half + 1) * width]
        total = total + contract_cols(part, columns_of(down_w, half, slice(0, width)))
    return total


def down_first_kernel(table, product, *refs):
    partner, down_w = refs[-2:]

    @pl.when(pl.program_id(0) == 0)
    def _():
        fill_blocks(table, refs[:-2], down_w)

    partner[...] = times_down(product, down_w).astype(BF16)


def down_kernel(product, down_w, own):
    own[...] = times_down(product, down_w)


def second_norm_kernel(unit_one, norms, part_own, part_got, cotangent, out, d_z, d_ffn, sums):
    normed = unit_one[...] * norms[0:1, :] + norms[2:3, :]
    n, inv = spread(normed + (part_own[...] + part_got[...].astype(F32)))
    gain = norms[1:2, :]
    out[...] = (n * gain + norms[3:4, :]).astype(BF16)
    c = cotangent[...].astype(F32)
    back = norm_back(gain * c, n, inv)
    d_z[...] = back
    d_ffn[...] = back.astype(BF16)
    add_sums(sums, c * n, c)


def add_sums(sums, gain_terms, bias_terms):
    @pl.when(pl.program_id(0) == 0)
    def _():
        sums[...] = jnp.zeros_like(sums)

    sums[0:1, :] += jnp.sum(gain_terms, axis=0, keepdims=True)
    sums[1:2, :] += jnp.sum(bias_terms, axis=0, keepdims=True)


def ffn_back_kernel(
    steps, own, partner, down_w, gate_w, value_w, active, slope, d_gate, d_up, back_own, back_partner
):
    i = pl.program_id(0)
    rows = pick_rows(i, steps, own, partner)
    width = down_w.shape[2]
    total = jnp.zeros((ROWS, D), F32)
    for half in range(2):
        for start in range(0, width, 256):
            span = slice(start, start + 256)
            out = slice(half * width + start, half * width + start + 256)
            d_product = dot(rows, columns_of(down_w, half, span))
            dg = (d_product * slope[:, out].astype(F32)).astype(BF16)
            du = (d_product * active[:, out].astype(F32)).astype(BF16)
            d_gate[:, out] = dg
            d_up[:, out] = du
            total = total + contract_cols(dg, columns_of(gate_w, half, span))
            total = total + contract_cols(du, columns_of(value_w, half, span))

    @pl.when(i < steps)
    def _():
        back_own[...] = total

    @pl.when(i >= steps)
    def _():
        back_partner[...] = total.astype(BF16)


def weight_grad_kernel(table, left_own, left_partner, right_a, right_b, *refs):
    i = pl.program_id(0)
    parts, blocks = refs[:-1], refs[-1]
    rows = left_own.shape[0]
    count, tall, cols = blocks.shape
    for half, right in enumerate((right_a, right_b)):
        value = contract_rows(left_own[...], right[:rows, :]) + contract_rows(left_partner[...], right[rows:, :])
        value = value.astype(BF16).reshape(count // 2, tall, cols)
        blocks[half * (count // 2) : (half + 1) * (count // 2)] = value
    span = pl.ds(pl.multiple_of(i * cols, cols), cols)
    each = count // len(parts)
    for k in range(count):
        parts[k // each][k % each, :, span] = blocks[table[k]]


def first_norm_back_kernel(
    place,
    unit_ref,
    inverse,
    norms,
    d_z,
    part_own,
    part_got,
    ctx_mine,
    ctx_other,
    w_mine,
    w_other,
    d_hidden,
    dctx_mine,
    dctx_other,
    grad_keep,
    grad_send,
    sums,
    grad,
):
    core = place[0]
    first = core == 0
    unit = unit_ref[...]
    d_normed = d_z[...] + (part_own[...] + part_got[...].astype(F32))
    back = norm_back(norms[0:1, :] * d_normed, unit, inverse[...])
    low = back.astype(BF16)
    d_hidden[...] = back
    add_sums(sums, d_normed * unit, d_normed)
    half, wide = w_mine.shape[0] // 2, w_mine.shape[2]
    low_mine = jnp.where(first, low[:, :wide], low[:, wide:])
    low_other = jnp.where(first, low[:, wide:], low[:, :wide])
    for head_core, out in ((core, dctx_mine), (1 - core, dctx_other)):
        near = w_mine[pl.ds(head_core * half, half)].reshape(D // 2, wide)
        far = w_other[pl.ds(pl.multiple_of(LONG + head_core * (D // 2), 128), D // 2), :]
        out[...] = (contract_cols(low_mine, near) + contract_cols(low_other, far)).astype(BF16)

    @pl.when(pl.program_id(0) == 0)
    def _():
        grad[...] = jnp.zeros_like(grad)

    shape = (half,) + grad.shape[1:]
    grad[pl.ds(core * half, half)] += contract_rows(ctx_mine[...], low).reshape(shape)
    grad[pl.ds((1 - core) * half, half)] += contract_rows(ctx_other[...], low).reshape(shape)

    @pl.when(pl.program_id(0) == pl.num_programs(0) - 1)
    def _():
        left, right = grad[:, :, :wide], grad[:, :, wide:]
        grad_keep[...] = jnp.where(first, left, right)
        grad_send[...] = jnp.where(first, right, left).astype(BF16)


def qkv_grad_kernel(table, left_own, left_partner, *refs):
    d_own, d_partner = refs[:3], refs[3:6]
    out_grad, sums_one, sums_two, near, far, blocks, norm_grad = refs[6:]
    i = pl.program_id(0)
    count, tall, cols = blocks.shape

    @pl.when(i == 0)
    def _():
        one, two = sums_one[...], sums_two[...]
        empty = jnp.zeros((norm_grad.shape[2] - 4, D), F32)
        stacked = jnp.concatenate([one[0:1], two[0:1], one[1:2], two[1:2], empty], axis=0)
        norm_grad[...] = stacked.T.astype(BF16).reshape(norm_grad.shape)

    for g in range(3):

        @pl.when(i == g)
        def _():
            value = contract_rows(left_own[...], d_own[g][...]) + contract_rows(left_partner[...], d_partner[g][...])
            blocks[...] = value.astype(BF16).reshape(blocks.shape)
            for k in range(count):
                target, place = (near if k < count // 2 else far), table[k]
                target[k % (count // 2), :, g * cols : (g + 1) * cols] = blocks[place]
                if g == 0:
                    start = 3 * cols
                    for more in (out_grad, norm_grad):
                        stop = start + more.shape[2]
                        target[k % (count // 2), :, start:stop] = more[place]
                        start = stop


def input_grad_kernel(d_query, d_key, d_value, weight, *refs):
    cols = d_query.shape[1]
    total = 0.0
    for g, left in enumerate((d_query, d_key, d_value)):
        tile = weight[:, :, g * cols : (g + 1) * cols].reshape(D, cols)
        total = total + contract_cols(left[...], tile)
    for more in refs[:-1]:
        total = total + more[...].astype(F32)
    refs[-1][...] = total.astype(refs[-1].dtype)


def pieces_kernel(place, here, there, got, qkv, out, gains, biases):
    first, own = place[0] == 0, place[1] == 1
    half = D // 2
    mine = jnp.where(own, here[...], there[...])
    for n in range(4):
        a, b = mine[:, n * half : (n + 1) * half].astype(F32), got[:, n * half : (n + 1) * half].astype(F32)
        target, start = (qkv, n * D) if n < 3 else (out, 0)
        target[:, start : start + half] = jnp.where(first, a, b)
        target[:, start + half : start + D] = jnp.where(first, b, a)
    rows = (mine[:, 4 * half :].astype(F32) + got[:, 4 * half :].astype(F32)).T
    gains[...] = rows[0:2]
    biases[...] = rows[2:4]


def by_core(core, mine, other, axis):
    first = core == 0
    return jnp.stack([jnp.where(first, mine, other), jnp.where(first, other, mine)], axis=axis)


def half_of(core, halves, axis):
    zero, one = (lax.index_in_dim(halves, k, axis, keepdims=False) for k in range(2))
    first = core == 0
    return jnp.where(first, zero, one), jnp.where(first, one, zero)


def plane_shards(
    wide,
    narrow,
    tokens,
    w_qkv,
    w_out,
    w_gate,
    w_value,
    w_down,
    norm_gains,
    norm_biases,
    long_count,
    cotangent,
):
    plane = Plane(wide, narrow)
    swap = plane.swap
    core, y_here = plane.core, plane.y
    rows = tokens.shape[0]
    steps = rows // ROWS
    tall = w_qkv.shape[0]
    blocks = wide * narrow // 2
    z_size = plane.size["z"]
    head_cols = D // 2
    width = w_gate.shape[1] // 2
    hidden = 2 * width
    pairs = head_cols // PAIR
    qkv_to = plane.tables(("z", "a", "b"), lambda z, x, y: (z * 2 + x) * 2 + y)
    ffn_to = plane.tables(("z", "a", "b"), lambda z, x, y: y * (2 * z_size) + z * 2 + x)
    back_to = plane.tables(("a", "z", "b"), lambda z, x, y: y * (2 * z_size) + z * 2 + x)
    down_to = plane.tables(("a", "b", "ring"), lambda z, x, y: y * (2 * z_size) + z * 2 + x)
    place = jnp.reshape(core, (1,)).astype(jnp.int32)
    first = core == 0

    def wholes(arrays):
        return [(v, whole(v.shape)) for v in arrays]

    def far(entries):
        return [entry + (True,) for entry in entries]

    def step_rows(cols):
        return pl.BlockSpec((ROWS, cols), lambda i: (i, 0))

    head_shape = (tall, 4 * head_cols + 128)
    head_part, head_send = kernel_call(
        split_kernel,
        (1,),
        [(place, smem())] + far(wholes([w_qkv, w_out, norm_gains, norm_biases])),
        [(head_shape, BF16, whole(head_shape))] * 2,
        name="split",
    )
    flag = jnp.broadcast_to(long_count.astype(F32), (8, 128))
    head_got, flag_got = fence(swap(head_send, "core"), swap(flag, "core"))
    head_part = jnp.where(y_here == core, head_part, head_got)
    head_parts = [head_part] + [swap(head_part, "z", k) for k in range(1, z_size)]
    ffn_parts = [after(w_gate, head_part), w_value, w_down.T]
    ffn_other = jnp.concatenate([jnp.where(first, v[:, width:], v[:, :width]) for v in ffn_parts], axis=1)
    ffn_got = swap(ffn_other, "core")
    flags = jnp.stack([long_count[0, 0], flag_got[0, 0].astype(jnp.int32)])
    slopes = lax.dynamic_slice_in_dim(alibi_slopes(HEADS), core * (HEADS // 2), HEADS // 2)

    def ffn_chip(n):
        v, got = ffn_parts[n], ffn_got[:, n * width : (n + 1) * width]
        mine = jnp.where(first, v[:, :width], v[:, width:])
        return jnp.concatenate([jnp.where(first, mine, got), jnp.where(first, got, mine)], axis=0)

    def doubled(value, step, *events):
        got = swap(value, "z", step)
        return jnp.concatenate(lax.optimization_barrier((value, got) + events)[:2], axis=0)

    def along_plane(held):
        near = swap(held, "a")
        return held, near, swap(held, "b")

    def joined(value, got):
        return jnp.concatenate([value, got], axis=0)

    gate_one, value_one, down_one = (ffn_chip(n)[None] for n in range(3))
    gate_got = swap(gate_one, "z", 1)
    down_got = swap(down_one, "a")
    *head_parts, gate_got, down_got = fence(*head_parts, gate_got, down_got)
    qkv_z = jnp.stack(head_parts)
    gate_two, down_two = joined(gate_one, gate_got), joined(down_one, down_got)

    head_near, head_far = swap(qkv_z, "a"), swap(qkv_z, "b")
    gate_got = swap(gate_two, "z", 2)
    value_got = swap(after(value_one, qkv_z), "z", 1)
    tokens_other = swap(after(tokens, qkv_z), "core")
    head_near, head_far, gate_got, value_got, tokens_other = fence(head_near, head_far, gate_got, value_got, tokens_other)
    gate_z, value_two = joined(gate_two, gate_got), joined(value_one, value_got)

    head_last = swap(head_near, "b")
    down_got = swap(after(down_two, head_near), "b")
    gate_near = swap(gate_z, "a")
    value_got = swap(value_two, "z", 2)
    head_last, down_got, gate_near, value_got = fence(head_last, down_got, gate_near, value_got)
    value_z, down_four = joined(value_two, value_got), joined(down_two, down_got)
    qkv_blocks = [qkv_z, head_near, head_far, head_last]

    gate_far, gate_last = swap(after(gate_z, head_last), "b"), swap(gate_near, "b")
    ring_one = swap(down_four, "next")
    block_row = (blocks, tall)
    mixed_own, mixed_partner, qkv_w, out_mine, norms = kernel_call(
        functools.partial(qkv_kernel, steps, 3, len(qkv_blocks)),
        (2 * steps,),
        [(qkv_to, smem())]
        + far([(tokens, own_rows(steps, D)), (tokens_other, partner_rows(steps, D))] + wholes(qkv_blocks)),
        far(
            [((rows, 3 * head_cols), BF16, own_rows(steps, 3 * head_cols))]
            + [((rows, 3 * head_cols), BF16, partner_rows(steps, 3 * head_cols))]
            + [(block_row + (n,), BF16, whole(block_row + (n,))) for n in (3 * head_cols, head_cols)]
        )
        + [((8, D), F32, whole((8, D)))],
        scratch=[pltpu.VMEM(block_row + (128,), BF16)],
        flops=2 * 2 * rows * D * 3 * head_cols,
        name="mixed",
    )
    def attend(block, mixed, extra=()):
        tall_out = rows + sum(v.size for v in extra) // head_cols
        return kernel_call(
            attend_kernel,
            (1,),
            [(jnp.array([0, block], jnp.int32), smem()), (flags, smem()), (slopes, smem())]
            + far(wholes([mixed, *extra])),
            [((tall_out, head_cols), BF16, whole((tall_out, head_cols))), ((rows, 128), F32, whole((rows, 128)), True)],
            scratch=[pltpu.VMEM((LONG, LONG), F32)],
            flops=4 * rows * LONG * D,
            name="attend",
            room=12,
        )

    ctx_send, logs_partner = attend(1, mixed_partner, [out_mine])
    gate_far, gate_last, ring_one, ctx_send = fence(gate_far, gate_last, ring_one, ctx_send)

    value_near, value_far = swap(value_z, "a"), swap(value_z, "b")
    ring_two = swap(ring_one, "next")
    ctx_got = swap(ctx_send, "core")
    ctx_mine, logs_own = attend(0, after(mixed_own, ctx_send))

    unit_one, inverse_one, low = kernel_call(
        first_norm_kernel,
        (steps,),
        [
            (place, smem()),
            (tokens, step_rows(D)),
            (ctx_mine, step_rows(head_cols)),
            (ctx_got, step_rows(head_cols)),
        ]
        + wholes([out_mine, ctx_got, norms]),
        [
            ((rows, D), F32, step_rows(D)),
            ((rows, 1), F32, step_rows(1)),
            ((rows, D), BF16, step_rows(D)),
        ],
        flops=2 * rows * D * D,
        name="first_norm",
    )
    value_near, value_far, ring_two, low = fence(value_near, value_far, ring_two, low)
    gate_blocks = [gate_z, gate_near, gate_far, gate_last]
    value_last = swap(value_near, "b")
    ring_three = swap(ring_two, "next")
    low_other = swap(low, "core")

    w_shape = (blocks, 2 * tall, width)
    both_rows = [(low, own_rows(steps, D)), (low_other, partner_rows(steps, D))]
    active, slope, gate_w = kernel_call(
        functools.partial(gate_kernel, steps, len(gate_blocks)),
        (2 * steps,),
        [(ffn_to, smem())] + both_rows + far(wholes(gate_blocks)),
        [((2 * rows, hidden), BF16, step_rows(hidden))] * 2 + [(w_shape, BF16, whole(w_shape))],
        name="gate",
    )
    value_last, active = fence(value_last, active)
    value_blocks = [value_z, value_near, value_far, value_last]
    down_blocks = [down_four, ring_one, ring_two, ring_three]
    product, slope, value_w = kernel_call(
        functools.partial(value_kernel, steps, len(value_blocks)),
        (2 * steps,),
        [(ffn_to, smem())] + both_rows + [(active, step_rows(hidden)), (slope, step_rows(hidden))] + wholes(value_blocks),
        [((2 * rows, hidden), BF16, step_rows(hidden))] * 2 + [(w_shape, BF16, whole(w_shape))],
        name="value",
    )
    part_send, down_w = kernel_call(
        down_first_kernel,
        (steps,),
        [(down_to, smem()), (product, pl.BlockSpec((ROWS, hidden), lambda i: (i + steps, 0)))] + wholes(down_blocks),
        [((rows, D), BF16, step_rows(D)), (w_shape, BF16, whole(w_shape))],
        name="down_first",
    )
    (part_own,) = kernel_call(
        down_kernel,
        (steps,),
        [(product, step_rows(hidden))] + wholes([down_w]),
        [((rows, D), F32, step_rows(D))],
        name="down",
    )
    part_got = swap(part_send, "core")
    layer_out, d_z, d_ffn, sums_two = kernel_call(
        second_norm_kernel,
        (steps,),
        [(unit_one, step_rows(D))]
        + wholes([norms])
        + [(part_own, step_rows(D)), (part_got, step_rows(D)), (cotangent, step_rows(D))],
        [
            ((rows, D), BF16, step_rows(D)),
            ((rows, D), F32, step_rows(D)),
            ((rows, D), BF16, step_rows(D)),
            ((8, D), F32, whole((8, D))),
        ],
        name="second_norm",
    )
    d_ffn_other = swap(d_ffn, "core")

    def weight_grad(left, left_other, right, to, parts):
        part = (blocks // parts, 2 * tall, width)
        cols = width // 3
        return kernel_call(
            weight_grad_kernel,
            (3,),
            [
                (to, smem()),
                (left, whole((rows, D))),
                (left_other, whole((rows, D))),
                (right, pl.BlockSpec((2 * rows, cols), lambda i: (0, i))),
                (right, pl.BlockSpec((2 * rows, cols), lambda i: (0, 3 + i))),
            ],
            [(part, BF16, whole(part))] * parts,
            scratch=[pltpu.VMEM((blocks, 2 * tall, cols), BF16)],
            flops=2 * 2 * rows * D * hidden,
            name="weight_grad",
        )

    def added(keep, got):
        return (keep.astype(F32) + got.astype(F32)).astype(BF16)

    def halves(keep, got):
        count = keep.shape[0] // 2
        return added(keep[:count], got[:count]), added(keep[count:], got[count:])

    def quarters(keep, got):
        return [added(keep[k], got[k]) for k in range(z_size)]

    down_parts = weight_grad(d_ffn, d_ffn_other, product, back_to, 2)
    d_gate, d_up, back_own, back_send = kernel_call(
        functools.partial(ffn_back_kernel, steps),
        (2 * steps,),
        [(after(d_ffn, down_parts[-1]), own_rows(steps, D)), (d_ffn_other, partner_rows(steps, D))]
        + wholes([down_w, gate_w, value_w])
        + [(active, step_rows(hidden)), (slope, step_rows(hidden))],
        [((2 * rows, hidden), BF16, step_rows(hidden))] * 2
        + [((rows, D), F32, own_rows(steps, D)), ((rows, D), BF16, partner_rows(steps, D))],
        flops=3 * 2 * 2 * rows * D * hidden,
        name="ffn_back",
    )
    down_got = swap(down_parts[1], "b")
    gate_keep, gate_send = weight_grad(after(low, back_send), low_other, d_gate, ffn_to, 2)
    down_got, back_send, gate_send = fence(down_got, back_send, gate_send)

    gate_got = swap(gate_send, "b")
    down_z = [added(down_parts[0][2 * k : 2 * k + 2], down_got[2 * k : 2 * k + 2]) for k in range(z_size)]
    down_got = swap(down_z[3], "z", 2)
    back_got = swap(back_send, "core")
    d_hidden, dctx_mine, dctx_send, out_keep, out_send, sums_one = kernel_call(
        first_norm_back_kernel,
        (steps,),
        [
            (place, smem()),
            (unit_one, step_rows(D)),
            (inverse_one, step_rows(1)),
            (norms, whole(norms.shape)),
            (d_z, step_rows(D)),
            (back_own, step_rows(D)),
            (back_got, step_rows(D)),
            (ctx_mine, step_rows(head_cols)),
            (ctx_got, step_rows(head_cols)),
        ]
        + wholes([out_mine, ctx_got]),
        [
            ((rows, D), F32, step_rows(D)),
            ((rows, head_cols), BF16, step_rows(head_cols)),
            ((rows, head_cols), BF16, step_rows(head_cols)),
            (out_mine.shape, F32, whole(out_mine.shape)),
            (out_mine.shape, BF16, whole(out_mine.shape)),
            ((8, D), F32, whole((8, D))),
        ],
        scratch=[pltpu.VMEM((blocks, tall, D), F32)],
        flops=2 * 2 * rows * D * D,
        name="first_norm_back",
    )
    def attend_back(block, mixed, d_context, logs):
        return kernel_call(
            attend_back_kernel,
            (1,),
            [(jnp.array([0, block], jnp.int32), smem()), (flags, smem()), (slopes, smem())]
            + far(wholes([mixed, logs]))
            + wholes([d_context]),
            [((rows, head_cols), BF16, whole((rows, head_cols)))] * 3,
            scratch=[pltpu.VMEM((LONG, LONG), F32)],
            name="attend_back",
            room=16,
        )

    d_own = attend_back(0, mixed_own, dctx_mine, logs_own)
    value_keep, value_send = weight_grad(after(low, d_own[0]), low_other, d_up, ffn_to, 2)
    down_got, gate_got, dctx_send, out_send, value_send = fence(down_got, gate_got, dctx_send, out_send, value_send)
    dctx_got, out_got = swap(dctx_send, "core"), swap(out_send, "core")
    value_got = swap(value_send, "b")
    gate_keep, gate_send = halves(gate_keep, gate_got)
    down_send = added(down_z[1], down_got)
    gate_got = swap(gate_send, "a")
    down_got = swap(after(down_z[2], gate_send), "z", 2)
    out_sum = (out_keep + out_got.astype(F32)).astype(BF16)

    d_partner = attend_back(1, mixed_partner, after(dctx_got, gate_send, down_send), logs_partner)
    grad_shape = (blocks // 2, tall, 4 * head_cols + 128)
    head_keep, head_send = kernel_call(
        qkv_grad_kernel,
        (3,),
        [(qkv_to, smem())]
        + wholes([tokens, tokens_other, *d_own, *d_partner, out_sum, sums_one, sums_two]),
        [(grad_shape, BF16, whole(grad_shape))] * 2,
        scratch=[pltpu.VMEM(block_row + (head_cols,), BF16), pltpu.VMEM(block_row + (128,), BF16)],
        name="qkv_grad",
    )
    down_got, gate_got, head_send = fence(down_got, gate_got, head_send)
    head_got = swap(head_send, "b")
    gate_parts = quarters(gate_keep, gate_got)
    value_keep, value_send = halves(value_keep, value_got)

    value_got = swap(value_send, "a")
    gate_sum = plane.sum_z(gate_parts)
    down_keep = added(down_z[0], down_got)

    def input_part(d_parts, more, dtype):
        return kernel_call(
            input_grad_kernel,
            (steps,),
            [(v, step_rows(head_cols)) for v in d_parts] + wholes([qkv_w]) + [(v, step_rows(D)) for v in more],
            [((rows, D), dtype, step_rows(D))],
            name="input_grad",
        )[0]

    in_send = input_part([after(d_partner[0], value_send, *gate_parts), *d_partner[1:]], [], BF16)
    head_got, value_got, gate_sum, down_send, in_send = fence(head_got, value_got, gate_sum, down_send, in_send)
    head_keep, head_send = halves(head_keep, head_got)
    value_keep, value_send = halves(value_keep, value_got)

    in_got = swap(in_send, "core")
    down_got = swap(down_send, "z", 1)
    head_got = swap(head_send, "a")
    value_got = swap(value_send, "z", 2)
    input_grad = input_part([after(d_own[0], head_send, value_send), *d_own[1:]], [d_hidden, in_got], F32)
    head_got, input_grad = fence(head_got, input_grad)
    head_parts = quarters(head_keep, head_got)
    value_got, down_got = after(value_got, *head_parts), after(down_got, *head_parts)
    value_keep, value_send = halves(value_keep, value_got)
    down_keep, down_send = halves(down_keep, down_got)
    value_got = swap(value_send, "z", 1)

    down_got = swap(down_send, "a")
    head_sum = plane.sum_z(head_parts)
    there = swap(head_sum, "y")
    value_got, down_got = after(value_got, there), after(down_got, there)
    grads = [gate_sum, added(value_keep[0], value_got[0]), added(down_keep[0], down_got[0])]

    def in_order(mine, other):
        return [jnp.where(first, mine, other), jnp.where(first, other, mine)]

    kept = [half_of(core, total.reshape(2, tall, width), 0) for total in grads]
    ffn_got = swap(jnp.concatenate([other for _, other in kept], axis=0), "core")
    ffn_pieces = [
        jnp.concatenate(in_order(mine, ffn_got[n * tall : (n + 1) * tall]), axis=1).astype(F32)
        for n, (mine, _) in enumerate(kept)
    ]
    gate_piece, value_piece, down_piece = ffn_pieces[0], ffn_pieces[1], ffn_pieces[2].T
    own = y_here == core
    got = swap(jnp.where(own, there, head_sum), "core")
    qkv_piece, out_piece, gains_piece, biases_piece = kernel_call(
        pieces_kernel,
        (1,),
        [(jnp.stack([core, own.astype(jnp.int32)]), smem())] + wholes([head_sum, there, got]),
        [((tall, 3 * D), F32, whole((tall, 3 * D))), ((tall, D), F32, whole((tall, D)))]
        + [((2, tall), F32, whole((2, tall)))] * 2,
        name="pieces",
    )
    return (
        layer_out,
        input_grad,
        qkv_piece,
        out_piece,
        gate_piece,
        value_piece,
        down_piece,
        gains_piece,
        biases_piece,
    )


def solution(mesh):
    wide, narrow = mesh.shape["wide"], mesh.shape["narrow"]
    placed = (
        P(("wide", "narrow"), None),
        P("wide", None),
        P("wide", None),
        P("wide", "narrow"),
        P("wide", "narrow"),
        P("narrow", "wide"),
        P(None, "wide"),
        P(None, "wide"),
        P("wide", "narrow"),
        P(("wide", "narrow"), None),
    )
    if narrow == 2 and wide % 16 == 0 and D % (16 * wide) == 0:
        body = functools.partial(plane_shards, wide, narrow)
    else:
        body = general_shards
    return jax.shard_map(
        body,
        mesh=mesh,
        in_specs=placed,
        out_specs=(
            P(("wide", "narrow"), None),
            P(("wide", "narrow"), None),
            P("wide", None),
            P("wide", None),
            P("wide", "narrow"),
            P("wide", "narrow"),
            P("narrow", "wide"),
            P(None, "wide"),
            P(None, "wide"),
        ),
        check_vma=False,
    )
```

```python
import functools

import jax
import jax.numpy as jnp
import numpy as np
from jax import lax
from jax.experimental import pallas as pl
from jax.experimental.pallas import tpu as pltpu
from jax.sharding import PartitionSpec as P

D = 768
HEADS = 12
HEAD_DIM = 64
LONG = 512
SHORT = 128


def norm_rows(values, gain_row, bias_row):
    center = jnp.mean(values, axis=-1, keepdims=True)
    shifted = values - center
    spread = jnp.mean(shifted * shifted, axis=-1, keepdims=True)
    return shifted * lax.rsqrt(spread + 1e-05) * gain_row + bias_row


def gelu_product(gate_in, value_in):
    return jax.nn.gelu(gate_in, approximate=False) * value_in


def alibi_slopes(heads):
    power = 1 << heads.bit_length() - 1
    first = [2.0 ** (-8.0 * (index + 1) / power) for index in range(power)]
    second = [2.0 ** (-8.0 * (2 * index + 1) / (2 * power)) for index in range(heads - power)]
    return jnp.array(first + second, dtype=jnp.float32)


def alibi_bias(span, heads):
    position = jnp.arange(span)
    distance = jnp.abs(position[:, None] - position[None, :]).astype(jnp.float32)
    slopes = alibi_slopes(heads)
    return slopes[:, None, None] * distance


def block_scores(query_g, key_g, span):
    width = query_g.shape[-1]
    scores = jnp.einsum(
        "bqhd,bkhd->bhqk", query_g, key_g, preferred_element_type=jnp.float32
    ) * width ** (-0.5)
    return scores - alibi_bias(span, query_g.shape[2])


def attend(query_rows, key_rows, value_rows, span):
    rows, heads, width = query_rows.shape
    groups = rows // span
    shape_g = (groups, span, heads, width)
    query_g = query_rows.reshape(shape_g)
    key_g = key_rows.reshape(shape_g)
    value_g = value_rows.reshape(shape_g)
    scores = block_scores(query_g, key_g, span)
    top = jnp.max(scores, axis=-1, keepdims=True)
    expd = jnp.exp(scores - top)
    total = jnp.sum(expd, axis=-1, keepdims=True)
    probs_low = (expd / total).astype(jnp.bfloat16)
    context = jnp.einsum("bhqk,bkhd->bqhd", probs_low, value_g, preferred_element_type=jnp.float32)
    log_total = jnp.transpose((top + jnp.log(total))[..., 0], (0, 2, 1)).reshape(rows, heads)
    return (context.reshape(rows, heads * width), log_total)


def attend_back(query_rows, key_rows, value_rows, log_total, d_context, span):
    rows, heads, width = query_rows.shape
    groups = rows // span
    shape_g = (groups, span, heads, width)
    query_g = query_rows.reshape(shape_g)
    key_g = key_rows.reshape(shape_g)
    value_g = value_rows.reshape(shape_g)
    d_context_g = d_context.reshape(shape_g)
    lse_g = jnp.transpose(log_total.reshape(groups, span, heads), (0, 2, 1))
    scores = block_scores(query_g, key_g, span)
    probs = jnp.exp(scores - lse_g[..., None])
    probs_low = probs.astype(jnp.bfloat16)
    d_probs = jnp.einsum(
        "bqhd,bkhd->bhqk", d_context_g, value_g, preferred_element_type=jnp.float32
    )
    d_values = jnp.einsum(
        "bhqk,bqhd->bkhd", probs_low, d_context_g, preferred_element_type=jnp.float32
    )
    row_dot = jnp.sum(probs * d_probs, axis=-1, keepdims=True)
    d_scores = (probs * (d_probs - row_dot)).astype(jnp.bfloat16)
    scale = width ** (-0.5)
    d_queries = (
        jnp.einsum("bhqk,bkhd->bqhd", d_scores, key_g, preferred_element_type=jnp.float32) * scale
    )
    d_keys = (
        jnp.einsum("bhqk,bqhd->bkhd", d_scores, query_g, preferred_element_type=jnp.float32) * scale
    )
    return jnp.stack([d_queries, d_keys, d_values], axis=2).reshape(rows, 3, heads, width)


def contract_rows(left, right):
    return lax.dot_general(
        left, right, (((0,), (0,)), ((), ())), preferred_element_type=jnp.float32
    )


def contract_cols(left, right):
    return lax.dot_general(
        left, right, (((1,), (1,)), ((), ())), preferred_element_type=jnp.float32
    )


def general_shards(
    tokens, w_qkv, w_out, w_gate, w_value, w_down, norm_gains, norm_biases, long_count, cotangent
):
    gathered = (
        lax.all_gather(w_qkv, "wide", axis=0, tiled=True),
        lax.all_gather(w_out, "wide", axis=0, tiled=True),
        lax.all_gather(w_gate, "wide", axis=0, tiled=True),
        lax.all_gather(w_value, "wide", axis=0, tiled=True),
        lax.all_gather(w_down, "wide", axis=1, tiled=True),
        lax.all_gather(norm_gains, "wide", axis=1, tiled=True),
        lax.all_gather(norm_biases, "wide", axis=1, tiled=True),
    )
    full_qkv, full_out, wide_gate, wide_value, wide_down, gains_all, biases_all = gathered
    gains_f = gains_all.astype(jnp.float32)
    biases_f = biases_all.astype(jnp.float32)
    rows_dev = tokens.shape[0]
    n_blocks = rows_dev // LONG
    long_here = long_count[0, 0]
    tokens_f = tokens.astype(jnp.float32)
    mixed = jnp.dot(tokens, full_qkv, preferred_element_type=jnp.float32).astype(jnp.bfloat16)
    heads_view = mixed.reshape(n_blocks, LONG, 3, HEADS, HEAD_DIM)
    query_blk = heads_view[:, :, 0]
    key_blk = heads_view[:, :, 1]
    value_blk = heads_view[:, :, 2]
    block_ids = jnp.arange(n_blocks)

    def forward_block(entry):
        block_id, query_rows, key_rows, value_rows = entry
        return lax.cond(
            block_id < long_here,
            lambda operands: attend(operands[0], operands[1], operands[2], LONG),
            lambda operands: attend(operands[0], operands[1], operands[2], SHORT),
            (query_rows, key_rows, value_rows),
        )

    context_f, lse_rows = lax.map(forward_block, (block_ids, query_blk, key_blk, value_blk))
    context = context_f.reshape(rows_dev, D).astype(jnp.bfloat16)
    branch = jnp.dot(context, full_out, preferred_element_type=jnp.float32)
    hidden_in = tokens_f + branch
    normed = norm_rows(hidden_in, gains_f[0], biases_f[0])
    normed_low = normed.astype(jnp.bfloat16)
    all_rows = lax.all_gather(normed_low, "narrow", axis=0, tiled=True)
    gate = jnp.dot(all_rows, wide_gate, preferred_element_type=jnp.float32)
    value_up = jnp.dot(all_rows, wide_value, preferred_element_type=jnp.float32)
    product_f, pull_product = jax.vjp(gelu_product, gate, value_up)
    product = product_f.astype(jnp.bfloat16)
    ffn_out = lax.psum_scatter(
        jnp.dot(product, wide_down, preferred_element_type=jnp.float32),
        "narrow",
        scatter_dimension=0,
        tiled=True,
    )
    out_in = normed + ffn_out
    layer_out, pull_second = jax.vjp(norm_rows, out_in, gains_f[1], biases_f[1])
    d_out, d_gain_two, d_bias_two = pull_second(cotangent.astype(jnp.float32))
    d_ffn = d_out.astype(jnp.bfloat16)
    d_rows = lax.all_gather(d_ffn, "narrow", axis=0, tiled=True)
    grad_down = contract_rows(product, d_rows)
    d_product = contract_cols(d_rows, wide_down)
    d_gate, d_up = pull_product(d_product)
    d_gate_low = d_gate.astype(jnp.bfloat16)
    d_up_low = d_up.astype(jnp.bfloat16)
    grad_gate = contract_rows(all_rows, d_gate_low)
    grad_value = contract_rows(all_rows, d_up_low)
    d_normed = lax.psum_scatter(
        contract_cols(d_gate_low, wide_gate) + contract_cols(d_up_low, wide_value),
        "narrow",
        scatter_dimension=0,
        tiled=True,
    )
    d_normed_total = d_out + d_normed
    unused_out, pull_first = jax.vjp(norm_rows, hidden_in, gains_f[0], biases_f[0])
    d_hidden, d_gain_one, d_bias_one = pull_first(d_normed_total)
    d_branch = d_hidden.astype(jnp.bfloat16)
    grad_out = contract_rows(context, d_branch)
    d_context = contract_cols(d_branch, full_out).astype(jnp.bfloat16)
    d_context_blk = d_context.reshape(n_blocks, LONG, HEADS, HEAD_DIM)

    def backward_block(entry):
        block_id, query_rows, key_rows, value_rows, log_total, d_ctx = entry
        return lax.cond(
            block_id < long_here,
            lambda operands: attend_back(
                operands[0], operands[1], operands[2], operands[3], operands[4], LONG
            ),
            lambda operands: attend_back(
                operands[0], operands[1], operands[2], operands[3], operands[4], SHORT
            ),
            (query_rows, key_rows, value_rows, log_total, d_ctx),
        )

    d_mixed_f = lax.map(
        backward_block, (block_ids, query_blk, key_blk, value_blk, lse_rows, d_context_blk)
    )
    d_mixed = d_mixed_f.reshape(rows_dev, 3 * D).astype(jnp.bfloat16)
    grad_qkv = contract_rows(tokens, d_mixed)
    input_grad = d_hidden + contract_cols(d_mixed, full_qkv)
    grad_gains = jnp.stack([d_gain_one, d_gain_two])
    grad_biases = jnp.stack([d_bias_one, d_bias_two])
    pieces = (
        lax.psum_scatter(
            grad_qkv.astype(jnp.bfloat16), "wide", scatter_dimension=0, tiled=True
        ).astype(jnp.float32),
        lax.psum_scatter(
            grad_out.astype(jnp.bfloat16), "wide", scatter_dimension=0, tiled=True
        ).astype(jnp.float32),
        lax.psum_scatter(
            grad_gate.astype(jnp.bfloat16), "wide", scatter_dimension=0, tiled=True
        ).astype(jnp.float32),
        lax.psum_scatter(
            grad_value.astype(jnp.bfloat16), "wide", scatter_dimension=0, tiled=True
        ).astype(jnp.float32),
        lax.psum_scatter(
            grad_down.astype(jnp.bfloat16), "wide", scatter_dimension=1, tiled=True
        ).astype(jnp.float32),
        lax.psum_scatter(
            grad_gains.astype(jnp.bfloat16), "wide", scatter_dimension=1, tiled=True
        ).astype(jnp.float32),
        lax.psum_scatter(
            grad_biases.astype(jnp.bfloat16), "wide", scatter_dimension=1, tiled=True
        ).astype(jnp.float32),
    )
    qkv_piece, out_piece, gate_piece, value_piece, down_piece, gains_piece, biases_piece = pieces
    qkv_piece, out_piece, gains_piece, biases_piece = (
        lax.psum(qkv_piece.astype(jnp.bfloat16), "narrow").astype(jnp.float32),
        lax.psum(out_piece.astype(jnp.bfloat16), "narrow").astype(jnp.float32),
        lax.psum(gains_piece.astype(jnp.bfloat16), "narrow").astype(jnp.float32),
        lax.psum(biases_piece.astype(jnp.bfloat16), "narrow").astype(jnp.float32),
    )
    return (
        layer_out.astype(jnp.bfloat16),
        input_grad,
        qkv_piece,
        out_piece,
        gate_piece,
        value_piece,
        down_piece,
        gains_piece,
        biases_piece,
    )


AXES = ("wide", "narrow")
F32 = jnp.float32
BF16 = jnp.bfloat16
MIB = 1024 * 1024
RING = (0, 1, 3, 2)
PAIR = 2 * HEAD_DIM


def dot(left, right):
    return jnp.dot(left, right, preferred_element_type=F32)


class Plane:
    def __init__(self, wide, narrow):
        self.size = {"z": wide // 4, "ring": len(RING), "a": 2, "b": 2, "core": 2, "y": narrow}
        self.pairs = {}
        count = wide * narrow
        for dim, size in self.size.items():
            for step in range(1, size) if dim != "ring" else ():
                self.pairs[dim, step] = [(i, self.partner(i, dim, step)) for i in range(count)]
        after_z = {z: RING[(n + 1) % len(RING)] for n, z in enumerate(RING)}
        self.pairs["next", 1] = [(i, i % 8 + 8 * after_z[i // 8]) for i in range(count)]
        self.pairs["prev", 1] = [(j, i) for i, j in self.pairs["next", 1]]
        w = lax.axis_index("wide")
        self.z, self.x, self.core = w // 4, (w // 2) % 2, w % 2
        self.y = lax.axis_index("narrow")

    @staticmethod
    def partner(i, dim, step):
        z, x, c, y = i // 8, (i // 4) % 2, (i // 2) % 2, i % 2
        if dim == "z":
            z ^= step
        elif dim == "core":
            c ^= 1
        elif dim == "y" or (dim == "a") == (c == 1):
            y ^= 1
        else:
            x ^= 1
        return ((z * 2 + x) * 2 + c) * 2 + y

    def swap(self, value, dim, step=1):
        return lax.ppermute(value, AXES, self.pairs[dim, step])

    def tables(self, order, numbered):
        sizes = [self.size[dim] for dim in order]
        number = np.arange(int(np.prod(sizes)))
        rest, digit = number, {}
        for dim, size in zip(order, sizes):
            digit[dim] = rest % size
            rest = rest // size
        first = self.core == 0
        a_here = jnp.where(first, self.x, self.y)
        b_here = jnp.where(first, self.y, self.x)
        if "ring" in digit:
            at = sum(jnp.where(self.z == z, n, 0) for n, z in enumerate(RING))
            z = sum(jnp.where((at - digit["ring"]) % len(RING) == n, z, 0) for n, z in enumerate(RING))
        else:
            z = digit["z"] ^ self.z
        a = digit["a"] ^ a_here
        b = digit["b"] ^ b_here
        x, y = jnp.where(first, a, b), jnp.where(first, b, a)
        return numbered(z, x, y).astype(jnp.int32)


def after(value, *events):
    return lax.optimization_barrier((value,) + events)[0]


def fence(*values):
    return lax.optimization_barrier(values)


def smem():
    return pl.BlockSpec(memory_space=pltpu.SMEM)


def whole(shape):
    zeros = (0,) * len(shape)
    return pl.BlockSpec(tuple(shape), lambda *_: zeros)


def kernel_call(body, grid, ins, outs, scratch=(), flops=0, name=None, room=6):
    blocks = [(v[1].block_shape, v[0].dtype) for v in ins] + [(v[2].block_shape, v[1]) for v in outs]
    held = sum(2 * int(np.prod(shape)) * np.dtype(d).itemsize for shape, d in blocks if shape is not None)
    held += sum(int(np.prod(v.shape)) * np.dtype(v.dtype).itemsize for v in scratch)
    return pl.pallas_call(
        body,
        grid=grid,
        in_specs=[v[1] for v in ins],
        out_specs=[v[2] for v in outs],
        out_shape=[(pltpu.HBM if more else jax.ShapeDtypeStruct)(s, d) for s, d, _, *more in outs],
        scratch_shapes=list(scratch),
        compiler_params=pltpu.CompilerParams(
            dimension_semantics=("arbitrary",) * len(grid), vmem_limit_bytes=held // 2 + room * MIB
        ),
        cost_estimate=pl.CostEstimate(flops=0, bytes_accessed=0, transcendentals=0),
        name=name,
    )(*[pltpu.with_memory_space_constraint(a, pltpu.HBM) if more else a for a, _, *more in ins])


ROWS = 512


def own_rows(steps, cols):
    return pl.BlockSpec((ROWS, cols), lambda i: (jnp.minimum(i, steps - 1), 0))


def partner_rows(steps, cols):
    return pl.BlockSpec((ROWS, cols), lambda i: (jnp.maximum(i - steps, 0), 0))


def pick_rows(i, steps, own_ref, partner_ref):
    return jnp.where(i < steps, own_ref[...], partner_ref[...])


def split_kernel(place, w_qkv, w_out, gains, biases, mine, send):
    first = place[0] == 0
    half = D // 2
    for n in range(4):
        source, start = (w_qkv, n * D) if n < 3 else (w_out, 0)
        low, high = source[:, start : start + half], source[:, start + half : start + D]
        mine[:, n * half : (n + 1) * half] = jnp.where(first, low, high)
        send[:, n * half : (n + 1) * half] = jnp.where(first, high, low)
    rows = jnp.concatenate([gains[...], biases[...]], axis=0).astype(F32)
    eye = jnp.where(
        lax.broadcasted_iota(jnp.int32, (128, rows.shape[0]), 0)
        == lax.broadcasted_iota(jnp.int32, (128, rows.shape[0]), 1),
        1.0,
        0.0,
    )
    norm_cols = contract_cols(rows.T.astype(BF16), eye.astype(BF16)).astype(BF16)
    mine[:, 4 * half :] = norm_cols
    send[:, 4 * half :] = norm_cols


def fill_blocks(table, pieces, weight, cols=slice(None)):
    count = pieces[0].shape[0]
    for n, piece in enumerate(pieces):
        for k in range(count):
            weight[table[n * count + k]] = piece[k, :, cols]


def qkv_kernel(steps, groups, pieces, table, own, partner, *refs):
    i = pl.program_id(0)
    parts = refs[:pieces]
    mixed_own, mixed_partner, weight, out_w, norms, table_t = refs[pieces:]
    cols, part = weight.shape[2], out_w.shape[2]
    tall = weight.shape[0] * weight.shape[1]

    @pl.when(i == 0)
    def _():
        fill_blocks(table, parts, weight, slice(0, cols))
        fill_blocks(table, parts, out_w, slice(cols, cols + part))
        fill_blocks(table, parts, table_t, slice(cols + part, None))
        norms[...] = table_t[...].reshape(tall, table_t.shape[2]).astype(F32).T[: norms.shape[0]]

    rows_here = pick_rows(i, steps, own, partner)
    for g in range(groups):
        span = slice(g * cols // groups, (g + 1) * cols // groups)
        tile = weight[:, :, span].reshape(tall, cols // groups)
        value = dot(rows_here, tile).astype(BF16)

        @pl.when(i < steps)
        def _():
            mixed_own[:, span] = value

        @pl.when(i >= steps)
        def _():
            mixed_partner[:, span] = value


def lane_masks():
    lane = lax.broadcasted_iota(jnp.int32, (1, PAIR), 1)
    return [lane < HEAD_DIM, lane >= HEAD_DIM]


def keep(mask, value):
    return jnp.where(mask, value, jnp.zeros_like(value))


def fill_distance(distance):
    row = lax.broadcasted_iota(jnp.int32, distance.shape, 0)
    col = lax.broadcasted_iota(jnp.int32, distance.shape, 1)
    distance[...] = jnp.abs(row - col).astype(F32)


def scores_of(queries, keys, slope, distance):
    raw = lax.dot_general(queries, keys, (((1,), (1,)), ((), ())), preferred_element_type=F32)
    return raw - slope * distance


def tiles(value, tall):
    return [value[n : n + tall] for n in range(0, value.shape[0], tall)]


def pair_cols(part, pair):
    return pl.ds(pl.multiple_of(part * (D // 2) + pair * PAIR, PAIR), PAIR)


def attend_kernel(place, flags, slopes, mixed, *refs):
    context, logs, distance = refs[-3:]
    masks = lane_masks()
    scale = HEAD_DIM**-0.5
    lane = lax.broadcasted_iota(jnp.int32, (1, 128), 1)
    fill_distance(distance)
    for extra in refs[:-3]:
        context[LONG:, :] = extra[...].reshape(context.shape[0] - LONG, context.shape[1])

    def run(is_long):
        tall = 2 * SHORT if is_long else LONG

        def one_pair(pair, _):
            q_all, k_all, v_all = (mixed[:, pair_cols(part, pair)] for part in range(3))
            totals = [0.0] * (LONG // tall)
            mine = (lambda v: [v]) if is_long else (lambda v: tiles(v, SHORT))
            jobs = []
            for head in range(2):
                slope = slopes[pair * 2 + head]
                q = (keep(masks[head], q_all) * scale).astype(BF16)
                v = keep(masks[head], v_all)
                for n in range(LONG // tall):
                    rows = slice(n * tall, (n + 1) * tall)
                    away = distance[rows, :] if is_long else distance[:SHORT, :SHORT]
                    s = [scores_of(a, b, slope, away) for a, b in zip(mine(q[rows]), mine(k_all))]
                    jobs.append((head, n, jnp.concatenate(s, axis=0), v))
            done = []
            for head, n, s, v in jobs:
                top = jnp.max(s, axis=-1, keepdims=True)
                e = jnp.exp(s - top)
                norm = jnp.sum(e, axis=-1, keepdims=True)
                done.append(((e * (1.0 / norm)).astype(BF16), top + jnp.log(norm)))
            for (head, n, s, v), (p, log) in zip(jobs, done):
                totals[n] = totals[n] + jnp.concatenate([dot(a, b) for a, b in zip(mine(p), mine(v))], axis=0)
                rows = slice(n * tall, (n + 1) * tall)
                logs[rows, :] = jnp.where(lane == pair * 2 + head, log, logs[rows, :])
            for n in range(LONG // tall):
                context[n * tall : (n + 1) * tall, pair_cols(0, pair)] = totals[n].astype(BF16)
            return 0

        lax.fori_loop(0, D // 2 // PAIR, one_pair, 0)

    logs[...] = jnp.zeros_like(logs)
    flag = flags[place[1]]

    @pl.when(flag > 0)
    def _():
        run(True)

    @pl.when(flag <= 0)
    def _():
        run(False)


def attend_back_kernel(place, flags, slopes, mixed, logs_ref, d_context, d_query, d_key, d_value, distance):
    masks = lane_masks()
    scale = HEAD_DIM**-0.5
    fill_distance(distance)

    def run(is_long):
        tall = 2 * SHORT if is_long else LONG
        logs = logs_ref[...]
        lane = lax.broadcasted_iota(jnp.int32, (1, 128), 1)

        def one_pair(pair, _):
            q_all, k_all, v_all = (mixed[:, pair_cols(part, pair)] for part in range(3))
            d_all = d_context[:, pair_cols(0, pair)]
            d_q, d_k, d_v = [0.0] * (LONG // tall), 0.0, 0.0
            group = SHORT if not is_long else tall
            jobs = []
            for head in range(2):
                slope = slopes[pair * 2 + head]
                q = (keep(masks[head], q_all) * scale).astype(BF16)
                k = (keep(masks[head], k_all) * scale).astype(BF16)
                d_c = keep(masks[head], d_all)
                log_all = jnp.sum(jnp.where(lane == pair * 2 + head, logs, 0.0), axis=-1, keepdims=True)
                for n in range(LONG // tall):
                    rows = slice(n * tall, (n + 1) * tall)
                    jobs.append((n, slope, q[rows], k, d_c[rows], log_all[rows], distance[rows, :] if is_long else distance[:SHORT, :SHORT]))
            mine = (lambda v: [v]) if is_long else (lambda v: tiles(v, SHORT))
            raw = []
            for n, slope, q, k, d_c, log_rows, away in jobs:
                s = jnp.concatenate([scores_of(a, b, slope, away) for a, b in zip(mine(q), mine(k_all))], axis=0)
                d_p = jnp.concatenate([contract_cols(a, b) for a, b in zip(mine(d_c), mine(v_all))], axis=0)
                raw.append((s, d_p))
            done = []
            for (n, slope, q, k, d_c, log_rows, away), (s, d_p) in zip(jobs, raw):
                p = jnp.exp(s - log_rows)
                d_s = (p * (d_p - jnp.sum(p * d_p, axis=-1, keepdims=True))).astype(BF16)
                done.append((d_s, p.astype(BF16)))
            for (n, slope, q, k, d_c, log_rows, away), (d_s, p) in zip(jobs, done):
                d_q[n] = d_q[n] + jnp.concatenate([dot(a, b) for a, b in zip(mine(d_s), mine(k))], axis=0)
                d_k = d_k + jnp.concatenate([dot(a.T, b) for a, b in zip(mine(q), mine(d_s))], axis=1)
                d_v = d_v + jnp.concatenate([dot(a.T, b) for a, b in zip(mine(d_c), mine(p))], axis=1)
            cols = pair_cols(0, pair)
            for n in range(LONG // tall):
                d_query[n * tall : (n + 1) * tall, cols] = d_q[n].astype(BF16)
            d_key[:, cols] = d_k.T.astype(BF16)
            d_value[:, cols] = d_v.T.astype(BF16)
            return 0

        lax.fori_loop(0, D // 2 // PAIR, one_pair, 0)

    flag = flags[place[1]]

    @pl.when(flag > 0)
    def _():
        run(True)

    @pl.when(flag <= 0)
    def _():
        run(False)


def spread(rows):
    center = jnp.mean(rows, axis=-1, keepdims=True)
    shifted = rows - center
    inverse = lax.rsqrt(jnp.mean(shifted * shifted, axis=-1, keepdims=True) + 1e-05)
    return shifted * inverse, inverse


def norm_back(e, unit, inverse):
    mean_e = jnp.mean(e, axis=-1, keepdims=True)
    mean_en = jnp.mean(e * unit, axis=-1, keepdims=True)
    return (e - mean_e - unit * mean_en) * inverse


def first_norm_kernel(place, tokens, ctx_mine, ctx_other, w_mine, w_other_rows, norms, unit, inverse, low):
    core = place[0]
    half = w_mine.shape[0] // 2
    wide = w_mine.shape[2]

    def branch(weight):
        return dot(ctx_mine[...], weight(core)) + dot(ctx_other[...], weight(1 - core))

    mine = branch(lambda c: w_mine[pl.ds(c * half, half)].reshape(D // 2, wide))
    other = branch(lambda c: w_other_rows[pl.ds(pl.multiple_of(LONG + c * (D // 2), 128), D // 2), :])
    first = core == 0
    added = jnp.concatenate([jnp.where(first, mine, other), jnp.where(first, other, mine)], axis=1)
    n, inv = spread(tokens[...].astype(F32) + added)
    unit[...] = n
    inverse[...] = inv
    low[...] = (n * norms[0:1, :] + norms[2:3, :]).astype(BF16)


def gelu_parts(x):
    phi = 0.5 + 0.5 * lax.erf(x * 0.5**0.5)
    return x * phi, phi + x * jnp.exp(-0.5 * (x * x)) * 0.3989422804014327


def columns_of(weight, half, span):
    count = weight.shape[0] // 2
    return weight[half * count : (half + 1) * count, :, span].reshape(D, span.stop - span.start)


def gate_kernel(steps, pieces, table, own, partner, *refs):
    i = pl.program_id(0)
    active, slope, gate_w = refs[pieces:]

    @pl.when(i == 0)
    def _():
        fill_blocks(table, refs[:pieces], gate_w)

    rows = pick_rows(i, steps, own, partner)
    width = gate_w.shape[2]
    for half in range(2):
        for start in range(0, width, 256):
            out = slice(half * width + start, half * width + start + 256)
            gate = dot(rows, columns_of(gate_w, half, slice(start, start + 256)))
            act, grad = gelu_parts(gate)
            active[:, out] = act.astype(BF16)
            slope[:, out] = grad.astype(BF16)


def value_kernel(steps, pieces, table, own, partner, active, slope, *refs):
    i = pl.program_id(0)
    product, scaled, value_w = refs[pieces:]

    @pl.when(i == 0)
    def _():
        fill_blocks(table, refs[:pieces], value_w)

    rows = pick_rows(i, steps, own, partner)
    width = value_w.shape[2]
    for half in range(2):
        for start in range(0, width, 256):
            out = slice(half * width + start, half * width + start + 256)
            up = dot(rows, columns_of(value_w, half, slice(start, start + 256)))
            product[:, out] = (active[:, out].astype(F32) * up).astype(BF16)
            scaled[:, out] = (slope[:, out].astype(F32) * up).astype(BF16)


def times_down(product, down_w):
    width = down_w.shape[2]
    total = 0.0
    for half in range(2):
        part = product[:, half * width : (half + 1) * width]
        total = total + contract_cols(part, columns_of(down_w, half, slice(0, width)))
    return total


def down_first_kernel(table, product, *refs):
    partner, down_w = refs[-2:]

    @pl.when(pl.program_id(0) == 0)
    def _():
        fill_blocks(table, refs[:-2], down_w)

    partner[...] = times_down(product, down_w).astype(BF16)


def down_kernel(product, down_w, own):
    own[...] = times_down(product, down_w)


def second_norm_kernel(unit_one, norms, part_own, part_got, cotangent, out, d_z, d_ffn, sums):
    normed = unit_one[...] * norms[0:1, :] + norms[2:3, :]
    n, inv = spread(normed + (part_own[...] + part_got[...].astype(F32)))
    gain = norms[1:2, :]
    out[...] = (n * gain + norms[3:4, :]).astype(BF16)
    c = cotangent[...].astype(F32)
    back = norm_back(gain * c, n, inv)
    d_z[...] = back
    d_ffn[...] = back.astype(BF16)
    add_sums(sums, c * n, c)


def add_sums(sums, gain_terms, bias_terms):
    @pl.when(pl.program_id(0) == 0)
    def _():
        sums[...] = jnp.zeros_like(sums)

    sums[0:1, :] += jnp.sum(gain_terms, axis=0, keepdims=True)
    sums[1:2, :] += jnp.sum(bias_terms, axis=0, keepdims=True)


def ffn_back_kernel(
    steps, own, partner, down_w, gate_w, value_w, active, slope, d_gate, d_up, back_own, back_partner
):
    i = pl.program_id(0)
    rows = pick_rows(i, steps, own, partner)
    width = down_w.shape[2]
    total = jnp.zeros((ROWS, D), F32)
    for half in range(2):
        for start in range(0, width, 256):
            span = slice(start, start + 256)
            out = slice(half * width + start, half * width + start + 256)
            d_product = dot(rows, columns_of(down_w, half, span))
            dg = (d_product * slope[:, out].astype(F32)).astype(BF16)
            du = (d_product * active[:, out].astype(F32)).astype(BF16)
            d_gate[:, out] = dg
            d_up[:, out] = du
            total = total + contract_cols(dg, columns_of(gate_w, half, span))
            total = total + contract_cols(du, columns_of(value_w, half, span))

    @pl.when(i < steps)
    def _():
        back_own[...] = total

    @pl.when(i >= steps)
    def _():
        back_partner[...] = total.astype(BF16)


def weight_grad_kernel(table, left_own, left_partner, right_a, right_b, *refs):
    i = pl.program_id(0)
    parts, blocks = refs[:-1], refs[-1]
    rows = left_own.shape[0]
    count, tall, cols = blocks.shape
    for half, right in enumerate((right_a, right_b)):
        value = contract_rows(left_own[...], right[:rows, :]) + contract_rows(left_partner[...], right[rows:, :])
        value = value.astype(BF16).reshape(count // 2, tall, cols)
        blocks[half * (count // 2) : (half + 1) * (count // 2)] = value
    span = pl.ds(pl.multiple_of(i * cols, cols), cols)
    each = count // len(parts)
    for k in range(count):
        parts[k // each][k % each, :, span] = blocks[table[k]]


def first_norm_back_kernel(
    place,
    unit_ref,
    inverse,
    norms,
    d_z,
    part_own,
    part_got,
    ctx_mine,
    ctx_other,
    w_mine,
    w_other,
    d_hidden,
    dctx_mine,
    dctx_other,
    grad_keep,
    grad_send,
    sums,
    grad,
):
    core = place[0]
    first = core == 0
    unit = unit_ref[...]
    d_normed = d_z[...] + (part_own[...] + part_got[...].astype(F32))
    back = norm_back(norms[0:1, :] * d_normed, unit, inverse[...])
    low = back.astype(BF16)
    d_hidden[...] = back
    add_sums(sums, d_normed * unit, d_normed)
    half, wide = w_mine.shape[0] // 2, w_mine.shape[2]
    low_mine = jnp.where(first, low[:, :wide], low[:, wide:])
    low_other = jnp.where(first, low[:, wide:], low[:, :wide])
    for head_core, out in ((core, dctx_mine), (1 - core, dctx_other)):
        near = w_mine[pl.ds(head_core * half, half)].reshape(D // 2, wide)
        far = w_other[pl.ds(pl.multiple_of(LONG + head_core * (D // 2), 128), D // 2), :]
        out[...] = (contract_cols(low_mine, near) + contract_cols(low_other, far)).astype(BF16)

    @pl.when(pl.program_id(0) == 0)
    def _():
        grad[...] = jnp.zeros_like(grad)

    shape = (half,) + grad.shape[1:]
    grad[pl.ds(core * half, half)] += contract_rows(ctx_mine[...], low).reshape(shape)
    grad[pl.ds((1 - core) * half, half)] += contract_rows(ctx_other[...], low).reshape(shape)

    @pl.when(pl.program_id(0) == pl.num_programs(0) - 1)
    def _():
        left, right = grad[:, :, :wide], grad[:, :, wide:]
        grad_keep[...] = jnp.where(first, left, right)
        grad_send[...] = jnp.where(first, right, left).astype(BF16)


def qkv_grad_kernel(table, left_own, left_partner, *refs):
    d_own, d_partner = refs[:3], refs[3:6]
    out_grad, sums_one, sums_two, near, far, blocks, norm_grad = refs[6:]
    i = pl.program_id(0)
    count, tall, cols = blocks.shape

    @pl.when(i == 0)
    def _():
        one, two = sums_one[...], sums_two[...]
        empty = jnp.zeros((norm_grad.shape[2] - 4, D), F32)
        stacked = jnp.concatenate([one[0:1], two[0:1], one[1:2], two[1:2], empty], axis=0)
        norm_grad[...] = stacked.T.astype(BF16).reshape(norm_grad.shape)

    for g in range(3):

        @pl.when(i == g)
        def _():
            value = contract_rows(left_own[...], d_own[g][...]) + contract_rows(left_partner[...], d_partner[g][...])
            blocks[...] = value.astype(BF16).reshape(blocks.shape)
            for k in range(count):
                target, place = (near if k < count // 2 else far), table[k]
                target[k % (count // 2), :, g * cols : (g + 1) * cols] = blocks[place]
                if g == 0:
                    start = 3 * cols
                    for more in (out_grad, norm_grad):
                        stop = start + more.shape[2]
                        target[k % (count // 2), :, start:stop] = more[place]
                        start = stop


def input_grad_kernel(d_query, d_key, d_value, weight, *refs):
    cols = d_query.shape[1]
    total = 0.0
    for g, left in enumerate((d_query, d_key, d_value)):
        tile = weight[:, :, g * cols : (g + 1) * cols].reshape(D, cols)
        total = total + contract_cols(left[...], tile)
    for more in refs[:-1]:
        total = total + more[...].astype(F32)
    refs[-1][...] = total.astype(refs[-1].dtype)


def pieces_kernel(place, here, there, got, qkv, out, gains, biases):
    first, own = place[0] == 0, place[1] == 1
    half = D // 2
    mine = jnp.where(own, here[...], there[...])
    for n in range(4):
        a, b = mine[:, n * half : (n + 1) * half].astype(F32), got[:, n * half : (n + 1) * half].astype(F32)
        target, start = (qkv, n * D) if n < 3 else (out, 0)
        target[:, start : start + half] = jnp.where(first, a, b)
        target[:, start + half : start + D] = jnp.where(first, b, a)
    rows = (mine[:, 4 * half :].astype(F32) + got[:, 4 * half :].astype(F32)).T
    gains[...] = rows[0:2]
    biases[...] = rows[2:4]


def by_core(core, mine, other, axis):
    first = core == 0
    return jnp.stack([jnp.where(first, mine, other), jnp.where(first, other, mine)], axis=axis)


def half_of(core, halves, axis):
    zero, one = (lax.index_in_dim(halves, k, axis, keepdims=False) for k in range(2))
    first = core == 0
    return jnp.where(first, zero, one), jnp.where(first, one, zero)


def plane_shards(
    wide,
    narrow,
    tokens,
    w_qkv,
    w_out,
    w_gate,
    w_value,
    w_down,
    norm_gains,
    norm_biases,
    long_count,
    cotangent,
):
    plane = Plane(wide, narrow)
    swap = plane.swap
    core, y_here = plane.core, plane.y
    rows = tokens.shape[0]
    steps = rows // ROWS
    tall = w_qkv.shape[0]
    blocks = wide * narrow // 2
    z_size = plane.size["z"]
    head_cols = D // 2
    width = w_gate.shape[1] // 2
    hidden = 2 * width
    pairs = head_cols // PAIR
    qkv_to = plane.tables(("z", "a", "b"), lambda z, x, y: (z * 2 + x) * 2 + y)
    ffn_to = plane.tables(("z", "a", "b"), lambda z, x, y: y * (2 * z_size) + z * 2 + x)
    back_to = plane.tables(("a", "z", "b"), lambda z, x, y: y * (2 * z_size) + z * 2 + x)
    down_to = plane.tables(("a", "b", "ring"), lambda z, x, y: y * (2 * z_size) + z * 2 + x)
    place = jnp.reshape(core, (1,)).astype(jnp.int32)
    first = core == 0

    def wholes(arrays):
        return [(v, whole(v.shape)) for v in arrays]

    def far(entries):
        return [entry + (True,) for entry in entries]

    def step_rows(cols):
        return pl.BlockSpec((ROWS, cols), lambda i: (i, 0))

    head_shape = (tall, 4 * head_cols + 128)
    head_part, head_send = kernel_call(
        split_kernel,
        (1,),
        [(place, smem())] + far(wholes([w_qkv, w_out, norm_gains, norm_biases])),
        [(head_shape, BF16, whole(head_shape))] * 2,
        name="split",
    )
    flag = jnp.broadcast_to(long_count.astype(F32), (8, 128))
    head_got, flag_got = fence(swap(head_send, "core"), swap(flag, "core"))
    head_part = jnp.where(y_here == core, head_part, head_got)
    head_parts = [head_part] + [swap(head_part, "z", k) for k in range(1, z_size)]
    ffn_parts = [after(w_gate, head_part), w_value, w_down.T]
    ffn_other = jnp.concatenate([jnp.where(first, v[:, width:], v[:, :width]) for v in ffn_parts], axis=1)
    ffn_got = swap(ffn_other, "core")
    flags = jnp.stack([long_count[0, 0], flag_got[0, 0].astype(jnp.int32)])
    slopes = lax.dynamic_slice_in_dim(alibi_slopes(HEADS), core * (HEADS // 2), HEADS // 2)

    def ffn_chip(n):
        v, got = ffn_parts[n], ffn_got[:, n * width : (n + 1) * width]
        mine = jnp.where(first, v[:, :width], v[:, width:])
        return jnp.concatenate([jnp.where(first, mine, got), jnp.where(first, got, mine)], axis=0)

    def doubled(value, step, *events):
        got = swap(value, "z", step)
        return jnp.concatenate(lax.optimization_barrier((value, got) + events)[:2], axis=0)

    def along_plane(held):
        near = swap(held, "a")
        return held, near, swap(held, "b")

    def joined(value, got):
        return jnp.concatenate([value, got], axis=0)

    gate_one, value_one, down_one = (ffn_chip(n)[None] for n in range(3))
    gate_got = swap(gate_one, "z", 1)
    down_got = swap(down_one, "a")
    *head_parts, gate_got, down_got = fence(*head_parts, gate_got, down_got)
    qkv_z = jnp.stack(head_parts)
    gate_two, down_two = joined(gate_one, gate_got), joined(down_one, down_got)

    head_near, head_far = swap(qkv_z, "a"), swap(qkv_z, "b")
    gate_got = swap(gate_two, "z", 2)
    value_got = swap(after(value_one, qkv_z), "z", 1)
    tokens_other = swap(after(tokens, qkv_z), "core")
    head_near, head_far, gate_got, value_got, tokens_other = fence(head_near, head_far, gate_got, value_got, tokens_other)
    gate_z, value_two = joined(gate_two, gate_got), joined(value_one, value_got)

    head_last = swap(head_near, "b")
    down_got = swap(after(down_two, head_near), "b")
    gate_near = swap(gate_z, "a")
    value_got = swap(value_two, "z", 2)
    head_last, down_got, gate_near, value_got = fence(head_last, down_got, gate_near, value_got)
    value_z, down_four = joined(value_two, value_got), joined(down_two, down_got)
    qkv_blocks = [qkv_z, head_near, head_far, head_last]

    gate_far, gate_last = swap(after(gate_z, head_last), "b"), swap(gate_near, "b")
    ring_one = swap(down_four, "next")
    block_row = (blocks, tall)
    mixed_own, mixed_partner, qkv_w, out_mine, norms = kernel_call(
        functools.partial(qkv_kernel, steps, 3, len(qkv_blocks)),
        (2 * steps,),
        [(qkv_to, smem())]
        + far([(tokens, own_rows(steps, D)), (tokens_other, partner_rows(steps, D))] + wholes(qkv_blocks)),
        far(
            [((rows, 3 * head_cols), BF16, own_rows(steps, 3 * head_cols))]
            + [((rows, 3 * head_cols), BF16, partner_rows(steps, 3 * head_cols))]
            + [(block_row + (n,), BF16, whole(block_row + (n,))) for n in (3 * head_cols, head_cols)]
        )
        + [((8, D), F32, whole((8, D)))],
        scratch=[pltpu.VMEM(block_row + (128,), BF16)],
        flops=2 * 2 * rows * D * 3 * head_cols,
        name="mixed",
    )
    def attend(block, mixed, extra=()):
        tall_out = rows + sum(v.size for v in extra) // head_cols
        return kernel_call(
            attend_kernel,
            (1,),
            [(jnp.array([0, block], jnp.int32), smem()), (flags, smem()), (slopes, smem())]
            + far(wholes([mixed, *extra])),
            [((tall_out, head_cols), BF16, whole((tall_out, head_cols))), ((rows, 128), F32, whole((rows, 128)), True)],
            scratch=[pltpu.VMEM((LONG, LONG), F32)],
            flops=4 * rows * LONG * D,
            name="attend",
            room=12,
        )

    ctx_send, logs_partner = attend(1, mixed_partner, [out_mine])
    gate_far, gate_last, ring_one, ctx_send = fence(gate_far, gate_last, ring_one, ctx_send)

    value_near, value_far = swap(value_z, "a"), swap(value_z, "b")
    ring_two = swap(ring_one, "next")
    ctx_got = swap(ctx_send, "core")
    ctx_mine, logs_own = attend(0, after(mixed_own, ctx_send))

    unit_one, inverse_one, low = kernel_call(
        first_norm_kernel,
        (steps,),
        [
            (place, smem()),
            (tokens, step_rows(D)),
            (ctx_mine, step_rows(head_cols)),
            (ctx_got, step_rows(head_cols)),
        ]
        + wholes([out_mine, ctx_got, norms]),
        [
            ((rows, D), F32, step_rows(D)),
            ((rows, 1), F32, step_rows(1)),
            ((rows, D), BF16, step_rows(D)),
        ],
        flops=2 * rows * D * D,
        name="first_norm",
    )
    value_near, value_far, ring_two, low = fence(value_near, value_far, ring_two, low)
    gate_blocks = [gate_z, gate_near, gate_far, gate_last]
    value_last = swap(value_near, "b")
    ring_three = swap(ring_two, "next")
    low_other = swap(low, "core")

    w_shape = (blocks, 2 * tall, width)
    both_rows = [(low, own_rows(steps, D)), (low_other, partner_rows(steps, D))]
    active, slope, gate_w = kernel_call(
        functools.partial(gate_kernel, steps, len(gate_blocks)),
        (2 * steps,),
        [(ffn_to, smem())] + both_rows + far(wholes(gate_blocks)),
        [((2 * rows, hidden), BF16, step_rows(hidden))] * 2 + [(w_shape, BF16, whole(w_shape))],
        name="gate",
    )
    value_last, active = fence(value_last, active)
    value_blocks = [value_z, value_near, value_far, value_last]
    down_blocks = [down_four, ring_one, ring_two, ring_three]
    product, slope, value_w = kernel_call(
        functools.partial(value_kernel, steps, len(value_blocks)),
        (2 * steps,),
        [(ffn_to, smem())] + both_rows + [(active, step_rows(hidden)), (slope, step_rows(hidden))] + wholes(value_blocks),
        [((2 * rows, hidden), BF16, step_rows(hidden))] * 2 + [(w_shape, BF16, whole(w_shape))],
        name="value",
    )
    part_send, down_w = kernel_call(
        down_first_kernel,
        (steps,),
        [(down_to, smem()), (product, pl.BlockSpec((ROWS, hidden), lambda i: (i + steps, 0)))] + wholes(down_blocks),
        [((rows, D), BF16, step_rows(D)), (w_shape, BF16, whole(w_shape))],
        name="down_first",
    )
    (part_own,) = kernel_call(
        down_kernel,
        (steps,),
        [(product, step_rows(hidden))] + wholes([down_w]),
        [((rows, D), F32, step_rows(D))],
        name="down",
    )
    part_got = swap(part_send, "core")
    layer_out, d_z, d_ffn, sums_two = kernel_call(
        second_norm_kernel,
        (steps,),
        [(unit_one, step_rows(D))]
        + wholes([norms])
        + [(part_own, step_rows(D)), (part_got, step_rows(D)), (cotangent, step_rows(D))],
        [
            ((rows, D), BF16, step_rows(D)),
            ((rows, D), F32, step_rows(D)),
            ((rows, D), BF16, step_rows(D)),
            ((8, D), F32, whole((8, D))),
        ],
        name="second_norm",
    )
    d_ffn_other = swap(d_ffn, "core")

    def weight_grad(left, left_other, right, to, parts):
        part = (blocks // parts, 2 * tall, width)
        cols = width // 3
        return kernel_call(
            weight_grad_kernel,
            (3,),
            [
                (to, smem()),
                (left, whole((rows, D))),
                (left_other, whole((rows, D))),
                (right, pl.BlockSpec((2 * rows, cols), lambda i: (0, i))),
                (right, pl.BlockSpec((2 * rows, cols), lambda i: (0, 3 + i))),
            ],
            [(part, BF16, whole(part))] * parts,
            scratch=[pltpu.VMEM((blocks, 2 * tall, cols), BF16)],
            flops=2 * 2 * rows * D * hidden,
            name="weight_grad",
        )

    def added(keep, got):
        return (keep.astype(F32) + got.astype(F32)).astype(BF16)

    def halves(keep, got):
        count = keep.shape[0] // 2
        return added(keep[:count], got[:count]), added(keep[count:], got[count:])

    def quarters(keep, got):
        return [added(keep[k], got[k]) for k in range(z_size)]

    down_parts = weight_grad(d_ffn, d_ffn_other, product, back_to, 2)
    d_gate, d_up, back_own, back_send = kernel_call(
        functools.partial(ffn_back_kernel, steps),
        (2 * steps,),
        [(after(d_ffn, down_parts[-1]), own_rows(steps, D)), (d_ffn_other, partner_rows(steps, D))]
        + wholes([down_w, gate_w, value_w])
        + [(active, step_rows(hidden)), (slope, step_rows(hidden))],
        [((2 * rows, hidden), BF16, step_rows(hidden))] * 2
        + [((rows, D), F32, own_rows(steps, D)), ((rows, D), BF16, partner_rows(steps, D))],
        flops=3 * 2 * 2 * rows * D * hidden,
        name="ffn_back",
    )
    down_got = swap(down_parts[1], "b")
    gate_keep, gate_send = weight_grad(after(low, back_send), low_other, d_gate, ffn_to, 2)
    down_got, back_send, gate_send = fence(down_got, back_send, gate_send)

    gate_got = swap(gate_send, "b")
    down_z = [added(down_parts[0][2 * k : 2 * k + 2], down_got[2 * k : 2 * k + 2]) for k in range(z_size)]
    down_got = swap(down_z[3], "z", 2)
    back_got = swap(back_send, "core")
    value_keep, value_send = weight_grad(after(low, gate_send), low_other, d_up, ffn_to, 2)
    value_got = swap(value_send, "b")
    back_got = after(back_got, value_send)
    d_hidden, dctx_mine, dctx_send, out_keep, out_send, sums_one = kernel_call(
        first_norm_back_kernel,
        (steps,),
        [
            (place, smem()),
            (unit_one, step_rows(D)),
            (inverse_one, step_rows(1)),
            (norms, whole(norms.shape)),
            (d_z, step_rows(D)),
            (back_own, step_rows(D)),
            (back_got, step_rows(D)),
            (ctx_mine, step_rows(head_cols)),
            (ctx_got, step_rows(head_cols)),
        ]
        + wholes([out_mine, ctx_got]),
        [
            ((rows, D), F32, step_rows(D)),
            ((rows, head_cols), BF16, step_rows(head_cols)),
            ((rows, head_cols), BF16, step_rows(head_cols)),
            (out_mine.shape, F32, whole(out_mine.shape)),
            (out_mine.shape, BF16, whole(out_mine.shape)),
            ((8, D), F32, whole((8, D))),
        ],
        scratch=[pltpu.VMEM((blocks, tall, D), F32)],
        flops=2 * 2 * rows * D * D,
        name="first_norm_back",
    )
    def attend_back(block, mixed, d_context, logs):
        return kernel_call(
            attend_back_kernel,
            (1,),
            [(jnp.array([0, block], jnp.int32), smem()), (flags, smem()), (slopes, smem())]
            + far(wholes([mixed, logs]))
            + wholes([d_context]),
            [((rows, head_cols), BF16, whole((rows, head_cols)))] * 3,
            scratch=[pltpu.VMEM((LONG, LONG), F32)],
            name="attend_back",
            room=16,
        )

    d_own = attend_back(0, mixed_own, dctx_mine, logs_own)
    down_got, gate_got, dctx_send, out_send, d_first = fence(down_got, gate_got, dctx_send, out_send, d_own[0])
    d_own = [d_first, *d_own[1:]]
    dctx_got, out_got = swap(dctx_send, "core"), swap(out_send, "core")
    gate_keep, gate_send = halves(gate_keep, gate_got)
    down_send = added(down_z[1], down_got)
    gate_got = swap(gate_send, "a")
    down_got = swap(after(down_z[2], gate_send), "z", 2)
    out_sum = (out_keep + out_got.astype(F32)).astype(BF16)

    d_partner = attend_back(1, mixed_partner, after(dctx_got, gate_send, down_send), logs_partner)
    grad_shape = (blocks // 2, tall, 4 * head_cols + 128)
    head_keep, head_send = kernel_call(
        qkv_grad_kernel,
        (3,),
        [(qkv_to, smem())]
        + wholes([tokens, tokens_other, *d_own, *d_partner, out_sum, sums_one, sums_two]),
        [(grad_shape, BF16, whole(grad_shape))] * 2,
        scratch=[pltpu.VMEM(block_row + (head_cols,), BF16), pltpu.VMEM(block_row + (128,), BF16)],
        name="qkv_grad",
    )
    down_got, gate_got, head_send = fence(down_got, gate_got, head_send)
    head_got = swap(head_send, "b")
    gate_keep, gate_send = halves(gate_keep, gate_got)
    value_keep, value_send = halves(value_keep, value_got)

    value_got = swap(value_send, "a")
    gate_got = swap(gate_send, "z", 2)
    down_keep = added(down_z[0], down_got)
    down_got = swap(down_send, "z", 1)

    def input_part(d_parts, more, dtype):
        return kernel_call(
            input_grad_kernel,
            (steps,),
            [(v, step_rows(head_cols)) for v in d_parts] + wholes([qkv_w]) + [(v, step_rows(D)) for v in more],
            [((rows, D), dtype, step_rows(D))],
            name="input_grad",
        )[0]

    in_send = input_part([after(d_partner[0], value_send, gate_send), *d_partner[1:]], [], BF16)
    head_got, value_got, gate_got, down_got, in_send = fence(head_got, value_got, gate_got, down_got, in_send)
    head_keep, head_send = halves(head_keep, head_got)
    value_keep, value_send = halves(value_keep, value_got)
    gate_keep, gate_send = halves(gate_keep, gate_got)
    down_keep, down_send = halves(down_keep, down_got)

    in_got = swap(in_send, "core")
    gate_got = swap(gate_send, "z", 1)
    down_got = swap(down_send, "a")
    head_got = swap(head_send, "a")
    value_got = swap(value_send, "z", 2)
    input_grad = input_part([after(d_own[0], head_send, value_send), *d_own[1:]], [d_hidden, in_got], F32)
    head_got, input_grad = fence(head_got, input_grad)
    head_parts = quarters(head_keep, head_got)
    value_got = after(value_got, *head_parts)
    value_keep, value_send = halves(value_keep, value_got)
    value_got = swap(value_send, "z", 1)

    head_got = [swap(head_parts[k], "z", k) for k in range(1, z_size)]
    value_got, gate_got, down_got, *head_got = fence(value_got, gate_got, down_got, *head_got)
    head_sum = head_parts[0].astype(F32)
    for part in head_got:
        head_sum = head_sum + part.astype(F32)
    head_sum = head_sum.astype(BF16)
    there = swap(head_sum, "y")
    gate_sum = added(gate_keep[0], gate_got[0])
    grads = [gate_sum, added(value_keep[0], value_got[0]), added(down_keep[0], down_got[0])]

    def in_order(mine, other):
        return [jnp.where(first, mine, other), jnp.where(first, other, mine)]

    kept = [half_of(core, total.reshape(2, tall, width), 0) for total in grads]
    ffn_got = swap(jnp.concatenate([other for _, other in kept], axis=0), "core")
    ffn_pieces = [
        jnp.concatenate(in_order(mine, ffn_got[n * tall : (n + 1) * tall]), axis=1).astype(F32)
        for n, (mine, _) in enumerate(kept)
    ]
    gate_piece, value_piece, down_piece = ffn_pieces[0], ffn_pieces[1], ffn_pieces[2].T
    there = after(there, gate_piece, value_piece, down_piece)
    own = y_here == core
    got = swap(jnp.where(own, there, head_sum), "core")
    qkv_piece, out_piece, gains_piece, biases_piece = kernel_call(
        pieces_kernel,
        (1,),
        [(jnp.stack([core, own.astype(jnp.int32)]), smem())] + wholes([head_sum, there, got]),
        [((tall, 3 * D), F32, whole((tall, 3 * D))), ((tall, D), F32, whole((tall, D)))]
        + [((2, tall), F32, whole((2, tall)))] * 2,
        name="pieces",
    )
    return (
        layer_out,
        input_grad,
        qkv_piece,
        out_piece,
        gate_piece,
        value_piece,
        down_piece,
        gains_piece,
        biases_piece,
    )


def solution(mesh):
    wide, narrow = mesh.shape["wide"], mesh.shape["narrow"]
    placed = (
        P(("wide", "narrow"), None),
        P("wide", None),
        P("wide", None),
        P("wide", "narrow"),
        P("wide", "narrow"),
        P("narrow", "wide"),
        P(None, "wide"),
        P(None, "wide"),
        P("wide", "narrow"),
        P(("wide", "narrow"), None),
    )
    if narrow == 2 and wide % 16 == 0 and D % (16 * wide) == 0:
        body = functools.partial(plane_shards, wide, narrow)
    else:
        body = general_shards
    return jax.shard_map(
        body,
        mesh=mesh,
        in_specs=placed,
        out_specs=(
            P(("wide", "narrow"), None),
            P(("wide", "narrow"), None),
            P("wide", None),
            P("wide", None),
            P("wide", "narrow"),
            P("wide", "narrow"),
            P("narrow", "wide"),
            P(None, "wide"),
            P(None, "wide"),
        ),
        check_vma=False,
    )
```

```python
import functools

import jax
import jax.numpy as jnp
import numpy as np
from jax import lax
from jax.experimental import pallas as pl
from jax.experimental.pallas import tpu as pltpu
from jax.sharding import PartitionSpec as P

D = 768
HEADS = 12
HEAD_DIM = 64
LONG = 512
SHORT = 128


def norm_rows(values, gain_row, bias_row):
    center = jnp.mean(values, axis=-1, keepdims=True)
    shifted = values - center
    spread = jnp.mean(shifted * shifted, axis=-1, keepdims=True)
    return shifted * lax.rsqrt(spread + 1e-05) * gain_row + bias_row


def gelu_product(gate_in, value_in):
    return jax.nn.gelu(gate_in, approximate=False) * value_in


def alibi_slopes(heads):
    power = 1 << heads.bit_length() - 1
    first = [2.0 ** (-8.0 * (index + 1) / power) for index in range(power)]
    second = [2.0 ** (-8.0 * (2 * index + 1) / (2 * power)) for index in range(heads - power)]
    return jnp.array(first + second, dtype=jnp.float32)


def alibi_bias(span, heads):
    position = jnp.arange(span)
    distance = jnp.abs(position[:, None] - position[None, :]).astype(jnp.float32)
    slopes = alibi_slopes(heads)
    return slopes[:, None, None] * distance


def block_scores(query_g, key_g, span):
    width = query_g.shape[-1]
    scores = jnp.einsum(
        "bqhd,bkhd->bhqk", query_g, key_g, preferred_element_type=jnp.float32
    ) * width ** (-0.5)
    return scores - alibi_bias(span, query_g.shape[2])


def attend(query_rows, key_rows, value_rows, span):
    rows, heads, width = query_rows.shape
    groups = rows // span
    shape_g = (groups, span, heads, width)
    query_g = query_rows.reshape(shape_g)
    key_g = key_rows.reshape(shape_g)
    value_g = value_rows.reshape(shape_g)
    scores = block_scores(query_g, key_g, span)
    top = jnp.max(scores, axis=-1, keepdims=True)
    expd = jnp.exp(scores - top)
    total = jnp.sum(expd, axis=-1, keepdims=True)
    probs_low = (expd / total).astype(jnp.bfloat16)
    context = jnp.einsum("bhqk,bkhd->bqhd", probs_low, value_g, preferred_element_type=jnp.float32)
    log_total = jnp.transpose((top + jnp.log(total))[..., 0], (0, 2, 1)).reshape(rows, heads)
    return (context.reshape(rows, heads * width), log_total)


def attend_back(query_rows, key_rows, value_rows, log_total, d_context, span):
    rows, heads, width = query_rows.shape
    groups = rows // span
    shape_g = (groups, span, heads, width)
    query_g = query_rows.reshape(shape_g)
    key_g = key_rows.reshape(shape_g)
    value_g = value_rows.reshape(shape_g)
    d_context_g = d_context.reshape(shape_g)
    lse_g = jnp.transpose(log_total.reshape(groups, span, heads), (0, 2, 1))
    scores = block_scores(query_g, key_g, span)
    probs = jnp.exp(scores - lse_g[..., None])
    probs_low = probs.astype(jnp.bfloat16)
    d_probs = jnp.einsum(
        "bqhd,bkhd->bhqk", d_context_g, value_g, preferred_element_type=jnp.float32
    )
    d_values = jnp.einsum(
        "bhqk,bqhd->bkhd", probs_low, d_context_g, preferred_element_type=jnp.float32
    )
    row_dot = jnp.sum(probs * d_probs, axis=-1, keepdims=True)
    d_scores = (probs * (d_probs - row_dot)).astype(jnp.bfloat16)
    scale = width ** (-0.5)
    d_queries = (
        jnp.einsum("bhqk,bkhd->bqhd", d_scores, key_g, preferred_element_type=jnp.float32) * scale
    )
    d_keys = (
        jnp.einsum("bhqk,bqhd->bkhd", d_scores, query_g, preferred_element_type=jnp.float32) * scale
    )
    return jnp.stack([d_queries, d_keys, d_values], axis=2).reshape(rows, 3, heads, width)


def contract_rows(left, right):
    return lax.dot_general(
        left, right, (((0,), (0,)), ((), ())), preferred_element_type=jnp.float32
    )


def contract_cols(left, right):
    return lax.dot_general(
        left, right, (((1,), (1,)), ((), ())), preferred_element_type=jnp.float32
    )


def general_shards(
    tokens, w_qkv, w_out, w_gate, w_value, w_down, norm_gains, norm_biases, long_count, cotangent
):
    gathered = (
        lax.all_gather(w_qkv, "wide", axis=0, tiled=True),
        lax.all_gather(w_out, "wide", axis=0, tiled=True),
        lax.all_gather(w_gate, "wide", axis=0, tiled=True),
        lax.all_gather(w_value, "wide", axis=0, tiled=True),
        lax.all_gather(w_down, "wide", axis=1, tiled=True),
        lax.all_gather(norm_gains, "wide", axis=1, tiled=True),
        lax.all_gather(norm_biases, "wide", axis=1, tiled=True),
    )
    full_qkv, full_out, wide_gate, wide_value, wide_down, gains_all, biases_all = gathered
    gains_f = gains_all.astype(jnp.float32)
    biases_f = biases_all.astype(jnp.float32)
    rows_dev = tokens.shape[0]
    n_blocks = rows_dev // LONG
    long_here = long_count[0, 0]
    tokens_f = tokens.astype(jnp.float32)
    mixed = jnp.dot(tokens, full_qkv, preferred_element_type=jnp.float32).astype(jnp.bfloat16)
    heads_view = mixed.reshape(n_blocks, LONG, 3, HEADS, HEAD_DIM)
    query_blk = heads_view[:, :, 0]
    key_blk = heads_view[:, :, 1]
    value_blk = heads_view[:, :, 2]
    block_ids = jnp.arange(n_blocks)

    def forward_block(entry):
        block_id, query_rows, key_rows, value_rows = entry
        return lax.cond(
            block_id < long_here,
            lambda operands: attend(operands[0], operands[1], operands[2], LONG),
            lambda operands: attend(operands[0], operands[1], operands[2], SHORT),
            (query_rows, key_rows, value_rows),
        )

    context_f, lse_rows = lax.map(forward_block, (block_ids, query_blk, key_blk, value_blk))
    context = context_f.reshape(rows_dev, D).astype(jnp.bfloat16)
    branch = jnp.dot(context, full_out, preferred_element_type=jnp.float32)
    hidden_in = tokens_f + branch
    normed = norm_rows(hidden_in, gains_f[0], biases_f[0])
    normed_low = normed.astype(jnp.bfloat16)
    all_rows = lax.all_gather(normed_low, "narrow", axis=0, tiled=True)
    gate = jnp.dot(all_rows, wide_gate, preferred_element_type=jnp.float32)
    value_up = jnp.dot(all_rows, wide_value, preferred_element_type=jnp.float32)
    product_f, pull_product = jax.vjp(gelu_product, gate, value_up)
    product = product_f.astype(jnp.bfloat16)
    ffn_out = lax.psum_scatter(
        jnp.dot(product, wide_down, preferred_element_type=jnp.float32),
        "narrow",
        scatter_dimension=0,
        tiled=True,
    )
    out_in = normed + ffn_out
    layer_out, pull_second = jax.vjp(norm_rows, out_in, gains_f[1], biases_f[1])
    d_out, d_gain_two, d_bias_two = pull_second(cotangent.astype(jnp.float32))
    d_ffn = d_out.astype(jnp.bfloat16)
    d_rows = lax.all_gather(d_ffn, "narrow", axis=0, tiled=True)
    grad_down = contract_rows(product, d_rows)
    d_product = contract_cols(d_rows, wide_down)
    d_gate, d_up = pull_product(d_product)
    d_gate_low = d_gate.astype(jnp.bfloat16)
    d_up_low = d_up.astype(jnp.bfloat16)
    grad_gate = contract_rows(all_rows, d_gate_low)
    grad_value = contract_rows(all_rows, d_up_low)
    d_normed = lax.psum_scatter(
        contract_cols(d_gate_low, wide_gate) + contract_cols(d_up_low, wide_value),
        "narrow",
        scatter_dimension=0,
        tiled=True,
    )
    d_normed_total = d_out + d_normed
    unused_out, pull_first = jax.vjp(norm_rows, hidden_in, gains_f[0], biases_f[0])
    d_hidden, d_gain_one, d_bias_one = pull_first(d_normed_total)
    d_branch = d_hidden.astype(jnp.bfloat16)
    grad_out = contract_rows(context, d_branch)
    d_context = contract_cols(d_branch, full_out).astype(jnp.bfloat16)
    d_context_blk = d_context.reshape(n_blocks, LONG, HEADS, HEAD_DIM)

    def backward_block(entry):
        block_id, query_rows, key_rows, value_rows, log_total, d_ctx = entry
        return lax.cond(
            block_id < long_here,
            lambda operands: attend_back(
                operands[0], operands[1], operands[2], operands[3], operands[4], LONG
            ),
            lambda operands: attend_back(
                operands[0], operands[1], operands[2], operands[3], operands[4], SHORT
            ),
            (query_rows, key_rows, value_rows, log_total, d_ctx),
        )

    d_mixed_f = lax.map(
        backward_block, (block_ids, query_blk, key_blk, value_blk, lse_rows, d_context_blk)
    )
    d_mixed = d_mixed_f.reshape(rows_dev, 3 * D).astype(jnp.bfloat16)
    grad_qkv = contract_rows(tokens, d_mixed)
    input_grad = d_hidden + contract_cols(d_mixed, full_qkv)
    grad_gains = jnp.stack([d_gain_one, d_gain_two])
    grad_biases = jnp.stack([d_bias_one, d_bias_two])
    pieces = (
        lax.psum_scatter(
            grad_qkv.astype(jnp.bfloat16), "wide", scatter_dimension=0, tiled=True
        ).astype(jnp.float32),
        lax.psum_scatter(
            grad_out.astype(jnp.bfloat16), "wide", scatter_dimension=0, tiled=True
        ).astype(jnp.float32),
        lax.psum_scatter(
            grad_gate.astype(jnp.bfloat16), "wide", scatter_dimension=0, tiled=True
        ).astype(jnp.float32),
        lax.psum_scatter(
            grad_value.astype(jnp.bfloat16), "wide", scatter_dimension=0, tiled=True
        ).astype(jnp.float32),
        lax.psum_scatter(
            grad_down.astype(jnp.bfloat16), "wide", scatter_dimension=1, tiled=True
        ).astype(jnp.float32),
        lax.psum_scatter(
            grad_gains.astype(jnp.bfloat16), "wide", scatter_dimension=1, tiled=True
        ).astype(jnp.float32),
        lax.psum_scatter(
            grad_biases.astype(jnp.bfloat16), "wide", scatter_dimension=1, tiled=True
        ).astype(jnp.float32),
    )
    qkv_piece, out_piece, gate_piece, value_piece, down_piece, gains_piece, biases_piece = pieces
    qkv_piece, out_piece, gains_piece, biases_piece = (
        lax.psum(qkv_piece.astype(jnp.bfloat16), "narrow").astype(jnp.float32),
        lax.psum(out_piece.astype(jnp.bfloat16), "narrow").astype(jnp.float32),
        lax.psum(gains_piece.astype(jnp.bfloat16), "narrow").astype(jnp.float32),
        lax.psum(biases_piece.astype(jnp.bfloat16), "narrow").astype(jnp.float32),
    )
    return (
        layer_out.astype(jnp.bfloat16),
        input_grad,
        qkv_piece,
        out_piece,
        gate_piece,
        value_piece,
        down_piece,
        gains_piece,
        biases_piece,
    )


AXES = ("wide", "narrow")
F32 = jnp.float32
BF16 = jnp.bfloat16
MIB = 1024 * 1024
RING = (0, 1, 3, 2)
PAIR = 2 * HEAD_DIM


def dot(left, right):
    return jnp.dot(left, right, preferred_element_type=F32)


class Plane:
    def __init__(self, wide, narrow):
        self.size = {"z": wide // 4, "ring": len(RING), "a": 2, "b": 2, "core": 2, "y": narrow}
        self.pairs = {}
        count = wide * narrow
        for dim, size in self.size.items():
            for step in range(1, size) if dim != "ring" else ():
                self.pairs[dim, step] = [(i, self.partner(i, dim, step)) for i in range(count)]
        after_z = {z: RING[(n + 1) % len(RING)] for n, z in enumerate(RING)}
        self.pairs["next", 1] = [(i, i % 8 + 8 * after_z[i // 8]) for i in range(count)]
        self.pairs["prev", 1] = [(j, i) for i, j in self.pairs["next", 1]]
        w = lax.axis_index("wide")
        self.z, self.x, self.core = w // 4, (w // 2) % 2, w % 2
        self.y = lax.axis_index("narrow")

    @staticmethod
    def partner(i, dim, step):
        z, x, c, y = i // 8, (i // 4) % 2, (i // 2) % 2, i % 2
        if dim == "z":
            z ^= step
        elif dim == "core":
            c ^= 1
        elif dim == "y" or (dim == "a") == (c == 1):
            y ^= 1
        else:
            x ^= 1
        return ((z * 2 + x) * 2 + c) * 2 + y

    def swap(self, value, dim, step=1):
        return lax.ppermute(value, AXES, self.pairs[dim, step])

    def tables(self, order, numbered):
        sizes = [self.size[dim] for dim in order]
        number = np.arange(int(np.prod(sizes)))
        rest, digit = number, {}
        for dim, size in zip(order, sizes):
            digit[dim] = rest % size
            rest = rest // size
        first = self.core == 0
        a_here = jnp.where(first, self.x, self.y)
        b_here = jnp.where(first, self.y, self.x)
        if "ring" in digit:
            at = sum(jnp.where(self.z == z, n, 0) for n, z in enumerate(RING))
            z = sum(jnp.where((at - digit["ring"]) % len(RING) == n, z, 0) for n, z in enumerate(RING))
        else:
            z = digit["z"] ^ self.z
        a = digit["a"] ^ a_here
        b = digit["b"] ^ b_here
        x, y = jnp.where(first, a, b), jnp.where(first, b, a)
        return numbered(z, x, y).astype(jnp.int32)


def after(value, *events):
    return lax.optimization_barrier((value,) + events)[0]


def fence(*values):
    return lax.optimization_barrier(values)


def smem():
    return pl.BlockSpec(memory_space=pltpu.SMEM)


def whole(shape):
    zeros = (0,) * len(shape)
    return pl.BlockSpec(tuple(shape), lambda *_: zeros)


def kernel_call(body, grid, ins, outs, scratch=(), flops=0, name=None, room=6):
    blocks = [(v[1].block_shape, v[0].dtype) for v in ins] + [(v[2].block_shape, v[1]) for v in outs]
    held = sum(2 * int(np.prod(shape)) * np.dtype(d).itemsize for shape, d in blocks if shape is not None)
    held += sum(int(np.prod(v.shape)) * np.dtype(v.dtype).itemsize for v in scratch)
    return pl.pallas_call(
        body,
        grid=grid,
        in_specs=[v[1] for v in ins],
        out_specs=[v[2] for v in outs],
        out_shape=[(pltpu.HBM if more else jax.ShapeDtypeStruct)(s, d) for s, d, _, *more in outs],
        scratch_shapes=list(scratch),
        compiler_params=pltpu.CompilerParams(
            dimension_semantics=("arbitrary",) * len(grid), vmem_limit_bytes=held // 2 + room * MIB
        ),
        cost_estimate=pl.CostEstimate(flops=0, bytes_accessed=0, transcendentals=0),
        name=name,
    )(*[pltpu.with_memory_space_constraint(a, pltpu.HBM) if more else a for a, _, *more in ins])


ROWS = 512


def own_rows(steps, cols):
    return pl.BlockSpec((ROWS, cols), lambda i: (jnp.minimum(i, steps - 1), 0))


def partner_rows(steps, cols):
    return pl.BlockSpec((ROWS, cols), lambda i: (jnp.maximum(i - steps, 0), 0))


def pick_rows(i, steps, own_ref, partner_ref):
    return jnp.where(i < steps, own_ref[...], partner_ref[...])


def split_kernel(place, w_qkv, w_out, gains, biases, mine, send):
    first = place[0] == 0
    half = D // 2
    for n in range(4):
        source, start = (w_qkv, n * D) if n < 3 else (w_out, 0)
        low, high = source[:, start : start + half], source[:, start + half : start + D]
        mine[:, n * half : (n + 1) * half] = jnp.where(first, low, high)
        send[:, n * half : (n + 1) * half] = jnp.where(first, high, low)
    rows = jnp.concatenate([gains[...], biases[...]], axis=0).astype(F32)
    eye = jnp.where(
        lax.broadcasted_iota(jnp.int32, (128, rows.shape[0]), 0)
        == lax.broadcasted_iota(jnp.int32, (128, rows.shape[0]), 1),
        1.0,
        0.0,
    )
    norm_cols = contract_cols(rows.T.astype(BF16), eye.astype(BF16)).astype(BF16)
    mine[:, 4 * half :] = norm_cols
    send[:, 4 * half :] = norm_cols


def fill_blocks(table, pieces, weight, cols=slice(None)):
    count = pieces[0].shape[0]
    for n, piece in enumerate(pieces):
        for k in range(count):
            weight[table[n * count + k]] = piece[k, :, cols]


def qkv_kernel(steps, groups, pieces, table, own, partner, *refs):
    i = pl.program_id(0)
    parts = refs[:pieces]
    mixed_own, mixed_partner, weight, out_w, norms, table_t = refs[pieces:]
    cols, part = weight.shape[2], out_w.shape[2]
    tall = weight.shape[0] * weight.shape[1]

    @pl.when(i == 0)
    def _():
        fill_blocks(table, parts, weight, slice(0, cols))
        fill_blocks(table, parts, out_w, slice(cols, cols + part))
        fill_blocks(table, parts, table_t, slice(cols + part, None))
        norms[...] = table_t[...].reshape(tall, table_t.shape[2]).astype(F32).T[: norms.shape[0]]

    rows_here = pick_rows(i, steps, own, partner)
    for g in range(groups):
        span = slice(g * cols // groups, (g + 1) * cols // groups)
        tile = weight[:, :, span].reshape(tall, cols // groups)
        value = dot(rows_here, tile).astype(BF16)

        @pl.when(i < steps)
        def _():
            mixed_own[:, span] = value

        @pl.when(i >= steps)
        def _():
            mixed_partner[:, span] = value


def lane_masks():
    lane = lax.broadcasted_iota(jnp.int32, (1, PAIR), 1)
    return [lane < HEAD_DIM, lane >= HEAD_DIM]


def keep(mask, value):
    return jnp.where(mask, value, jnp.zeros_like(value))


def fill_distance(distance):
    row = lax.broadcasted_iota(jnp.int32, distance.shape, 0)
    col = lax.broadcasted_iota(jnp.int32, distance.shape, 1)
    distance[...] = jnp.abs(row - col).astype(F32)


def scores_of(queries, keys, slope, distance):
    raw = lax.dot_general(queries, keys, (((1,), (1,)), ((), ())), preferred_element_type=F32)
    return raw - slope * distance


def tiles(value, tall):
    return [value[n : n + tall] for n in range(0, value.shape[0], tall)]


def pair_cols(part, pair):
    return pl.ds(pl.multiple_of(part * (D // 2) + pair * PAIR, PAIR), PAIR)


def attend_kernel(place, flags, slopes, mixed, *refs):
    context, logs, distance = refs[-3:]
    masks = lane_masks()
    scale = HEAD_DIM**-0.5
    lane = lax.broadcasted_iota(jnp.int32, (1, 128), 1)
    fill_distance(distance)
    for extra in refs[:-3]:
        context[LONG:, :] = extra[...].reshape(context.shape[0] - LONG, context.shape[1])

    def run(is_long):
        tall = 2 * SHORT if is_long else LONG

        def one_pair(pair, _):
            q_all, k_all, v_all = (mixed[:, pair_cols(part, pair)] for part in range(3))
            totals = [0.0] * (LONG // tall)
            mine = (lambda v: [v]) if is_long else (lambda v: tiles(v, SHORT))
            jobs = []
            for head in range(2):
                slope = slopes[pair * 2 + head]
                q = (keep(masks[head], q_all) * scale).astype(BF16)
                v = keep(masks[head], v_all)
                for n in range(LONG // tall):
                    rows = slice(n * tall, (n + 1) * tall)
                    away = distance[rows, :] if is_long else distance[:SHORT, :SHORT]
                    s = [scores_of(a, b, slope, away) for a, b in zip(mine(q[rows]), mine(k_all))]
                    jobs.append((head, n, jnp.concatenate(s, axis=0), v))
            done = []
            for head, n, s, v in jobs:
                top = jnp.max(s, axis=-1, keepdims=True)
                e = jnp.exp(s - top)
                norm = jnp.sum(e, axis=-1, keepdims=True)
                done.append(((e * (1.0 / norm)).astype(BF16), top + jnp.log(norm)))
            for (head, n, s, v), (p, log) in zip(jobs, done):
                totals[n] = totals[n] + jnp.concatenate([dot(a, b) for a, b in zip(mine(p), mine(v))], axis=0)
                rows = slice(n * tall, (n + 1) * tall)
                logs[rows, :] = jnp.where(lane == pair * 2 + head, log, logs[rows, :])
            for n in range(LONG // tall):
                context[n * tall : (n + 1) * tall, pair_cols(0, pair)] = totals[n].astype(BF16)
            return 0

        lax.fori_loop(0, D // 2 // PAIR, one_pair, 0)

    logs[...] = jnp.zeros_like(logs)
    flag = flags[place[1]]

    @pl.when(flag > 0)
    def _():
        run(True)

    @pl.when(flag <= 0)
    def _():
        run(False)


def attend_back_kernel(place, flags, slopes, mixed, logs_ref, d_context, d_query, d_key, d_value, distance):
    masks = lane_masks()
    scale = HEAD_DIM**-0.5
    fill_distance(distance)

    def run(is_long):
        tall = 2 * SHORT if is_long else LONG
        logs = logs_ref[...]
        lane = lax.broadcasted_iota(jnp.int32, (1, 128), 1)

        def one_pair(pair, _):
            q_all, k_all, v_all = (mixed[:, pair_cols(part, pair)] for part in range(3))
            d_all = d_context[:, pair_cols(0, pair)]
            d_q, d_k, d_v = [0.0] * (LONG // tall), 0.0, 0.0
            group = SHORT if not is_long else tall
            jobs = []
            for head in range(2):
                slope = slopes[pair * 2 + head]
                q = (keep(masks[head], q_all) * scale).astype(BF16)
                k = (keep(masks[head], k_all) * scale).astype(BF16)
                d_c = keep(masks[head], d_all)
                log_all = jnp.sum(jnp.where(lane == pair * 2 + head, logs, 0.0), axis=-1, keepdims=True)
                for n in range(LONG // tall):
                    rows = slice(n * tall, (n + 1) * tall)
                    jobs.append((n, slope, q[rows], k, d_c[rows], log_all[rows], distance[rows, :] if is_long else distance[:SHORT, :SHORT]))
            mine = (lambda v: [v]) if is_long else (lambda v: tiles(v, SHORT))
            raw = []
            for n, slope, q, k, d_c, log_rows, away in jobs:
                s = jnp.concatenate([scores_of(a, b, slope, away) for a, b in zip(mine(q), mine(k_all))], axis=0)
                d_p = jnp.concatenate([contract_cols(a, b) for a, b in zip(mine(d_c), mine(v_all))], axis=0)
                raw.append((s, d_p))
            done = []
            for (n, slope, q, k, d_c, log_rows, away), (s, d_p) in zip(jobs, raw):
                p = jnp.exp(s - log_rows)
                d_s = (p * (d_p - jnp.sum(p * d_p, axis=-1, keepdims=True))).astype(BF16)
                done.append((d_s, p.astype(BF16)))
            for (n, slope, q, k, d_c, log_rows, away), (d_s, p) in zip(jobs, done):
                d_q[n] = d_q[n] + jnp.concatenate([dot(a, b) for a, b in zip(mine(d_s), mine(k))], axis=0)
                d_k = d_k + jnp.concatenate([dot(a.T, b) for a, b in zip(mine(q), mine(d_s))], axis=1)
                d_v = d_v + jnp.concatenate([dot(a.T, b) for a, b in zip(mine(d_c), mine(p))], axis=1)
            cols = pair_cols(0, pair)
            for n in range(LONG // tall):
                d_query[n * tall : (n + 1) * tall, cols] = d_q[n].astype(BF16)
            d_key[:, cols] = d_k.T.astype(BF16)
            d_value[:, cols] = d_v.T.astype(BF16)
            return 0

        lax.fori_loop(0, D // 2 // PAIR, one_pair, 0)

    flag = flags[place[1]]

    @pl.when(flag > 0)
    def _():
        run(True)

    @pl.when(flag <= 0)
    def _():
        run(False)


def spread(rows):
    center = jnp.mean(rows, axis=-1, keepdims=True)
    shifted = rows - center
    inverse = lax.rsqrt(jnp.mean(shifted * shifted, axis=-1, keepdims=True) + 1e-05)
    return shifted * inverse, inverse


def norm_back(e, unit, inverse):
    mean_e = jnp.mean(e, axis=-1, keepdims=True)
    mean_en = jnp.mean(e * unit, axis=-1, keepdims=True)
    return (e - mean_e - unit * mean_en) * inverse


def first_norm_kernel(place, tokens, ctx_mine, ctx_other, w_mine, w_other_rows, norms, unit, inverse, low):
    core = place[0]
    half = w_mine.shape[0] // 2
    wide = w_mine.shape[2]

    def branch(weight):
        return dot(ctx_mine[...], weight(core)) + dot(ctx_other[...], weight(1 - core))

    mine = branch(lambda c: w_mine[pl.ds(c * half, half)].reshape(D // 2, wide))
    other = branch(lambda c: w_other_rows[pl.ds(pl.multiple_of(LONG + c * (D // 2), 128), D // 2), :])
    first = core == 0
    added = jnp.concatenate([jnp.where(first, mine, other), jnp.where(first, other, mine)], axis=1)
    n, inv = spread(tokens[...].astype(F32) + added)
    unit[...] = n
    inverse[...] = inv
    low[...] = (n * norms[0:1, :] + norms[2:3, :]).astype(BF16)


def gelu_parts(x):
    phi = 0.5 + 0.5 * lax.erf(x * 0.5**0.5)
    return x * phi, phi + x * jnp.exp(-0.5 * (x * x)) * 0.3989422804014327


def columns_of(weight, half, span):
    count = weight.shape[0] // 2
    return weight[half * count : (half + 1) * count, :, span].reshape(D, span.stop - span.start)


def gate_kernel(steps, pieces, table, own, partner, *refs):
    i = pl.program_id(0)
    active, slope, gate_w = refs[pieces:]

    @pl.when(i == 0)
    def _():
        fill_blocks(table, refs[:pieces], gate_w)

    rows = pick_rows(i, steps, own, partner)
    width = gate_w.shape[2]
    for half in range(2):
        for start in range(0, width, 256):
            out = slice(half * width + start, half * width + start + 256)
            gate = dot(rows, columns_of(gate_w, half, slice(start, start + 256)))
            act, grad = gelu_parts(gate)
            active[:, out] = act.astype(BF16)
            slope[:, out] = grad.astype(BF16)


def value_kernel(steps, pieces, table, own, partner, active, slope, *refs):
    i = pl.program_id(0)
    product, scaled, value_w = refs[pieces:]

    @pl.when(i == 0)
    def _():
        fill_blocks(table, refs[:pieces], value_w)

    rows = pick_rows(i, steps, own, partner)
    width = value_w.shape[2]
    for half in range(2):
        for start in range(0, width, 256):
            out = slice(half * width + start, half * width + start + 256)
            up = dot(rows, columns_of(value_w, half, slice(start, start + 256)))
            product[:, out] = (active[:, out].astype(F32) * up).astype(BF16)
            scaled[:, out] = (slope[:, out].astype(F32) * up).astype(BF16)


def times_down(product, down_w):
    width = down_w.shape[2]
    total = 0.0
    for half in range(2):
        part = product[:, half * width : (half + 1) * width]
        total = total + contract_cols(part, columns_of(down_w, half, slice(0, width)))
    return total


def down_first_kernel(table, product, *refs):
    partner, down_w = refs[-2:]

    @pl.when(pl.program_id(0) == 0)
    def _():
        fill_blocks(table, refs[:-2], down_w)

    partner[...] = times_down(product, down_w).astype(BF16)


def down_kernel(product, down_w, own):
    own[...] = times_down(product, down_w)


def second_norm_kernel(unit_one, norms, part_own, part_got, cotangent, out, d_z, d_ffn, sums):
    normed = unit_one[...] * norms[0:1, :] + norms[2:3, :]
    n, inv = spread(normed + (part_own[...] + part_got[...].astype(F32)))
    gain = norms[1:2, :]
    out[...] = (n * gain + norms[3:4, :]).astype(BF16)
    c = cotangent[...].astype(F32)
    back = norm_back(gain * c, n, inv)
    d_z[...] = back
    d_ffn[...] = back.astype(BF16)
    add_sums(sums, c * n, c)


def add_sums(sums, gain_terms, bias_terms):
    @pl.when(pl.program_id(0) == 0)
    def _():
        sums[...] = jnp.zeros_like(sums)

    sums[0:1, :] += jnp.sum(gain_terms, axis=0, keepdims=True)
    sums[1:2, :] += jnp.sum(bias_terms, axis=0, keepdims=True)


def ffn_back_kernel(
    steps, own, partner, down_w, gate_w, value_w, active, slope, d_gate, d_up, back_own, back_partner
):
    i = pl.program_id(0)
    rows = pick_rows(i, steps, own, partner)
    width = down_w.shape[2]
    for half in range(2):
        for start in range(0, width, 256):
            span = slice(start, start + 256)
            out = slice(half * width + start, half * width + start + 256)
            d_product = dot(rows, columns_of(down_w, half, span))
            d_gate[:, out] = (d_product * slope[:, out].astype(F32)).astype(BF16)
            d_up[:, out] = (d_product * active[:, out].astype(F32)).astype(BF16)
    total = 0.0
    for half in range(2):
        out = slice(half * width, (half + 1) * width)
        span = slice(0, width)
        total = total + contract_cols(d_gate[:, out], columns_of(gate_w, half, span))
        total = total + contract_cols(d_up[:, out], columns_of(value_w, half, span))

    @pl.when(i < steps)
    def _():
        back_own[...] = total

    @pl.when(i >= steps)
    def _():
        back_partner[...] = total.astype(BF16)


def weight_grad_kernel(table, left_own, left_partner, right_a, right_b, *refs):
    i = pl.program_id(0)
    parts, blocks = refs[:-1], refs[-1]
    rows = left_own.shape[0]
    count, tall, cols = blocks.shape
    for half, right in enumerate((right_a, right_b)):
        value = contract_rows(left_own[...], right[:rows, :]) + contract_rows(left_partner[...], right[rows:, :])
        value = value.astype(BF16).reshape(count // 2, tall, cols)
        blocks[half * (count // 2) : (half + 1) * (count // 2)] = value
    span = pl.ds(pl.multiple_of(i * cols, cols), cols)
    each = count // len(parts)
    for k in range(count):
        parts[k // each][k % each, :, span] = blocks[table[k]]


def first_norm_back_kernel(
    place,
    unit_ref,
    inverse,
    norms,
    d_z,
    part_own,
    part_got,
    ctx_mine,
    ctx_other,
    w_mine,
    w_other,
    d_hidden,
    dctx_mine,
    dctx_other,
    grad_keep,
    grad_send,
    sums,
    grad,
):
    core = place[0]
    first = core == 0
    unit = unit_ref[...]
    d_normed = d_z[...] + (part_own[...] + part_got[...].astype(F32))
    back = norm_back(norms[0:1, :] * d_normed, unit, inverse[...])
    low = back.astype(BF16)
    d_hidden[...] = back
    add_sums(sums, d_normed * unit, d_normed)
    half, wide = w_mine.shape[0] // 2, w_mine.shape[2]
    low_mine = jnp.where(first, low[:, :wide], low[:, wide:])
    low_other = jnp.where(first, low[:, wide:], low[:, :wide])
    for head_core, out in ((core, dctx_mine), (1 - core, dctx_other)):
        near = w_mine[pl.ds(head_core * half, half)].reshape(D // 2, wide)
        far = w_other[pl.ds(pl.multiple_of(LONG + head_core * (D // 2), 128), D // 2), :]
        out[...] = (contract_cols(low_mine, near) + contract_cols(low_other, far)).astype(BF16)

    @pl.when(pl.program_id(0) == 0)
    def _():
        grad[...] = jnp.zeros_like(grad)

    shape = (half,) + grad.shape[1:]
    grad[pl.ds(core * half, half)] += contract_rows(ctx_mine[...], low).reshape(shape)
    grad[pl.ds((1 - core) * half, half)] += contract_rows(ctx_other[...], low).reshape(shape)

    @pl.when(pl.program_id(0) == pl.num_programs(0) - 1)
    def _():
        left, right = grad[:, :, :wide], grad[:, :, wide:]
        grad_keep[...] = jnp.where(first, left, right)
        grad_send[...] = jnp.where(first, right, left).astype(BF16)


def qkv_grad_kernel(table, left_own, left_partner, *refs):
    d_own, d_partner = refs[:3], refs[3:6]
    out_grad, sums_one, sums_two, near, far, blocks, norm_grad = refs[6:]
    i = pl.program_id(0)
    count, tall, cols = blocks.shape

    @pl.when(i == 0)
    def _():
        one, two = sums_one[...], sums_two[...]
        empty = jnp.zeros((norm_grad.shape[2] - 4, D), F32)
        stacked = jnp.concatenate([one[0:1], two[0:1], one[1:2], two[1:2], empty], axis=0)
        norm_grad[...] = stacked.T.astype(BF16).reshape(norm_grad.shape)

    for g in range(3):

        @pl.when(i == g)
        def _():
            value = contract_rows(left_own[...], d_own[g][...]) + contract_rows(left_partner[...], d_partner[g][...])
            blocks[...] = value.astype(BF16).reshape(blocks.shape)
            for k in range(count):
                target, place = (near if k < count // 2 else far), table[k]
                target[k % (count // 2), :, g * cols : (g + 1) * cols] = blocks[place]
                if g == 0:
                    start = 3 * cols
                    for more in (out_grad, norm_grad):
                        stop = start + more.shape[2]
                        target[k % (count // 2), :, start:stop] = more[place]
                        start = stop


def input_grad_kernel(d_query, d_key, d_value, weight, *refs):
    cols = d_query.shape[1]
    total = 0.0
    for g, left in enumerate((d_query, d_key, d_value)):
        tile = weight[:, :, g * cols : (g + 1) * cols].reshape(D, cols)
        total = total + contract_cols(left[...], tile)
    for more in refs[:-1]:
        total = total + more[...].astype(F32)
    refs[-1][...] = total.astype(refs[-1].dtype)


def pieces_kernel(place, here, there, got, qkv, out, gains, biases):
    first, own = place[0] == 0, place[1] == 1
    half = D // 2
    mine = jnp.where(own, here[...], there[...])
    for n in range(4):
        a, b = mine[:, n * half : (n + 1) * half].astype(F32), got[:, n * half : (n + 1) * half].astype(F32)
        target, start = (qkv, n * D) if n < 3 else (out, 0)
        target[:, start : start + half] = jnp.where(first, a, b)
        target[:, start + half : start + D] = jnp.where(first, b, a)
    rows = (mine[:, 4 * half :].astype(F32) + got[:, 4 * half :].astype(F32)).T
    gains[...] = rows[0:2]
    biases[...] = rows[2:4]


def by_core(core, mine, other, axis):
    first = core == 0
    return jnp.stack([jnp.where(first, mine, other), jnp.where(first, other, mine)], axis=axis)


def half_of(core, halves, axis):
    zero, one = (lax.index_in_dim(halves, k, axis, keepdims=False) for k in range(2))
    first = core == 0
    return jnp.where(first, zero, one), jnp.where(first, one, zero)


def plane_shards(
    wide,
    narrow,
    tokens,
    w_qkv,
    w_out,
    w_gate,
    w_value,
    w_down,
    norm_gains,
    norm_biases,
    long_count,
    cotangent,
):
    plane = Plane(wide, narrow)
    swap = plane.swap
    core, y_here = plane.core, plane.y
    rows = tokens.shape[0]
    steps = rows // ROWS
    tall = w_qkv.shape[0]
    blocks = wide * narrow // 2
    z_size = plane.size["z"]
    head_cols = D // 2
    width = w_gate.shape[1] // 2
    hidden = 2 * width
    pairs = head_cols // PAIR
    qkv_to = plane.tables(("z", "a", "b"), lambda z, x, y: (z * 2 + x) * 2 + y)
    ffn_to = plane.tables(("z", "a", "b"), lambda z, x, y: y * (2 * z_size) + z * 2 + x)
    back_to = plane.tables(("a", "z", "b"), lambda z, x, y: y * (2 * z_size) + z * 2 + x)
    down_to = plane.tables(("a", "b", "ring"), lambda z, x, y: y * (2 * z_size) + z * 2 + x)
    place = jnp.reshape(core, (1,)).astype(jnp.int32)
    first = core == 0

    def wholes(arrays):
        return [(v, whole(v.shape)) for v in arrays]

    def far(entries):
        return [entry + (True,) for entry in entries]

    def step_rows(cols):
        return pl.BlockSpec((ROWS, cols), lambda i: (i, 0))

    head_shape = (tall, 4 * head_cols + 128)
    head_part, head_send = kernel_call(
        split_kernel,
        (1,),
        [(place, smem())] + far(wholes([w_qkv, w_out, norm_gains, norm_biases])),
        [(head_shape, BF16, whole(head_shape))] * 2,
        name="split",
    )
    flag = jnp.broadcast_to(long_count.astype(F32), (8, 128))
    head_got, flag_got = fence(swap(head_send, "core"), swap(flag, "core"))
    head_part = jnp.where(y_here == core, head_part, head_got)
    head_parts = [head_part] + [swap(head_part, "z", k) for k in range(1, z_size)]
    ffn_parts = [after(w_gate, head_part), w_value, w_down.T]
    ffn_other = jnp.concatenate([jnp.where(first, v[:, width:], v[:, :width]) for v in ffn_parts], axis=1)
    ffn_got = swap(ffn_other, "core")
    flags = jnp.stack([long_count[0, 0], flag_got[0, 0].astype(jnp.int32)])
    slopes = lax.dynamic_slice_in_dim(alibi_slopes(HEADS), core * (HEADS // 2), HEADS // 2)

    def ffn_chip(n):
        v, got = ffn_parts[n], ffn_got[:, n * width : (n + 1) * width]
        mine = jnp.where(first, v[:, :width], v[:, width:])
        return jnp.concatenate([jnp.where(first, mine, got), jnp.where(first, got, mine)], axis=0)

    def doubled(value, step, *events):
        got = swap(value, "z", step)
        return jnp.concatenate(lax.optimization_barrier((value, got) + events)[:2], axis=0)

    def along_plane(held):
        near = swap(held, "a")
        return held, near, swap(held, "b")

    def joined(value, got):
        return jnp.concatenate([value, got], axis=0)

    gate_one, value_one, down_one = (ffn_chip(n)[None] for n in range(3))
    gate_got = swap(gate_one, "z", 1)
    down_got = swap(down_one, "a")
    *head_parts, gate_got, down_got = fence(*head_parts, gate_got, down_got)
    qkv_z = jnp.stack(head_parts)
    gate_two, down_two = joined(gate_one, gate_got), joined(down_one, down_got)

    head_near, head_far = swap(qkv_z, "a"), swap(qkv_z, "b")
    gate_got = swap(gate_two, "z", 2)
    value_got = swap(after(value_one, qkv_z), "z", 1)
    tokens_other = swap(after(tokens, qkv_z), "core")
    head_near, head_far, gate_got, value_got, tokens_other = fence(head_near, head_far, gate_got, value_got, tokens_other)
    gate_z, value_two = joined(gate_two, gate_got), joined(value_one, value_got)

    head_last = swap(head_near, "b")
    down_got = swap(after(down_two, head_near), "b")
    gate_near = swap(gate_z, "a")
    value_got = swap(value_two, "z", 2)
    head_last, down_got, gate_near, value_got = fence(head_last, down_got, gate_near, value_got)
    value_z, down_four = joined(value_two, value_got), joined(down_two, down_got)
    qkv_blocks = [qkv_z, head_near, head_far, head_last]

    gate_far, gate_last = swap(after(gate_z, head_last), "b"), swap(gate_near, "b")
    ring_one = swap(down_four, "next")
    block_row = (blocks, tall)
    mixed_own, mixed_partner, qkv_w, out_mine, norms = kernel_call(
        functools.partial(qkv_kernel, steps, 3, len(qkv_blocks)),
        (2 * steps,),
        [(qkv_to, smem())]
        + far([(tokens, own_rows(steps, D)), (tokens_other, partner_rows(steps, D))] + wholes(qkv_blocks)),
        far(
            [((rows, 3 * head_cols), BF16, own_rows(steps, 3 * head_cols))]
            + [((rows, 3 * head_cols), BF16, partner_rows(steps, 3 * head_cols))]
            + [(block_row + (n,), BF16, whole(block_row + (n,))) for n in (3 * head_cols, head_cols)]
        )
        + [((8, D), F32, whole((8, D)))],
        scratch=[pltpu.VMEM(block_row + (128,), BF16)],
        flops=2 * 2 * rows * D * 3 * head_cols,
        name="mixed",
    )
    def attend(block, mixed, extra=()):
        tall_out = rows + sum(v.size for v in extra) // head_cols
        return kernel_call(
            attend_kernel,
            (1,),
            [(jnp.array([0, block], jnp.int32), smem()), (flags, smem()), (slopes, smem())]
            + far(wholes([mixed, *extra])),
            [((tall_out, head_cols), BF16, whole((tall_out, head_cols))), ((rows, 128), F32, whole((rows, 128)), True)],
            scratch=[pltpu.VMEM((LONG, LONG), F32)],
            flops=4 * rows * LONG * D,
            name="attend",
            room=12,
        )

    ctx_send, logs_partner = attend(1, mixed_partner, [out_mine])
    gate_far, gate_last, ring_one, ctx_send = fence(gate_far, gate_last, ring_one, ctx_send)

    value_near, value_far = swap(value_z, "a"), swap(value_z, "b")
    ring_two = swap(ring_one, "next")
    ctx_got = swap(ctx_send, "core")
    ctx_mine, logs_own = attend(0, after(mixed_own, ctx_send))

    unit_one, inverse_one, low = kernel_call(
        first_norm_kernel,
        (steps,),
        [
            (place, smem()),
            (tokens, step_rows(D)),
            (ctx_mine, step_rows(head_cols)),
            (ctx_got, step_rows(head_cols)),
        ]
        + wholes([out_mine, ctx_got, norms]),
        [
            ((rows, D), F32, step_rows(D)),
            ((rows, 1), F32, step_rows(1)),
            ((rows, D), BF16, step_rows(D)),
        ],
        flops=2 * rows * D * D,
        name="first_norm",
    )
    value_near, low = fence(value_near, low)
    gate_blocks = [gate_z, gate_near, gate_far, gate_last]
    value_last = swap(value_near, "b")
    ring_three = swap(ring_two, "next")
    low_other = swap(low, "core")

    w_shape = (blocks, 2 * tall, width)
    both_rows = [(low, own_rows(steps, D)), (low_other, partner_rows(steps, D))]
    active, slope, gate_w = kernel_call(
        functools.partial(gate_kernel, steps, len(gate_blocks)),
        (2 * steps,),
        [(ffn_to, smem())] + both_rows + far(wholes(gate_blocks)),
        [((2 * rows, hidden), BF16, step_rows(hidden))] * 2 + [(w_shape, BF16, whole(w_shape))],
        name="gate",
    )
    value_last, active = fence(value_last, active)
    value_blocks = [value_z, value_near, value_far, value_last]
    down_blocks = [down_four, ring_one, ring_two, ring_three]
    product, slope, value_w = kernel_call(
        functools.partial(value_kernel, steps, len(value_blocks)),
        (2 * steps,),
        [(ffn_to, smem())] + both_rows + [(active, step_rows(hidden)), (slope, step_rows(hidden))] + wholes(value_blocks),
        [((2 * rows, hidden), BF16, step_rows(hidden))] * 2 + [(w_shape, BF16, whole(w_shape))],
        name="value",
    )
    part_send, down_w = kernel_call(
        down_first_kernel,
        (steps,),
        [(down_to, smem()), (product, pl.BlockSpec((ROWS, hidden), lambda i: (i + steps, 0)))] + wholes(down_blocks),
        [((rows, D), BF16, step_rows(D)), (w_shape, BF16, whole(w_shape))],
        name="down_first",
    )
    (part_own,) = kernel_call(
        down_kernel,
        (steps,),
        [(product, step_rows(hidden))] + wholes([down_w]),
        [((rows, D), F32, step_rows(D))],
        name="down",
    )
    part_got = swap(part_send, "core")
    layer_out, d_z, d_ffn, sums_two = kernel_call(
        second_norm_kernel,
        (steps,),
        [(unit_one, step_rows(D))]
        + wholes([norms])
        + [(part_own, step_rows(D)), (part_got, step_rows(D)), (cotangent, step_rows(D))],
        [
            ((rows, D), BF16, step_rows(D)),
            ((rows, D), F32, step_rows(D)),
            ((rows, D), BF16, step_rows(D)),
            ((8, D), F32, whole((8, D))),
        ],
        name="second_norm",
    )
    d_ffn_other = swap(d_ffn, "core")

    def weight_grad(left, left_other, right, to, parts):
        part = (blocks // parts, 2 * tall, width)
        cols = width // 3
        return kernel_call(
            weight_grad_kernel,
            (3,),
            [
                (to, smem()),
                (left, whole((rows, D))),
                (left_other, whole((rows, D))),
                (right, pl.BlockSpec((2 * rows, cols), lambda i: (0, i))),
                (right, pl.BlockSpec((2 * rows, cols), lambda i: (0, 3 + i))),
            ],
            [(part, BF16, whole(part))] * parts,
            scratch=[pltpu.VMEM((blocks, 2 * tall, cols), BF16)],
            flops=2 * 2 * rows * D * hidden,
            name="weight_grad",
        )

    def added(keep, got):
        return (keep.astype(F32) + got.astype(F32)).astype(BF16)

    def halves(keep, got):
        count = keep.shape[0] // 2
        return added(keep[:count], got[:count]), added(keep[count:], got[count:])

    def quarters(keep, got):
        return [added(keep[k], got[k]) for k in range(z_size)]

    down_parts = weight_grad(d_ffn, d_ffn_other, product, back_to, 2)
    d_gate, d_up, back_own, back_send = kernel_call(
        functools.partial(ffn_back_kernel, steps),
        (2 * steps,),
        [(after(d_ffn, down_parts[-1]), own_rows(steps, D)), (d_ffn_other, partner_rows(steps, D))]
        + wholes([down_w, gate_w, value_w])
        + [(active, step_rows(hidden)), (slope, step_rows(hidden))],
        [((2 * rows, hidden), BF16, step_rows(hidden))] * 2
        + [((rows, D), F32, own_rows(steps, D)), ((rows, D), BF16, partner_rows(steps, D))],
        flops=3 * 2 * 2 * rows * D * hidden,
        name="ffn_back",
    )
    down_got = swap(down_parts[1], "b")
    gate_keep, gate_send = weight_grad(after(low, back_send), low_other, d_gate, ffn_to, 2)
    back_send, gate_send = fence(back_send, gate_send)

    gate_got = swap(gate_send, "b")
    down_z = [added(down_parts[0][2 * k : 2 * k + 2], down_got[2 * k : 2 * k + 2]) for k in range(z_size)]
    down_got = swap(down_z[3], "z", 2)
    back_got = swap(back_send, "core")
    value_keep, value_send = weight_grad(after(low, gate_send), low_other, d_up, ffn_to, 2)
    value_got = swap(value_send, "b")
    back_got = after(back_got, value_send)
    d_hidden, dctx_mine, dctx_send, out_keep, out_send, sums_one = kernel_call(
        first_norm_back_kernel,
        (steps,),
        [
            (place, smem()),
            (unit_one, step_rows(D)),
            (inverse_one, step_rows(1)),
            (norms, whole(norms.shape)),
            (d_z, step_rows(D)),
            (back_own, step_rows(D)),
            (back_got, step_rows(D)),
            (ctx_mine, step_rows(head_cols)),
            (ctx_got, step_rows(head_cols)),
        ]
        + wholes([out_mine, ctx_got]),
        [
            ((rows, D), F32, step_rows(D)),
            ((rows, head_cols), BF16, step_rows(head_cols)),
            ((rows, head_cols), BF16, step_rows(head_cols)),
            (out_mine.shape, F32, whole(out_mine.shape)),
            (out_mine.shape, BF16, whole(out_mine.shape)),
            ((8, D), F32, whole((8, D))),
        ],
        scratch=[pltpu.VMEM((blocks, tall, D), F32)],
        flops=2 * 2 * rows * D * D,
        name="first_norm_back",
    )
    def attend_back(block, mixed, d_context, logs):
        return kernel_call(
            attend_back_kernel,
            (1,),
            [(jnp.array([0, block], jnp.int32), smem()), (flags, smem()), (slopes, smem())]
            + far(wholes([mixed, logs]))
            + wholes([d_context]),
            [((rows, head_cols), BF16, whole((rows, head_cols)))] * 3,
            scratch=[pltpu.VMEM((LONG, LONG), F32)],
            name="attend_back",
            room=16,
        )

    d_own = attend_back(0, mixed_own, dctx_mine, logs_own)
    down_got, gate_got, dctx_send, out_send, d_first = fence(down_got, gate_got, dctx_send, out_send, d_own[0])
    d_own = [d_first, *d_own[1:]]
    dctx_got, out_got = swap(dctx_send, "core"), swap(out_send, "core")
    gate_keep, gate_send = halves(gate_keep, gate_got)
    down_send = added(down_z[1], down_got)
    gate_got = swap(gate_send, "a")
    down_got = swap(after(down_z[2], gate_send), "z", 2)
    out_sum = (out_keep + out_got.astype(F32)).astype(BF16)

    d_partner = attend_back(1, mixed_partner, after(dctx_got, gate_send, down_send), logs_partner)
    grad_shape = (blocks // 2, tall, 4 * head_cols + 128)
    head_keep, head_send = kernel_call(
        qkv_grad_kernel,
        (3,),
        [(qkv_to, smem())]
        + wholes([tokens, tokens_other, *d_own, *d_partner, out_sum, sums_one, sums_two]),
        [(grad_shape, BF16, whole(grad_shape))] * 2,
        scratch=[pltpu.VMEM(block_row + (head_cols,), BF16), pltpu.VMEM(block_row + (128,), BF16)],
        name="qkv_grad",
    )
    down_got, gate_got, head_send = fence(down_got, gate_got, head_send)
    head_got = swap(head_send, "b")
    gate_keep, gate_send = halves(gate_keep, gate_got)
    value_keep, value_send = halves(value_keep, value_got)

    value_got = swap(value_send, "a")
    gate_got = swap(gate_send, "z", 2)
    down_keep = added(down_z[0], down_got)
    down_got = swap(down_send, "z", 1)

    def input_part(d_parts, more, dtype):
        return kernel_call(
            input_grad_kernel,
            (steps,),
            [(v, step_rows(head_cols)) for v in d_parts] + wholes([qkv_w]) + [(v, step_rows(D)) for v in more],
            [((rows, D), dtype, step_rows(D))],
            name="input_grad",
        )[0]

    in_send = input_part([after(d_partner[0], value_send, gate_send), *d_partner[1:]], [], BF16)
    head_got, value_got, gate_got, down_got, in_send = fence(head_got, value_got, gate_got, down_got, in_send)
    head_keep, head_send = halves(head_keep, head_got)
    value_keep, value_send = halves(value_keep, value_got)
    gate_keep, gate_send = halves(gate_keep, gate_got)
    down_keep, down_send = halves(down_keep, down_got)

    in_got = swap(in_send, "core")
    gate_got = swap(gate_send, "z", 1)
    down_got = swap(down_send, "a")
    head_got = swap(head_send, "a")
    value_got = swap(value_send, "z", 2)
    input_grad = input_part([after(d_own[0], head_send, value_send), *d_own[1:]], [d_hidden, in_got], F32)
    head_got, input_grad = fence(head_got, input_grad)
    head_parts = quarters(head_keep, head_got)
    value_got = after(value_got, *head_parts)
    value_keep, value_send = halves(value_keep, value_got)
    value_got = swap(value_send, "z", 1)

    head_got = [swap(head_parts[k], "z", k) for k in range(1, z_size)]
    value_got, gate_got, down_got, *head_got = fence(value_got, gate_got, down_got, *head_got)
    head_sum = head_parts[0].astype(F32)
    for part in head_got:
        head_sum = head_sum + part.astype(F32)
    head_sum = head_sum.astype(BF16)
    there = swap(head_sum, "y")
    gate_sum = added(gate_keep[0], gate_got[0])
    grads = [gate_sum, added(value_keep[0], value_got[0]), added(down_keep[0], down_got[0])]

    def in_order(mine, other):
        return [jnp.where(first, mine, other), jnp.where(first, other, mine)]

    kept = [half_of(core, total.reshape(2, tall, width), 0) for total in grads]
    ffn_got = swap(jnp.concatenate([other for _, other in kept], axis=0), "core")
    ffn_pieces = [
        jnp.concatenate(in_order(mine, ffn_got[n * tall : (n + 1) * tall]), axis=1).astype(F32)
        for n, (mine, _) in enumerate(kept)
    ]
    gate_piece, value_piece, down_piece = ffn_pieces[0], ffn_pieces[1], ffn_pieces[2].T
    there = after(there, gate_piece, value_piece, down_piece)
    own = y_here == core
    got = swap(jnp.where(own, there, head_sum), "core")
    qkv_piece, out_piece, gains_piece, biases_piece = kernel_call(
        pieces_kernel,
        (1,),
        [(jnp.stack([core, own.astype(jnp.int32)]), smem())] + wholes([head_sum, there, got]),
        [((tall, 3 * D), F32, whole((tall, 3 * D))), ((tall, D), F32, whole((tall, D)))]
        + [((2, tall), F32, whole((2, tall)))] * 2,
        name="pieces",
    )
    return (
        layer_out,
        input_grad,
        qkv_piece,
        out_piece,
        gate_piece,
        value_piece,
        down_piece,
        gains_piece,
        biases_piece,
    )


def solution(mesh):
    wide, narrow = mesh.shape["wide"], mesh.shape["narrow"]
    placed = (
        P(("wide", "narrow"), None),
        P("wide", None),
        P("wide", None),
        P("wide", "narrow"),
        P("wide", "narrow"),
        P("narrow", "wide"),
        P(None, "wide"),
        P(None, "wide"),
        P("wide", "narrow"),
        P(("wide", "narrow"), None),
    )
    if narrow == 2 and wide % 16 == 0 and D % (16 * wide) == 0:
        body = functools.partial(plane_shards, wide, narrow)
    else:
        body = general_shards
    return jax.shard_map(
        body,
        mesh=mesh,
        in_specs=placed,
        out_specs=(
            P(("wide", "narrow"), None),
            P(("wide", "narrow"), None),
            P("wide", None),
            P("wide", None),
            P("wide", "narrow"),
            P("wide", "narrow"),
            P("narrow", "wide"),
            P(None, "wide"),
            P(None, "wide"),
        ),
        check_vma=False,
    )
```

```python
import functools

import jax
import jax.numpy as jnp
import numpy as np
from jax import lax
from jax.experimental import pallas as pl
from jax.experimental.pallas import tpu as pltpu
from jax.sharding import PartitionSpec as P

D = 768
HEADS = 12
HEAD_DIM = 64
LONG = 512
SHORT = 128


def norm_rows(values, gain_row, bias_row):
    center = jnp.mean(values, axis=-1, keepdims=True)
    shifted = values - center
    spread = jnp.mean(shifted * shifted, axis=-1, keepdims=True)
    return shifted * lax.rsqrt(spread + 1e-05) * gain_row + bias_row


def gelu_product(gate_in, value_in):
    return jax.nn.gelu(gate_in, approximate=False) * value_in


def alibi_slopes(heads):
    power = 1 << heads.bit_length() - 1
    first = [2.0 ** (-8.0 * (index + 1) / power) for index in range(power)]
    second = [2.0 ** (-8.0 * (2 * index + 1) / (2 * power)) for index in range(heads - power)]
    return jnp.array(first + second, dtype=jnp.float32)


def alibi_bias(span, heads):
    position = jnp.arange(span)
    distance = jnp.abs(position[:, None] - position[None, :]).astype(jnp.float32)
    slopes = alibi_slopes(heads)
    return slopes[:, None, None] * distance


def block_scores(query_g, key_g, span):
    width = query_g.shape[-1]
    scores = jnp.einsum(
        "bqhd,bkhd->bhqk", query_g, key_g, preferred_element_type=jnp.float32
    ) * width ** (-0.5)
    return scores - alibi_bias(span, query_g.shape[2])


def attend(query_rows, key_rows, value_rows, span):
    rows, heads, width = query_rows.shape
    groups = rows // span
    shape_g = (groups, span, heads, width)
    query_g = query_rows.reshape(shape_g)
    key_g = key_rows.reshape(shape_g)
    value_g = value_rows.reshape(shape_g)
    scores = block_scores(query_g, key_g, span)
    top = jnp.max(scores, axis=-1, keepdims=True)
    expd = jnp.exp(scores - top)
    total = jnp.sum(expd, axis=-1, keepdims=True)
    probs_low = (expd / total).astype(jnp.bfloat16)
    context = jnp.einsum("bhqk,bkhd->bqhd", probs_low, value_g, preferred_element_type=jnp.float32)
    log_total = jnp.transpose((top + jnp.log(total))[..., 0], (0, 2, 1)).reshape(rows, heads)
    return (context.reshape(rows, heads * width), log_total)


def attend_back(query_rows, key_rows, value_rows, log_total, d_context, span):
    rows, heads, width = query_rows.shape
    groups = rows // span
    shape_g = (groups, span, heads, width)
    query_g = query_rows.reshape(shape_g)
    key_g = key_rows.reshape(shape_g)
    value_g = value_rows.reshape(shape_g)
    d_context_g = d_context.reshape(shape_g)
    lse_g = jnp.transpose(log_total.reshape(groups, span, heads), (0, 2, 1))
    scores = block_scores(query_g, key_g, span)
    probs = jnp.exp(scores - lse_g[..., None])
    probs_low = probs.astype(jnp.bfloat16)
    d_probs = jnp.einsum(
        "bqhd,bkhd->bhqk", d_context_g, value_g, preferred_element_type=jnp.float32
    )
    d_values = jnp.einsum(
        "bhqk,bqhd->bkhd", probs_low, d_context_g, preferred_element_type=jnp.float32
    )
    row_dot = jnp.sum(probs * d_probs, axis=-1, keepdims=True)
    d_scores = (probs * (d_probs - row_dot)).astype(jnp.bfloat16)
    scale = width ** (-0.5)
    d_queries = (
        jnp.einsum("bhqk,bkhd->bqhd", d_scores, key_g, preferred_element_type=jnp.float32) * scale
    )
    d_keys = (
        jnp.einsum("bhqk,bqhd->bkhd", d_scores, query_g, preferred_element_type=jnp.float32) * scale
    )
    return jnp.stack([d_queries, d_keys, d_values], axis=2).reshape(rows, 3, heads, width)


def contract_rows(left, right):
    return lax.dot_general(
        left, right, (((0,), (0,)), ((), ())), preferred_element_type=jnp.float32
    )


def contract_cols(left, right):
    return lax.dot_general(
        left, right, (((1,), (1,)), ((), ())), preferred_element_type=jnp.float32
    )


def general_shards(
    tokens, w_qkv, w_out, w_gate, w_value, w_down, norm_gains, norm_biases, long_count, cotangent
):
    gathered = (
        lax.all_gather(w_qkv, "wide", axis=0, tiled=True),
        lax.all_gather(w_out, "wide", axis=0, tiled=True),
        lax.all_gather(w_gate, "wide", axis=0, tiled=True),
        lax.all_gather(w_value, "wide", axis=0, tiled=True),
        lax.all_gather(w_down, "wide", axis=1, tiled=True),
        lax.all_gather(norm_gains, "wide", axis=1, tiled=True),
        lax.all_gather(norm_biases, "wide", axis=1, tiled=True),
    )
    full_qkv, full_out, wide_gate, wide_value, wide_down, gains_all, biases_all = gathered
    gains_f = gains_all.astype(jnp.float32)
    biases_f = biases_all.astype(jnp.float32)
    rows_dev = tokens.shape[0]
    n_blocks = rows_dev // LONG
    long_here = long_count[0, 0]
    tokens_f = tokens.astype(jnp.float32)
    mixed = jnp.dot(tokens, full_qkv, preferred_element_type=jnp.float32).astype(jnp.bfloat16)
    heads_view = mixed.reshape(n_blocks, LONG, 3, HEADS, HEAD_DIM)
    query_blk = heads_view[:, :, 0]
    key_blk = heads_view[:, :, 1]
    value_blk = heads_view[:, :, 2]
    block_ids = jnp.arange(n_blocks)

    def forward_block(entry):
        block_id, query_rows, key_rows, value_rows = entry
        return lax.cond(
            block_id < long_here,
            lambda operands: attend(operands[0], operands[1], operands[2], LONG),
            lambda operands: attend(operands[0], operands[1], operands[2], SHORT),
            (query_rows, key_rows, value_rows),
        )

    context_f, lse_rows = lax.map(forward_block, (block_ids, query_blk, key_blk, value_blk))
    context = context_f.reshape(rows_dev, D).astype(jnp.bfloat16)
    branch = jnp.dot(context, full_out, preferred_element_type=jnp.float32)
    hidden_in = tokens_f + branch
    normed = norm_rows(hidden_in, gains_f[0], biases_f[0])
    normed_low = normed.astype(jnp.bfloat16)
    all_rows = lax.all_gather(normed_low, "narrow", axis=0, tiled=True)
    gate = jnp.dot(all_rows, wide_gate, preferred_element_type=jnp.float32)
    value_up = jnp.dot(all_rows, wide_value, preferred_element_type=jnp.float32)
    product_f, pull_product = jax.vjp(gelu_product, gate, value_up)
    product = product_f.astype(jnp.bfloat16)
    ffn_out = lax.psum_scatter(
        jnp.dot(product, wide_down, preferred_element_type=jnp.float32),
        "narrow",
        scatter_dimension=0,
        tiled=True,
    )
    out_in = normed + ffn_out
    layer_out, pull_second = jax.vjp(norm_rows, out_in, gains_f[1], biases_f[1])
    d_out, d_gain_two, d_bias_two = pull_second(cotangent.astype(jnp.float32))
    d_ffn = d_out.astype(jnp.bfloat16)
    d_rows = lax.all_gather(d_ffn, "narrow", axis=0, tiled=True)
    grad_down = contract_rows(product, d_rows)
    d_product = contract_cols(d_rows, wide_down)
    d_gate, d_up = pull_product(d_product)
    d_gate_low = d_gate.astype(jnp.bfloat16)
    d_up_low = d_up.astype(jnp.bfloat16)
    grad_gate = contract_rows(all_rows, d_gate_low)
    grad_value = contract_rows(all_rows, d_up_low)
    d_normed = lax.psum_scatter(
        contract_cols(d_gate_low, wide_gate) + contract_cols(d_up_low, wide_value),
        "narrow",
        scatter_dimension=0,
        tiled=True,
    )
    d_normed_total = d_out + d_normed
    unused_out, pull_first = jax.vjp(norm_rows, hidden_in, gains_f[0], biases_f[0])
    d_hidden, d_gain_one, d_bias_one = pull_first(d_normed_total)
    d_branch = d_hidden.astype(jnp.bfloat16)
    grad_out = contract_rows(context, d_branch)
    d_context = contract_cols(d_branch, full_out).astype(jnp.bfloat16)
    d_context_blk = d_context.reshape(n_blocks, LONG, HEADS, HEAD_DIM)

    def backward_block(entry):
        block_id, query_rows, key_rows, value_rows, log_total, d_ctx = entry
        return lax.cond(
            block_id < long_here,
            lambda operands: attend_back(
                operands[0], operands[1], operands[2], operands[3], operands[4], LONG
            ),
            lambda operands: attend_back(
                operands[0], operands[1], operands[2], operands[3], operands[4], SHORT
            ),
            (query_rows, key_rows, value_rows, log_total, d_ctx),
        )

    d_mixed_f = lax.map(
        backward_block, (block_ids, query_blk, key_blk, value_blk, lse_rows, d_context_blk)
    )
    d_mixed = d_mixed_f.reshape(rows_dev, 3 * D).astype(jnp.bfloat16)
    grad_qkv = contract_rows(tokens, d_mixed)
    input_grad = d_hidden + contract_cols(d_mixed, full_qkv)
    grad_gains = jnp.stack([d_gain_one, d_gain_two])
    grad_biases = jnp.stack([d_bias_one, d_bias_two])
    pieces = (
        lax.psum_scatter(
            grad_qkv.astype(jnp.bfloat16), "wide", scatter_dimension=0, tiled=True
        ).astype(jnp.float32),
        lax.psum_scatter(
            grad_out.astype(jnp.bfloat16), "wide", scatter_dimension=0, tiled=True
        ).astype(jnp.float32),
        lax.psum_scatter(
            grad_gate.astype(jnp.bfloat16), "wide", scatter_dimension=0, tiled=True
        ).astype(jnp.float32),
        lax.psum_scatter(
            grad_value.astype(jnp.bfloat16), "wide", scatter_dimension=0, tiled=True
        ).astype(jnp.float32),
        lax.psum_scatter(
            grad_down.astype(jnp.bfloat16), "wide", scatter_dimension=1, tiled=True
        ).astype(jnp.float32),
        lax.psum_scatter(
            grad_gains.astype(jnp.bfloat16), "wide", scatter_dimension=1, tiled=True
        ).astype(jnp.float32),
        lax.psum_scatter(
            grad_biases.astype(jnp.bfloat16), "wide", scatter_dimension=1, tiled=True
        ).astype(jnp.float32),
    )
    qkv_piece, out_piece, gate_piece, value_piece, down_piece, gains_piece, biases_piece = pieces
    qkv_piece, out_piece, gains_piece, biases_piece = (
        lax.psum(qkv_piece.astype(jnp.bfloat16), "narrow").astype(jnp.float32),
        lax.psum(out_piece.astype(jnp.bfloat16), "narrow").astype(jnp.float32),
        lax.psum(gains_piece.astype(jnp.bfloat16), "narrow").astype(jnp.float32),
        lax.psum(biases_piece.astype(jnp.bfloat16), "narrow").astype(jnp.float32),
    )
    return (
        layer_out.astype(jnp.bfloat16),
        input_grad,
        qkv_piece,
        out_piece,
        gate_piece,
        value_piece,
        down_piece,
        gains_piece,
        biases_piece,
    )


AXES = ("wide", "narrow")
F32 = jnp.float32
BF16 = jnp.bfloat16
MIB = 1024 * 1024
RING = (0, 1, 3, 2)
PAIR = 2 * HEAD_DIM


def dot(left, right):
    return jnp.dot(left, right, preferred_element_type=F32)


class Plane:
    def __init__(self, wide, narrow):
        self.size = {"z": wide // 4, "ring": len(RING), "a": 2, "b": 2, "core": 2, "y": narrow}
        self.pairs = {}
        count = wide * narrow
        for dim, size in self.size.items():
            for step in range(1, size) if dim != "ring" else ():
                self.pairs[dim, step] = [(i, self.partner(i, dim, step)) for i in range(count)]
        after_z = {z: RING[(n + 1) % len(RING)] for n, z in enumerate(RING)}
        self.pairs["next", 1] = [(i, i % 8 + 8 * after_z[i // 8]) for i in range(count)]
        self.pairs["prev", 1] = [(j, i) for i, j in self.pairs["next", 1]]
        w = lax.axis_index("wide")
        self.z, self.x, self.core = w // 4, (w // 2) % 2, w % 2
        self.y = lax.axis_index("narrow")

    @staticmethod
    def partner(i, dim, step):
        z, x, c, y = i // 8, (i // 4) % 2, (i // 2) % 2, i % 2
        if dim == "z":
            z ^= step
        elif dim == "core":
            c ^= 1
        elif dim == "y" or (dim == "a") == (c == 1):
            y ^= 1
        else:
            x ^= 1
        return ((z * 2 + x) * 2 + c) * 2 + y

    def swap(self, value, dim, step=1):
        return lax.ppermute(value, AXES, self.pairs[dim, step])

    def tables(self, order, numbered):
        sizes = [self.size[dim] for dim in order]
        number = np.arange(int(np.prod(sizes)))
        rest, digit = number, {}
        for dim, size in zip(order, sizes):
            digit[dim] = rest % size
            rest = rest // size
        first = self.core == 0
        a_here = jnp.where(first, self.x, self.y)
        b_here = jnp.where(first, self.y, self.x)
        if "ring" in digit:
            at = sum(jnp.where(self.z == z, n, 0) for n, z in enumerate(RING))
            z = sum(jnp.where((at - digit["ring"]) % len(RING) == n, z, 0) for n, z in enumerate(RING))
        else:
            z = digit["z"] ^ self.z
        a = digit["a"] ^ a_here
        b = digit["b"] ^ b_here
        x, y = jnp.where(first, a, b), jnp.where(first, b, a)
        return numbered(z, x, y).astype(jnp.int32)


def after(value, *events):
    return lax.optimization_barrier((value,) + events)[0]


def fence(*values):
    return lax.optimization_barrier(values)


def smem():
    return pl.BlockSpec(memory_space=pltpu.SMEM)


def whole(shape):
    zeros = (0,) * len(shape)
    return pl.BlockSpec(tuple(shape), lambda *_: zeros)


def kernel_call(body, grid, ins, outs, scratch=(), flops=0, name=None, room=6):
    blocks = [(v[1].block_shape, v[0].dtype) for v in ins] + [(v[2].block_shape, v[1]) for v in outs]
    held = sum(2 * int(np.prod(shape)) * np.dtype(d).itemsize for shape, d in blocks if shape is not None)
    held += sum(int(np.prod(v.shape)) * np.dtype(v.dtype).itemsize for v in scratch)
    return pl.pallas_call(
        body,
        grid=grid,
        in_specs=[v[1] for v in ins],
        out_specs=[v[2] for v in outs],
        out_shape=[(pltpu.HBM if more else jax.ShapeDtypeStruct)(s, d) for s, d, _, *more in outs],
        scratch_shapes=list(scratch),
        compiler_params=pltpu.CompilerParams(
            dimension_semantics=("arbitrary",) * len(grid), vmem_limit_bytes=held // 2 + room * MIB
        ),
        cost_estimate=pl.CostEstimate(flops=0, bytes_accessed=0, transcendentals=0),
        name=name,
    )(*[pltpu.with_memory_space_constraint(a, pltpu.HBM) if more else a for a, _, *more in ins])


ROWS = 512


def own_rows(steps, cols):
    return pl.BlockSpec((ROWS, cols), lambda i: (jnp.minimum(i, steps - 1), 0))


def partner_rows(steps, cols):
    return pl.BlockSpec((ROWS, cols), lambda i: (jnp.maximum(i - steps, 0), 0))


def pick_rows(i, steps, own_ref, partner_ref):
    return jnp.where(i < steps, own_ref[...], partner_ref[...])


def split_kernel(place, w_qkv, w_out, gains, biases, mine, send):
    first = place[0] == 0
    half = D // 2
    for n in range(4):
        source, start = (w_qkv, n * D) if n < 3 else (w_out, 0)
        low, high = source[:, start : start + half], source[:, start + half : start + D]
        mine[:, n * half : (n + 1) * half] = jnp.where(first, low, high)
        send[:, n * half : (n + 1) * half] = jnp.where(first, high, low)
    rows = jnp.concatenate([gains[...], biases[...]], axis=0).astype(F32)
    eye = jnp.where(
        lax.broadcasted_iota(jnp.int32, (128, rows.shape[0]), 0)
        == lax.broadcasted_iota(jnp.int32, (128, rows.shape[0]), 1),
        1.0,
        0.0,
    )
    norm_cols = contract_cols(rows.T.astype(BF16), eye.astype(BF16)).astype(BF16)
    mine[:, 4 * half :] = norm_cols
    send[:, 4 * half :] = norm_cols


def fill_blocks(table, pieces, weight, cols=slice(None)):
    count = pieces[0].shape[0]
    for n, piece in enumerate(pieces):
        for k in range(count):
            weight[table[n * count + k]] = piece[k, :, cols]


def qkv_kernel(steps, groups, pieces, table, own, partner, *refs):
    i = pl.program_id(0)
    parts = refs[:pieces]
    mixed_own, mixed_partner, weight, out_w, norms, table_t = refs[pieces:]
    cols, part = weight.shape[2], out_w.shape[2]
    tall = weight.shape[0] * weight.shape[1]

    @pl.when(i == 0)
    def _():
        fill_blocks(table, parts, weight, slice(0, cols))
        fill_blocks(table, parts, out_w, slice(cols, cols + part))
        fill_blocks(table, parts, table_t, slice(cols + part, None))
        norms[...] = table_t[...].reshape(tall, table_t.shape[2]).astype(F32).T[: norms.shape[0]]

    rows_here = pick_rows(i, steps, own, partner)
    for g in range(groups):
        span = slice(g * cols // groups, (g + 1) * cols // groups)
        tile = weight[:, :, span].reshape(tall, cols // groups)
        value = dot(rows_here, tile).astype(BF16)

        @pl.when(i < steps)
        def _():
            mixed_own[:, span] = value

        @pl.when(i >= steps)
        def _():
            mixed_partner[:, span] = value


def lane_masks():
    lane = lax.broadcasted_iota(jnp.int32, (1, PAIR), 1)
    return [lane < HEAD_DIM, lane >= HEAD_DIM]


def keep(mask, value):
    return jnp.where(mask, value, jnp.zeros_like(value))


def fill_distance(distance):
    row = lax.broadcasted_iota(jnp.int32, distance.shape, 0)
    col = lax.broadcasted_iota(jnp.int32, distance.shape, 1)
    distance[...] = jnp.abs(row - col).astype(F32)


def scores_of(queries, keys, slope, distance):
    raw = lax.dot_general(queries, keys, (((1,), (1,)), ((), ())), preferred_element_type=F32)
    return raw - slope * distance


def tiles(value, tall):
    return [value[n : n + tall] for n in range(0, value.shape[0], tall)]


def pair_cols(part, pair):
    return pl.ds(pl.multiple_of(part * (D // 2) + pair * PAIR, PAIR), PAIR)


def attend_kernel(place, flags, slopes, mixed, *refs):
    context, logs, distance = refs[-3:]
    masks = lane_masks()
    scale = HEAD_DIM**-0.5
    lane = lax.broadcasted_iota(jnp.int32, (1, 128), 1)
    fill_distance(distance)
    for extra in refs[:-3]:
        context[LONG:, :] = extra[...].reshape(context.shape[0] - LONG, context.shape[1])

    def run(is_long):
        tall = 2 * SHORT if is_long else LONG

        def one_pair(pair, _):
            q_all, k_all, v_all = (mixed[:, pair_cols(part, pair)] for part in range(3))
            totals = [0.0] * (LONG // tall)
            mine = (lambda v: [v]) if is_long else (lambda v: tiles(v, SHORT))
            jobs = []
            for head in range(2):
                slope = slopes[pair * 2 + head]
                q = (keep(masks[head], q_all) * scale).astype(BF16)
                v = keep(masks[head], v_all)
                for n in range(LONG // tall):
                    rows = slice(n * tall, (n + 1) * tall)
                    away = distance[rows, :] if is_long else distance[:SHORT, :SHORT]
                    s = [scores_of(a, b, slope, away) for a, b in zip(mine(q[rows]), mine(k_all))]
                    jobs.append((head, n, jnp.concatenate(s, axis=0), v))
            done = []
            for head, n, s, v in jobs:
                top = jnp.max(s, axis=-1, keepdims=True)
                e = jnp.exp(s - top)
                norm = jnp.sum(e, axis=-1, keepdims=True)
                done.append(((e * (1.0 / norm)).astype(BF16), top + jnp.log(norm)))
            for (head, n, s, v), (p, log) in zip(jobs, done):
                totals[n] = totals[n] + jnp.concatenate([dot(a, b) for a, b in zip(mine(p), mine(v))], axis=0)
                rows = slice(n * tall, (n + 1) * tall)
                logs[rows, :] = jnp.where(lane == pair * 2 + head, log, logs[rows, :])
            for n in range(LONG // tall):
                context[n * tall : (n + 1) * tall, pair_cols(0, pair)] = totals[n].astype(BF16)
            return 0

        lax.fori_loop(0, D // 2 // PAIR, one_pair, 0)

    logs[...] = jnp.zeros_like(logs)
    flag = flags[place[1]]

    @pl.when(flag > 0)
    def _():
        run(True)

    @pl.when(flag <= 0)
    def _():
        run(False)


def attend_back_kernel(place, flags, slopes, mixed, logs_ref, d_context, d_query, d_key, d_value, distance):
    masks = lane_masks()
    scale = HEAD_DIM**-0.5
    fill_distance(distance)

    def run(is_long):
        tall = 2 * SHORT if is_long else LONG
        logs = logs_ref[...]
        lane = lax.broadcasted_iota(jnp.int32, (1, 128), 1)

        def one_pair(pair, _):
            q_all, k_all, v_all = (mixed[:, pair_cols(part, pair)] for part in range(3))
            d_all = d_context[:, pair_cols(0, pair)]
            d_q, d_k, d_v = [0.0] * (LONG // tall), 0.0, 0.0
            group = SHORT if not is_long else tall
            jobs = []
            for head in range(2):
                slope = slopes[pair * 2 + head]
                q = (keep(masks[head], q_all) * scale).astype(BF16)
                k = (keep(masks[head], k_all) * scale).astype(BF16)
                d_c = keep(masks[head], d_all)
                log_all = jnp.sum(jnp.where(lane == pair * 2 + head, logs, 0.0), axis=-1, keepdims=True)
                for n in range(LONG // tall):
                    rows = slice(n * tall, (n + 1) * tall)
                    jobs.append((n, slope, q[rows], k, d_c[rows], log_all[rows], distance[rows, :] if is_long else distance[:SHORT, :SHORT]))
            mine = (lambda v: [v]) if is_long else (lambda v: tiles(v, SHORT))
            raw = []
            for n, slope, q, k, d_c, log_rows, away in jobs:
                s = jnp.concatenate([scores_of(a, b, slope, away) for a, b in zip(mine(q), mine(k_all))], axis=0)
                d_p = jnp.concatenate([contract_cols(a, b) for a, b in zip(mine(d_c), mine(v_all))], axis=0)
                raw.append((s, d_p))
            done = []
            for (n, slope, q, k, d_c, log_rows, away), (s, d_p) in zip(jobs, raw):
                p = jnp.exp(s - log_rows)
                d_s = (p * (d_p - jnp.sum(p * d_p, axis=-1, keepdims=True))).astype(BF16)
                done.append((d_s, p.astype(BF16)))
            for (n, slope, q, k, d_c, log_rows, away), (d_s, p) in zip(jobs, done):
                d_q[n] = d_q[n] + jnp.concatenate([dot(a, b) for a, b in zip(mine(d_s), mine(k))], axis=0)
                d_k = d_k + jnp.concatenate([dot(a.T, b) for a, b in zip(mine(q), mine(d_s))], axis=1)
                d_v = d_v + jnp.concatenate([dot(a.T, b) for a, b in zip(mine(d_c), mine(p))], axis=1)
            cols = pair_cols(0, pair)
            for n in range(LONG // tall):
                d_query[n * tall : (n + 1) * tall, cols] = d_q[n].astype(BF16)
            d_key[:, cols] = d_k.T.astype(BF16)
            d_value[:, cols] = d_v.T.astype(BF16)
            return 0

        lax.fori_loop(0, D // 2 // PAIR, one_pair, 0)

    flag = flags[place[1]]

    @pl.when(flag > 0)
    def _():
        run(True)

    @pl.when(flag <= 0)
    def _():
        run(False)


def spread(rows):
    center = jnp.mean(rows, axis=-1, keepdims=True)
    shifted = rows - center
    inverse = lax.rsqrt(jnp.mean(shifted * shifted, axis=-1, keepdims=True) + 1e-05)
    return shifted * inverse, inverse


def norm_back(e, unit, inverse):
    mean_e = jnp.mean(e, axis=-1, keepdims=True)
    mean_en = jnp.mean(e * unit, axis=-1, keepdims=True)
    return (e - mean_e - unit * mean_en) * inverse


def first_norm_kernel(place, tokens, ctx_mine, ctx_other, w_mine, w_other_rows, norms, unit, inverse, low):
    core = place[0]
    half = w_mine.shape[0] // 2
    wide = w_mine.shape[2]

    def branch(weight):
        return dot(ctx_mine[...], weight(core)) + dot(ctx_other[...], weight(1 - core))

    mine = branch(lambda c: w_mine[pl.ds(c * half, half)].reshape(D // 2, wide))
    other = branch(lambda c: w_other_rows[pl.ds(pl.multiple_of(LONG + c * (D // 2), 128), D // 2), :])
    first = core == 0
    added = jnp.concatenate([jnp.where(first, mine, other), jnp.where(first, other, mine)], axis=1)
    n, inv = spread(tokens[...].astype(F32) + added)
    unit[...] = n
    inverse[...] = inv
    low[...] = (n * norms[0:1, :] + norms[2:3, :]).astype(BF16)


def gelu_parts(x):
    phi = 0.5 + 0.5 * lax.erf(x * 0.5**0.5)
    return x * phi, phi + x * jnp.exp(-0.5 * (x * x)) * 0.3989422804014327


def columns_of(weight, half, span):
    count = weight.shape[0] // 2
    return weight[half * count : (half + 1) * count, :, span].reshape(D, span.stop - span.start)


def gate_kernel(steps, pieces, table, own, partner, *refs):
    i = pl.program_id(0)
    active, slope, gate_w = refs[pieces:]

    @pl.when(i == 0)
    def _():
        fill_blocks(table, refs[:pieces], gate_w)

    rows = pick_rows(i, steps, own, partner)
    width = gate_w.shape[2]
    for half in range(2):
        for start in range(0, width, 256):
            out = slice(half * width + start, half * width + start + 256)
            gate = dot(rows, columns_of(gate_w, half, slice(start, start + 256)))
            act, grad = gelu_parts(gate)
            active[:, out] = act.astype(BF16)
            slope[:, out] = grad.astype(BF16)


def value_kernel(steps, pieces, table, own, partner, active, slope, *refs):
    i = pl.program_id(0)
    product, scaled, value_w = refs[pieces:]

    @pl.when(i == 0)
    def _():
        fill_blocks(table, refs[:pieces], value_w)

    rows = pick_rows(i, steps, own, partner)
    width = value_w.shape[2]
    for half in range(2):
        for start in range(0, width, 256):
            out = slice(half * width + start, half * width + start + 256)
            up = dot(rows, columns_of(value_w, half, slice(start, start + 256)))
            product[:, out] = (active[:, out].astype(F32) * up).astype(BF16)
            scaled[:, out] = (slope[:, out].astype(F32) * up).astype(BF16)


def times_down(product, down_w):
    width = down_w.shape[2]
    total = 0.0
    for half in range(2):
        part = product[:, half * width : (half + 1) * width]
        total = total + contract_cols(part, columns_of(down_w, half, slice(0, width)))
    return total


def down_first_kernel(table, product, *refs):
    partner, down_w = refs[-2:]

    @pl.when(pl.program_id(0) == 0)
    def _():
        fill_blocks(table, refs[:-2], down_w)

    partner[...] = times_down(product, down_w).astype(BF16)


def down_kernel(product, down_w, own):
    own[...] = times_down(product, down_w)


def second_norm_kernel(unit_one, norms, part_own, part_got, cotangent, out, d_z, d_ffn, sums):
    normed = unit_one[...] * norms[0:1, :] + norms[2:3, :]
    n, inv = spread(normed + (part_own[...] + part_got[...].astype(F32)))
    gain = norms[1:2, :]
    out[...] = (n * gain + norms[3:4, :]).astype(BF16)
    c = cotangent[...].astype(F32)
    back = norm_back(gain * c, n, inv)
    d_z[...] = back
    d_ffn[...] = back.astype(BF16)
    add_sums(sums, c * n, c)


def add_sums(sums, gain_terms, bias_terms):
    @pl.when(pl.program_id(0) == 0)
    def _():
        sums[...] = jnp.zeros_like(sums)

    sums[0:1, :] += jnp.sum(gain_terms, axis=0, keepdims=True)
    sums[1:2, :] += jnp.sum(bias_terms, axis=0, keepdims=True)


def ffn_back_kernel(
    steps, own, partner, down_w, gate_w, value_w, active, slope, d_gate, d_up, back_own, back_partner
):
    i = pl.program_id(0)
    rows = pick_rows(i, steps, own, partner)
    width = down_w.shape[2]
    for half in range(2):
        for start in range(0, width, 256):
            span = slice(start, start + 256)
            out = slice(half * width + start, half * width + start + 256)
            d_product = dot(rows, columns_of(down_w, half, span))
            d_gate[:, out] = (d_product * slope[:, out].astype(F32)).astype(BF16)
            d_up[:, out] = (d_product * active[:, out].astype(F32)).astype(BF16)
    total = 0.0
    for half in range(2):
        out = slice(half * width, (half + 1) * width)
        span = slice(0, width)
        total = total + contract_cols(d_gate[:, out], columns_of(gate_w, half, span))
        total = total + contract_cols(d_up[:, out], columns_of(value_w, half, span))

    @pl.when(i < steps)
    def _():
        back_own[...] = total

    @pl.when(i >= steps)
    def _():
        back_partner[...] = total.astype(BF16)


def weight_grad_kernel(table, left_own, left_partner, right_a, right_b, *refs):
    i = pl.program_id(0)
    parts, blocks = refs[:-1], refs[-1]
    rows = left_own.shape[0]
    count, tall, cols = blocks.shape
    for half, right in enumerate((right_a, right_b)):
        value = contract_rows(left_own[...], right[:rows, :]) + contract_rows(left_partner[...], right[rows:, :])
        value = value.astype(BF16).reshape(count // 2, tall, cols)
        blocks[half * (count // 2) : (half + 1) * (count // 2)] = value
    span = pl.ds(pl.multiple_of(i * cols, cols), cols)
    each = count // len(parts)
    for k in range(count):
        parts[k // each][k % each, :, span] = blocks[table[k]]


def first_norm_back_kernel(
    place,
    unit_ref,
    inverse,
    norms,
    d_z,
    part_own,
    part_got,
    ctx_mine,
    ctx_other,
    w_mine,
    w_other,
    d_hidden,
    dctx_mine,
    dctx_other,
    grad_keep,
    grad_send,
    sums,
    grad,
):
    core = place[0]
    first = core == 0
    unit = unit_ref[...]
    d_normed = d_z[...] + (part_own[...] + part_got[...].astype(F32))
    back = norm_back(norms[0:1, :] * d_normed, unit, inverse[...])
    low = back.astype(BF16)
    d_hidden[...] = back
    add_sums(sums, d_normed * unit, d_normed)
    half, wide = w_mine.shape[0] // 2, w_mine.shape[2]
    low_mine = jnp.where(first, low[:, :wide], low[:, wide:])
    low_other = jnp.where(first, low[:, wide:], low[:, :wide])
    for head_core, out in ((core, dctx_mine), (1 - core, dctx_other)):
        near = w_mine[pl.ds(head_core * half, half)].reshape(D // 2, wide)
        far = w_other[pl.ds(pl.multiple_of(LONG + head_core * (D // 2), 128), D // 2), :]
        out[...] = (contract_cols(low_mine, near) + contract_cols(low_other, far)).astype(BF16)

    @pl.when(pl.program_id(0) == 0)
    def _():
        grad[...] = jnp.zeros_like(grad)

    shape = (half,) + grad.shape[1:]
    grad[pl.ds(core * half, half)] += contract_rows(ctx_mine[...], low).reshape(shape)
    grad[pl.ds((1 - core) * half, half)] += contract_rows(ctx_other[...], low).reshape(shape)

    @pl.when(pl.program_id(0) == pl.num_programs(0) - 1)
    def _():
        left, right = grad[:, :, :wide], grad[:, :, wide:]
        grad_keep[...] = jnp.where(first, left, right)
        grad_send[...] = jnp.where(first, right, left).astype(BF16)


def qkv_grad_kernel(table, left_own, left_partner, *refs):
    d_own, d_partner = refs[:3], refs[3:6]
    out_grad, sums_one, sums_two, near, far, blocks, norm_grad = refs[6:]
    i = pl.program_id(0)
    count, tall, cols = blocks.shape

    @pl.when(i == 0)
    def _():
        one, two = sums_one[...], sums_two[...]
        empty = jnp.zeros((norm_grad.shape[2] - 4, D), F32)
        stacked = jnp.concatenate([one[0:1], two[0:1], one[1:2], two[1:2], empty], axis=0)
        norm_grad[...] = stacked.T.astype(BF16).reshape(norm_grad.shape)

    for g in range(3):

        @pl.when(i == g)
        def _():
            value = contract_rows(left_own[...], d_own[g][...]) + contract_rows(left_partner[...], d_partner[g][...])
            blocks[...] = value.astype(BF16).reshape(blocks.shape)
            for k in range(count):
                target, place = (near if k < count // 2 else far), table[k]
                target[k % (count // 2), :, g * cols : (g + 1) * cols] = blocks[place]
                if g == 0:
                    start = 3 * cols
                    for more in (out_grad, norm_grad):
                        stop = start + more.shape[2]
                        target[k % (count // 2), :, start:stop] = more[place]
                        start = stop


def input_grad_kernel(d_query, d_key, d_value, weight, *refs):
    cols = d_query.shape[1]
    total = 0.0
    for g, left in enumerate((d_query, d_key, d_value)):
        tile = weight[:, :, g * cols : (g + 1) * cols].reshape(D, cols)
        total = total + contract_cols(left[...], tile)
    for more in refs[:-1]:
        total = total + more[...].astype(F32)
    refs[-1][...] = total.astype(refs[-1].dtype)


def pieces_kernel(place, here, there, got, qkv, out, gains, biases):
    first, own = place[0] == 0, place[1] == 1
    half = D // 2
    mine = jnp.where(own, here[...], there[...])
    for n in range(4):
        a, b = mine[:, n * half : (n + 1) * half].astype(F32), got[:, n * half : (n + 1) * half].astype(F32)
        target, start = (qkv, n * D) if n < 3 else (out, 0)
        target[:, start : start + half] = jnp.where(first, a, b)
        target[:, start + half : start + D] = jnp.where(first, b, a)
    rows = (mine[:, 4 * half :].astype(F32) + got[:, 4 * half :].astype(F32)).T
    gains[...] = rows[0:2]
    biases[...] = rows[2:4]


def by_core(core, mine, other, axis):
    first = core == 0
    return jnp.stack([jnp.where(first, mine, other), jnp.where(first, other, mine)], axis=axis)


def half_of(core, halves, axis):
    zero, one = (lax.index_in_dim(halves, k, axis, keepdims=False) for k in range(2))
    first = core == 0
    return jnp.where(first, zero, one), jnp.where(first, one, zero)


def plane_shards(
    wide,
    narrow,
    tokens,
    w_qkv,
    w_out,
    w_gate,
    w_value,
    w_down,
    norm_gains,
    norm_biases,
    long_count,
    cotangent,
):
    plane = Plane(wide, narrow)
    swap = plane.swap
    core, y_here = plane.core, plane.y
    rows = tokens.shape[0]
    steps = rows // ROWS
    tall = w_qkv.shape[0]
    blocks = wide * narrow // 2
    z_size = plane.size["z"]
    head_cols = D // 2
    width = w_gate.shape[1] // 2
    hidden = 2 * width
    pairs = head_cols // PAIR
    qkv_to = plane.tables(("z", "a", "b"), lambda z, x, y: (z * 2 + x) * 2 + y)
    ffn_to = plane.tables(("z", "a", "b"), lambda z, x, y: y * (2 * z_size) + z * 2 + x)
    back_to = plane.tables(("a", "z", "b"), lambda z, x, y: y * (2 * z_size) + z * 2 + x)
    down_to = plane.tables(("a", "b", "ring"), lambda z, x, y: y * (2 * z_size) + z * 2 + x)
    place = jnp.reshape(core, (1,)).astype(jnp.int32)
    first = core == 0

    def wholes(arrays):
        return [(v, whole(v.shape)) for v in arrays]

    def far(entries):
        return [entry + (True,) for entry in entries]

    def step_rows(cols):
        return pl.BlockSpec((ROWS, cols), lambda i: (i, 0))

    head_shape = (tall, 4 * head_cols + 128)
    head_part, head_send = kernel_call(
        split_kernel,
        (1,),
        [(place, smem())] + far(wholes([w_qkv, w_out, norm_gains, norm_biases])),
        [(head_shape, BF16, whole(head_shape))] * 2,
        name="split",
    )
    flag = jnp.broadcast_to(long_count.astype(F32), (8, 128))
    head_got, flag_got = fence(swap(head_send, "core"), swap(flag, "core"))
    head_part = jnp.where(y_here == core, head_part, head_got)
    head_parts = [head_part] + [swap(head_part, "z", k) for k in range(1, z_size)]
    ffn_parts = [after(w_gate, head_part), w_value, w_down.T]
    ffn_other = jnp.concatenate([jnp.where(first, v[:, width:], v[:, :width]) for v in ffn_parts], axis=1)
    ffn_got = swap(ffn_other, "core")
    flags = jnp.stack([long_count[0, 0], flag_got[0, 0].astype(jnp.int32)])
    slopes = lax.dynamic_slice_in_dim(alibi_slopes(HEADS), core * (HEADS // 2), HEADS // 2)

    def ffn_chip(n):
        v, got = ffn_parts[n], ffn_got[:, n * width : (n + 1) * width]
        mine = jnp.where(first, v[:, :width], v[:, width:])
        return jnp.concatenate([jnp.where(first, mine, got), jnp.where(first, got, mine)], axis=0)

    def doubled(value, step, *events):
        got = swap(value, "z", step)
        return jnp.concatenate(lax.optimization_barrier((value, got) + events)[:2], axis=0)

    def along_plane(held):
        near = swap(held, "a")
        return held, near, swap(held, "b")

    def joined(value, got):
        return jnp.concatenate([value, got], axis=0)

    gate_one, value_one, down_one = (ffn_chip(n)[None] for n in range(3))
    gate_got = swap(gate_one, "z", 1)
    down_got = swap(down_one, "a")
    *head_parts, gate_got, down_got = fence(*head_parts, gate_got, down_got)
    qkv_z = jnp.stack(head_parts)
    gate_two, down_two = joined(gate_one, gate_got), joined(down_one, down_got)

    head_near, head_far = swap(qkv_z, "a"), swap(qkv_z, "b")
    gate_got = swap(gate_two, "z", 2)
    value_got = swap(after(value_one, qkv_z), "z", 1)
    tokens_other = swap(after(tokens, qkv_z), "core")
    head_near, head_far, gate_got, value_got, tokens_other = fence(head_near, head_far, gate_got, value_got, tokens_other)
    gate_z, value_two = joined(gate_two, gate_got), joined(value_one, value_got)

    head_last = swap(head_near, "b")
    down_got = swap(after(down_two, head_near), "b")
    gate_near = swap(gate_z, "a")
    value_got = swap(value_two, "z", 2)
    head_last, down_got, gate_near, value_got = fence(head_last, down_got, gate_near, value_got)
    value_z, down_four = joined(value_two, value_got), joined(down_two, down_got)
    qkv_blocks = [qkv_z, head_near, head_far, head_last]

    gate_far, gate_last = swap(after(gate_z, head_last), "b"), swap(gate_near, "b")
    ring_one = swap(down_four, "next")
    block_row = (blocks, tall)
    mixed_own, mixed_partner, qkv_w, out_mine, norms = kernel_call(
        functools.partial(qkv_kernel, steps, 3, len(qkv_blocks)),
        (2 * steps,),
        [(qkv_to, smem())]
        + far([(tokens, own_rows(steps, D)), (tokens_other, partner_rows(steps, D))] + wholes(qkv_blocks)),
        far(
            [((rows, 3 * head_cols), BF16, own_rows(steps, 3 * head_cols))]
            + [((rows, 3 * head_cols), BF16, partner_rows(steps, 3 * head_cols))]
            + [(block_row + (n,), BF16, whole(block_row + (n,))) for n in (3 * head_cols, head_cols)]
        )
        + [((8, D), F32, whole((8, D)))],
        scratch=[pltpu.VMEM(block_row + (128,), BF16)],
        flops=2 * 2 * rows * D * 3 * head_cols,
        name="mixed",
    )
    def attend(block, mixed, extra=()):
        tall_out = rows + sum(v.size for v in extra) // head_cols
        return kernel_call(
            attend_kernel,
            (1,),
            [(jnp.array([0, block], jnp.int32), smem()), (flags, smem()), (slopes, smem())]
            + far(wholes([mixed, *extra])),
            [((tall_out, head_cols), BF16, whole((tall_out, head_cols))), ((rows, 128), F32, whole((rows, 128)), True)],
            scratch=[pltpu.VMEM((LONG, LONG), F32)],
            flops=4 * rows * LONG * D,
            name="attend",
            room=12,
        )

    ctx_send, logs_partner = attend(1, mixed_partner, [out_mine])
    gate_far, gate_last, ring_one, ctx_send = fence(gate_far, gate_last, ring_one, ctx_send)

    value_near, value_far = swap(value_z, "a"), swap(value_z, "b")
    ring_two = swap(ring_one, "next")
    ctx_got = swap(ctx_send, "core")
    ctx_mine, logs_own = attend(0, after(mixed_own, ctx_send))

    unit_one, inverse_one, low = kernel_call(
        first_norm_kernel,
        (steps,),
        [
            (place, smem()),
            (tokens, step_rows(D)),
            (ctx_mine, step_rows(head_cols)),
            (ctx_got, step_rows(head_cols)),
        ]
        + wholes([out_mine, ctx_got, norms]),
        [
            ((rows, D), F32, step_rows(D)),
            ((rows, 1), F32, step_rows(1)),
            ((rows, D), BF16, step_rows(D)),
        ],
        flops=2 * rows * D * D,
        name="first_norm",
    )
    value_near, low = fence(value_near, low)
    gate_blocks = [gate_z, gate_near, gate_far, gate_last]
    value_last = swap(value_near, "b")
    ring_three = swap(ring_two, "next")
    low_other = swap(low, "core")

    w_shape = (blocks, 2 * tall, width)
    both_rows = [(low, own_rows(steps, D)), (low_other, partner_rows(steps, D))]
    active, slope, gate_w = kernel_call(
        functools.partial(gate_kernel, steps, len(gate_blocks)),
        (2 * steps,),
        [(ffn_to, smem())] + both_rows + far(wholes(gate_blocks)),
        [((2 * rows, hidden), BF16, step_rows(hidden))] * 2 + [(w_shape, BF16, whole(w_shape))],
        name="gate",
    )
    value_last, active = fence(value_last, active)
    value_blocks = [value_z, value_near, value_far, value_last]
    down_blocks = [down_four, ring_one, ring_two, ring_three]
    product, slope, value_w = kernel_call(
        functools.partial(value_kernel, steps, len(value_blocks)),
        (2 * steps,),
        [(ffn_to, smem())] + both_rows + [(active, step_rows(hidden)), (slope, step_rows(hidden))] + wholes(value_blocks),
        [((2 * rows, hidden), BF16, step_rows(hidden))] * 2 + [(w_shape, BF16, whole(w_shape))],
        name="value",
    )
    part_send, down_w = kernel_call(
        down_first_kernel,
        (steps,),
        [(down_to, smem()), (product, pl.BlockSpec((ROWS, hidden), lambda i: (i + steps, 0)))] + wholes(down_blocks),
        [((rows, D), BF16, step_rows(D)), (w_shape, BF16, whole(w_shape))],
        name="down_first",
    )
    (part_own,) = kernel_call(
        down_kernel,
        (steps,),
        [(product, step_rows(hidden))] + wholes([down_w]),
        [((rows, D), F32, step_rows(D))],
        name="down",
    )
    part_got = swap(part_send, "core")
    layer_out, d_z, d_ffn, sums_two = kernel_call(
        second_norm_kernel,
        (steps,),
        [(unit_one, step_rows(D))]
        + wholes([norms])
        + [(part_own, step_rows(D)), (part_got, step_rows(D)), (cotangent, step_rows(D))],
        [
            ((rows, D), BF16, step_rows(D)),
            ((rows, D), F32, step_rows(D)),
            ((rows, D), BF16, step_rows(D)),
            ((8, D), F32, whole((8, D))),
        ],
        name="second_norm",
    )
    d_ffn_other = swap(d_ffn, "core")

    def weight_grad(left, left_other, right, to, parts):
        part = (blocks // parts, 2 * tall, width)
        cols = width // 3
        return kernel_call(
            weight_grad_kernel,
            (3,),
            [
                (to, smem()),
                (left, whole((rows, D))),
                (left_other, whole((rows, D))),
                (right, pl.BlockSpec((2 * rows, cols), lambda i: (0, i))),
                (right, pl.BlockSpec((2 * rows, cols), lambda i: (0, 3 + i))),
            ],
            [(part, BF16, whole(part))] * parts,
            scratch=[pltpu.VMEM((blocks, 2 * tall, cols), BF16)],
            flops=2 * 2 * rows * D * hidden,
            name="weight_grad",
        )

    def added(keep, got):
        return (keep.astype(F32) + got.astype(F32)).astype(BF16)

    def halves(keep, got):
        count = keep.shape[0] // 2
        return added(keep[:count], got[:count]), added(keep[count:], got[count:])

    def quarters(keep, got):
        return [added(keep[k], got[k]) for k in range(z_size)]

    down_parts = weight_grad(d_ffn, d_ffn_other, product, back_to, 2)
    d_gate, d_up, back_own, back_send = kernel_call(
        functools.partial(ffn_back_kernel, steps),
        (2 * steps,),
        [(after(d_ffn, down_parts[-1]), own_rows(steps, D)), (d_ffn_other, partner_rows(steps, D))]
        + wholes([down_w, gate_w, value_w])
        + [(active, step_rows(hidden)), (slope, step_rows(hidden))],
        [((2 * rows, hidden), BF16, step_rows(hidden))] * 2
        + [((rows, D), F32, own_rows(steps, D)), ((rows, D), BF16, partner_rows(steps, D))],
        flops=3 * 2 * 2 * rows * D * hidden,
        name="ffn_back",
    )
    down_got = swap(down_parts[1], "b")
    gate_keep, gate_send = weight_grad(after(low, back_send), low_other, d_gate, ffn_to, 2)
    back_send, gate_send = fence(back_send, gate_send)

    gate_got = swap(gate_send, "b")
    down_z = [added(down_parts[0][2 * k : 2 * k + 2], down_got[2 * k : 2 * k + 2]) for k in range(z_size)]
    down_got = swap(down_z[3], "z", 2)
    back_got = swap(back_send, "core")
    value_keep, value_send = weight_grad(after(low, gate_send), low_other, d_up, ffn_to, 2)
    value_got = swap(value_send, "b")
    back_got = after(back_got, value_send)
    d_hidden, dctx_mine, dctx_send, out_keep, out_send, sums_one = kernel_call(
        first_norm_back_kernel,
        (steps,),
        [
            (place, smem()),
            (unit_one, step_rows(D)),
            (inverse_one, step_rows(1)),
            (norms, whole(norms.shape)),
            (d_z, step_rows(D)),
            (back_own, step_rows(D)),
            (back_got, step_rows(D)),
            (ctx_mine, step_rows(head_cols)),
            (ctx_got, step_rows(head_cols)),
        ]
        + wholes([out_mine, ctx_got]),
        [
            ((rows, D), F32, step_rows(D)),
            ((rows, head_cols), BF16, step_rows(head_cols)),
            ((rows, head_cols), BF16, step_rows(head_cols)),
            (out_mine.shape, F32, whole(out_mine.shape)),
            (out_mine.shape, BF16, whole(out_mine.shape)),
            ((8, D), F32, whole((8, D))),
        ],
        scratch=[pltpu.VMEM((blocks, tall, D), F32)],
        flops=2 * 2 * rows * D * D,
        name="first_norm_back",
    )
    def attend_back(block, mixed, d_context, logs):
        return kernel_call(
            attend_back_kernel,
            (1,),
            [(jnp.array([0, block], jnp.int32), smem()), (flags, smem()), (slopes, smem())]
            + far(wholes([mixed, logs]))
            + wholes([d_context]),
            [((rows, head_cols), BF16, whole((rows, head_cols)))] * 3,
            scratch=[pltpu.VMEM((LONG, LONG), F32)],
            name="attend_back",
            room=16,
        )

    d_own = attend_back(0, mixed_own, dctx_mine, logs_own)
    down_got, gate_got, dctx_send, out_send, d_first = fence(down_got, gate_got, dctx_send, out_send, d_own[0])
    d_own = [d_first, *d_own[1:]]
    dctx_got, out_got = swap(dctx_send, "core"), swap(out_send, "core")
    gate_keep, gate_send = halves(gate_keep, gate_got)
    down_send = added(down_z[1], down_got)
    gate_got = swap(gate_send, "a")
    down_got = swap(after(down_z[2], gate_send), "z", 2)
    out_sum = (out_keep + out_got.astype(F32)).astype(BF16)

    d_partner = attend_back(1, mixed_partner, after(dctx_got, gate_send, down_send), logs_partner)
    grad_shape = (blocks // 2, tall, 4 * head_cols + 128)
    head_keep, head_send = kernel_call(
        qkv_grad_kernel,
        (3,),
        [(qkv_to, smem())]
        + wholes([tokens, tokens_other, *d_own, *d_partner, out_sum, sums_one, sums_two]),
        [(grad_shape, BF16, whole(grad_shape))] * 2,
        scratch=[pltpu.VMEM(block_row + (head_cols,), BF16), pltpu.VMEM(block_row + (128,), BF16)],
        name="qkv_grad",
    )
    down_got, gate_got, head_send = fence(down_got, gate_got, head_send)
    head_got = swap(head_send, "b")
    gate_keep, gate_send = halves(gate_keep, gate_got)
    value_keep, value_send = halves(value_keep, value_got)

    value_got = swap(value_send, "a")
    gate_got = swap(gate_send, "z", 2)
    down_keep = added(down_z[0], down_got)
    down_got = swap(down_send, "z", 1)

    def input_part(d_parts, more, dtype):
        return kernel_call(
            input_grad_kernel,
            (steps,),
            [(v, step_rows(head_cols)) for v in d_parts] + wholes([qkv_w]) + [(v, step_rows(D)) for v in more],
            [((rows, D), dtype, step_rows(D))],
            name="input_grad",
        )[0]

    in_send = input_part([after(d_partner[0], value_send, gate_send), *d_partner[1:]], [], BF16)
    head_got, gate_got, down_got, in_send = fence(head_got, gate_got, down_got, in_send)
    head_keep, head_send = halves(head_keep, head_got)
    value_keep, value_send = halves(value_keep, value_got)
    gate_keep, gate_send = halves(gate_keep, gate_got)
    down_keep, down_send = halves(down_keep, down_got)

    in_got = swap(in_send, "core")
    gate_got = swap(gate_send, "z", 1)
    down_got = swap(down_send, "a")
    head_got = swap(head_send, "a")
    value_got = swap(value_send, "z", 2)
    input_grad = input_part([after(d_own[0], head_send, value_send), *d_own[1:]], [d_hidden, in_got], F32)
    head_got, input_grad = fence(head_got, input_grad)
    head_parts = quarters(head_keep, head_got)
    value_got = after(value_got, *head_parts)
    value_keep, value_send = halves(value_keep, value_got)
    value_got = swap(value_send, "z", 1)

    head_got = [swap(head_parts[k], "z", k) for k in range(1, z_size)]
    value_got, gate_got, down_got, *head_got = fence(value_got, gate_got, down_got, *head_got)
    head_sum = head_parts[0].astype(F32)
    for part in head_got:
        head_sum = head_sum + part.astype(F32)
    head_sum = head_sum.astype(BF16)
    there = swap(head_sum, "y")
    gate_sum = added(gate_keep[0], gate_got[0])
    grads = [gate_sum, added(value_keep[0], value_got[0]), added(down_keep[0], down_got[0])]

    def in_order(mine, other):
        return [jnp.where(first, mine, other), jnp.where(first, other, mine)]

    kept = [half_of(core, total.reshape(2, tall, width), 0) for total in grads]
    ffn_got = swap(jnp.concatenate([other for _, other in kept], axis=0), "core")
    ffn_pieces = [
        jnp.concatenate(in_order(mine, ffn_got[n * tall : (n + 1) * tall]), axis=1).astype(F32)
        for n, (mine, _) in enumerate(kept)
    ]
    gate_piece, value_piece, down_piece = ffn_pieces[0], ffn_pieces[1], ffn_pieces[2].T
    there = after(there, gate_piece, value_piece, down_piece)
    own = y_here == core
    got = swap(jnp.where(own, there, head_sum), "core")
    qkv_piece, out_piece, gains_piece, biases_piece = kernel_call(
        pieces_kernel,
        (1,),
        [(jnp.stack([core, own.astype(jnp.int32)]), smem())] + wholes([head_sum, there, got]),
        [((tall, 3 * D), F32, whole((tall, 3 * D))), ((tall, D), F32, whole((tall, D)))]
        + [((2, tall), F32, whole((2, tall)))] * 2,
        name="pieces",
    )
    return (
        layer_out,
        input_grad,
        qkv_piece,
        out_piece,
        gate_piece,
        value_piece,
        down_piece,
        gains_piece,
        biases_piece,
    )


def solution(mesh):
    wide, narrow = mesh.shape["wide"], mesh.shape["narrow"]
    placed = (
        P(("wide", "narrow"), None),
        P("wide", None),
        P("wide", None),
        P("wide", "narrow"),
        P("wide", "narrow"),
        P("narrow", "wide"),
        P(None, "wide"),
        P(None, "wide"),
        P("wide", "narrow"),
        P(("wide", "narrow"), None),
    )
    if narrow == 2 and wide % 16 == 0 and D % (16 * wide) == 0:
        body = functools.partial(plane_shards, wide, narrow)
    else:
        body = general_shards
    return jax.shard_map(
        body,
        mesh=mesh,
        in_specs=placed,
        out_specs=(
            P(("wide", "narrow"), None),
            P(("wide", "narrow"), None),
            P("wide", None),
            P("wide", None),
            P("wide", "narrow"),
            P("wide", "narrow"),
            P("narrow", "wide"),
            P(None, "wide"),
            P(None, "wide"),
        ),
        check_vma=False,
    )
```

```python
import functools

import jax
import jax.numpy as jnp
import numpy as np
from jax import lax
from jax.experimental import pallas as pl
from jax.experimental.pallas import tpu as pltpu
from jax.sharding import PartitionSpec as P

D = 768
HEADS = 12
HEAD_DIM = 64
LONG = 512
SHORT = 128


def norm_rows(values, gain_row, bias_row):
    center = jnp.mean(values, axis=-1, keepdims=True)
    shifted = values - center
    spread = jnp.mean(shifted * shifted, axis=-1, keepdims=True)
    return shifted * lax.rsqrt(spread + 1e-05) * gain_row + bias_row


def gelu_product(gate_in, value_in):
    return jax.nn.gelu(gate_in, approximate=False) * value_in


def alibi_slopes(heads):
    power = 1 << heads.bit_length() - 1
    first = [2.0 ** (-8.0 * (index + 1) / power) for index in range(power)]
    second = [2.0 ** (-8.0 * (2 * index + 1) / (2 * power)) for index in range(heads - power)]
    return jnp.array(first + second, dtype=jnp.float32)


def alibi_bias(span, heads):
    position = jnp.arange(span)
    distance = jnp.abs(position[:, None] - position[None, :]).astype(jnp.float32)
    slopes = alibi_slopes(heads)
    return slopes[:, None, None] * distance


def block_scores(query_g, key_g, span):
    width = query_g.shape[-1]
    scores = jnp.einsum(
        "bqhd,bkhd->bhqk", query_g, key_g, preferred_element_type=jnp.float32
    ) * width ** (-0.5)
    return scores - alibi_bias(span, query_g.shape[2])


def attend(query_rows, key_rows, value_rows, span):
    rows, heads, width = query_rows.shape
    groups = rows // span
    shape_g = (groups, span, heads, width)
    query_g = query_rows.reshape(shape_g)
    key_g = key_rows.reshape(shape_g)
    value_g = value_rows.reshape(shape_g)
    scores = block_scores(query_g, key_g, span)
    top = jnp.max(scores, axis=-1, keepdims=True)
    expd = jnp.exp(scores - top)
    total = jnp.sum(expd, axis=-1, keepdims=True)
    probs_low = (expd / total).astype(jnp.bfloat16)
    context = jnp.einsum("bhqk,bkhd->bqhd", probs_low, value_g, preferred_element_type=jnp.float32)
    log_total = jnp.transpose((top + jnp.log(total))[..., 0], (0, 2, 1)).reshape(rows, heads)
    return (context.reshape(rows, heads * width), log_total)


def attend_back(query_rows, key_rows, value_rows, log_total, d_context, span):
    rows, heads, width = query_rows.shape
    groups = rows // span
    shape_g = (groups, span, heads, width)
    query_g = query_rows.reshape(shape_g)
    key_g = key_rows.reshape(shape_g)
    value_g = value_rows.reshape(shape_g)
    d_context_g = d_context.reshape(shape_g)
    lse_g = jnp.transpose(log_total.reshape(groups, span, heads), (0, 2, 1))
    scores = block_scores(query_g, key_g, span)
    probs = jnp.exp(scores - lse_g[..., None])
    probs_low = probs.astype(jnp.bfloat16)
    d_probs = jnp.einsum(
        "bqhd,bkhd->bhqk", d_context_g, value_g, preferred_element_type=jnp.float32
    )
    d_values = jnp.einsum(
        "bhqk,bqhd->bkhd", probs_low, d_context_g, preferred_element_type=jnp.float32
    )
    row_dot = jnp.sum(probs * d_probs, axis=-1, keepdims=True)
    d_scores = (probs * (d_probs - row_dot)).astype(jnp.bfloat16)
    scale = width ** (-0.5)
    d_queries = (
        jnp.einsum("bhqk,bkhd->bqhd", d_scores, key_g, preferred_element_type=jnp.float32) * scale
    )
    d_keys = (
        jnp.einsum("bhqk,bqhd->bkhd", d_scores, query_g, preferred_element_type=jnp.float32) * scale
    )
    return jnp.stack([d_queries, d_keys, d_values], axis=2).reshape(rows, 3, heads, width)


def contract_rows(left, right):
    return lax.dot_general(
        left, right, (((0,), (0,)), ((), ())), preferred_element_type=jnp.float32
    )


def contract_cols(left, right):
    return lax.dot_general(
        left, right, (((1,), (1,)), ((), ())), preferred_element_type=jnp.float32
    )


def general_shards(
    tokens, w_qkv, w_out, w_gate, w_value, w_down, norm_gains, norm_biases, long_count, cotangent
):
    gathered = (
        lax.all_gather(w_qkv, "wide", axis=0, tiled=True),
        lax.all_gather(w_out, "wide", axis=0, tiled=True),
        lax.all_gather(w_gate, "wide", axis=0, tiled=True),
        lax.all_gather(w_value, "wide", axis=0, tiled=True),
        lax.all_gather(w_down, "wide", axis=1, tiled=True),
        lax.all_gather(norm_gains, "wide", axis=1, tiled=True),
        lax.all_gather(norm_biases, "wide", axis=1, tiled=True),
    )
    full_qkv, full_out, wide_gate, wide_value, wide_down, gains_all, biases_all = gathered
    gains_f = gains_all.astype(jnp.float32)
    biases_f = biases_all.astype(jnp.float32)
    rows_dev = tokens.shape[0]
    n_blocks = rows_dev // LONG
    long_here = long_count[0, 0]
    tokens_f = tokens.astype(jnp.float32)
    mixed = jnp.dot(tokens, full_qkv, preferred_element_type=jnp.float32).astype(jnp.bfloat16)
    heads_view = mixed.reshape(n_blocks, LONG, 3, HEADS, HEAD_DIM)
    query_blk = heads_view[:, :, 0]
    key_blk = heads_view[:, :, 1]
    value_blk = heads_view[:, :, 2]
    block_ids = jnp.arange(n_blocks)

    def forward_block(entry):
        block_id, query_rows, key_rows, value_rows = entry
        return lax.cond(
            block_id < long_here,
            lambda operands: attend(operands[0], operands[1], operands[2], LONG),
            lambda operands: attend(operands[0], operands[1], operands[2], SHORT),
            (query_rows, key_rows, value_rows),
        )

    context_f, lse_rows = lax.map(forward_block, (block_ids, query_blk, key_blk, value_blk))
    context = context_f.reshape(rows_dev, D).astype(jnp.bfloat16)
    branch = jnp.dot(context, full_out, preferred_element_type=jnp.float32)
    hidden_in = tokens_f + branch
    normed = norm_rows(hidden_in, gains_f[0], biases_f[0])
    normed_low = normed.astype(jnp.bfloat16)
    all_rows = lax.all_gather(normed_low, "narrow", axis=0, tiled=True)
    gate = jnp.dot(all_rows, wide_gate, preferred_element_type=jnp.float32)
    value_up = jnp.dot(all_rows, wide_value, preferred_element_type=jnp.float32)
    product_f, pull_product = jax.vjp(gelu_product, gate, value_up)
    product = product_f.astype(jnp.bfloat16)
    ffn_out = lax.psum_scatter(
        jnp.dot(product, wide_down, preferred_element_type=jnp.float32),
        "narrow",
        scatter_dimension=0,
        tiled=True,
    )
    out_in = normed + ffn_out
    layer_out, pull_second = jax.vjp(norm_rows, out_in, gains_f[1], biases_f[1])
    d_out, d_gain_two, d_bias_two = pull_second(cotangent.astype(jnp.float32))
    d_ffn = d_out.astype(jnp.bfloat16)
    d_rows = lax.all_gather(d_ffn, "narrow", axis=0, tiled=True)
    grad_down = contract_rows(product, d_rows)
    d_product = contract_cols(d_rows, wide_down)
    d_gate, d_up = pull_product(d_product)
    d_gate_low = d_gate.astype(jnp.bfloat16)
    d_up_low = d_up.astype(jnp.bfloat16)
    grad_gate = contract_rows(all_rows, d_gate_low)
    grad_value = contract_rows(all_rows, d_up_low)
    d_normed = lax.psum_scatter(
        contract_cols(d_gate_low, wide_gate) + contract_cols(d_up_low, wide_value),
        "narrow",
        scatter_dimension=0,
        tiled=True,
    )
    d_normed_total = d_out + d_normed
    unused_out, pull_first = jax.vjp(norm_rows, hidden_in, gains_f[0], biases_f[0])
    d_hidden, d_gain_one, d_bias_one = pull_first(d_normed_total)
    d_branch = d_hidden.astype(jnp.bfloat16)
    grad_out = contract_rows(context, d_branch)
    d_context = contract_cols(d_branch, full_out).astype(jnp.bfloat16)
    d_context_blk = d_context.reshape(n_blocks, LONG, HEADS, HEAD_DIM)

    def backward_block(entry):
        block_id, query_rows, key_rows, value_rows, log_total, d_ctx = entry
        return lax.cond(
            block_id < long_here,
            lambda operands: attend_back(
                operands[0], operands[1], operands[2], operands[3], operands[4], LONG
            ),
            lambda operands: attend_back(
                operands[0], operands[1], operands[2], operands[3], operands[4], SHORT
            ),
            (query_rows, key_rows, value_rows, log_total, d_ctx),
        )

    d_mixed_f = lax.map(
        backward_block, (block_ids, query_blk, key_blk, value_blk, lse_rows, d_context_blk)
    )
    d_mixed = d_mixed_f.reshape(rows_dev, 3 * D).astype(jnp.bfloat16)
    grad_qkv = contract_rows(tokens, d_mixed)
    input_grad = d_hidden + contract_cols(d_mixed, full_qkv)
    grad_gains = jnp.stack([d_gain_one, d_gain_two])
    grad_biases = jnp.stack([d_bias_one, d_bias_two])
    pieces = (
        lax.psum_scatter(
            grad_qkv.astype(jnp.bfloat16), "wide", scatter_dimension=0, tiled=True
        ).astype(jnp.float32),
        lax.psum_scatter(
            grad_out.astype(jnp.bfloat16), "wide", scatter_dimension=0, tiled=True
        ).astype(jnp.float32),
        lax.psum_scatter(
            grad_gate.astype(jnp.bfloat16), "wide", scatter_dimension=0, tiled=True
        ).astype(jnp.float32),
        lax.psum_scatter(
            grad_value.astype(jnp.bfloat16), "wide", scatter_dimension=0, tiled=True
        ).astype(jnp.float32),
        lax.psum_scatter(
            grad_down.astype(jnp.bfloat16), "wide", scatter_dimension=1, tiled=True
        ).astype(jnp.float32),
        lax.psum_scatter(
            grad_gains.astype(jnp.bfloat16), "wide", scatter_dimension=1, tiled=True
        ).astype(jnp.float32),
        lax.psum_scatter(
            grad_biases.astype(jnp.bfloat16), "wide", scatter_dimension=1, tiled=True
        ).astype(jnp.float32),
    )
    qkv_piece, out_piece, gate_piece, value_piece, down_piece, gains_piece, biases_piece = pieces
    qkv_piece, out_piece, gains_piece, biases_piece = (
        lax.psum(qkv_piece.astype(jnp.bfloat16), "narrow").astype(jnp.float32),
        lax.psum(out_piece.astype(jnp.bfloat16), "narrow").astype(jnp.float32),
        lax.psum(gains_piece.astype(jnp.bfloat16), "narrow").astype(jnp.float32),
        lax.psum(biases_piece.astype(jnp.bfloat16), "narrow").astype(jnp.float32),
    )
    return (
        layer_out.astype(jnp.bfloat16),
        input_grad,
        qkv_piece,
        out_piece,
        gate_piece,
        value_piece,
        down_piece,
        gains_piece,
        biases_piece,
    )


AXES = ("wide", "narrow")
F32 = jnp.float32
BF16 = jnp.bfloat16
MIB = 1024 * 1024
RING = (0, 1, 3, 2)
PAIR = 2 * HEAD_DIM


def dot(left, right):
    return jnp.dot(left, right, preferred_element_type=F32)


class Plane:
    def __init__(self, wide, narrow):
        self.size = {"z": wide // 4, "ring": len(RING), "a": 2, "b": 2, "core": 2, "y": narrow}
        self.pairs = {}
        count = wide * narrow
        for dim, size in self.size.items():
            for step in range(1, size) if dim != "ring" else ():
                self.pairs[dim, step] = [(i, self.partner(i, dim, step)) for i in range(count)]
        after_z = {z: RING[(n + 1) % len(RING)] for n, z in enumerate(RING)}
        self.pairs["next", 1] = [(i, i % 8 + 8 * after_z[i // 8]) for i in range(count)]
        self.pairs["prev", 1] = [(j, i) for i, j in self.pairs["next", 1]]
        w = lax.axis_index("wide")
        self.z, self.x, self.core = w // 4, (w // 2) % 2, w % 2
        self.y = lax.axis_index("narrow")

    @staticmethod
    def partner(i, dim, step):
        z, x, c, y = i // 8, (i // 4) % 2, (i // 2) % 2, i % 2
        if dim == "z":
            z ^= step
        elif dim == "core":
            c ^= 1
        elif dim == "y" or (dim == "a") == (c == 1):
            y ^= 1
        else:
            x ^= 1
        return ((z * 2 + x) * 2 + c) * 2 + y

    def swap(self, value, dim, step=1):
        return lax.ppermute(value, AXES, self.pairs[dim, step])

    def tables(self, order, numbered):
        sizes = [self.size[dim] for dim in order]
        number = np.arange(int(np.prod(sizes)))
        rest, digit = number, {}
        for dim, size in zip(order, sizes):
            digit[dim] = rest % size
            rest = rest // size
        first = self.core == 0
        a_here = jnp.where(first, self.x, self.y)
        b_here = jnp.where(first, self.y, self.x)
        if "ring" in digit:
            at = sum(jnp.where(self.z == z, n, 0) for n, z in enumerate(RING))
            z = sum(jnp.where((at - digit["ring"]) % len(RING) == n, z, 0) for n, z in enumerate(RING))
        else:
            z = digit["z"] ^ self.z
        a = digit["a"] ^ a_here
        b = digit["b"] ^ b_here
        x, y = jnp.where(first, a, b), jnp.where(first, b, a)
        return numbered(z, x, y).astype(jnp.int32)


def after(value, *events):
    return lax.optimization_barrier((value,) + events)[0]


def fence(*values):
    return lax.optimization_barrier(values)


def smem():
    return pl.BlockSpec(memory_space=pltpu.SMEM)


def whole(shape):
    zeros = (0,) * len(shape)
    return pl.BlockSpec(tuple(shape), lambda *_: zeros)


def kernel_call(body, grid, ins, outs, scratch=(), flops=0, name=None, room=6):
    blocks = [(v[1].block_shape, v[0].dtype) for v in ins] + [(v[2].block_shape, v[1]) for v in outs]
    held = sum(2 * int(np.prod(shape)) * np.dtype(d).itemsize for shape, d in blocks if shape is not None)
    held += sum(int(np.prod(v.shape)) * np.dtype(v.dtype).itemsize for v in scratch)
    return pl.pallas_call(
        body,
        grid=grid,
        in_specs=[v[1] for v in ins],
        out_specs=[v[2] for v in outs],
        out_shape=[(pltpu.HBM if more else jax.ShapeDtypeStruct)(s, d) for s, d, _, *more in outs],
        scratch_shapes=list(scratch),
        compiler_params=pltpu.CompilerParams(
            dimension_semantics=("arbitrary",) * len(grid), vmem_limit_bytes=held // 2 + room * MIB
        ),
        cost_estimate=pl.CostEstimate(flops=0, bytes_accessed=0, transcendentals=0),
        name=name,
    )(*[pltpu.with_memory_space_constraint(a, pltpu.HBM) if more else a for a, _, *more in ins])


ROWS = 512


def own_rows(steps, cols):
    return pl.BlockSpec((ROWS, cols), lambda i: (jnp.minimum(i, steps - 1), 0))


def partner_rows(steps, cols):
    return pl.BlockSpec((ROWS, cols), lambda i: (jnp.maximum(i - steps, 0), 0))


def pick_rows(i, steps, own_ref, partner_ref):
    return jnp.where(i < steps, own_ref[...], partner_ref[...])


def split_kernel(place, w_qkv, w_out, gains, biases, mine, send):
    first = place[0] == 0
    half = D // 2
    for n in range(4):
        source, start = (w_qkv, n * D) if n < 3 else (w_out, 0)
        low, high = source[:, start : start + half], source[:, start + half : start + D]
        mine[:, n * half : (n + 1) * half] = jnp.where(first, low, high)
        send[:, n * half : (n + 1) * half] = jnp.where(first, high, low)
    rows = jnp.concatenate([gains[...], biases[...]], axis=0).astype(F32)
    eye = jnp.where(
        lax.broadcasted_iota(jnp.int32, (128, rows.shape[0]), 0)
        == lax.broadcasted_iota(jnp.int32, (128, rows.shape[0]), 1),
        1.0,
        0.0,
    )
    norm_cols = contract_cols(rows.T.astype(BF16), eye.astype(BF16)).astype(BF16)
    mine[:, 4 * half :] = norm_cols
    send[:, 4 * half :] = norm_cols


def fill_blocks(table, pieces, weight, cols=slice(None)):
    count = pieces[0].shape[0]
    for n, piece in enumerate(pieces):
        for k in range(count):
            weight[table[n * count + k]] = piece[k, :, cols]


def qkv_kernel(steps, groups, pieces, table, own, partner, *refs):
    i = pl.program_id(0)
    parts = refs[:pieces]
    mixed_own, mixed_partner, weight, out_w, norms, table_t = refs[pieces:]
    cols, part = weight.shape[2], out_w.shape[2]
    tall = weight.shape[0] * weight.shape[1]

    @pl.when(i == 0)
    def _():
        fill_blocks(table, parts, weight, slice(0, cols))
        fill_blocks(table, parts, out_w, slice(cols, cols + part))
        fill_blocks(table, parts, table_t, slice(cols + part, None))
        norms[...] = table_t[...].reshape(tall, table_t.shape[2]).astype(F32).T[: norms.shape[0]]

    rows_here = pick_rows(i, steps, own, partner)
    for g in range(groups):
        span = slice(g * cols // groups, (g + 1) * cols // groups)
        tile = weight[:, :, span].reshape(tall, cols // groups)
        value = dot(rows_here, tile).astype(BF16)

        @pl.when(i < steps)
        def _():
            mixed_own[:, span] = value

        @pl.when(i >= steps)
        def _():
            mixed_partner[:, span] = value


def lane_masks():
    lane = lax.broadcasted_iota(jnp.int32, (1, PAIR), 1)
    return [lane < HEAD_DIM, lane >= HEAD_DIM]


def keep(mask, value):
    return jnp.where(mask, value, jnp.zeros_like(value))


def fill_distance(distance):
    row = lax.broadcasted_iota(jnp.int32, distance.shape, 0)
    col = lax.broadcasted_iota(jnp.int32, distance.shape, 1)
    distance[...] = jnp.abs(row - col).astype(F32)


def scores_of(queries, keys, slope, distance):
    raw = lax.dot_general(queries, keys, (((1,), (1,)), ((), ())), preferred_element_type=F32)
    return raw - slope * distance


def tiles(value, tall):
    return [value[n : n + tall] for n in range(0, value.shape[0], tall)]


def pair_cols(part, pair):
    return pl.ds(pl.multiple_of(part * (D // 2) + pair * PAIR, PAIR), PAIR)


def attend_kernel(place, flags, slopes, mixed, *refs):
    context, logs, distance = refs[-3:]
    masks = lane_masks()
    scale = HEAD_DIM**-0.5
    lane = lax.broadcasted_iota(jnp.int32, (1, 128), 1)
    fill_distance(distance)
    for extra in refs[:-3]:
        context[LONG:, :] = extra[...].reshape(context.shape[0] - LONG, context.shape[1])

    def run(is_long):
        tall = 2 * SHORT if is_long else LONG

        def one_pair(pair, _):
            q_all, k_all, v_all = (mixed[:, pair_cols(part, pair)] for part in range(3))
            totals = [0.0] * (LONG // tall)
            mine = (lambda v: [v]) if is_long else (lambda v: tiles(v, SHORT))
            jobs = []
            for head in range(2):
                slope = slopes[pair * 2 + head]
                q = (keep(masks[head], q_all) * scale).astype(BF16)
                v = keep(masks[head], v_all)
                for n in range(LONG // tall):
                    rows = slice(n * tall, (n + 1) * tall)
                    away = distance[rows, :] if is_long else distance[:SHORT, :SHORT]
                    s = [scores_of(a, b, slope, away) for a, b in zip(mine(q[rows]), mine(k_all))]
                    jobs.append((head, n, jnp.concatenate(s, axis=0), v))
            done = []
            for head, n, s, v in jobs:
                top = jnp.max(s, axis=-1, keepdims=True)
                e = jnp.exp(s - top)
                norm = jnp.sum(e, axis=-1, keepdims=True)
                done.append(((e * (1.0 / norm)).astype(BF16), top + jnp.log(norm)))
            for (head, n, s, v), (p, log) in zip(jobs, done):
                totals[n] = totals[n] + jnp.concatenate([dot(a, b) for a, b in zip(mine(p), mine(v))], axis=0)
                rows = slice(n * tall, (n + 1) * tall)
                logs[rows, :] = jnp.where(lane == pair * 2 + head, log, logs[rows, :])
            for n in range(LONG // tall):
                context[n * tall : (n + 1) * tall, pair_cols(0, pair)] = totals[n].astype(BF16)
            return 0

        lax.fori_loop(0, D // 2 // PAIR, one_pair, 0)

    logs[...] = jnp.zeros_like(logs)
    flag = flags[place[1]]

    @pl.when(flag > 0)
    def _():
        run(True)

    @pl.when(flag <= 0)
    def _():
        run(False)


def attend_back_kernel(place, flags, slopes, mixed, logs_ref, d_context, d_query, d_key, d_value, distance):
    masks = lane_masks()
    scale = HEAD_DIM**-0.5
    fill_distance(distance)

    def run(is_long):
        tall = 2 * SHORT if is_long else LONG
        logs = logs_ref[...]
        lane = lax.broadcasted_iota(jnp.int32, (1, 128), 1)

        def one_pair(pair, _):
            q_all, k_all, v_all = (mixed[:, pair_cols(part, pair)] for part in range(3))
            d_all = d_context[:, pair_cols(0, pair)]
            d_q, d_k, d_v = [0.0] * (LONG // tall), 0.0, 0.0
            group = SHORT if not is_long else tall
            jobs = []
            for head in range(2):
                slope = slopes[pair * 2 + head]
                q = (keep(masks[head], q_all) * scale).astype(BF16)
                k = (keep(masks[head], k_all) * scale).astype(BF16)
                d_c = keep(masks[head], d_all)
                log_all = jnp.sum(jnp.where(lane == pair * 2 + head, logs, 0.0), axis=-1, keepdims=True)
                for n in range(LONG // tall):
                    rows = slice(n * tall, (n + 1) * tall)
                    jobs.append((n, slope, q[rows], k, d_c[rows], log_all[rows], distance[rows, :] if is_long else distance[:SHORT, :SHORT]))
            mine = (lambda v: [v]) if is_long else (lambda v: tiles(v, SHORT))
            raw = []
            for n, slope, q, k, d_c, log_rows, away in jobs:
                s = jnp.concatenate([scores_of(a, b, slope, away) for a, b in zip(mine(q), mine(k_all))], axis=0)
                d_p = jnp.concatenate([contract_cols(a, b) for a, b in zip(mine(d_c), mine(v_all))], axis=0)
                raw.append((s, d_p))
            done = []
            for (n, slope, q, k, d_c, log_rows, away), (s, d_p) in zip(jobs, raw):
                p = jnp.exp(s - log_rows)
                d_s = (p * (d_p - jnp.sum(p * d_p, axis=-1, keepdims=True))).astype(BF16)
                done.append((d_s, p.astype(BF16)))
            for (n, slope, q, k, d_c, log_rows, away), (d_s, p) in zip(jobs, done):
                d_q[n] = d_q[n] + jnp.concatenate([dot(a, b) for a, b in zip(mine(d_s), mine(k))], axis=0)
                d_k = d_k + jnp.concatenate([dot(a.T, b) for a, b in zip(mine(q), mine(d_s))], axis=1)
                d_v = d_v + jnp.concatenate([dot(a.T, b) for a, b in zip(mine(d_c), mine(p))], axis=1)
            cols = pair_cols(0, pair)
            for n in range(LONG // tall):
                d_query[n * tall : (n + 1) * tall, cols] = d_q[n].astype(BF16)
            d_key[:, cols] = d_k.T.astype(BF16)
            d_value[:, cols] = d_v.T.astype(BF16)
            return 0

        lax.fori_loop(0, D // 2 // PAIR, one_pair, 0)

    flag = flags[place[1]]

    @pl.when(flag > 0)
    def _():
        run(True)

    @pl.when(flag <= 0)
    def _():
        run(False)


def spread(rows):
    center = jnp.mean(rows, axis=-1, keepdims=True)
    shifted = rows - center
    inverse = lax.rsqrt(jnp.mean(shifted * shifted, axis=-1, keepdims=True) + 1e-05)
    return shifted * inverse, inverse


def norm_back(e, unit, inverse):
    mean_e = jnp.mean(e, axis=-1, keepdims=True)
    mean_en = jnp.mean(e * unit, axis=-1, keepdims=True)
    return (e - mean_e - unit * mean_en) * inverse


def first_norm_kernel(place, tokens, ctx_mine, ctx_other, w_mine, w_other_rows, norms, unit, inverse, low):
    core = place[0]
    half = w_mine.shape[0] // 2
    wide = w_mine.shape[2]

    def branch(weight):
        return dot(ctx_mine[...], weight(core)) + dot(ctx_other[...], weight(1 - core))

    mine = branch(lambda c: w_mine[pl.ds(c * half, half)].reshape(D // 2, wide))
    other = branch(lambda c: w_other_rows[pl.ds(pl.multiple_of(LONG + c * (D // 2), 128), D // 2), :])
    first = core == 0
    added = jnp.concatenate([jnp.where(first, mine, other), jnp.where(first, other, mine)], axis=1)
    n, inv = spread(tokens[...].astype(F32) + added)
    unit[...] = n
    inverse[...] = inv
    low[...] = (n * norms[0:1, :] + norms[2:3, :]).astype(BF16)


def gelu_parts(x):
    phi = 0.5 + 0.5 * lax.erf(x * 0.5**0.5)
    return x * phi, phi + x * jnp.exp(-0.5 * (x * x)) * 0.3989422804014327


def columns_of(weight, half, span):
    count = weight.shape[0] // 2
    return weight[half * count : (half + 1) * count, :, span].reshape(D, span.stop - span.start)


def gate_kernel(steps, pieces, table, own, partner, *refs):
    i = pl.program_id(0)
    active, slope, gate_w = refs[pieces:]

    @pl.when(i == 0)
    def _():
        fill_blocks(table, refs[:pieces], gate_w)

    rows = pick_rows(i, steps, own, partner)
    width = gate_w.shape[2]
    for half in range(2):
        for start in range(0, width, 256):
            out = slice(half * width + start, half * width + start + 256)
            gate = dot(rows, columns_of(gate_w, half, slice(start, start + 256)))
            act, grad = gelu_parts(gate)
            active[:, out] = act.astype(BF16)
            slope[:, out] = grad.astype(BF16)


def value_kernel(steps, pieces, table, own, partner, active, slope, *refs):
    i = pl.program_id(0)
    product, scaled, value_w = refs[pieces:]

    @pl.when(i == 0)
    def _():
        fill_blocks(table, refs[:pieces], value_w)

    rows = pick_rows(i, steps, own, partner)
    width = value_w.shape[2]
    for half in range(2):
        for start in range(0, width, 256):
            out = slice(half * width + start, half * width + start + 256)
            up = dot(rows, columns_of(value_w, half, slice(start, start + 256)))
            product[:, out] = (active[:, out].astype(F32) * up).astype(BF16)
            scaled[:, out] = (slope[:, out].astype(F32) * up).astype(BF16)


def times_down(product, down_w):
    width = down_w.shape[2]
    total = 0.0
    for half in range(2):
        part = product[:, half * width : (half + 1) * width]
        total = total + contract_cols(part, columns_of(down_w, half, slice(0, width)))
    return total


def down_first_kernel(table, product, *refs):
    partner, down_w = refs[-2:]

    @pl.when(pl.program_id(0) == 0)
    def _():
        fill_blocks(table, refs[:-2], down_w)

    partner[...] = times_down(product, down_w).astype(BF16)


def down_kernel(product, down_w, own):
    own[...] = times_down(product, down_w)


def second_norm_kernel(unit_one, norms, part_own, part_got, cotangent, out, d_z, d_ffn, sums):
    normed = unit_one[...] * norms[0:1, :] + norms[2:3, :]
    n, inv = spread(normed + (part_own[...] + part_got[...].astype(F32)))
    gain = norms[1:2, :]
    out[...] = (n * gain + norms[3:4, :]).astype(BF16)
    c = cotangent[...].astype(F32)
    back = norm_back(gain * c, n, inv)
    d_z[...] = back
    d_ffn[...] = back.astype(BF16)
    add_sums(sums, c * n, c)


def add_sums(sums, gain_terms, bias_terms):
    @pl.when(pl.program_id(0) == 0)
    def _():
        sums[...] = jnp.zeros_like(sums)

    sums[0:1, :] += jnp.sum(gain_terms, axis=0, keepdims=True)
    sums[1:2, :] += jnp.sum(bias_terms, axis=0, keepdims=True)


def ffn_back_kernel(
    steps, own, partner, down_w, gate_w, value_w, active, slope, d_gate, d_up, back_own, back_partner
):
    i = pl.program_id(0)
    rows = pick_rows(i, steps, own, partner)
    width = down_w.shape[2]
    for half in range(2):
        for start in range(0, width, 256):
            span = slice(start, start + 256)
            out = slice(half * width + start, half * width + start + 256)
            d_product = dot(rows, columns_of(down_w, half, span))
            d_gate[:, out] = (d_product * slope[:, out].astype(F32)).astype(BF16)
            d_up[:, out] = (d_product * active[:, out].astype(F32)).astype(BF16)
    total = 0.0
    for half in range(2):
        out = slice(half * width, (half + 1) * width)
        span = slice(0, width)
        total = total + contract_cols(d_gate[:, out], columns_of(gate_w, half, span))
        total = total + contract_cols(d_up[:, out], columns_of(value_w, half, span))

    @pl.when(i < steps)
    def _():
        back_own[...] = total

    @pl.when(i >= steps)
    def _():
        back_partner[...] = total.astype(BF16)


def weight_grad_kernel(table, left_own, left_partner, right_a, right_b, *refs):
    i = pl.program_id(0)
    parts, blocks = refs[:-1], refs[-1]
    rows = left_own.shape[0]
    count, tall, cols = blocks.shape
    for half, right in enumerate((right_a, right_b)):
        value = contract_rows(left_own[...], right[:rows, :]) + contract_rows(left_partner[...], right[rows:, :])
        value = value.astype(BF16).reshape(count // 2, tall, cols)
        blocks[half * (count // 2) : (half + 1) * (count // 2)] = value
    span = pl.ds(pl.multiple_of(i * cols, cols), cols)
    each = count // len(parts)
    for k in range(count):
        parts[k // each][k % each, :, span] = blocks[table[k]]


def first_norm_back_kernel(
    place,
    unit_ref,
    inverse,
    norms,
    d_z,
    part_own,
    part_got,
    ctx_mine,
    ctx_other,
    w_mine,
    w_other,
    d_hidden,
    dctx_mine,
    dctx_other,
    grad_keep,
    grad_send,
    sums,
    grad,
):
    core = place[0]
    first = core == 0
    unit = unit_ref[...]
    d_normed = d_z[...] + (part_own[...] + part_got[...].astype(F32))
    back = norm_back(norms[0:1, :] * d_normed, unit, inverse[...])
    low = back.astype(BF16)
    d_hidden[...] = back
    add_sums(sums, d_normed * unit, d_normed)
    half, wide = w_mine.shape[0] // 2, w_mine.shape[2]
    low_mine = jnp.where(first, low[:, :wide], low[:, wide:])
    low_other = jnp.where(first, low[:, wide:], low[:, :wide])
    for head_core, out in ((core, dctx_mine), (1 - core, dctx_other)):
        near = w_mine[pl.ds(head_core * half, half)].reshape(D // 2, wide)
        far = w_other[pl.ds(pl.multiple_of(LONG + head_core * (D // 2), 128), D // 2), :]
        out[...] = (contract_cols(low_mine, near) + contract_cols(low_other, far)).astype(BF16)

    @pl.when(pl.program_id(0) == 0)
    def _():
        grad[...] = jnp.zeros_like(grad)

    shape = (half,) + grad.shape[1:]
    grad[pl.ds(core * half, half)] += contract_rows(ctx_mine[...], low).reshape(shape)
    grad[pl.ds((1 - core) * half, half)] += contract_rows(ctx_other[...], low).reshape(shape)

    @pl.when(pl.program_id(0) == pl.num_programs(0) - 1)
    def _():
        left, right = grad[:, :, :wide], grad[:, :, wide:]
        grad_keep[...] = jnp.where(first, left, right)
        grad_send[...] = jnp.where(first, right, left).astype(BF16)


def qkv_grad_kernel(table, left_own, left_partner, *refs):
    d_own, d_partner = refs[:3], refs[3:6]
    out_grad, sums_one, sums_two, near, far, blocks, norm_grad = refs[6:]
    i = pl.program_id(0)
    count, tall, cols = blocks.shape

    @pl.when(i == 0)
    def _():
        one, two = sums_one[...], sums_two[...]
        empty = jnp.zeros((norm_grad.shape[2] - 4, D), F32)
        stacked = jnp.concatenate([one[0:1], two[0:1], one[1:2], two[1:2], empty], axis=0)
        norm_grad[...] = stacked.T.astype(BF16).reshape(norm_grad.shape)

    for g in range(3):

        @pl.when(i == g)
        def _():
            value = contract_rows(left_own[...], d_own[g][...]) + contract_rows(left_partner[...], d_partner[g][...])
            blocks[...] = value.astype(BF16).reshape(blocks.shape)
            for k in range(count):
                target, place = (near if k < count // 2 else far), table[k]
                target[k % (count // 2), :, g * cols : (g + 1) * cols] = blocks[place]
                if g == 0:
                    start = 3 * cols
                    for more in (out_grad, norm_grad):
                        stop = start + more.shape[2]
                        target[k % (count // 2), :, start:stop] = more[place]
                        start = stop


def input_grad_kernel(d_query, d_key, d_value, weight, *refs):
    cols = d_query.shape[1]
    total = 0.0
    for g, left in enumerate((d_query, d_key, d_value)):
        tile = weight[:, :, g * cols : (g + 1) * cols].reshape(D, cols)
        total = total + contract_cols(left[...], tile)
    for more in refs[:-1]:
        total = total + more[...].astype(F32)
    refs[-1][...] = total.astype(refs[-1].dtype)


def pieces_kernel(place, here, there, got, qkv, out, gains, biases):
    first, own = place[0] == 0, place[1] == 1
    half = D // 2
    mine = jnp.where(own, here[...], there[...])
    for n in range(4):
        a, b = mine[:, n * half : (n + 1) * half].astype(F32), got[:, n * half : (n + 1) * half].astype(F32)
        target, start = (qkv, n * D) if n < 3 else (out, 0)
        target[:, start : start + half] = jnp.where(first, a, b)
        target[:, start + half : start + D] = jnp.where(first, b, a)
    rows = (mine[:, 4 * half :].astype(F32) + got[:, 4 * half :].astype(F32)).T
    gains[...] = rows[0:2]
    biases[...] = rows[2:4]


def by_core(core, mine, other, axis):
    first = core == 0
    return jnp.stack([jnp.where(first, mine, other), jnp.where(first, other, mine)], axis=axis)


def half_of(core, halves, axis):
    zero, one = (lax.index_in_dim(halves, k, axis, keepdims=False) for k in range(2))
    first = core == 0
    return jnp.where(first, zero, one), jnp.where(first, one, zero)


def plane_shards(
    wide,
    narrow,
    tokens,
    w_qkv,
    w_out,
    w_gate,
    w_value,
    w_down,
    norm_gains,
    norm_biases,
    long_count,
    cotangent,
):
    plane = Plane(wide, narrow)
    swap = plane.swap
    core, y_here = plane.core, plane.y
    rows = tokens.shape[0]
    steps = rows // ROWS
    tall = w_qkv.shape[0]
    blocks = wide * narrow // 2
    z_size = plane.size["z"]
    head_cols = D // 2
    width = w_gate.shape[1] // 2
    hidden = 2 * width
    pairs = head_cols // PAIR
    qkv_to = plane.tables(("z", "a", "b"), lambda z, x, y: (z * 2 + x) * 2 + y)
    ffn_to = plane.tables(("z", "a", "b"), lambda z, x, y: y * (2 * z_size) + z * 2 + x)
    back_to = plane.tables(("a", "z", "b"), lambda z, x, y: y * (2 * z_size) + z * 2 + x)
    down_to = plane.tables(("a", "b", "ring"), lambda z, x, y: y * (2 * z_size) + z * 2 + x)
    place = jnp.reshape(core, (1,)).astype(jnp.int32)
    first = core == 0

    def wholes(arrays):
        return [(v, whole(v.shape)) for v in arrays]

    def far(entries):
        return [entry + (True,) for entry in entries]

    def step_rows(cols):
        return pl.BlockSpec((ROWS, cols), lambda i: (i, 0))

    head_shape = (tall, 4 * head_cols + 128)
    head_part, head_send = kernel_call(
        split_kernel,
        (1,),
        [(place, smem())] + far(wholes([w_qkv, w_out, norm_gains, norm_biases])),
        [(head_shape, BF16, whole(head_shape))] * 2,
        name="split",
    )
    flag = jnp.broadcast_to(long_count.astype(F32), (8, 128))
    head_got, flag_got = fence(swap(head_send, "core"), swap(flag, "core"))
    head_part = jnp.where(y_here == core, head_part, head_got)
    head_parts = [head_part] + [swap(head_part, "z", k) for k in range(1, z_size)]
    ffn_parts = [after(w_gate, head_part), w_value, w_down.T]
    ffn_other = jnp.concatenate([jnp.where(first, v[:, width:], v[:, :width]) for v in ffn_parts], axis=1)
    ffn_got = swap(ffn_other, "core")
    flags = jnp.stack([long_count[0, 0], flag_got[0, 0].astype(jnp.int32)])
    slopes = lax.dynamic_slice_in_dim(alibi_slopes(HEADS), core * (HEADS // 2), HEADS // 2)

    def ffn_chip(n):
        v, got = ffn_parts[n], ffn_got[:, n * width : (n + 1) * width]
        mine = jnp.where(first, v[:, :width], v[:, width:])
        return jnp.concatenate([jnp.where(first, mine, got), jnp.where(first, got, mine)], axis=0)

    def doubled(value, step, *events):
        got = swap(value, "z", step)
        return jnp.concatenate(lax.optimization_barrier((value, got) + events)[:2], axis=0)

    def along_plane(held):
        near = swap(held, "a")
        return held, near, swap(held, "b")

    def joined(value, got):
        return jnp.concatenate([value, got], axis=0)

    gate_one, value_one, down_one = (ffn_chip(n)[None] for n in range(3))
    gate_got = swap(gate_one, "z", 1)
    down_got = swap(down_one, "a")
    *head_parts, gate_got, down_got = fence(*head_parts, gate_got, down_got)
    qkv_z = jnp.stack(head_parts)
    gate_two, down_two = joined(gate_one, gate_got), joined(down_one, down_got)

    head_near, head_far = swap(qkv_z, "a"), swap(qkv_z, "b")
    gate_got = swap(gate_two, "z", 2)
    value_got = swap(after(value_one, qkv_z), "z", 1)
    tokens_other = swap(after(tokens, qkv_z), "core")
    head_near, head_far, gate_got, value_got, tokens_other = fence(head_near, head_far, gate_got, value_got, tokens_other)
    gate_z, value_two = joined(gate_two, gate_got), joined(value_one, value_got)

    head_last = swap(head_near, "b")
    down_got = swap(after(down_two, head_near), "b")
    gate_near = swap(gate_z, "a")
    value_got = swap(value_two, "z", 2)
    head_last, down_got, gate_near, value_got = fence(head_last, down_got, gate_near, value_got)
    value_z, down_four = joined(value_two, value_got), joined(down_two, down_got)
    qkv_blocks = [qkv_z, head_near, head_far, head_last]

    gate_far, gate_last = swap(after(gate_z, head_last), "b"), swap(gate_near, "b")
    ring_one = swap(down_four, "next")
    block_row = (blocks, tall)
    mixed_own, mixed_partner, qkv_w, out_mine, norms = kernel_call(
        functools.partial(qkv_kernel, steps, 3, len(qkv_blocks)),
        (2 * steps,),
        [(qkv_to, smem())]
        + far([(tokens, own_rows(steps, D)), (tokens_other, partner_rows(steps, D))])
        + wholes(qkv_blocks[:1])
        + far(wholes(qkv_blocks[1:])),
        far(
            [((rows, 3 * head_cols), BF16, own_rows(steps, 3 * head_cols))]
            + [((rows, 3 * head_cols), BF16, partner_rows(steps, 3 * head_cols))]
            + [(block_row + (n,), BF16, whole(block_row + (n,))) for n in (3 * head_cols, head_cols)]
        )
        + [((8, D), F32, whole((8, D)))],
        scratch=[pltpu.VMEM(block_row + (128,), BF16)],
        flops=2 * 2 * rows * D * 3 * head_cols,
        name="mixed",
    )
    def attend(block, mixed, extra=()):
        tall_out = rows + sum(v.size for v in extra) // head_cols
        return kernel_call(
            attend_kernel,
            (1,),
            [(jnp.array([0, block], jnp.int32), smem()), (flags, smem()), (slopes, smem())]
            + far(wholes([mixed, *extra])),
            [((tall_out, head_cols), BF16, whole((tall_out, head_cols))), ((rows, 128), F32, whole((rows, 128)), True)],
            scratch=[pltpu.VMEM((LONG, LONG), F32)],
            flops=4 * rows * LONG * D,
            name="attend",
            room=12,
        )

    ctx_send, logs_partner = attend(1, mixed_partner, [out_mine])
    gate_far, gate_last, ring_one, ctx_send = fence(gate_far, gate_last, ring_one, ctx_send)

    value_near, value_far = swap(value_z, "a"), swap(value_z, "b")
    ring_two = swap(ring_one, "next")
    ctx_got = swap(ctx_send, "core")
    ctx_mine, logs_own = attend(0, after(mixed_own, ctx_send))

    unit_one, inverse_one, low = kernel_call(
        first_norm_kernel,
        (steps,),
        [
            (place, smem()),
            (tokens, step_rows(D)),
            (ctx_mine, step_rows(head_cols)),
            (ctx_got, step_rows(head_cols)),
        ]
        + wholes([out_mine, ctx_got, norms]),
        [
            ((rows, D), F32, step_rows(D)),
            ((rows, 1), F32, step_rows(1)),
            ((rows, D), BF16, step_rows(D)),
        ],
        flops=2 * rows * D * D,
        name="first_norm",
    )
    value_near, low = fence(value_near, low)
    gate_blocks = [gate_z, gate_near, gate_far, gate_last]
    value_last = swap(value_near, "b")
    ring_three = swap(ring_two, "next")
    low_other = swap(low, "core")

    w_shape = (blocks, 2 * tall, width)
    both_rows = [(low, own_rows(steps, D)), (low_other, partner_rows(steps, D))]
    active, slope, gate_w = kernel_call(
        functools.partial(gate_kernel, steps, len(gate_blocks)),
        (2 * steps,),
        [(ffn_to, smem())] + both_rows + far(wholes(gate_blocks)),
        [((2 * rows, hidden), BF16, step_rows(hidden))] * 2 + [(w_shape, BF16, whole(w_shape))],
        name="gate",
    )
    value_last, active = fence(value_last, active)
    value_blocks = [value_z, value_near, value_far, value_last]
    down_blocks = [down_four, ring_one, ring_two, ring_three]
    product, slope, value_w = kernel_call(
        functools.partial(value_kernel, steps, len(value_blocks)),
        (2 * steps,),
        [(ffn_to, smem())] + both_rows + [(active, step_rows(hidden)), (slope, step_rows(hidden))] + wholes(value_blocks),
        [((2 * rows, hidden), BF16, step_rows(hidden))] * 2 + [(w_shape, BF16, whole(w_shape))],
        name="value",
    )
    part_send, down_w = kernel_call(
        down_first_kernel,
        (steps,),
        [(down_to, smem()), (product, pl.BlockSpec((ROWS, hidden), lambda i: (i + steps, 0)))] + wholes(down_blocks),
        [((rows, D), BF16, step_rows(D)), (w_shape, BF16, whole(w_shape))],
        name="down_first",
    )
    (part_own,) = kernel_call(
        down_kernel,
        (steps,),
        [(product, step_rows(hidden))] + wholes([down_w]),
        [((rows, D), F32, step_rows(D))],
        name="down",
    )
    part_got = swap(part_send, "core")
    layer_out, d_z, d_ffn, sums_two = kernel_call(
        second_norm_kernel,
        (steps,),
        [(unit_one, step_rows(D))]
        + wholes([norms])
        + [(part_own, step_rows(D)), (part_got, step_rows(D)), (cotangent, step_rows(D))],
        [
            ((rows, D), BF16, step_rows(D)),
            ((rows, D), F32, step_rows(D)),
            ((rows, D), BF16, step_rows(D)),
            ((8, D), F32, whole((8, D))),
        ],
        name="second_norm",
    )
    d_ffn_other = swap(d_ffn, "core")

    def weight_grad(left, left_other, right, to, parts):
        part = (blocks // parts, 2 * tall, width)
        cols = width // 3
        return kernel_call(
            weight_grad_kernel,
            (3,),
            [
                (to, smem()),
                (left, whole((rows, D))),
                (left_other, whole((rows, D))),
                (right, pl.BlockSpec((2 * rows, cols), lambda i: (0, i))),
                (right, pl.BlockSpec((2 * rows, cols), lambda i: (0, 3 + i))),
            ],
            [(part, BF16, whole(part))] * parts,
            scratch=[pltpu.VMEM((blocks, 2 * tall, cols), BF16)],
            flops=2 * 2 * rows * D * hidden,
            name="weight_grad",
        )

    def added(keep, got):
        return (keep.astype(F32) + got.astype(F32)).astype(BF16)

    def halves(keep, got):
        count = keep.shape[0] // 2
        return added(keep[:count], got[:count]), added(keep[count:], got[count:])

    def quarters(keep, got):
        return [added(keep[k], got[k]) for k in range(z_size)]

    down_parts = weight_grad(d_ffn, d_ffn_other, product, back_to, 2)
    d_gate, d_up, back_own, back_send = kernel_call(
        functools.partial(ffn_back_kernel, steps),
        (2 * steps,),
        [(after(d_ffn, down_parts[-1]), own_rows(steps, D)), (d_ffn_other, partner_rows(steps, D))]
        + wholes([down_w, gate_w, value_w])
        + [(active, step_rows(hidden)), (slope, step_rows(hidden))],
        [((2 * rows, hidden), BF16, step_rows(hidden))] * 2
        + [((rows, D), F32, own_rows(steps, D)), ((rows, D), BF16, partner_rows(steps, D))],
        flops=3 * 2 * 2 * rows * D * hidden,
        name="ffn_back",
    )
    down_got = swap(down_parts[1], "b")
    gate_keep, gate_send = weight_grad(after(low, back_send), low_other, d_gate, ffn_to, 2)
    back_send, gate_send = fence(back_send, gate_send)

    gate_got = swap(gate_send, "b")
    down_z = [added(down_parts[0][2 * k : 2 * k + 2], down_got[2 * k : 2 * k + 2]) for k in range(z_size)]
    down_got = swap(down_z[3], "z", 2)
    back_got = swap(back_send, "core")
    value_keep, value_send = weight_grad(after(low, gate_send), low_other, d_up, ffn_to, 2)
    value_got = swap(value_send, "b")
    back_got = after(back_got, value_send)
    d_hidden, dctx_mine, dctx_send, out_keep, out_send, sums_one = kernel_call(
        first_norm_back_kernel,
        (steps,),
        [
            (place, smem()),
            (unit_one, step_rows(D)),
            (inverse_one, step_rows(1)),
            (norms, whole(norms.shape)),
            (d_z, step_rows(D)),
            (back_own, step_rows(D)),
            (back_got, step_rows(D)),
            (ctx_mine, step_rows(head_cols)),
            (ctx_got, step_rows(head_cols)),
        ]
        + wholes([out_mine, ctx_got]),
        [
            ((rows, D), F32, step_rows(D)),
            ((rows, head_cols), BF16, step_rows(head_cols)),
            ((rows, head_cols), BF16, step_rows(head_cols)),
            (out_mine.shape, F32, whole(out_mine.shape)),
            (out_mine.shape, BF16, whole(out_mine.shape)),
            ((8, D), F32, whole((8, D))),
        ],
        scratch=[pltpu.VMEM((blocks, tall, D), F32)],
        flops=2 * 2 * rows * D * D,
        name="first_norm_back",
    )
    def attend_back(block, mixed, d_context, logs):
        return kernel_call(
            attend_back_kernel,
            (1,),
            [(jnp.array([0, block], jnp.int32), smem()), (flags, smem()), (slopes, smem())]
            + far(wholes([mixed, logs]))
            + wholes([d_context]),
            [((rows, head_cols), BF16, whole((rows, head_cols)))] * 3,
            scratch=[pltpu.VMEM((LONG, LONG), F32)],
            name="attend_back",
            room=16,
        )

    d_own = attend_back(0, mixed_own, dctx_mine, logs_own)
    down_got, dctx_send, out_send, d_first = fence(down_got, dctx_send, out_send, d_own[0])
    d_own = [d_first, *d_own[1:]]
    dctx_got, out_got = swap(dctx_send, "core"), swap(out_send, "core")
    gate_keep, gate_send = halves(gate_keep, gate_got)
    down_send = added(down_z[1], down_got)
    gate_got = swap(gate_send, "a")
    down_got = swap(after(down_z[2], gate_send), "z", 2)
    out_sum = (out_keep + out_got.astype(F32)).astype(BF16)

    d_partner = attend_back(1, mixed_partner, after(dctx_got, gate_send, down_send), logs_partner)
    grad_shape = (blocks // 2, tall, 4 * head_cols + 128)
    head_keep, head_send = kernel_call(
        qkv_grad_kernel,
        (3,),
        [(qkv_to, smem())]
        + wholes([tokens, tokens_other, *d_own, *d_partner, out_sum, sums_one, sums_two]),
        [(grad_shape, BF16, whole(grad_shape))] * 2,
        scratch=[pltpu.VMEM(block_row + (head_cols,), BF16), pltpu.VMEM(block_row + (128,), BF16)],
        name="qkv_grad",
    )
    down_got, gate_got, head_send = fence(down_got, gate_got, head_send)
    head_got = swap(head_send, "b")
    gate_keep, gate_send = halves(gate_keep, gate_got)
    value_keep, value_send = halves(value_keep, value_got)

    value_got = swap(value_send, "a")
    gate_got = swap(gate_send, "z", 2)
    down_keep = added(down_z[0], down_got)
    down_got = swap(down_send, "z", 1)

    def input_part(d_parts, more, dtype):
        return kernel_call(
            input_grad_kernel,
            (steps,),
            [(v, step_rows(head_cols)) for v in d_parts] + wholes([qkv_w]) + [(v, step_rows(D)) for v in more],
            [((rows, D), dtype, step_rows(D))],
            name="input_grad",
        )[0]

    in_send = input_part([after(d_partner[0], value_send, gate_send), *d_partner[1:]], [], BF16)
    head_got, gate_got, down_got, in_send = fence(head_got, gate_got, down_got, in_send)
    head_keep, head_send = halves(head_keep, head_got)
    value_keep, value_send = halves(value_keep, value_got)
    gate_keep, gate_send = halves(gate_keep, gate_got)
    down_keep, down_send = halves(down_keep, down_got)

    in_got = swap(in_send, "core")
    gate_got = swap(gate_send, "z", 1)
    down_got = swap(down_send, "a")
    head_got = swap(head_send, "a")
    value_got = swap(value_send, "z", 2)
    input_grad = input_part([after(d_own[0], head_send, value_send), *d_own[1:]], [d_hidden, in_got], F32)
    head_got, input_grad = fence(head_got, input_grad)
    head_parts = quarters(head_keep, head_got)
    value_got = after(value_got, *head_parts)
    value_keep, value_send = halves(value_keep, value_got)
    value_got = swap(value_send, "z", 1)

    head_got = [swap(head_parts[k], "z", k) for k in range(1, z_size)]
    value_got, gate_got, down_got, *head_got = fence(value_got, gate_got, down_got, *head_got)
    head_sum = head_parts[0].astype(F32)
    for part in head_got:
        head_sum = head_sum + part.astype(F32)
    head_sum = head_sum.astype(BF16)
    there = swap(head_sum, "y")
    gate_sum = added(gate_keep[0], gate_got[0])
    grads = [gate_sum, added(value_keep[0], value_got[0]), added(down_keep[0], down_got[0])]

    def in_order(mine, other):
        return [jnp.where(first, mine, other), jnp.where(first, other, mine)]

    kept = [half_of(core, total.reshape(2, tall, width), 0) for total in grads]
    ffn_got = swap(jnp.concatenate([other for _, other in kept], axis=0), "core")
    ffn_pieces = [
        jnp.concatenate(in_order(mine, ffn_got[n * tall : (n + 1) * tall]), axis=1).astype(F32)
        for n, (mine, _) in enumerate(kept)
    ]
    gate_piece, value_piece, down_piece = ffn_pieces[0], ffn_pieces[1], ffn_pieces[2].T
    there = after(there, gate_piece, value_piece, down_piece)
    own = y_here == core
    got = swap(jnp.where(own, there, head_sum), "core")
    qkv_piece, out_piece, gains_piece, biases_piece = kernel_call(
        pieces_kernel,
        (1,),
        [(jnp.stack([core, own.astype(jnp.int32)]), smem())] + wholes([head_sum, there, got]),
        [((tall, 3 * D), F32, whole((tall, 3 * D))), ((tall, D), F32, whole((tall, D)))]
        + [((2, tall), F32, whole((2, tall)))] * 2,
        name="pieces",
    )
    return (
        layer_out,
        input_grad,
        qkv_piece,
        out_piece,
        gate_piece,
        value_piece,
        down_piece,
        gains_piece,
        biases_piece,
    )


def solution(mesh):
    wide, narrow = mesh.shape["wide"], mesh.shape["narrow"]
    placed = (
        P(("wide", "narrow"), None),
        P("wide", None),
        P("wide", None),
        P("wide", "narrow"),
        P("wide", "narrow"),
        P("narrow", "wide"),
        P(None, "wide"),
        P(None, "wide"),
        P("wide", "narrow"),
        P(("wide", "narrow"), None),
    )
    if narrow == 2 and wide % 16 == 0 and D % (16 * wide) == 0:
        body = functools.partial(plane_shards, wide, narrow)
    else:
        body = general_shards
    return jax.shard_map(
        body,
        mesh=mesh,
        in_specs=placed,
        out_specs=(
            P(("wide", "narrow"), None),
            P(("wide", "narrow"), None),
            P("wide", None),
            P("wide", None),
            P("wide", "narrow"),
            P("wide", "narrow"),
            P("narrow", "wide"),
            P(None, "wide"),
            P(None, "wide"),
        ),
        check_vma=False,
    )
```
